32 devices in a mesh: shots: 2 (over y), track: 8 (over z, x), depth: 2 (over core).
Axes of the slice: x: 2, y: 2, z: 4, core: 2. Of those that a mesh axis runs over, the one named last changes fastest.
Arguments:
- velocity: float32 [4, 512, 512], P('shots', 'track', 'depth'), parts along dimension 0, may hold values from -6 to 6
- stress: float32 [6, 512, 512], P('shots', 'track', 'depth'), parts along dimension 0, may hold values from -6 to 6
- adjoint_velocity: float32 [4, 512, 512], P('shots', 'track', 'depth'), parts along dimension 0, may hold values from -6 to 6
- adjoint_stress: float32 [6, 512, 512], P('shots', 'track', 'depth'), parts along dimension 0, may hold values from -6 to 6
- buoyancy: float32 [512, 512], P('track', 'depth'), may hold values from 0.3 to 0.8
- lame_lambda: float32 [512, 512], P('track', 'depth'), may hold values from 0.05 to 0.2
- shear_modulus: float32 [512, 512], P('track', 'depth'), may hold values from 0.05 to 0.2
- observed: float32 [8, 2048], P('shots', 'track'), parts along dimension 0, may hold values from -6 to 6
- owner_track: int32 [2048, 1], P('track'), may hold values from 0 to 7; in each aligned block of 256 rows (0 to 255, 256 to 511, ...) at most 64 rows name the same one
- fibre_cell: int32 [2048], P('track'), may hold values from 0 to 255
Outputs:
- gradient_lambda: float32 [1024, 512], P(('shots', 'track'), 'depth'), parts along dimension 0
- gradient_mu: float32 [1024, 512], P(('shots', 'track'), 'depth'), parts along dimension 0
- velocity_end: float32 [4, 512, 512], P('shots', 'track', 'depth'), parts along dimension 0
- residual_traces: float32 [8, 2048], P(('shots', 'depth'), 'track'), parts along dimension 0
The draws below stay inside these ranges and needn't reach their ends.
There are 2 independent parts, one for each index of `shots`. The reference program is written for one: setup_inputs(seed, part) draws one part's arguments, and reference() takes and returns one part's arrays. A program takes and returns all parts, laid end to end along the dimension named above; an argument that names none is the same for every part. Nothing has to cross between parts.
Inputs may be any that keep to these rules, and one draw needn't show every extreme that they name: `owner_track`: among the channels of one index of track, no slab is named by more than 64 of them, a bound that some block reaches.
All inputs are finite; a program needn't handle non-finite values.
Results may differ from the reference program's by a relative error of at most 0.00002.
Values sent between devices are 32-bit elements; how exact they have to be, the bound alone decides.
No kernel may reach another device: no remote copies, remote signals or barrier semaphores. Data moves between devices by JAX's collectives and lax.ppermute only.
A program may use at most 64 MiB of HBM per device.

```python
import math
import jax
import jax.numpy as jnp
import numpy as np
from jax import lax

CX = 64
CH_DEV = 256
NT = 4
FIBRE_ROWS = 4
NX = 512
NZ = 512
NCH = 2048
CAP = 64
N_TRACK = 8


def set_ends(values, own_key, low, high):
    index_at = [jax.random.randint(jax.random.fold_in(own_key, axis), (), 0, length) for axis, length in enumerate(values.shape)]
    longest = values.shape.index(max(values.shape))
    beside = index_at[:longest] + [(index_at[longest] + 1) % values.shape[longest]] + index_at[longest + 1:]
    return values.at[tuple(index_at)].set(low).at[tuple(beside)].set(high)


def level_of(own_key, dims, cuts, low, largest):
    gain, own = 1.0, jax.random.fold_in(own_key, 6)
    for dim, shards_of in cuts:
        steps = jnp.exp(jax.random.uniform(jax.random.fold_in(own, dim), (shards_of,), jnp.float32, low / len(cuts), largest / len(cuts)))
        gain = gain * jnp.repeat(steps, dims[dim] // shards_of).reshape([-1 if axis == dim else 1 for axis in range(len(dims))])
    return gain


def assign_block(key, own, number, rows, number_of, top, reach, slope):
    sequence = jax.random.permutation(key, number_of)
    heavy_load, common = shares(number_of, rows * top, reach, slope, True), shares(number_of, rows * top, reach, slope, False)
    places = jnp.arange(number_of)

    def named(tallies, offset_by):
        used = int((tallies > 0).sum())
        fixed = max(1, used // 4)
        passed = fixed + (places - fixed + offset_by * (used - fixed)) % max(1, number_of - fixed)
        return jnp.zeros((number_of,), jnp.int32).at[sequence[jnp.where(places < fixed, places, passed)]].set(jnp.asarray(tallies, jnp.int32))

    tallies = jnp.where(number % 4 == 0, named(heavy_load, number // 4), named(common, number - number // 4 - 1))
    mixed = jax.random.permutation(jax.random.fold_in(own, 3), number_of)
    source_of, taker = mixed[0:number_of // 2 * 2:2], mixed[1:number_of // 2 * 2:2]
    margin = jnp.minimum(tallies[source_of] - 1, reach - tallies[taker]) // 2
    margin = jnp.where((source_of == sequence[0]) | (taker == sequence[0]) | (tallies[taker] == 0), 0, jnp.maximum(margin, 0))
    passed = jax.random.randint(jax.random.fold_in(own, 4), (number_of // 2,), 0, 1 << 20) % (margin + 1)
    tallies = tallies.at[source_of].add(-passed).at[taker].add(passed)
    labels = jnp.searchsorted(jnp.cumsum(tallies), jnp.arange(rows * top), side="right").astype(jnp.int32)
    table = labels.reshape(top, rows).T
    table = table[jax.random.permutation(jax.random.fold_in(own, 1), rows)]
    offset_by = jax.random.randint(jax.random.fold_in(own, 2), (rows, 1), 0, top)
    return jnp.take_along_axis(table, (jnp.arange(top)[None, :] + offset_by) % top, axis=1)


def shares(number_of, total, limit, skew, full):
    weights = [(1 << 20) // math.isqrt(rank ** skew) + 1 for rank in range(1, number_of + 1)]
    largest = limit if full else min(limit, max(-(-total // number_of), total * weights[0] // sum(weights)))
    least = 1 if total - largest >= number_of - 1 else 0
    holding, spare = [largest] + [least] * (number_of - 1), total - largest - least * (number_of - 1)
    while spare > 0:
        movable = [i for i in range(1, number_of) if holding[i] < largest] or [i for i in range(1, number_of) if holding[i] < limit]
        whole, left = sum([weights[i] for i in movable]), spare
        for i in movable:
            more = min(limit - holding[i], max(1, left * weights[i] // whole), spare)
            holding[i] = holding[i] + more
            spare = spare - more
    return np.array(holding)


def noise(key, dims, width, reach, split=(), dtype=jnp.bfloat16):
    drawn = width * jax.random.normal(key, dims, jnp.float32)
    if split:
        drawn = drawn * level_of(key, dims, split, -0.22, 0.18)
    return jnp.clip(drawn, -reach, reach).astype(dtype)


def setup_inputs(seed: int = 0, part: int = 0) -> dict:
    arg_keys = jax.random.split(jax.random.key(seed), 11)
    part_splits = jax.random.split(jax.random.fold_in(arg_keys[10], part), 11)
    velocity = noise(part_splits[0], (2, NX, NZ), 1.0, 6.0, ((1, 8), (2, 2)), jnp.float32)
    stress = noise(part_splits[1], (3, NX, NZ), 1.0, 6.0, ((1, 8), (2, 2)), jnp.float32)
    adjoint_velocity = noise(part_splits[2], (2, NX, NZ), 1.0, 6.0, ((1, 8), (2, 2)), jnp.float32)
    adjoint_stress = noise(part_splits[3], (3, NX, NZ), 1.0, 6.0, ((1, 8), (2, 2)), jnp.float32)
    buoyancy = jnp.clip(jnp.exp(math.log(0.8) - 0.98082923 * jax.random.uniform(arg_keys[4], (NX, NZ), jnp.float32) ** level_of(arg_keys[4], (NX, NZ), ((0, 8), (1, 2)), -0.2, 0.2)), 0.3, 0.8)
    lame_lambda = jnp.clip(jnp.exp(math.log(0.2) - 1.3862944 * jax.random.uniform(arg_keys[5], (NX, NZ), jnp.float32) ** level_of(arg_keys[5], (NX, NZ), ((0, 8), (1, 2)), -0.2, 0.2)), 0.05, 0.2)
    shear_modulus = jnp.clip(jnp.exp(math.log(0.2) - 1.3862944 * jax.random.uniform(arg_keys[6], (NX, NZ), jnp.float32) ** level_of(arg_keys[6], (NX, NZ), ((0, 8), (1, 2)), -0.2, 0.2)), 0.05, 0.2)
    observed = noise(part_splits[7], (NT, NCH), 1.0, 6.0, ((1, 8),), jnp.float32)
    owner_track_keys = jax.random.split(jax.random.fold_in(arg_keys[8], 1), NCH // CH_DEV)
    owner_track_turns = jax.random.permutation(jax.random.fold_in(arg_keys[8], 3), NCH // CH_DEV)
    owner_track = jax.vmap(lambda own, number: assign_block(jax.random.fold_in(arg_keys[8], 2), own, number, CH_DEV, N_TRACK, 1, CAP, 2))(owner_track_keys, owner_track_turns).reshape((NCH, 1))
    fibre_cell = set_ends(jax.random.randint(arg_keys[9], (NCH,), 0, CX * FIBRE_ROWS), jax.random.fold_in(arg_keys[9], 1), 0, (CX * FIBRE_ROWS) - 1).astype(jnp.int32)
    return dict(velocity=velocity, stress=stress, adjoint_velocity=adjoint_velocity, adjoint_stress=adjoint_stress, buoyancy=buoyancy, lame_lambda=lame_lambda, shear_modulus=shear_modulus, observed=observed, owner_track=owner_track, fibre_cell=fibre_cell)


NEAR_WEIGHT = 9.0 / 8.0
FAR_WEIGHT = -1.0 / 24.0


def window_of(field, start_at, cut_count, dim_index):
    return lax.slice_in_dim(field, start_at, start_at + cut_count, axis=dim_index)


def ahead_diff(field, dim_index):
    cut_count = field.shape[dim_index] - 4
    return NEAR_WEIGHT * (window_of(field, 3, cut_count, dim_index) - window_of(field, 2, cut_count, dim_index)) + FAR_WEIGHT * (window_of(field, 4, cut_count, dim_index) - window_of(field, 1, cut_count, dim_index))


def behind_diff(field, dim_index):
    cut_count = field.shape[dim_index] - 4
    return NEAR_WEIGHT * (window_of(field, 2, cut_count, dim_index) - window_of(field, 1, cut_count, dim_index)) + FAR_WEIGHT * (window_of(field, 3, cut_count, dim_index) - window_of(field, 0, cut_count, dim_index))


def widen(field):
    return jnp.pad(field, ((2, 2), (2, 2)))


def advance(fields, buoyancy, lame_lambda, shear_modulus, modulus):
    press_along, press_down, press_shear = widen(fields[2]), widen(fields[3]), widen(fields[4])
    speed_along = fields[0] + buoyancy * (behind_diff(press_along, 0)[:, 2:-2] + behind_diff(press_shear, 1)[2:-2, :])
    speed_down = fields[1] + buoyancy * (ahead_diff(press_shear, 0)[:, 2:-2] + ahead_diff(press_down, 1)[2:-2, :])
    wide_along, wide_down = widen(speed_along), widen(speed_down)
    strain_along = ahead_diff(wide_along, 0)[:, 2:-2]
    strain_down = behind_diff(wide_down, 1)[2:-2, :]
    shear_rate = ahead_diff(wide_along, 1)[2:-2, :] + behind_diff(wide_down, 0)[:, 2:-2]
    new_xx = fields[2] + modulus * strain_along + lame_lambda * strain_down
    new_zz = fields[3] + lame_lambda * strain_along + modulus * strain_down
    new_xz = fields[4] + shear_modulus * shear_rate
    return jnp.stack([speed_along, speed_down, new_xx, new_zz, new_xz]), (strain_along, strain_down, shear_rate)


def reference(velocity, stress, adjoint_velocity, adjoint_stress, buoyancy, lame_lambda, shear_modulus, observed, owner_track, fibre_cell):
    modulus = lame_lambda + 2.0 * shear_modulus
    along_cell = owner_track[:, 0] * CX + fibre_cell // FIBRE_ROWS
    flat_cell = (along_cell * NZ + fibre_cell % FIBRE_ROWS).astype(jnp.int32)
    fields = jnp.concatenate([velocity, stress], axis=0)
    saved = []
    records = []
    for step_index in range(NT):
        fields, strains = advance(fields, buoyancy, lame_lambda, shear_modulus, modulus)
        saved.append(strains)
        records.append(strains[0].reshape(-1)[flat_cell])
    recorded = jnp.stack(records)
    residual = recorded - observed
    adjoint = jnp.concatenate([adjoint_velocity, adjoint_stress], axis=0)
    gradient_lambda = jnp.zeros((NX, NZ), jnp.float32)
    gradient_mu = jnp.zeros((NX, NZ), jnp.float32)
    for back_index in range(NT):
        moment = NT - 1 - back_index
        press = adjoint[2].reshape(-1).at[flat_cell].add(residual[moment])
        adjoint = adjoint.at[2].set(press.reshape(NX, NZ))
        adjoint, adjoint_strains = advance(adjoint, buoyancy, lame_lambda, shear_modulus, modulus)
        fwd_along, fwd_down, fwd_shear = saved[moment]
        adj_along, adj_down, adj_shear = adjoint_strains
        gradient_lambda = gradient_lambda + (fwd_along + fwd_down) * (adj_along + adj_down)
        gradient_mu = gradient_mu + 2.0 * (fwd_along * adj_along + fwd_down * adj_down) + fwd_shear * adj_shear
    return gradient_lambda, gradient_mu, fields[0:2], residual
```

```python
import jax
import jax.numpy as jnp
from jax import lax
from jax.experimental import pallas as pl
from jax.experimental.pallas import tpu as pltpu
from jax.sharding import PartitionSpec as P

FIBRE_ROWS = 4
NEAR = 9.0 / 8.0
RATIO = -1.0 / 27.0
HALO = 12
EDGE = 16
LANES = 128
PAD = 8
FIELDS = 13
STRIP = 16
OWN = LANES - 2 * HALO
VMEM = pltpu.VMEM


def lane_ids(rows):
    return lax.broadcasted_iota(jnp.int32, (rows, LANES), 1)


def params():
    return pltpu.CompilerParams(vmem_limit_bytes=40 * 1024 * 1024)


def field_refs(velocity, stress, adj_velocity, adj_stress, buoyancy, lame, shear):
    return (
        [velocity.at[i] for i in range(2)]
        + [stress.at[i] for i in range(3)]
        + [adj_velocity.at[i] for i in range(2)]
        + [adj_stress.at[i] for i in range(3)]
        + [buoyancy, lame, shear]
    )


def pack_kernel(*refs):
    fields = field_refs(*refs[:7])
    obs, along, row, depth_out, even_out, odd_out, strip_out = refs[7:]
    depth = lax.axis_index("depth")
    even = lax.rem(lax.axis_index("track"), 2) == 0
    rows = fields[0].shape[0]
    lane = lane_ids(rows)
    packed = [jnp.zeros((rows, LANES), jnp.float32) for _ in range(2)]
    strip = jnp.zeros((rows, LANES), jnp.float32)
    for f, ref in enumerate(fields):
        first, last = ref[:, :LANES], ref[:, LANES:]
        spot = EDGE * (f % 8)
        here = (lane >= spot) & (lane < spot + EDGE)
        edge = jnp.where(depth == 0, last, first)
        shift = lax.rem(spot + EDGE * (1 - depth), LANES)
        packed[f // 8] = jnp.where(here, pltpu.roll(edge, shift, 1), packed[f // 8])
        if f < 5 or f >= 10:
            k = f if f < 5 else f - 5
            mine = (lane >= STRIP * k) & (lane < STRIP * (k + 1))
            strip = jnp.where(mine, pltpu.roll(first, STRIP * k, 1), strip)
        low, high = ref[:HALO, :], ref[rows - HALO :, :]
        at = EDGE + HALO * f
        even_out[at : at + HALO, :] = jnp.where(even, high, low)
        odd_out[at : at + HALO, :] = jnp.where(even, low, high)
    tail = EDGE + HALO * FIELDS
    for out in (even_out, odd_out):
        out[:EDGE, :] = jnp.zeros((EDGE, 2 * LANES), jnp.float32)
        out[tail:, :] = jnp.zeros((out.shape[0] - tail, 2 * LANES), jnp.float32)
    depth_out[:, :LANES] = packed[0]
    depth_out[:, LANES:] = packed[1]
    turned = strip.T
    half = LANES // 2
    strip_out[:half, :] = jnp.concatenate([turned[:half], turned[half:]], axis=1)
    strip_out[half : half + 4, :] = obs[:, :LANES]
    strip_out[half + 4 : half + 8, :] = obs[:, LANES:]
    strip_out[half + 8 : half + 9, :] = along[:, :LANES].astype(jnp.float32)
    strip_out[half + 9 : half + 10, :] = along[:, LANES:].astype(jnp.float32)
    strip_out[half + 10 : half + 11, :] = row[:, :LANES].astype(jnp.float32)
    strip_out[half + 11 : half + 12, :] = row[:, LANES:].astype(jnp.float32)
    strip_out[half + 12 :, :] = jnp.zeros((4, LANES), jnp.float32)


def corner_kernel(got, even_in, odd_in, even_out, odd_out, sems):
    rows = got.shape[0]
    is_odd = lax.rem(lax.axis_index("track"), 2)
    high, low = (rows - EDGE) * (1 - is_odd), (rows - EDGE) * is_odd
    one = pltpu.make_async_copy(
        got.at[pl.ds(pl.multiple_of(high, EDGE), EDGE), :], even_out.at[pl.ds(0, EDGE), :], sems.at[0]
    )
    two = pltpu.make_async_copy(
        got.at[pl.ds(pl.multiple_of(low, EDGE), EDGE), :], odd_out.at[pl.ds(0, EDGE), :], sems.at[1]
    )
    one.start()
    two.start()
    one.wait()
    two.wait()


def turn(value, by):
    return pltpu.roll(value, by % LANES, 1)


def surface_kernel(tracks, columns, got, obs, along, row, inject_out, residual_out, state, media, rate):
    depth = lax.axis_index("depth")
    start = lax.axis_index("track") * columns - EDGE
    channels = obs.shape[1]
    grid_end = tracks * columns
    windows = -(-grid_end // OWN)
    lane = lane_ids(STRIP)
    state[...] = jnp.zeros(state.shape, jnp.float32)
    media[...] = jnp.zeros(media.shape, jnp.float32)
    own_along = along[...]

    def window(number, total):
        begin = number * OWN - HALO
        base = (begin + columns) // columns - 1
        offset = begin - base * columns
        part = lax.div(offset + lane, columns)
        where_x = begin + lane
        inside = (where_x >= 0) & (where_x < grid_end)
        half = LANES // 2
        for k in range(8):
            value = jnp.zeros((STRIP, LANES), jnp.float32)
            top = STRIP * (k % 4)
            for step in range(3):
                who = jnp.clip(base + step, 0, tracks - 1)
                block = got[2 * who, top : top + STRIP, :]
                shift = lax.rem(4 * LANES - offset + columns * step - half * (k // 4), LANES)
                value = jnp.where(part == step, pltpu.roll(block, shift, 1), value)
            value = jnp.where(inside, value, 0.0)
            if k < 5:
                state[k, PAD : PAD + STRIP, :] = value
            elif k == 5:
                media[0, :STRIP, :] = NEAR * value
            elif k == 6:
                lame = value
            else:
                media[1, :STRIP, :] = NEAR * (lame + 2.0 * value)
                media[2, :STRIP, :] = NEAR * lame
                media[3, :STRIP, :] = NEAR * value

        def at(f, r, by=0):
            return state[f, PAD + r + by : PAD + r + by + 8, :]

        strains = []
        for moment in range(4):
            for r in (0, 8) if moment < 2 else (0,):
                xx, xz, zz = at(2, r), at(4, r), at(3, r)
                near = (xx - turn(xx, 1)) + (xz - at(4, r, -1))
                far = (turn(xx, -1) - turn(xx, 2)) + (at(4, r, 1) - at(4, r, -2))
                b = media[0, r : r + 8, :]
                state[0, PAD + r : PAD + r + 8, :] = at(0, r) + b * (near + RATIO * far)
                if moment < 3:
                    near = (turn(xz, -1) - xz) + (at(3, r, 1) - zz)
                    far = (turn(xz, -2) - turn(xz, 1)) + (at(3, r, 2) - at(3, r, -1))
                    state[1, PAD + r : PAD + r + 8, :] = at(1, r) + b * (near + RATIO * far)
            for r in (0, 8) if moment < 1 else (0,):
                vx, vz = at(0, r), at(1, r)
                exx = (turn(vx, -1) - vx) + RATIO * (turn(vx, -2) - turn(vx, 1))
                if r == 0:
                    strains.append(NEAR * exx)
                if moment < 3:
                    ezz = (vz - at(1, r, -1)) + RATIO * (at(1, r, 1) - at(1, r, -2))
                    near = (at(0, r, 1) - vx) + (vz - turn(vz, 1))
                    far = (at(0, r, 2) - at(0, r, -1)) + (turn(vz, -1) - turn(vz, 2))
                    shear = near + RATIO * far
                    whole, lam, mu = (media[i, r : r + 8, :] for i in (1, 2, 3))
                    state[2, PAD + r : PAD + r + 8, :] = at(2, r) + (whole * exx + lam * ezz)
                    state[3, PAD + r : PAD + r + 8, :] = at(3, r) + (lam * exx + whole * ezz)
                    state[4, PAD + r : PAD + r + 8, :] = at(4, r) + mu * shear
        lane32 = lane_ids(32)
        mine = (lane32 >= HALO) & (lane32 < HALO + OWN)
        image = jnp.where(mine, jnp.concatenate(strains, axis=0), 0.0)
        spot = begin + lax.broadcasted_iota(jnp.int32, (LANES, channels), 0)
        hot = (spot == own_along).astype(jnp.float32)
        spot = begin + lax.broadcasted_iota(jnp.int32, (LANES, LANES), 0)
        pick = (spot == start + lax.broadcasted_iota(jnp.int32, (LANES, LANES), 1)).astype(jnp.float32)
        both = jnp.concatenate([hot, pick], axis=1)
        rate[...] += jnp.dot(
            image, both, precision=lax.Precision.HIGHEST, preferred_element_type=jnp.float32
        )
        return total

    rate[...] = jnp.zeros(rate.shape, jnp.float32)
    if windows <= 8:
        for number in range(windows):
            window(number, 0)
    else:
        lax.fori_loop(0, windows, window, 0)

    half = LANES // 2
    group = 8

    def images(number, total):
        weights, hots = [], []
        for k in range(group):
            who = 2 * (number * group + k)
            for h in range(2):
                chan_along = got[who, half + 8 + h : half + 9 + h, :]
                chan_row = got[who, half + 10 + h : half + 11 + h, :]
                mask = lax.broadcasted_iota(jnp.int32, (8, LANES), 0).astype(jnp.float32) == chan_row
                pieces = [
                    jnp.where(mask, got[who, half + 4 * h + t : half + 4 * h + t + 1, :], 0.0) for t in range(4)
                ]
                weights.append(jnp.concatenate(pieces + [mask.astype(jnp.float32)], axis=0))
                spot = (start + lax.broadcasted_iota(jnp.int32, (LANES, LANES), 0)).astype(jnp.float32)
                hots.append((spot == chan_along).astype(jnp.float32))
        return total + lax.dot_general(
            jnp.concatenate(weights, axis=1),
            jnp.concatenate(hots, axis=1),
            (((1,), (1,)), ((), ())),
            precision=lax.Precision.HIGHEST,
            preferred_element_type=jnp.float32,
        )

    total = jnp.zeros((40, LANES), jnp.float32)
    if tracks <= group:
        total = images(0, total)
    else:
        total = lax.fori_loop(0, tracks // group, images, total)
    count = total[32:40]
    rows = [
        count * rate[8 * t : 8 * t + 8, channels:] - total[8 * t : 8 * t + 8] for t in range(4)
    ]
    turned = jnp.concatenate(rows + [jnp.zeros((LANES - 32, LANES), jnp.float32)], axis=0).T
    window_rows = inject_out.shape[1]
    lane_w = lane_ids(window_rows)
    keep = (lane_w >= EDGE) & (lane_w < EDGE + 8) & (depth == 0)
    for t in range(4):
        inject_out[t] = jnp.where(keep, turn(turned[:window_rows], EDGE - 8 * t), 0.0)
    mask = lax.broadcasted_iota(jnp.int32, (8, channels), 0) == row[...]
    traces = [
        jnp.sum(jnp.where(mask, rate[8 * t : 8 * t + 8, :channels], 0.0), axis=0, keepdims=True)
        - obs[t : t + 1, :]
        for t in range(4)
    ]
    residual_out[...] = jnp.where(
        depth == 0, jnp.concatenate(traces[:2], axis=0), jnp.concatenate(traces[2:], axis=0)
    )


def main_kernel(*refs):
    fields = field_refs(*refs[:7])
    got_depth, got_even, got_odd, inject = refs[7:11]
    lambda_out, mu_out, end_out = refs[11:14]
    state, media, saved, sums = refs[14:]
    rows = fields[0].shape[0]
    depth = lax.axis_index("depth")
    even = lax.rem(lax.axis_index("track"), 2) == 0
    extent = rows + 2 * EDGE
    tiles = extent // 8
    edge_tiles = EDGE // 8

    zero_pad = jnp.zeros((PAD, LANES), jnp.float32)
    for f in range(10):
        for p in range(3):
            state[f, p, :PAD, :] = zero_pad
            state[f, p, PAD + extent :, :] = zero_pad

    def place(f, at, first, last, halo):
        count = first.shape[0]
        lane = lane_ids(count)
        spot = EDGE * (f % 8)
        shift = lax.rem(LANES - spot + (LANES - EDGE) * (1 - depth), LANES)
        beside = pltpu.roll(halo, shift, 1)
        return [
            jnp.where(lane >= EDGE, turn(first, EDGE), jnp.where(depth == 1, beside, 0.0)),
            jnp.where(lane < LANES // 2, turn(first, LANES // 2), turn(last, LANES // 2)),
            jnp.where(lane < LANES - EDGE, turn(last, -EDGE), jnp.where(depth == 0, beside, 0.0)),
        ]

    def put(f, at, planes):
        count = planes[0].shape[0]
        for p in range(3):
            if f < 10:
                state[f, p, PAD + at : PAD + at + count, :] = planes[p]
            elif f == 10:
                media[0, p, at : at + count, :] = NEAR * planes[p]
            elif f == 11:
                media[2, p, at : at + count, :] = NEAR * planes[p]
            else:
                mu = NEAR * planes[p]
                media[3, p, at : at + count, :] = mu
                media[1, p, at : at + count, :] = media[2, p, at : at + count, :] + 2.0 * mu

    for f, ref in enumerate(fields):
        col = LANES * (f // 8)
        low = EDGE + HALO * f - (EDGE - HALO)
        high = EDGE + HALO * f
        left = jnp.where(even, got_odd[low : low + EDGE, :], got_even[low : low + EDGE, :])
        left_halo = jnp.where(even, got_odd[:EDGE, col : col + LANES], got_even[:EDGE, col : col + LANES])
        right = jnp.where(even, got_even[high : high + EDGE, :], got_odd[high : high + EDGE, :])
        right_halo = jnp.where(even, got_even[:EDGE, col : col + LANES], got_odd[:EDGE, col : col + LANES])
        put(f, 0, place(f, 0, left[:, :LANES], left[:, LANES:], left_halo))
        put(
            f,
            EDGE,
            place(f, EDGE, ref[:, :LANES], ref[:, LANES:], got_depth[:, col : col + LANES]),
        )
        put(f, EDGE + rows, place(f, EDGE + rows, right[:, :LANES], right[:, LANES:], right_halo))

    def velocities(g, lo, hi):
        def body(i, carry):
            r = pl.multiple_of(i * 8, 8)
            for p in range(3):

                def at(f, by=0):
                    return state[g + f, p, pl.ds(r + PAD + by, 8), :]

                xx, xz, zz = at(2), at(4), at(3)
                b = media[0, p, pl.ds(r, 8), :]
                near = (xx - at(2, -1)) + (xz - turn(xz, 1))
                far = (at(2, 1) - at(2, -2)) + (turn(xz, -1) - turn(xz, 2))
                state[g, p, pl.ds(r + PAD, 8), :] = at(0) + b * (near + RATIO * far)
                near = (at(4, 1) - xz) + (turn(zz, -1) - zz)
                far = (at(4, 2) - at(4, -1)) + (turn(zz, -2) - turn(zz, 1))
                state[g + 1, p, pl.ds(r + PAD, 8), :] = at(1) + b * (near + RATIO * far)
            return carry

        lax.fori_loop(lo, hi, body, 0)

    def stresses(g, lo, hi, update, keep):
        def body(i, carry):
            r = pl.multiple_of(i * 8, 8)
            for p in range(3):

                def at(f, by=0):
                    return state[g + f, p, pl.ds(r + PAD + by, 8), :]

                vx, vz = at(0), at(1)
                exx = (at(0, 1) - vx) + RATIO * (at(0, 2) - at(0, -1))
                ezz = (vz - turn(vz, 1)) + RATIO * (turn(vz, -1) - turn(vz, 2))
                near = (turn(vx, -1) - vx) + (vz - at(1, -1))
                far = (turn(vx, -2) - turn(vx, 1)) + (at(1, 1) - at(1, -2))
                shear = near + RATIO * far
                keep(p, r, exx, ezz, shear)
                if update:
                    whole, lam, mu = (media[k, p, pl.ds(r, 8), :] for k in (1, 2, 3))
                    state[g + 2, p, pl.ds(r + PAD, 8), :] = at(2) + (whole * exx + lam * ezz)
                    state[g + 3, p, pl.ds(r + PAD, 8), :] = at(3) + (lam * exx + whole * ezz)
                    state[g + 4, p, pl.ds(r + PAD, 8), :] = at(4) + mu * shear
            return carry

        lax.fori_loop(lo, hi, body, 0)

    def spans(step):
        if step == 0:
            return (0, tiles), (0, tiles)
        if step < 3:
            return (1, tiles - 1), (1, tiles - 1)
        return (1, tiles - 1), (edge_tiles, tiles - edge_tiles)

    for step in range(4):
        fast, slow = spans(step)
        velocities(0, *fast)

        def save(p, r, exx, ezz, shear, step=step):
            saved[step, 0, p, pl.ds(r, 8), :] = exx
            saved[step, 1, p, pl.ds(r, 8), :] = ezz
            saved[step, 2, p, pl.ds(r, 8), :] = shear

        stresses(0, *slow, step < 3, save)

    def joined(planes):
        lane = lane_ids(planes[0].shape[0])
        middle = turn(planes[1], LANES // 2)
        return (
            jnp.where(lane < 88, turn(planes[0], -EDGE), middle),
            jnp.where(lane < 40, middle, turn(planes[2], EDGE)),
        )

    top = PAD + EDGE
    for f in range(2):
        first, last = joined([state[f, p, top : top + rows, :] for p in range(3)])
        end_out[f, :, :LANES] = first
        end_out[f, :, LANES:] = last

    sums[...] = jnp.zeros(sums.shape, jnp.float32)
    for step in range(4):
        fast, slow = spans(step)
        moment = 3 - step
        state[7, 0, PAD : PAD + extent, :] += inject[moment]
        velocities(5, *fast)

        def gather(p, r, exx, ezz, shear, moment=moment):
            fxx, fzz, fxz = (saved[moment, k, p, pl.ds(r, 8), :] for k in range(3))
            sums[0, p, pl.ds(r, 8), :] += (fxx + fzz) * (exx + ezz)
            sums[1, p, pl.ds(r, 8), :] += 2.0 * (fxx * exx + fzz * ezz) + fxz * shear

        stresses(5, *slow, step < 3, gather)

    for k, out in enumerate((lambda_out, mu_out)):
        first, last = joined([sums[k, p, EDGE : EDGE + rows, :] for p in range(3)])
        out[:, :LANES] = (NEAR * NEAR) * first
        out[:, LANES:] = (NEAR * NEAR) * last


def per_device(
    velocity,
    stress,
    adjoint_velocity,
    adjoint_stress,
    buoyancy,
    lame_lambda,
    shear_modulus,
    observed,
    owner_track,
    fibre_cell,
):
    tracks = lax.axis_size("track")
    rows, depth_cells = buoyancy.shape
    moments, channels = observed.shape
    f32 = jnp.float32
    cell = fibre_cell.reshape(1, channels)
    along = owner_track.reshape(1, channels) * rows + cell // FIBRE_ROWS
    fibre_row = cell % FIBRE_ROWS
    arrays = (velocity, stress, adjoint_velocity, adjoint_stress, buoyancy, lame_lambda, shear_modulus)
    length = EDGE + HALO * FIELDS
    length = length + (-length) % 8
    edges = jax.ShapeDtypeStruct((length, depth_cells), f32)
    inside = pl.BlockSpec(memory_space=VMEM)
    anywhere = pl.BlockSpec(memory_space=pl.ANY)

    to_depth, to_even, to_odd, strip = pl.pallas_call(
        pack_kernel,
        out_shape=(
            jax.ShapeDtypeStruct((rows, depth_cells), f32),
            edges,
            edges,
            jax.ShapeDtypeStruct((LANES // 2 + 16, LANES), f32),
        ),
        in_specs=[inside] * 10,
        out_specs=(inside,) * 4,
        compiler_params=params(),
        name="pack",
    )(*arrays, observed, along, fibre_row)

    strips = lax.all_gather(strip, ("track", "depth"), axis=0, tiled=False)
    got_depth = lax.ppermute(to_depth, "depth", [(0, 1), (1, 0)])
    to_even, to_odd = pl.pallas_call(
        corner_kernel,
        out_shape=(edges, edges),
        in_specs=[anywhere] * 3,
        out_specs=(anywhere,) * 2,
        input_output_aliases={1: 0, 2: 1},
        scratch_shapes=[pltpu.SemaphoreType.DMA((2,))],
        compiler_params=params(),
        name="corners",
    )(got_depth, to_even, to_odd)
    swap = lambda k: [pair for i in range(k, tracks - 1, 2) for pair in ((i, i + 1), (i + 1, i))]
    got_odd = lax.ppermute(to_odd, "track", swap(1))
    got_even = lax.ppermute(to_even, "track", swap(0))

    extent = rows + 2 * EDGE
    inject, residual = pl.pallas_call(
        lambda *refs: surface_kernel(tracks, rows, *refs),
        out_shape=(
            jax.ShapeDtypeStruct((moments, extent, LANES), f32),
            jax.ShapeDtypeStruct((moments // 2, channels), f32),
        ),
        in_specs=[inside] * 4,
        out_specs=(inside,) * 2,
        scratch_shapes=[
            VMEM((5, 2 * PAD + STRIP, LANES), f32),
            VMEM((4, STRIP, LANES), f32),
            VMEM((32, channels + LANES), f32),
        ],
        compiler_params=params(),
        name="surface",
    )(strips, observed, along, fibre_row)

    block = jax.ShapeDtypeStruct((rows, depth_cells), f32)
    gradient_lambda, gradient_mu, velocity_end = pl.pallas_call(
        main_kernel,
        out_shape=(block, block, jax.ShapeDtypeStruct(velocity.shape, f32)),
        in_specs=[inside] * 11,
        out_specs=(inside,) * 3,
        scratch_shapes=[
            VMEM((10, 3, extent + 2 * PAD, LANES), f32),
            VMEM((4, 3, extent, LANES), f32),
            VMEM((4, 3, 3, extent, LANES), f32),
            VMEM((2, 3, extent, LANES), f32),
        ],
        compiler_params=params(),
        name="window",
    )(*arrays, got_depth, got_even, got_odd, inject)
    return gradient_lambda, gradient_mu, velocity_end, residual


def solution(mesh):
    return jax.shard_map(
        per_device,
        mesh=mesh,
        in_specs=(
            P("shots", "track", "depth"),
            P("shots", "track", "depth"),
            P("shots", "track", "depth"),
            P("shots", "track", "depth"),
            P("track", "depth"),
            P("track", "depth"),
            P("track", "depth"),
            P("shots", "track"),
            P("track", None),
            P("track"),
        ),
        out_specs=(
            P(("shots", "track"), "depth"),
            P(("shots", "track"), "depth"),
            P("shots", "track", "depth"),
            P(("shots", "depth"), "track"),
        ),
        check_vma=False,
    )
```

```python
import jax
import jax.numpy as jnp
from jax import lax
from jax.experimental import pallas as pl
from jax.experimental.pallas import tpu as pltpu
from jax.sharding import PartitionSpec as P

FIBRE_ROWS = 4
NEAR = 9.0 / 8.0
RATIO = -1.0 / 27.0
HALO = 12
EDGE = 16
LANES = 128
PAD = 8
FIELDS = 13
MOMENTS = 4
IMAGE = MOMENTS * FIBRE_ROWS
NOTE = 24
VMEM = pltpu.VMEM
F32 = jnp.float32
BF16 = jnp.bfloat16


def lane_ids(rows):
    return lax.broadcasted_iota(jnp.int32, (rows, LANES), 1)


def row_ids(rows, columns):
    return lax.broadcasted_iota(jnp.int32, (rows, columns), 0)


def params():
    return pltpu.CompilerParams(vmem_limit_bytes=40 * 1024 * 1024)


def turn(value, by):
    return pltpu.roll(value, by % LANES, 1)


def is_even():
    return lax.rem(lax.axis_index("track"), 2) == 0


def fetch(sources, targets, sems):
    copies = [pltpu.make_async_copy(s, t, sems.at[i]) for i, (s, t) in enumerate(zip(sources, targets))]
    for copy in copies:
        copy.start()
    return copies


def field_refs(velocity, stress, adj_velocity, adj_stress, buoyancy, lame, shear):
    return (
        [velocity.at[i] for i in range(2)]
        + [stress.at[i] for i in range(3)]
        + [adj_velocity.at[i] for i in range(2)]
        + [adj_stress.at[i] for i in range(3)]
        + [buoyancy, lame, shear]
    )


def pack_kernel(*refs):
    sources, (depth_out, even_out, odd_out), held, sems = refs[:7], refs[7:10], refs[10:17], refs[17]
    copies = fetch(sources, held, sems)
    depth = lax.axis_index("depth")
    even = is_even()
    fields = field_refs(*held)
    rows = fields[0].shape[0]
    lane = lane_ids(rows)
    tail = EDGE + HALO * FIELDS
    for out in (even_out, odd_out):
        out[:EDGE, :] = jnp.zeros((EDGE, 2 * LANES), F32)
        out[tail:, :] = jnp.zeros((out.shape[0] - tail, 2 * LANES), F32)
    for copy in copies:
        copy.wait()
    packed = [jnp.zeros((rows, LANES), F32) for _ in range(2)]
    for f, ref in enumerate(fields):
        first, last = ref[:, :LANES], ref[:, LANES:]
        spot = EDGE * (f % 8)
        here = (lane >= spot) & (lane < spot + EDGE)
        edge = jnp.where(depth == 0, last, first)
        shift = lax.rem(spot + EDGE * (1 - depth), LANES)
        packed[f // 8] = jnp.where(here, pltpu.roll(edge, shift, 1), packed[f // 8])
        low, high = ref[:HALO, :], ref[rows - HALO :, :]
        at = EDGE + HALO * f
        even_out[at : at + HALO, :] = jnp.where(even, high, low)
        odd_out[at : at + HALO, :] = jnp.where(even, low, high)
    depth_out[:, :LANES] = packed[0]
    depth_out[:, LANES:] = packed[1]


def corner_kernel(got, even_in, odd_in, even_out, odd_out, sems):
    rows = got.shape[0]
    is_odd = lax.rem(lax.axis_index("track"), 2)
    high, low = (rows - EDGE) * (1 - is_odd), (rows - EDGE) * is_odd
    one = pltpu.make_async_copy(
        got.at[pl.ds(pl.multiple_of(high, EDGE), EDGE), :], even_out.at[pl.ds(0, EDGE), :], sems.at[0]
    )
    two = pltpu.make_async_copy(
        got.at[pl.ds(pl.multiple_of(low, EDGE), EDGE), :], odd_out.at[pl.ds(0, EDGE), :], sems.at[1]
    )
    one.start()
    two.start()
    one.wait()
    two.wait()


def windows(f, first, last, halo):
    depth = lax.axis_index("depth")
    lane = lane_ids(first.shape[0])
    shift = lax.rem(LANES - EDGE * (f % 8) + (LANES - EDGE) * (1 - depth), LANES)
    beside = pltpu.roll(halo, shift, 1)
    return [
        jnp.where(lane >= EDGE, turn(first, EDGE), jnp.where(depth == 1, beside, 0.0)),
        jnp.where(lane < LANES // 2, turn(first, LANES // 2), turn(last, LANES // 2)),
        jnp.where(lane < LANES - EDGE, turn(last, -EDGE), jnp.where(depth == 0, beside, 0.0)),
    ]


def joined(planes):
    lane = lane_ids(planes[0].shape[0])
    middle = turn(planes[1], LANES // 2)
    return (
        jnp.where(lane < 88, turn(planes[0], -EDGE), middle),
        jnp.where(lane < 40, middle, turn(planes[2], EDGE)),
    )


def own_kernel(*refs):
    sources, got_depth, planes_out, held, sems = refs[:7], refs[7], refs[8], refs[9:16], refs[16]
    for copy in fetch(sources, held, sems):
        copy.wait()
    for f, ref in enumerate(field_refs(*held)):
        col = LANES * (f // 8)
        planes = windows(f, ref[:, :LANES], ref[:, LANES:], got_depth[:, col : col + LANES])
        for p in range(3):
            planes_out[f, p] = planes[p]


def halo_windows(f, got_even, got_odd):
    even = is_even()
    col = LANES * (f // 8)
    high = EDGE + HALO * f
    low = high - (EDGE - HALO)
    corner_even, corner_odd = got_even[:EDGE, col : col + LANES], got_odd[:EDGE, col : col + LANES]
    left = jnp.where(even, got_odd[low : low + EDGE, :], got_even[low : low + EDGE, :])
    right = jnp.where(even, got_even[high : high + EDGE, :], got_odd[high : high + EDGE, :])
    left_halo = jnp.where(even, corner_odd, corner_even)
    right_halo = jnp.where(even, corner_even, corner_odd)
    return (
        windows(f, left[:, :LANES], left[:, LANES:], left_halo),
        windows(f, right[:, :LANES], right[:, LANES:], right_halo),
    )


def load_state(state, own, got_even, got_odd, base):
    rows = own.shape[2]
    extent = rows + 2 * EDGE
    for f in range(5):
        below, above = halo_windows(base + f, got_even, got_odd)
        for p in range(3):
            state[f, p, :PAD, :] = jnp.zeros((PAD, LANES), F32)
            state[f, p, PAD : PAD + EDGE, :] = below[p]
            state[f, p, PAD + EDGE : PAD + EDGE + rows, :] = own[base + f, p]
            state[f, p, PAD + EDGE + rows : PAD + extent, :] = above[p]
            state[f, p, PAD + extent :, :] = jnp.zeros((PAD, LANES), F32)


def velocities(state, media, span):
    for r in range(8 * span[0], 8 * span[1], 8):
        for p in range(3):

            def at(f, by=0):
                return state[f, p, r + PAD + by : r + PAD + by + 8, :]

            xx, xz, zz = at(2), at(4), at(3)
            b = media[0, p, r : r + 8, :]
            near = (xx - at(2, -1)) + (xz - turn(xz, 1))
            far = (at(2, 1) - at(2, -2)) + (turn(xz, -1) - turn(xz, 2))
            state[0, p, r + PAD : r + PAD + 8, :] = at(0) + b * (near + RATIO * far)
            near = (at(4, 1) - xz) + (turn(zz, -1) - zz)
            far = (at(4, 2) - at(4, -1)) + (turn(zz, -2) - turn(zz, 1))
            state[1, p, r + PAD : r + PAD + 8, :] = at(1) + b * (near + RATIO * far)


def stresses(state, media, span, update, keep):
    for r in range(8 * span[0], 8 * span[1], 8):
        for p in range(3):

            def at(f, by=0):
                return state[f, p, r + PAD + by : r + PAD + by + 8, :]

            vx, vz = at(0), at(1)
            exx = (at(0, 1) - vx) + RATIO * (at(0, 2) - at(0, -1))
            ezz = (vz - turn(vz, 1)) + RATIO * (turn(vz, -1) - turn(vz, 2))
            near = (turn(vx, -1) - vx) + (vz - at(1, -1))
            far = (turn(vx, -2) - turn(vx, 1)) + (at(1, 1) - at(1, -2))
            shear = near + RATIO * far
            keep(p, r - EDGE, exx, ezz, shear)
            if update:
                whole, lam, mu = (media[k, p, r : r + 8, :] for k in (1, 2, 3))
                state[2, p, r + PAD : r + PAD + 8, :] = at(2) + (whole * exx + lam * ezz)
                state[3, p, r + PAD : r + PAD + 8, :] = at(3) + (lam * exx + whole * ezz)
                state[4, p, r + PAD : r + PAD + 8, :] = at(4) + mu * shear


def spans(step, rows):
    tiles = (rows + 2 * EDGE) // 8
    if step == 0:
        return (0, tiles), (0, tiles)
    inner = (1, tiles - 1)
    return inner, inner if step < MOMENTS - 1 else (EDGE // 8, tiles - EDGE // 8)


def forward_kernel(
    own, got_even, got_odd, obs, owner, cell, media, saved, end_out, note_out, state, small, numbers, sems
):
    copies = fetch((obs, owner, cell), (small, numbers.at[0], numbers.at[1]), sems)
    rows = own.shape[2]
    extent = rows + 2 * EDGE
    parts = []
    for f in (10, 11, 12):
        below, above = halo_windows(f, got_even, got_odd)
        parts.append([(below[p], own[f, p], above[p]) for p in range(3)])
    for p in range(3):
        for k, at in enumerate((0, EDGE, EDGE + rows)):
            b, lam, mu = (NEAR * parts[i][p][k] for i in range(3))
            span = slice(at, at + b.shape[0])
            media[0, p, span, :] = b
            media[1, p, span, :] = lam + 2.0 * mu
            media[2, p, span, :] = lam
            media[3, p, span, :] = mu
    load_state(state, own, got_even, got_odd, 0)
    for step in range(MOMENTS):
        fast, slow = spans(step, rows)
        velocities(state, media, fast)

        def save(p, r, exx, ezz, shear):
            if 0 <= r < rows:
                saved[step, 0, p, r : r + 8, :] = exx
                saved[step, 1, p, r : r + 8, :] = ezz
                saved[step, 2, p, r : r + 8, :] = shear

        stresses(state, media, slow, step < MOMENTS - 1, save)

    top = PAD + EDGE
    for f in range(2):
        first, last = joined([state[f, p, top : top + rows, :] for p in range(3)])
        end_out[f, :, :LANES] = first
        end_out[f, :, LANES:] = last

    lane = lane_ids(rows)
    image = jnp.zeros((rows, LANES), F32)
    for step in range(MOMENTS):
        spot = FIBRE_ROWS * step
        here = (lane >= spot) & (lane < spot + FIBRE_ROWS)
        image = jnp.where(here, NEAR * turn(saved[step, 0, 0], spot - EDGE), image)
    turned = image.T
    for copy in copies:
        copy.wait()
    along = numbers[0] * rows + lax.shift_right_logical(numbers[1], 2)
    row = numbers[1] & 3
    half = IMAGE // 2
    block = jnp.concatenate(
        [
            jnp.concatenate([turned[:half], turned[half:IMAGE]], axis=1),
            jnp.concatenate([small[:, :LANES], small[:, LANES:]], axis=0),
            along[:, :LANES].astype(F32),
            along[:, LANES:].astype(F32),
            row[:, :LANES].astype(F32),
            row[:, LANES:].astype(F32),
            jnp.zeros((4, LANES), F32),
        ],
        axis=0,
    )
    note_out[...] = jnp.broadcast_to(block[None], note_out.shape)


def three(value):
    high = value.astype(BF16)
    rest = value - high.astype(F32)
    middle = rest.astype(BF16)
    low = (rest - middle.astype(F32)).astype(BF16)
    return [high, middle, low]


def add_up(value):
    return (value[2 * IMAGE : 3 * IMAGE] + value[IMAGE : 2 * IMAGE]) + value[:IMAGE]


def channel_sums(tracks, rows, notes, own_along):
    start = lax.axis_index("track") * rows - EDGE
    group = min(8, tracks)
    channels = own_along.shape[1]
    lane = lane_ids(8)
    half = LANES // 2
    wanted = jnp.concatenate([own_along, start + lax.broadcasted_iota(jnp.int32, (1, LANES), 1)], axis=1)
    row16 = row_ids(IMAGE, LANES)

    def body(number, carry):
        rate, image = carry
        base = number * group
        firsts, lasts = [], []
        for k in range(0, group, 2):
            a, b = notes[2 * (base + k), :8, :], notes[2 * (base + k + 1), :8, :]
            firsts.append(jnp.where(lane < half, a, turn(b, half)))
            lasts.append(jnp.where(lane < half, turn(a, half), b))
        strains = jnp.concatenate([jnp.concatenate(firsts, axis=1), jnp.concatenate(lasts, axis=1)], axis=0)
        spot = base * rows + row_ids(group * rows, channels + LANES)
        hot = (spot == wanted).astype(F32).astype(BF16)
        rate = rate + jnp.dot(jnp.concatenate(three(strains), axis=0), hot, preferred_element_type=F32)
        weights, hots = [], []
        for k in range(group):
            who = 2 * (base + k)
            for h in range(2):
                along = notes[who, 16 + h : 17 + h, :]
                mask = (row16 & 3).astype(F32) == notes[who, 18 + h : 19 + h, :]
                seen = [notes[who, 8 + 4 * h + t : 9 + 4 * h + t, :] for t in range(MOMENTS)]
                value = jnp.where(
                    row16 < 8,
                    jnp.where(row16 < 4, seen[0], seen[1]),
                    jnp.where(row16 < 12, seen[2], seen[3]),
                )
                pieces = three(jnp.where(mask, value, 0.0)) + [mask.astype(F32).astype(BF16)]
                weights.append(jnp.concatenate(pieces, axis=0))
                spot = (start + row_ids(LANES, LANES)).astype(F32)
                hots.append((spot == along).astype(F32).astype(BF16))
        image = image + lax.dot_general(
            jnp.concatenate(weights, axis=1),
            jnp.concatenate(hots, axis=1),
            (((1,), (1,)), ((), ())),
            preferred_element_type=F32,
        )
        return rate, image

    carry = jnp.zeros((3 * IMAGE, channels + LANES), F32), jnp.zeros((4 * IMAGE, LANES), F32)
    if tracks == group:
        carry = body(0, carry)
    else:
        carry = lax.fori_loop(0, tracks // group, body, carry)
    rate, image = carry
    return add_up(rate), add_up(image), image[3 * IMAGE :]


def adjoint_kernel(
    tracks, own, got_even, got_odd, media, saved, notes, obs, owner, cell,
    lambda_out, mu_out, residual_out, state, sums, small, numbers, sems,
):
    copies = fetch((obs, owner, cell), (small, numbers.at[0], numbers.at[1]), sems)
    rows = own.shape[2]
    extent = rows + 2 * EDGE
    depth = lax.axis_index("depth")
    load_state(state, own, got_even, got_odd, 5)
    sums[...] = jnp.zeros(sums.shape, F32)
    for copy in copies:
        copy.wait()
    along = numbers[0] * rows + lax.shift_right_logical(numbers[1], 2)
    row = numbers[1] & 3
    rate, seen, count = channel_sums(tracks, rows, notes, along)
    channels = along.shape[1]
    at_own = jnp.where((row_ids(IMAGE, channels) & 3) == row, rate[:, :channels], 0.0)
    traces = [
        jnp.sum(at_own[4 * t : 4 * t + 4], axis=0, keepdims=True) - small[t : t + 1, :] for t in range(MOMENTS)
    ]
    residual_out[...] = jnp.where(
        depth == 0, jnp.concatenate(traces[:2], axis=0), jnp.concatenate(traces[2:], axis=0)
    )
    sources = count * rate[:, channels:] - seen
    turned = jnp.concatenate([sources, jnp.zeros((LANES - IMAGE, LANES), F32)], axis=0).T[:extent]
    lane = lane_ids(extent)
    here = (lane >= EDGE) & (lane < EDGE + FIBRE_ROWS) & (depth == 0)

    for step in range(MOMENTS):
        fast, slow = spans(step, rows)
        moment = MOMENTS - 1 - step
        added = jnp.where(here, turn(turned, EDGE - FIBRE_ROWS * moment), 0.0)
        state[2, 0, PAD : PAD + extent, :] += added
        velocities(state, media, fast)

        def gather(p, r, exx, ezz, shear):
            if 0 <= r < rows:
                fxx, fzz, fxz = (saved[moment, k, p, r : r + 8, :] for k in range(3))
                sums[0, p, r : r + 8, :] += (fxx + fzz) * (exx + ezz)
                sums[1, p, r : r + 8, :] += 2.0 * (fxx * exx + fzz * ezz) + fxz * shear

        stresses(state, media, slow, step < MOMENTS - 1, gather)

    for k, out in enumerate((lambda_out, mu_out)):
        first, last = joined([sums[k, p] for p in range(3)])
        out[:, :LANES] = (NEAR * NEAR) * first
        out[:, LANES:] = (NEAR * NEAR) * last


def per_device(
    velocity,
    stress,
    adjoint_velocity,
    adjoint_stress,
    buoyancy,
    lame_lambda,
    shear_modulus,
    observed,
    owner_track,
    fibre_cell,
):
    tracks = lax.axis_size("track")
    rows, depth_cells = buoyancy.shape
    moments, channels = observed.shape
    owner = owner_track.reshape(1, channels)
    cell = fibre_cell.reshape(1, channels)
    arrays = (velocity, stress, adjoint_velocity, adjoint_stress, buoyancy, lame_lambda, shear_modulus)
    length = EDGE + HALO * FIELDS
    length = length + (-length) % 8
    extent = rows + 2 * EDGE
    block = jax.ShapeDtypeStruct((rows, depth_cells), F32)
    edges = jax.ShapeDtypeStruct((length, depth_cells), F32)
    inside = pl.BlockSpec(memory_space=VMEM)
    outside = pl.BlockSpec(memory_space=pltpu.HBM)
    anywhere = pl.BlockSpec(memory_space=pl.ANY)
    held = [VMEM(a.shape, F32) for a in arrays]
    channel_scratch = [
        VMEM((moments, channels), F32),
        VMEM((2, 1, channels), jnp.int32),
        pltpu.SemaphoreType.DMA((3,)),
    ]

    to_depth, to_even, to_odd = pl.pallas_call(
        pack_kernel,
        out_shape=(block, edges, edges),
        in_specs=[outside] * 7,
        out_specs=(inside,) * 3,
        scratch_shapes=held + [pltpu.SemaphoreType.DMA((7,))],
        compiler_params=params(),
        name="pack",
    )(*arrays)

    got_depth = lax.ppermute(to_depth, "depth", [(0, 1), (1, 0)])
    to_even, to_odd = pl.pallas_call(
        corner_kernel,
        out_shape=(edges, edges),
        in_specs=[anywhere] * 3,
        out_specs=(anywhere,) * 2,
        input_output_aliases={1: 0, 2: 1},
        scratch_shapes=[pltpu.SemaphoreType.DMA((2,))],
        compiler_params=params(),
        name="corners",
    )(got_depth, to_even, to_odd)
    swap = lambda k: [pair for i in range(k, tracks - 1, 2) for pair in ((i, i + 1), (i + 1, i))]
    got_odd = lax.ppermute(to_odd, "track", swap(1))
    got_even = lax.ppermute(to_even, "track", swap(0))

    own = pl.pallas_call(
        own_kernel,
        out_shape=jax.ShapeDtypeStruct((FIELDS, 3, rows, LANES), F32),
        in_specs=[outside] * 7 + [inside],
        out_specs=inside,
        scratch_shapes=held + [pltpu.SemaphoreType.DMA((7,))],
        compiler_params=params(),
        name="own_planes",
    )(*arrays, got_depth)

    devices = tracks * lax.axis_size("depth")
    media, saved, velocity_end, note = pl.pallas_call(
        forward_kernel,
        out_shape=(
            jax.ShapeDtypeStruct((4, 3, extent, LANES), F32),
            jax.ShapeDtypeStruct((moments, 3, 3, rows, LANES), F32),
            jax.ShapeDtypeStruct(velocity.shape, F32),
            jax.ShapeDtypeStruct((devices, NOTE, LANES), F32),
        ),
        in_specs=[inside] * 3 + [outside] * 3,
        out_specs=(inside,) * 4,
        scratch_shapes=[VMEM((5, 3, extent + 2 * PAD, LANES), F32)] + channel_scratch,
        compiler_params=params(),
        name="forward",
    )(own, got_even, got_odd, observed, owner, cell)

    notes = lax.all_to_all(note, ("track", "depth"), split_axis=0, concat_axis=0, tiled=True)

    gradient_lambda, gradient_mu, residual = pl.pallas_call(
        lambda *refs: adjoint_kernel(tracks, *refs),
        out_shape=(block, block, jax.ShapeDtypeStruct((moments // 2, channels), F32)),
        in_specs=[inside] * 6 + [outside] * 3,
        out_specs=(inside,) * 3,
        scratch_shapes=[
            VMEM((5, 3, extent + 2 * PAD, LANES), F32),
            VMEM((2, 3, rows, LANES), F32),
        ]
        + channel_scratch,
        compiler_params=params(),
        name="adjoint",
    )(own, got_even, got_odd, media, saved, notes, observed, owner, cell)
    return gradient_lambda, gradient_mu, velocity_end, residual


def solution(mesh):
    return jax.shard_map(
        per_device,
        mesh=mesh,
        in_specs=(
            P("shots", "track", "depth"),
            P("shots", "track", "depth"),
            P("shots", "track", "depth"),
            P("shots", "track", "depth"),
            P("track", "depth"),
            P("track", "depth"),
            P("track", "depth"),
            P("shots", "track"),
            P("track", None),
            P("track"),
        ),
        out_specs=(
            P(("shots", "track"), "depth"),
            P(("shots", "track"), "depth"),
            P("shots", "track", "depth"),
            P(("shots", "depth"), "track"),
        ),
        check_vma=False,
    )
```

```python
import jax
import jax.numpy as jnp
from jax import lax
from jax.experimental import pallas as pl
from jax.experimental.pallas import tpu as pltpu
from jax.sharding import PartitionSpec as P

FIBRE_ROWS = 4
NEAR = 9.0 / 8.0
RATIO = -1.0 / 27.0
HALO = 12
EDGE = 16
LANES = 128
PAD = 8
FORWARD = 8
ADJOINT = 5
FIELDS = FORWARD + ADJOINT
MOMENTS = 4
IMAGE = MOMENTS * FIBRE_ROWS
NOTE = 24
VMEM = pltpu.VMEM
F32 = jnp.float32
BF16 = jnp.bfloat16


def lane_ids(rows):
    return lax.broadcasted_iota(jnp.int32, (rows, LANES), 1)


def row_ids(rows, columns):
    return lax.broadcasted_iota(jnp.int32, (rows, columns), 0)


def params():
    return pltpu.CompilerParams(vmem_limit_bytes=40 * 1024 * 1024)


def cost(microseconds):
    return pl.CostEstimate(flops=0, bytes_accessed=int(microseconds * 3.5e6), transcendentals=0)


def turn(value, by):
    return pltpu.roll(value, by % LANES, 1)


def is_even():
    return lax.rem(lax.axis_index("track"), 2) == 0


def fetch(sources, targets, sems):
    copies = [pltpu.make_async_copy(s, t, sems.at[i]) for i, (s, t) in enumerate(zip(sources, targets))]
    for copy in copies:
        copy.start()
    return copies


def field_refs(velocity, stress, adj_velocity, adj_stress, buoyancy, lame, shear):
    return (
        [velocity.at[i] for i in range(2)]
        + [stress.at[i] for i in range(3)]
        + [buoyancy, lame, shear]
        + [adj_velocity.at[i] for i in range(2)]
        + [adj_stress.at[i] for i in range(3)]
    )


def pack_kernel(*refs):
    sources, depth_out, edge_outs, held, sems = refs[:7], refs[7], refs[8:12], refs[12:19], refs[19]
    copies = fetch(sources, held, sems)
    depth = lax.axis_index("depth")
    even = is_even()
    fields = field_refs(*held)
    rows = fields[0].shape[0]
    lane = lane_ids(rows)
    for i, out in enumerate(edge_outs):
        tail = EDGE + HALO * (FORWARD, ADJOINT)[i // 2]
        out[:EDGE, :] = jnp.zeros((EDGE, 2 * LANES), F32)
        out[tail:, :] = jnp.zeros((out.shape[0] - tail, 2 * LANES), F32)
    for copy in copies:
        copy.wait()
    packed = [jnp.zeros((rows, LANES), F32) for _ in range(2)]
    for f, ref in enumerate(fields):
        first, last = ref[:, :LANES], ref[:, LANES:]
        group, place = divmod(f, FORWARD)
        spot = EDGE * place
        here = (lane >= spot) & (lane < spot + EDGE)
        edge = jnp.where(depth == 0, last, first)
        shift = lax.rem(spot + EDGE * (1 - depth), LANES)
        packed[group] = jnp.where(here, pltpu.roll(edge, shift, 1), packed[group])
        low, high = ref[:HALO, :], ref[rows - HALO :, :]
        at = EDGE + HALO * place
        edge_outs[2 * group][at : at + HALO, :] = jnp.where(even, high, low)
        edge_outs[2 * group + 1][at : at + HALO, :] = jnp.where(even, low, high)
    depth_out[:, :LANES] = packed[0]
    depth_out[:, LANES:] = packed[1]


def corner_kernel(got, *refs):
    outs, sems = refs[4:8], refs[8]
    rows = got.shape[0]
    is_odd = lax.rem(lax.axis_index("track"), 2)
    high, low = (rows - EDGE) * (1 - is_odd), (rows - EDGE) * is_odd
    copies = []
    for i, out in enumerate(outs):
        row = pl.multiple_of(low if i % 2 else high, EDGE)
        source = got.at[pl.ds(row, EDGE), pl.ds(LANES * (i // 2), LANES)]
        copies.append(pltpu.make_async_copy(source, out.at[pl.ds(0, EDGE), pl.ds(0, LANES)], sems.at[i]))
    for copy in copies:
        copy.start()
    for copy in copies:
        copy.wait()


def windows(f, first, last, halo):
    depth = lax.axis_index("depth")
    lane = lane_ids(first.shape[0])
    shift = lax.rem(LANES - EDGE * (f % FORWARD) + (LANES - EDGE) * (1 - depth), LANES)
    beside = pltpu.roll(halo, shift, 1)
    return [
        jnp.where(lane >= EDGE, turn(first, EDGE), jnp.where(depth == 1, beside, 0.0)),
        jnp.where(lane < LANES // 2, turn(first, LANES // 2), turn(last, LANES // 2)),
        jnp.where(lane < LANES - EDGE, turn(last, -EDGE), jnp.where(depth == 0, beside, 0.0)),
    ]


def joined(planes):
    lane = lane_ids(planes[0].shape[0])
    middle = turn(planes[1], LANES // 2)
    return (
        jnp.where(lane < 88, turn(planes[0], -EDGE), middle),
        jnp.where(lane < 40, middle, turn(planes[2], EDGE)),
    )


def own_kernel(*refs):
    sources, got_depth, planes_out, held, sems = refs[:7], refs[7], refs[8], refs[9:16], refs[16]
    for copy in fetch(sources, held, sems):
        copy.wait()
    for f, ref in enumerate(field_refs(*held)):
        col = LANES * (f // FORWARD)
        planes = windows(f, ref[:, :LANES], ref[:, LANES:], got_depth[:, col : col + LANES])
        for p in range(3):
            planes_out[f, p] = planes[p]


def halo_windows(f, got_even, got_odd):
    even = is_even()
    high = EDGE + HALO * (f % FORWARD)
    low = high - (EDGE - HALO)
    corner_even, corner_odd = got_even[:EDGE, :LANES], got_odd[:EDGE, :LANES]
    left = jnp.where(even, got_odd[low : low + EDGE, :], got_even[low : low + EDGE, :])
    right = jnp.where(even, got_even[high : high + EDGE, :], got_odd[high : high + EDGE, :])
    left_halo = jnp.where(even, corner_odd, corner_even)
    right_halo = jnp.where(even, corner_even, corner_odd)
    return (
        windows(f, left[:, :LANES], left[:, LANES:], left_halo),
        windows(f, right[:, :LANES], right[:, LANES:], right_halo),
    )


def load_state(state, own, got_even, got_odd, base):
    rows = own.shape[2]
    extent = rows + 2 * EDGE
    for f in range(5):
        below, above = halo_windows(base + f, got_even, got_odd)
        for p in range(3):
            state[f, p, :PAD, :] = jnp.zeros((PAD, LANES), F32)
            state[f, p, PAD : PAD + EDGE, :] = below[p]
            state[f, p, PAD + EDGE : PAD + EDGE + rows, :] = own[base + f, p]
            state[f, p, PAD + EDGE + rows : PAD + extent, :] = above[p]
            state[f, p, PAD + extent :, :] = jnp.zeros((PAD, LANES), F32)


def velocities(state, media, span):
    for r in range(8 * span[0], 8 * span[1], 8):
        for p in range(3):

            def at(f, by=0):
                return state[f, p, r + PAD + by : r + PAD + by + 8, :]

            xx, xz, zz = at(2), at(4), at(3)
            b = media[0, p, r : r + 8, :]
            near = (xx - at(2, -1)) + (xz - turn(xz, 1))
            far = (at(2, 1) - at(2, -2)) + (turn(xz, -1) - turn(xz, 2))
            state[0, p, r + PAD : r + PAD + 8, :] = at(0) + b * (near + RATIO * far)
            near = (at(4, 1) - xz) + (turn(zz, -1) - zz)
            far = (at(4, 2) - at(4, -1)) + (turn(zz, -2) - turn(zz, 1))
            state[1, p, r + PAD : r + PAD + 8, :] = at(1) + b * (near + RATIO * far)


def stresses(state, media, span, update, keep):
    for r in range(8 * span[0], 8 * span[1], 8):
        for p in range(3):

            def at(f, by=0):
                return state[f, p, r + PAD + by : r + PAD + by + 8, :]

            vx, vz = at(0), at(1)
            exx = (at(0, 1) - vx) + RATIO * (at(0, 2) - at(0, -1))
            ezz = (vz - turn(vz, 1)) + RATIO * (turn(vz, -1) - turn(vz, 2))
            near = (turn(vx, -1) - vx) + (vz - at(1, -1))
            far = (turn(vx, -2) - turn(vx, 1)) + (at(1, 1) - at(1, -2))
            shear = near + RATIO * far
            keep(p, r - EDGE, exx, ezz, shear)
            if update:
                whole, lam, mu = (media[k, p, r : r + 8, :] for k in (1, 2, 3))
                state[2, p, r + PAD : r + PAD + 8, :] = at(2) + (whole * exx + lam * ezz)
                state[3, p, r + PAD : r + PAD + 8, :] = at(3) + (lam * exx + whole * ezz)
                state[4, p, r + PAD : r + PAD + 8, :] = at(4) + mu * shear


def spans(step, rows):
    tiles = (rows + 2 * EDGE) // 8
    if step == 0:
        return (0, tiles), (0, tiles)
    inner = (1, tiles - 1)
    return inner, inner if step < MOMENTS - 1 else (EDGE // 8, tiles - EDGE // 8)


def forward_kernel(own, got_even, got_odd, media, saved, end_out, image_out, state):
    rows = own.shape[2]
    parts = []
    for f in (5, 6, 7):
        below, above = halo_windows(f, got_even, got_odd)
        parts.append([(below[p], own[f, p], above[p]) for p in range(3)])
    for p in range(3):
        for k, at in enumerate((0, EDGE, EDGE + rows)):
            b, lam, mu = (NEAR * parts[i][p][k] for i in range(3))
            span = slice(at, at + b.shape[0])
            media[0, p, span, :] = b
            media[1, p, span, :] = lam + 2.0 * mu
            media[2, p, span, :] = lam
            media[3, p, span, :] = mu
    load_state(state, own, got_even, got_odd, 0)
    for step in range(MOMENTS):
        fast, slow = spans(step, rows)
        velocities(state, media, fast)

        def save(p, r, exx, ezz, shear):
            if 0 <= r < rows:
                saved[step, 0, p, r : r + 8, :] = exx
                saved[step, 1, p, r : r + 8, :] = ezz
                saved[step, 2, p, r : r + 8, :] = shear

        stresses(state, media, slow, step < MOMENTS - 1, save)

    top = PAD + EDGE
    for f in range(2):
        first, last = joined([state[f, p, top : top + rows, :] for p in range(3)])
        end_out[f, :, :LANES] = first
        end_out[f, :, LANES:] = last

    lane = lane_ids(rows)
    image = jnp.zeros((rows, LANES), F32)
    for step in range(MOMENTS):
        spot = FIBRE_ROWS * step
        here = (lane >= spot) & (lane < spot + FIBRE_ROWS)
        image = jnp.where(here, NEAR * turn(saved[step, 0, 0], spot - EDGE), image)
    turned = image.T
    half = IMAGE // 2
    image_out[...] = jnp.concatenate([turned[:half], turned[half:IMAGE]], axis=1)


def note_kernel(rows, adj_even, adj_odd, image, image_beside, obs, owner, cell, note_out, small, numbers, sems):
    copies = fetch((obs, owner, cell), (small, numbers.at[0], numbers.at[1]), sems)
    depth = lax.axis_index("depth")
    for copy in copies:
        copy.wait()
    along = numbers[0] * rows + lax.shift_right_logical(numbers[1], 2)
    row = numbers[1] & 3
    block = jnp.concatenate(
        [
            jnp.where(depth == 0, image[...], image_beside[...]),
            jnp.concatenate([small[:, :LANES], small[:, LANES:]], axis=0),
            along[:, :LANES].astype(F32),
            along[:, LANES:].astype(F32),
            row[:, :LANES].astype(F32),
            row[:, LANES:].astype(F32),
            jnp.zeros((4, LANES), F32),
        ],
        axis=0,
    )
    note_out[...] = jnp.broadcast_to(block[None], note_out.shape)


def three(value):
    high = value.astype(BF16)
    rest = value - high.astype(F32)
    middle = rest.astype(BF16)
    low = (rest - middle.astype(F32)).astype(BF16)
    return [high, middle, low]


def add_up(value):
    return (value[2 * IMAGE : 3 * IMAGE] + value[IMAGE : 2 * IMAGE]) + value[:IMAGE]


def channel_sums(tracks, rows, notes, own_along):
    start = lax.axis_index("track") * rows - EDGE
    group = min(8, tracks)
    channels = own_along.shape[1]
    lane = lane_ids(8)
    half = LANES // 2
    wanted = jnp.concatenate([own_along, start + lax.broadcasted_iota(jnp.int32, (1, LANES), 1)], axis=1)
    row16 = row_ids(IMAGE, LANES)

    def body(number, carry):
        rate, image = carry
        base = number * group
        firsts, lasts = [], []
        for k in range(0, group, 2):
            a, b = notes[base + k, :8, :], notes[base + k + 1, :8, :]
            firsts.append(jnp.where(lane < half, a, turn(b, half)))
            lasts.append(jnp.where(lane < half, turn(a, half), b))
        strains = jnp.concatenate([jnp.concatenate(firsts, axis=1), jnp.concatenate(lasts, axis=1)], axis=0)
        spot = base * rows + row_ids(group * rows, channels + LANES)
        hot = (spot == wanted).astype(F32).astype(BF16)
        rate = rate + jnp.dot(jnp.concatenate(three(strains), axis=0), hot, preferred_element_type=F32)
        weights, hots = [], []
        for k in range(group):
            who = base + k
            for h in range(2):
                along = notes[who, 16 + h : 17 + h, :]
                mask = (row16 & 3).astype(F32) == notes[who, 18 + h : 19 + h, :]
                seen = [notes[who, 8 + 4 * h + t : 9 + 4 * h + t, :] for t in range(MOMENTS)]
                value = jnp.where(
                    row16 < 8,
                    jnp.where(row16 < 4, seen[0], seen[1]),
                    jnp.where(row16 < 12, seen[2], seen[3]),
                )
                pieces = three(jnp.where(mask, value, 0.0)) + [mask.astype(F32).astype(BF16)]
                weights.append(jnp.concatenate(pieces, axis=0))
                spot = (start + row_ids(LANES, LANES)).astype(F32)
                hots.append((spot == along).astype(F32).astype(BF16))
        image = image + lax.dot_general(
            jnp.concatenate(weights, axis=1),
            jnp.concatenate(hots, axis=1),
            (((1,), (1,)), ((), ())),
            preferred_element_type=F32,
        )
        return rate, image

    carry = jnp.zeros((3 * IMAGE, channels + LANES), F32), jnp.zeros((4 * IMAGE, LANES), F32)
    if tracks == group:
        carry = body(0, carry)
    else:
        carry = lax.fori_loop(0, tracks // group, body, carry)
    rate, image = carry
    return add_up(rate), add_up(image), image[3 * IMAGE :]


def adjoint_kernel(
    tracks, own, got_even, got_odd, media, saved, notes, obs, owner, cell,
    lambda_out, mu_out, residual_out, state, sums, small, numbers, sems,
):
    copies = fetch((obs, owner, cell), (small, numbers.at[0], numbers.at[1]), sems)
    rows = own.shape[2]
    extent = rows + 2 * EDGE
    depth = lax.axis_index("depth")
    load_state(state, own, got_even, got_odd, FORWARD)
    sums[...] = jnp.zeros(sums.shape, F32)
    for copy in copies:
        copy.wait()
    along = numbers[0] * rows + lax.shift_right_logical(numbers[1], 2)
    row = numbers[1] & 3
    rate, seen, count = channel_sums(tracks, rows, notes, along)
    channels = along.shape[1]
    at_own = jnp.where((row_ids(IMAGE, channels) & 3) == row, rate[:, :channels], 0.0)
    traces = [
        jnp.sum(at_own[4 * t : 4 * t + 4], axis=0, keepdims=True) - small[t : t + 1, :] for t in range(MOMENTS)
    ]
    residual_out[...] = jnp.where(
        depth == 0, jnp.concatenate(traces[:2], axis=0), jnp.concatenate(traces[2:], axis=0)
    )
    sources = count * rate[:, channels:] - seen
    turned = jnp.concatenate([sources, jnp.zeros((LANES - IMAGE, LANES), F32)], axis=0).T[:extent]
    lane = lane_ids(extent)
    here = (lane >= EDGE) & (lane < EDGE + FIBRE_ROWS) & (depth == 0)

    for step in range(MOMENTS):
        fast, slow = spans(step, rows)
        moment = MOMENTS - 1 - step
        added = jnp.where(here, turn(turned, EDGE - FIBRE_ROWS * moment), 0.0)
        state[2, 0, PAD : PAD + extent, :] += added
        velocities(state, media, fast)

        def gather(p, r, exx, ezz, shear):
            if 0 <= r < rows:
                fxx, fzz, fxz = (saved[moment, k, p, r : r + 8, :] for k in range(3))
                sums[0, p, r : r + 8, :] += (fxx + fzz) * (exx + ezz)
                sums[1, p, r : r + 8, :] += 2.0 * (fxx * exx + fzz * ezz) + fxz * shear

        stresses(state, media, slow, step < MOMENTS - 1, gather)

    for k, out in enumerate((lambda_out, mu_out)):
        first, last = joined([sums[k, p] for p in range(3)])
        out[:, :LANES] = (NEAR * NEAR) * first
        out[:, LANES:] = (NEAR * NEAR) * last


def per_device(
    velocity,
    stress,
    adjoint_velocity,
    adjoint_stress,
    buoyancy,
    lame_lambda,
    shear_modulus,
    observed,
    owner_track,
    fibre_cell,
):
    tracks = lax.axis_size("track")
    rows, depth_cells = buoyancy.shape
    moments, channels = observed.shape
    owner = owner_track.reshape(1, channels)
    cell = fibre_cell.reshape(1, channels)
    pinned = lambda array: pltpu.with_memory_space_constraint(array, pltpu.HBM)
    arrays = (velocity, stress, adjoint_velocity, adjoint_stress, buoyancy, lame_lambda, shear_modulus)
    arrays = tuple(pinned(array) for array in arrays)
    channel_arrays = (pinned(observed), pinned(owner), pinned(cell))
    extent = rows + 2 * EDGE
    block = jax.ShapeDtypeStruct((rows, depth_cells), F32)
    lengths = [EDGE + HALO * count + EDGE - HALO for count in (FORWARD, ADJOINT)]
    edges = [jax.ShapeDtypeStruct((length + (-length) % 8, depth_cells), F32) for length in lengths]
    edges = (edges[0], edges[0], edges[1], edges[1])
    inside = pl.BlockSpec(memory_space=VMEM)
    outside = pl.BlockSpec(memory_space=pltpu.HBM)
    anywhere = pl.BlockSpec(memory_space=pl.ANY)
    held = [VMEM(a.shape, F32) for a in arrays]
    channel_scratch = [
        VMEM((moments, channels), F32),
        VMEM((2, 1, channels), jnp.int32),
        pltpu.SemaphoreType.DMA((3,)),
    ]

    to_depth, *to_track = pl.pallas_call(
        pack_kernel,
        out_shape=(block,) + edges,
        in_specs=[outside] * 7,
        out_specs=(inside,) * 5,
        scratch_shapes=held + [pltpu.SemaphoreType.DMA((7,))],
        compiler_params=params(),
        cost_estimate=cost(2),
        name="pack",
    )(*arrays)

    depth_swap = [(0, 1), (1, 0)]
    got_depth = lax.ppermute(to_depth, "depth", depth_swap)
    to_track = pl.pallas_call(
        corner_kernel,
        out_shape=edges,
        in_specs=[anywhere] * 5,
        out_specs=(anywhere,) * 4,
        input_output_aliases={1: 0, 2: 1, 3: 2, 4: 3},
        scratch_shapes=[pltpu.SemaphoreType.DMA((4,))],
        compiler_params=params(),
        name="corners",
    )(got_depth, *to_track)
    swap = lambda k: [pair for i in range(k, tracks - 1, 2) for pair in ((i, i + 1), (i + 1, i))]
    fwd_odd = lax.ppermute(to_track[1], "track", swap(1))
    fwd_even = lax.ppermute(to_track[0], "track", swap(0))
    adj_odd = lax.ppermute(to_track[3], "track", swap(1))
    adj_even = lax.ppermute(to_track[2], "track", swap(0))

    own = pl.pallas_call(
        own_kernel,
        out_shape=jax.ShapeDtypeStruct((FIELDS, 3, rows, LANES), F32),
        in_specs=[outside] * 7 + [inside],
        out_specs=inside,
        scratch_shapes=held + [pltpu.SemaphoreType.DMA((7,))],
        compiler_params=params(),
        cost_estimate=cost(2),
        name="own_planes",
    )(*arrays, got_depth)

    media, saved, velocity_end, image = pl.pallas_call(
        forward_kernel,
        out_shape=(
            jax.ShapeDtypeStruct((4, 3, extent, LANES), F32),
            jax.ShapeDtypeStruct((moments, 3, 3, rows, LANES), F32),
            jax.ShapeDtypeStruct(velocity.shape, F32),
            jax.ShapeDtypeStruct((IMAGE // 2, LANES), F32),
        ),
        in_specs=[inside] * 3,
        out_specs=(inside,) * 4,
        scratch_shapes=[VMEM((5, 3, extent + 2 * PAD, LANES), F32)],
        compiler_params=params(),
        cost_estimate=cost(3),
        name="forward",
    )(own, fwd_even, fwd_odd)

    image_beside = lax.ppermute(image, "depth", depth_swap)
    note = pl.pallas_call(
        lambda *refs: note_kernel(rows, *refs),
        out_shape=jax.ShapeDtypeStruct((tracks, NOTE, LANES), F32),
        in_specs=[anywhere] * 2 + [inside] * 2 + [outside] * 3,
        out_specs=inside,
        scratch_shapes=channel_scratch,
        compiler_params=params(),
        cost_estimate=cost(1),
        name="note",
    )(adj_even, adj_odd, image, image_beside, *channel_arrays)
    notes = lax.all_to_all(note, "track", split_axis=0, concat_axis=0, tiled=True)

    gradient_lambda, gradient_mu, residual = pl.pallas_call(
        lambda *refs: adjoint_kernel(tracks, *refs),
        out_shape=(block, block, jax.ShapeDtypeStruct((moments // 2, channels), F32)),
        in_specs=[inside] * 6 + [outside] * 3,
        out_specs=(inside,) * 3,
        scratch_shapes=[
            VMEM((5, 3, extent + 2 * PAD, LANES), F32),
            VMEM((2, 3, rows, LANES), F32),
        ]
        + channel_scratch,
        compiler_params=params(),
        cost_estimate=cost(4),
        name="adjoint",
    )(own, adj_even, adj_odd, media, saved, notes, *channel_arrays)
    return gradient_lambda, gradient_mu, velocity_end, residual


def solution(mesh):
    return jax.shard_map(
        per_device,
        mesh=mesh,
        in_specs=(
            P("shots", "track", "depth"),
            P("shots", "track", "depth"),
            P("shots", "track", "depth"),
            P("shots", "track", "depth"),
            P("track", "depth"),
            P("track", "depth"),
            P("track", "depth"),
            P("shots", "track"),
            P("track", None),
            P("track"),
        ),
        out_specs=(
            P(("shots", "track"), "depth"),
            P(("shots", "track"), "depth"),
            P("shots", "track", "depth"),
            P(("shots", "depth"), "track"),
        ),
        check_vma=False,
    )
```

```python
import jax
import jax.numpy as jnp
from jax import lax
from jax.experimental import pallas as pl
from jax.experimental.pallas import tpu as pltpu
from jax.sharding import PartitionSpec as P

FIBRE_ROWS = 4
NEAR = 9.0 / 8.0
RATIO = -1.0 / 27.0
HALO = 12
EDGE = 16
LANES = 128
PAD = 8
FORWARD = 8
ADJOINT = 5
FIELDS = FORWARD + ADJOINT
MOMENTS = 4
IMAGE = MOMENTS * FIBRE_ROWS
NOTE = 16
VMEM = pltpu.VMEM
F32 = jnp.float32
BF16 = jnp.bfloat16


def lane_ids(rows):
    return lax.broadcasted_iota(jnp.int32, (rows, LANES), 1)


def row_ids(rows, columns):
    return lax.broadcasted_iota(jnp.int32, (rows, columns), 0)


def params():
    return pltpu.CompilerParams(vmem_limit_bytes=40 * 1024 * 1024)


def cost(microseconds):
    return pl.CostEstimate(flops=0, bytes_accessed=int(microseconds * 3.5e6), transcendentals=0)


def turn(value, by):
    return pltpu.roll(value, by % LANES, 1)


def is_even():
    return lax.rem(lax.axis_index("track"), 2) == 0


def fetch(sources, targets, sems):
    copies = [pltpu.make_async_copy(s, t, sems.at[i]) for i, (s, t) in enumerate(zip(sources, targets))]
    for copy in copies:
        copy.start()
    return copies


def field_refs(velocity, stress, adj_velocity, adj_stress, buoyancy, lame, shear):
    return (
        [velocity.at[i] for i in range(2)]
        + [stress.at[i] for i in range(3)]
        + [buoyancy, lame, shear]
        + [adj_velocity.at[i] for i in range(2)]
        + [adj_stress.at[i] for i in range(3)]
    )


def pack_kernel(*refs):
    sources, depth_out, edge_outs, held, sems = refs[:7], refs[7], refs[8:10], refs[10:17], refs[17]
    copies = fetch(sources, held, sems)
    depth = lax.axis_index("depth")
    even = is_even()
    fields = field_refs(*held)
    rows = fields[0].shape[0]
    lane = lane_ids(rows)
    tail = EDGE + HALO * FIELDS
    for out in edge_outs:
        out[:EDGE, :] = jnp.zeros((EDGE, 2 * LANES), F32)
        out[tail:, :] = jnp.zeros((out.shape[0] - tail, 2 * LANES), F32)
    for copy in copies:
        copy.wait()
    packed = [jnp.zeros((rows, LANES), F32) for _ in range(2)]
    for f, ref in enumerate(fields):
        first, last = ref[:, :LANES], ref[:, LANES:]
        group, place = divmod(f, FORWARD)
        spot = EDGE * place
        here = (lane >= spot) & (lane < spot + EDGE)
        edge = jnp.where(depth == 0, last, first)
        shift = lax.rem(spot + EDGE * (1 - depth), LANES)
        packed[group] = jnp.where(here, pltpu.roll(edge, shift, 1), packed[group])
        low, high = ref[:HALO, :], ref[rows - HALO :, :]
        at = EDGE + HALO * f
        edge_outs[0][at : at + HALO, :] = jnp.where(even, high, low)
        edge_outs[1][at : at + HALO, :] = jnp.where(even, low, high)
    depth_out[:, :LANES] = packed[0]
    depth_out[:, LANES:] = packed[1]


def corner_kernel(got, even_in, odd_in, even_out, odd_out, sems):
    rows = got.shape[0]
    is_odd = lax.rem(lax.axis_index("track"), 2)
    high, low = (rows - EDGE) * (1 - is_odd), (rows - EDGE) * is_odd
    one = pltpu.make_async_copy(
        got.at[pl.ds(pl.multiple_of(high, EDGE), EDGE), :], even_out.at[pl.ds(0, EDGE), :], sems.at[0]
    )
    two = pltpu.make_async_copy(
        got.at[pl.ds(pl.multiple_of(low, EDGE), EDGE), :], odd_out.at[pl.ds(0, EDGE), :], sems.at[1]
    )
    one.start()
    two.start()
    one.wait()
    two.wait()


def windows(f, first, last, halo):
    depth = lax.axis_index("depth")
    lane = lane_ids(first.shape[0])
    shift = lax.rem(LANES - EDGE * (f % FORWARD) + (LANES - EDGE) * (1 - depth), LANES)
    beside = pltpu.roll(halo, shift, 1)
    return [
        jnp.where(lane >= EDGE, turn(first, EDGE), jnp.where(depth == 1, beside, 0.0)),
        jnp.where(lane < LANES // 2, turn(first, LANES // 2), turn(last, LANES // 2)),
        jnp.where(lane < LANES - EDGE, turn(last, -EDGE), jnp.where(depth == 0, beside, 0.0)),
    ]


def joined(planes):
    lane = lane_ids(planes[0].shape[0])
    middle = turn(planes[1], LANES // 2)
    return (
        jnp.where(lane < 88, turn(planes[0], -EDGE), middle),
        jnp.where(lane < 40, middle, turn(planes[2], EDGE)),
    )


def own_kernel(*refs):
    sources, got_depth, planes_out, held, sems = refs[:7], refs[7], refs[8], refs[9:16], refs[16]
    for copy in fetch(sources, held, sems):
        copy.wait()
    for f, ref in enumerate(field_refs(*held)):
        col = LANES * (f // FORWARD)
        planes = windows(f, ref[:, :LANES], ref[:, LANES:], got_depth[:, col : col + LANES])
        for p in range(3):
            planes_out[f, p] = planes[p]


def halo_windows(f, got_even, got_odd):
    even = is_even()
    high = EDGE + HALO * f
    low = high - (EDGE - HALO)
    col = LANES * (f // FORWARD)
    corner_even, corner_odd = got_even[:EDGE, col : col + LANES], got_odd[:EDGE, col : col + LANES]
    left = jnp.where(even, got_odd[low : low + EDGE, :], got_even[low : low + EDGE, :])
    right = jnp.where(even, got_even[high : high + EDGE, :], got_odd[high : high + EDGE, :])
    left_halo = jnp.where(even, corner_odd, corner_even)
    right_halo = jnp.where(even, corner_even, corner_odd)
    return (
        windows(f, left[:, :LANES], left[:, LANES:], left_halo),
        windows(f, right[:, :LANES], right[:, LANES:], right_halo),
    )


def load_state(state, own, got_even, got_odd, base):
    rows = own.shape[2]
    extent = rows + 2 * EDGE
    for f in range(5):
        below, above = halo_windows(base + f, got_even, got_odd)
        for p in range(3):
            state[f, p, :PAD, :] = jnp.zeros((PAD, LANES), F32)
            state[f, p, PAD : PAD + EDGE, :] = below[p]
            state[f, p, PAD + EDGE : PAD + EDGE + rows, :] = own[base + f, p]
            state[f, p, PAD + EDGE + rows : PAD + extent, :] = above[p]
            state[f, p, PAD + extent :, :] = jnp.zeros((PAD, LANES), F32)


def velocities(state, media, span):
    for r in range(8 * span[0], 8 * span[1], 8):
        for p in range(3):

            def at(f, by=0):
                return state[f, p, r + PAD + by : r + PAD + by + 8, :]

            xx, xz, zz = at(2), at(4), at(3)
            b = media[0, p, r : r + 8, :]
            near = (xx - at(2, -1)) + (xz - turn(xz, 1))
            far = (at(2, 1) - at(2, -2)) + (turn(xz, -1) - turn(xz, 2))
            state[0, p, r + PAD : r + PAD + 8, :] = at(0) + b * (near + RATIO * far)
            near = (at(4, 1) - xz) + (turn(zz, -1) - zz)
            far = (at(4, 2) - at(4, -1)) + (turn(zz, -2) - turn(zz, 1))
            state[1, p, r + PAD : r + PAD + 8, :] = at(1) + b * (near + RATIO * far)


def stresses(state, media, span, update, keep):
    for r in range(8 * span[0], 8 * span[1], 8):
        for p in range(3):

            def at(f, by=0):
                return state[f, p, r + PAD + by : r + PAD + by + 8, :]

            vx, vz = at(0), at(1)
            exx = (at(0, 1) - vx) + RATIO * (at(0, 2) - at(0, -1))
            ezz = (vz - turn(vz, 1)) + RATIO * (turn(vz, -1) - turn(vz, 2))
            near = (turn(vx, -1) - vx) + (vz - at(1, -1))
            far = (turn(vx, -2) - turn(vx, 1)) + (at(1, 1) - at(1, -2))
            shear = near + RATIO * far
            keep(p, r - EDGE, exx, ezz, shear)
            if update:
                whole, lam, mu = (media[k, p, r : r + 8, :] for k in (1, 2, 3))
                state[2, p, r + PAD : r + PAD + 8, :] = at(2) + (whole * exx + lam * ezz)
                state[3, p, r + PAD : r + PAD + 8, :] = at(3) + (lam * exx + whole * ezz)
                state[4, p, r + PAD : r + PAD + 8, :] = at(4) + mu * shear


def spans(step, rows):
    tiles = (rows + 2 * EDGE) // 8
    if step == 0:
        return (0, tiles), (0, tiles)
    inner = (1, tiles - 1)
    return inner, inner if step < MOMENTS - 1 else (EDGE // 8, tiles - EDGE // 8)


def forward_kernel(
    own, got_even, got_odd, obs, owner, cell, media, saved, end_out, note_out, state, small, numbers, sems
):
    copies = fetch((obs, owner, cell), (small, numbers.at[0], numbers.at[1]), sems)
    rows = own.shape[2]
    parts = []
    for f in (5, 6, 7):
        below, above = halo_windows(f, got_even, got_odd)
        parts.append([(below[p], own[f, p], above[p]) for p in range(3)])
    for p in range(3):
        for k, at in enumerate((0, EDGE, EDGE + rows)):
            b, lam, mu = (NEAR * parts[i][p][k] for i in range(3))
            span = slice(at, at + b.shape[0])
            media[0, p, span, :] = b
            media[1, p, span, :] = lam + 2.0 * mu
            media[2, p, span, :] = lam
            media[3, p, span, :] = mu
    load_state(state, own, got_even, got_odd, 0)
    for step in range(MOMENTS):
        fast, slow = spans(step, rows)
        velocities(state, media, fast)

        def save(p, r, exx, ezz, shear):
            if 0 <= r < rows:
                saved[step, 0, p, r : r + 8, :] = exx
                saved[step, 1, p, r : r + 8, :] = ezz
                saved[step, 2, p, r : r + 8, :] = shear

        stresses(state, media, slow, step < MOMENTS - 1, save)

    top = PAD + EDGE
    for f in range(2):
        first, last = joined([state[f, p, top : top + rows, :] for p in range(3)])
        end_out[f, :, :LANES] = first
        end_out[f, :, LANES:] = last

    lane = lane_ids(rows)
    image = jnp.zeros((rows, LANES), F32)
    for step in range(MOMENTS):
        spot = FIBRE_ROWS * step
        here = (lane >= spot) & (lane < spot + FIBRE_ROWS)
        image = jnp.where(here, NEAR * turn(saved[step, 0, 0], spot - EDGE), image)
    turned = image.T
    half = IMAGE // 2
    rates = jnp.concatenate([turned[:half], turned[half:IMAGE]], axis=1)
    for copy in copies:
        copy.wait()
    seen = jnp.concatenate([small[:, :LANES], small[:, LANES:]], axis=0)
    along, row = channel_cells(numbers, rows)
    note_out[:half, :] = jnp.where(lax.axis_index("depth") == 0, rates, seen)
    for i, value in enumerate((along[:, :LANES], along[:, LANES:], row[:, :LANES], row[:, LANES:])):
        note_out[half + i : half + i + 1, :] = value.astype(F32)
    note_out[half + 4 :, :] = jnp.zeros((NOTE - half - 4, LANES), F32)


def channel_cells(numbers, rows):
    return numbers[0] * rows + lax.shift_right_logical(numbers[1], 2), numbers[1] & 3


def three(value):
    high = value.astype(BF16)
    rest = value - high.astype(F32)
    middle = rest.astype(BF16)
    low = (rest - middle.astype(F32)).astype(BF16)
    return [high, middle, low]


def add_up(value):
    return (value[2 * IMAGE : 3 * IMAGE] + value[IMAGE : 2 * IMAGE]) + value[:IMAGE]


def channel_sums(tracks, rows, notes, own_along):
    start = lax.axis_index("track") * rows - EDGE
    group = min(8, tracks)
    channels = own_along.shape[1]
    lane = lane_ids(8)
    half = LANES // 2
    wanted = jnp.concatenate([own_along, start + lax.broadcasted_iota(jnp.int32, (1, LANES), 1)], axis=1)
    row16 = row_ids(IMAGE, LANES)

    def body(number, carry):
        rate, image = carry
        base = number * group
        firsts, lasts = [], []
        for k in range(0, group, 2):
            a, b = notes[2 * (base + k), :8, :], notes[2 * (base + k + 1), :8, :]
            firsts.append(jnp.where(lane < half, a, turn(b, half)))
            lasts.append(jnp.where(lane < half, turn(a, half), b))
        strains = jnp.concatenate([jnp.concatenate(firsts, axis=1), jnp.concatenate(lasts, axis=1)], axis=0)
        spot = base * rows + row_ids(group * rows, channels + LANES)
        hot = (spot == wanted).astype(F32).astype(BF16)
        rate = rate + jnp.dot(jnp.concatenate(three(strains), axis=0), hot, preferred_element_type=F32)
        weights, hots = [], []
        for k in range(group):
            who = 2 * (base + k)
            for h in range(2):
                along = notes[who, 8 + h : 9 + h, :]
                mask = (row16 & 3).astype(F32) == notes[who, 10 + h : 11 + h, :]
                seen = [notes[who + 1, 4 * h + t : 4 * h + t + 1, :] for t in range(MOMENTS)]
                value = jnp.where(
                    row16 < 8,
                    jnp.where(row16 < 4, seen[0], seen[1]),
                    jnp.where(row16 < 12, seen[2], seen[3]),
                )
                pieces = three(jnp.where(mask, value, 0.0)) + [mask.astype(F32).astype(BF16)]
                weights.append(jnp.concatenate(pieces, axis=0))
                spot = (start + row_ids(LANES, LANES)).astype(F32)
                hots.append((spot == along).astype(F32).astype(BF16))
        image = image + lax.dot_general(
            jnp.concatenate(weights, axis=1),
            jnp.concatenate(hots, axis=1),
            (((1,), (1,)), ((), ())),
            preferred_element_type=F32,
        )
        return rate, image

    carry = jnp.zeros((3 * IMAGE, channels + LANES), F32), jnp.zeros((4 * IMAGE, LANES), F32)
    if tracks == group:
        carry = body(0, carry)
    else:
        carry = lax.fori_loop(0, tracks // group, body, carry)
    rate, image = carry
    return add_up(rate), add_up(image), image[3 * IMAGE :]


def adjoint_kernel(
    tracks, own, got_even, got_odd, media, saved, notes, obs, owner, cell,
    lambda_out, mu_out, residual_out, state, sums, small, numbers, sems,
):
    copies = fetch((obs, owner, cell), (small, numbers.at[0], numbers.at[1]), sems)
    rows = own.shape[2]
    extent = rows + 2 * EDGE
    depth = lax.axis_index("depth")
    load_state(state, own, got_even, got_odd, FORWARD)
    sums[...] = jnp.zeros(sums.shape, F32)
    for copy in copies:
        copy.wait()
    along, row = channel_cells(numbers, rows)
    rate, seen, count = channel_sums(tracks, rows, notes, along)
    channels = along.shape[1]
    at_own = jnp.where((row_ids(IMAGE, channels) & 3) == row, rate[:, :channels], 0.0)
    traces = [
        jnp.sum(at_own[4 * t : 4 * t + 4], axis=0, keepdims=True) - small[t : t + 1, :] for t in range(MOMENTS)
    ]
    residual_out[...] = jnp.where(
        depth == 0, jnp.concatenate(traces[:2], axis=0), jnp.concatenate(traces[2:], axis=0)
    )
    sources = count * rate[:, channels:] - seen
    turned = jnp.concatenate([sources, jnp.zeros((LANES - IMAGE, LANES), F32)], axis=0).T[:extent]
    lane = lane_ids(extent)
    here = (lane >= EDGE) & (lane < EDGE + FIBRE_ROWS) & (depth == 0)

    for step in range(MOMENTS):
        fast, slow = spans(step, rows)
        moment = MOMENTS - 1 - step
        added = jnp.where(here, turn(turned, EDGE - FIBRE_ROWS * moment), 0.0)
        state[2, 0, PAD : PAD + extent, :] += added
        velocities(state, media, fast)

        def gather(p, r, exx, ezz, shear):
            if 0 <= r < rows:
                fxx, fzz, fxz = (saved[moment, k, p, r : r + 8, :] for k in range(3))
                sums[0, p, r : r + 8, :] += (fxx + fzz) * (exx + ezz)
                sums[1, p, r : r + 8, :] += 2.0 * (fxx * exx + fzz * ezz) + fxz * shear

        stresses(state, media, slow, step < MOMENTS - 1, gather)

    for k, out in enumerate((lambda_out, mu_out)):
        first, last = joined([sums[k, p] for p in range(3)])
        out[:, :LANES] = (NEAR * NEAR) * first
        out[:, LANES:] = (NEAR * NEAR) * last


def per_device(
    velocity,
    stress,
    adjoint_velocity,
    adjoint_stress,
    buoyancy,
    lame_lambda,
    shear_modulus,
    observed,
    owner_track,
    fibre_cell,
):
    tracks = lax.axis_size("track")
    rows, depth_cells = buoyancy.shape
    moments, channels = observed.shape
    owner = owner_track.reshape(1, channels)
    cell = fibre_cell.reshape(1, channels)
    pinned = lambda array: pltpu.with_memory_space_constraint(array, pltpu.HBM)
    arrays = (velocity, stress, adjoint_velocity, adjoint_stress, buoyancy, lame_lambda, shear_modulus)
    arrays = tuple(pinned(array) for array in arrays)
    channel_arrays = (pinned(observed), pinned(owner), pinned(cell))
    extent = rows + 2 * EDGE
    block = jax.ShapeDtypeStruct((rows, depth_cells), F32)
    length = EDGE + HALO * FIELDS + EDGE - HALO
    edges = jax.ShapeDtypeStruct((length + (-length) % 8, depth_cells), F32)
    inside = pl.BlockSpec(memory_space=VMEM)
    outside = pl.BlockSpec(memory_space=pltpu.HBM)
    anywhere = pl.BlockSpec(memory_space=pl.ANY)
    held = [VMEM(a.shape, F32) for a in arrays]
    channel_scratch = [
        VMEM((moments, channels), F32),
        VMEM((2, 1, channels), jnp.int32),
        pltpu.SemaphoreType.DMA((3,)),
    ]

    to_depth, *to_track = pl.pallas_call(
        pack_kernel,
        out_shape=(block, edges, edges),
        in_specs=[outside] * 7,
        out_specs=(inside,) * 3,
        scratch_shapes=held + [pltpu.SemaphoreType.DMA((7,))],
        compiler_params=params(),
        cost_estimate=cost(2),
        name="pack",
    )(*arrays)

    depth_swap = [(0, 1), (1, 0)]
    got_depth = lax.ppermute(to_depth, "depth", depth_swap)
    to_track = pl.pallas_call(
        corner_kernel,
        out_shape=(edges, edges),
        in_specs=[anywhere] * 3,
        out_specs=(anywhere,) * 2,
        input_output_aliases={1: 0, 2: 1},
        scratch_shapes=[pltpu.SemaphoreType.DMA((2,))],
        compiler_params=params(),
        name="corners",
    )(got_depth, *to_track)
    swap = lambda k: [pair for i in range(k, tracks - 1, 2) for pair in ((i, i + 1), (i + 1, i))]
    got_odd = lax.ppermute(to_track[1], "track", swap(1))
    got_even = lax.ppermute(to_track[0], "track", swap(0))

    own = pl.pallas_call(
        own_kernel,
        out_shape=jax.ShapeDtypeStruct((FIELDS, 3, rows, LANES), F32),
        in_specs=[outside] * 7 + [inside],
        out_specs=inside,
        scratch_shapes=held + [pltpu.SemaphoreType.DMA((7,))],
        compiler_params=params(),
        cost_estimate=cost(2),
        name="own_planes",
    )(*arrays, got_depth)

    media, saved, velocity_end, note = pl.pallas_call(
        forward_kernel,
        out_shape=(
            jax.ShapeDtypeStruct((4, 3, extent, LANES), F32),
            jax.ShapeDtypeStruct((moments, 3, 3, rows, LANES), F32),
            jax.ShapeDtypeStruct(velocity.shape, F32),
            jax.ShapeDtypeStruct((NOTE, LANES), F32),
        ),
        in_specs=[inside] * 3 + [outside] * 3,
        out_specs=(inside,) * 4,
        scratch_shapes=[VMEM((5, 3, extent + 2 * PAD, LANES), F32)] + channel_scratch,
        compiler_params=params(),
        cost_estimate=cost(3),
        name="forward",
    )(own, got_even, got_odd, *channel_arrays)

    notes = lax.all_gather(note, ("track", "depth"), axis=0, tiled=False)

    gradient_lambda, gradient_mu, residual = pl.pallas_call(
        lambda *refs: adjoint_kernel(tracks, *refs),
        out_shape=(block, block, jax.ShapeDtypeStruct((moments // 2, channels), F32)),
        in_specs=[inside] * 6 + [outside] * 3,
        out_specs=(inside,) * 3,
        scratch_shapes=[
            VMEM((5, 3, extent + 2 * PAD, LANES), F32),
            VMEM((2, 3, rows, LANES), F32),
        ]
        + channel_scratch,
        compiler_params=params(),
        cost_estimate=cost(4),
        name="adjoint",
    )(own, got_even, got_odd, media, saved, notes, *channel_arrays)
    return gradient_lambda, gradient_mu, velocity_end, residual


def solution(mesh):
    return jax.shard_map(
        per_device,
        mesh=mesh,
        in_specs=(
            P("shots", "track", "depth"),
            P("shots", "track", "depth"),
            P("shots", "track", "depth"),
            P("shots", "track", "depth"),
            P("track", "depth"),
            P("track", "depth"),
            P("track", "depth"),
            P("shots", "track"),
            P("track", None),
            P("track"),
        ),
        out_specs=(
            P(("shots", "track"), "depth"),
            P(("shots", "track"), "depth"),
            P("shots", "track", "depth"),
            P(("shots", "depth"), "track"),
        ),
        check_vma=False,
    )
```

```python
import jax
import jax.numpy as jnp
from jax import lax
from jax.experimental import pallas as pl
from jax.experimental.pallas import tpu as pltpu
from jax.sharding import PartitionSpec as P

FIBRE_ROWS = 4
NEAR = 9.0 / 8.0
RATIO = -1.0 / 27.0
HALO = 12
EDGE = 16
LANES = 128
PAD = 8
FORWARD = 8
ADJOINT = 5
FIELDS = FORWARD + ADJOINT
MOMENTS = 4
IMAGE = MOMENTS * FIBRE_ROWS
VMEM = pltpu.VMEM
F32 = jnp.float32
BF16 = jnp.bfloat16


def lane_ids(rows):
    return lax.broadcasted_iota(jnp.int32, (rows, LANES), 1)


def row_ids(rows, columns):
    return lax.broadcasted_iota(jnp.int32, (rows, columns), 0)


def params():
    return pltpu.CompilerParams(vmem_limit_bytes=40 * 1024 * 1024)


def cost(microseconds):
    return pl.CostEstimate(flops=0, bytes_accessed=int(microseconds * 3.5e6), transcendentals=0)


def turn(value, by):
    return pltpu.roll(value, by % LANES, 1)


def is_even():
    return lax.rem(lax.axis_index("track"), 2) == 0


def fetch(sources, targets, sems):
    copies = [pltpu.make_async_copy(s, t, sems.at[i]) for i, (s, t) in enumerate(zip(sources, targets))]
    for copy in copies:
        copy.start()
    return copies


def field_refs(velocity, stress, adj_velocity, adj_stress, buoyancy, lame, shear):
    return (
        [velocity.at[i] for i in range(2)]
        + [stress.at[i] for i in range(3)]
        + [buoyancy, lame, shear]
        + [adj_velocity.at[i] for i in range(2)]
        + [adj_stress.at[i] for i in range(3)]
    )


def pack_kernel(*refs):
    sources, depth_out, edge_outs, held, sems = refs[:7], refs[7], refs[8:10], refs[10:17], refs[17]
    copies = fetch(sources, held, sems)
    depth = lax.axis_index("depth")
    even = is_even()
    fields = field_refs(*held)
    rows = fields[0].shape[0]
    lane = lane_ids(rows)
    tail = EDGE + HALO * FIELDS
    for out in edge_outs:
        out[:EDGE, :] = jnp.zeros((EDGE, 2 * LANES), F32)
        out[tail:, :] = jnp.zeros((out.shape[0] - tail, 2 * LANES), F32)
    for copy in copies:
        copy.wait()
    packed = [jnp.zeros((rows, LANES), F32) for _ in range(2)]
    for f, ref in enumerate(fields):
        first, last = ref[:, :LANES], ref[:, LANES:]
        group, place = divmod(f, FORWARD)
        spot = EDGE * place
        here = (lane >= spot) & (lane < spot + EDGE)
        edge = jnp.where(depth == 0, last, first)
        shift = lax.rem(spot + EDGE * (1 - depth), LANES)
        packed[group] = jnp.where(here, pltpu.roll(edge, shift, 1), packed[group])
        low, high = ref[:HALO, :], ref[rows - HALO :, :]
        at = EDGE + HALO * f
        edge_outs[0][at : at + HALO, :] = jnp.where(even, high, low)
        edge_outs[1][at : at + HALO, :] = jnp.where(even, low, high)
    depth_out[:, :LANES] = packed[0]
    depth_out[:, LANES:] = packed[1]


def corner_kernel(got, even_in, odd_in, even_out, odd_out, sems):
    rows = got.shape[0]
    is_odd = lax.rem(lax.axis_index("track"), 2)
    high, low = (rows - EDGE) * (1 - is_odd), (rows - EDGE) * is_odd
    one = pltpu.make_async_copy(
        got.at[pl.ds(pl.multiple_of(high, EDGE), EDGE), :], even_out.at[pl.ds(0, EDGE), :], sems.at[0]
    )
    two = pltpu.make_async_copy(
        got.at[pl.ds(pl.multiple_of(low, EDGE), EDGE), :], odd_out.at[pl.ds(0, EDGE), :], sems.at[1]
    )
    one.start()
    two.start()
    one.wait()
    two.wait()


def windows(f, first, last, halo):
    depth = lax.axis_index("depth")
    lane = lane_ids(first.shape[0])
    shift = lax.rem(LANES - EDGE * (f % FORWARD) + (LANES - EDGE) * (1 - depth), LANES)
    beside = pltpu.roll(halo, shift, 1)
    return [
        jnp.where(lane >= EDGE, turn(first, EDGE), jnp.where(depth == 1, beside, 0.0)),
        jnp.where(lane < LANES // 2, turn(first, LANES // 2), turn(last, LANES // 2)),
        jnp.where(lane < LANES - EDGE, turn(last, -EDGE), jnp.where(depth == 0, beside, 0.0)),
    ]


def joined(planes):
    lane = lane_ids(planes[0].shape[0])
    middle = turn(planes[1], LANES // 2)
    return (
        jnp.where(lane < 88, turn(planes[0], -EDGE), middle),
        jnp.where(lane < 40, middle, turn(planes[2], EDGE)),
    )


def own_kernel(*refs):
    sources, got_depth, planes_out, held, sems = refs[:7], refs[7], refs[8], refs[9:16], refs[16]
    for copy in fetch(sources, held, sems):
        copy.wait()
    for f, ref in enumerate(field_refs(*held)):
        col = LANES * (f // FORWARD)
        planes = windows(f, ref[:, :LANES], ref[:, LANES:], got_depth[:, col : col + LANES])
        for p in range(3):
            planes_out[f, p] = planes[p]


def halo_windows(f, got_even, got_odd):
    even = is_even()
    high = EDGE + HALO * f
    low = high - (EDGE - HALO)
    col = LANES * (f // FORWARD)
    corner_even, corner_odd = got_even[:EDGE, col : col + LANES], got_odd[:EDGE, col : col + LANES]
    left = jnp.where(even, got_odd[low : low + EDGE, :], got_even[low : low + EDGE, :])
    right = jnp.where(even, got_even[high : high + EDGE, :], got_odd[high : high + EDGE, :])
    left_halo = jnp.where(even, corner_odd, corner_even)
    right_halo = jnp.where(even, corner_even, corner_odd)
    return (
        windows(f, left[:, :LANES], left[:, LANES:], left_halo),
        windows(f, right[:, :LANES], right[:, LANES:], right_halo),
    )


def load_state(state, own, got_even, got_odd, base):
    rows = own.shape[2]
    extent = rows + 2 * EDGE
    for f in range(5):
        below, above = halo_windows(base + f, got_even, got_odd)
        for p in range(3):
            state[f, p, :PAD, :] = jnp.zeros((PAD, LANES), F32)
            state[f, p, PAD : PAD + EDGE, :] = below[p]
            state[f, p, PAD + EDGE : PAD + EDGE + rows, :] = own[base + f, p]
            state[f, p, PAD + EDGE + rows : PAD + extent, :] = above[p]
            state[f, p, PAD + extent :, :] = jnp.zeros((PAD, LANES), F32)


def velocities(state, media, span):
    for r in range(8 * span[0], 8 * span[1], 8):
        for p in range(3):

            def at(f, by=0):
                return state[f, p, r + PAD + by : r + PAD + by + 8, :]

            xx, xz, zz = at(2), at(4), at(3)
            b = media[0, p, r : r + 8, :]
            near = (xx - at(2, -1)) + (xz - turn(xz, 1))
            far = (at(2, 1) - at(2, -2)) + (turn(xz, -1) - turn(xz, 2))
            state[0, p, r + PAD : r + PAD + 8, :] = at(0) + b * (near + RATIO * far)
            near = (at(4, 1) - xz) + (turn(zz, -1) - zz)
            far = (at(4, 2) - at(4, -1)) + (turn(zz, -2) - turn(zz, 1))
            state[1, p, r + PAD : r + PAD + 8, :] = at(1) + b * (near + RATIO * far)


def stresses(state, media, span, update, keep):
    for r in range(8 * span[0], 8 * span[1], 8):
        for p in range(3):

            def at(f, by=0):
                return state[f, p, r + PAD + by : r + PAD + by + 8, :]

            vx, vz = at(0), at(1)
            exx = (at(0, 1) - vx) + RATIO * (at(0, 2) - at(0, -1))
            ezz = (vz - turn(vz, 1)) + RATIO * (turn(vz, -1) - turn(vz, 2))
            near = (turn(vx, -1) - vx) + (vz - at(1, -1))
            far = (turn(vx, -2) - turn(vx, 1)) + (at(1, 1) - at(1, -2))
            shear = near + RATIO * far
            keep(p, r - EDGE, exx, ezz, shear)
            if update:
                whole, lam, mu = (media[k, p, r : r + 8, :] for k in (1, 2, 3))
                state[2, p, r + PAD : r + PAD + 8, :] = at(2) + (whole * exx + lam * ezz)
                state[3, p, r + PAD : r + PAD + 8, :] = at(3) + (lam * exx + whole * ezz)
                state[4, p, r + PAD : r + PAD + 8, :] = at(4) + mu * shear


def spans(step, rows):
    tiles = (rows + 2 * EDGE) // 8
    if step == 0:
        return (0, tiles), (0, tiles)
    inner = (1, tiles - 1)
    return inner, inner if step < MOMENTS - 1 else (EDGE // 8, tiles - EDGE // 8)


def forward_kernel(
    own, got_even, got_odd, obs, owner, cell, media, saved, end_out, note_out, state, small, numbers, sems
):
    copies = fetch((obs, owner, cell), (small, numbers.at[0], numbers.at[1]), sems)
    rows = own.shape[2]
    parts = []
    for f in (5, 6, 7):
        below, above = halo_windows(f, got_even, got_odd)
        parts.append([(below[p], own[f, p], above[p]) for p in range(3)])
    for p in range(3):
        for k, at in enumerate((0, EDGE, EDGE + rows)):
            b, lam, mu = (NEAR * parts[i][p][k] for i in range(3))
            span = slice(at, at + b.shape[0])
            media[0, p, span, :] = b
            media[1, p, span, :] = lam + 2.0 * mu
            media[2, p, span, :] = lam
            media[3, p, span, :] = mu
    load_state(state, own, got_even, got_odd, 0)
    for step in range(MOMENTS):
        fast, slow = spans(step, rows)
        velocities(state, media, fast)

        def save(p, r, exx, ezz, shear):
            if 0 <= r < rows:
                saved[step, 0, p, r : r + 8, :] = exx
                saved[step, 1, p, r : r + 8, :] = ezz
                saved[step, 2, p, r : r + 8, :] = shear

        stresses(state, media, slow, step < MOMENTS - 1, save)

    top = PAD + EDGE
    for f in range(2):
        first, last = joined([state[f, p, top : top + rows, :] for p in range(3)])
        end_out[f, :, :LANES] = first
        end_out[f, :, LANES:] = last

    lane = lane_ids(rows)
    image = jnp.zeros((rows, LANES), F32)
    for step in range(MOMENTS):
        spot = FIBRE_ROWS * step
        here = (lane >= spot) & (lane < spot + FIBRE_ROWS)
        image = jnp.where(here, NEAR * turn(saved[step, 0, 0], spot - EDGE), image)
    turned = image.T
    half = IMAGE // 2
    rates = jnp.concatenate([turned[:half], turned[half:IMAGE]], axis=1)
    for copy in copies:
        copy.wait()
    seen = jnp.concatenate([small[:, :LANES], small[:, LANES:]], axis=0)
    along, row = channel_cells(numbers, rows)
    mine = jnp.where(lax.axis_index("depth") == 0, rates, seen)
    cells = jnp.concatenate([along[:, :LANES], along[:, LANES:], row[:, :LANES], row[:, LANES:]], axis=0)
    for i, value in enumerate((mine[:4], mine[4:], cells.astype(F32))):
        note_out[:, i] = jnp.broadcast_to(value[None], (note_out.shape[0], 4, LANES))


def channel_cells(numbers, rows):
    return numbers[0] * rows + lax.shift_right_logical(numbers[1], 2), numbers[1] & 3


def three(value):
    high = value.astype(BF16)
    rest = value - high.astype(F32)
    middle = rest.astype(BF16)
    low = (rest - middle.astype(F32)).astype(BF16)
    return [high, middle, low]


def add_up(value):
    return (value[2 * IMAGE : 3 * IMAGE] + value[IMAGE : 2 * IMAGE]) + value[:IMAGE]


def channel_sums(tracks, rows, notes, beside, own_along):
    start = lax.axis_index("track") * rows - EDGE
    surface = lax.axis_index("depth") == 0
    group = min(8, tracks)
    channels = own_along.shape[1]
    lane = lane_ids(8)
    half = LANES // 2
    wanted = jnp.concatenate([own_along, start + lax.broadcasted_iota(jnp.int32, (1, LANES), 1)], axis=1)
    row16 = row_ids(IMAGE, LANES)

    def body(number, carry):
        rate, image = carry
        base = number * group
        firsts, lasts = [], []
        mine = [[notes[base + k, i] for i in range(3)] for k in range(group)]
        other = [[beside[base + k, i] for i in range(3)] for k in range(group)]
        rates = [
            jnp.concatenate([jnp.where(surface, m[i], o[i]) for i in range(2)], axis=0) for m, o in zip(mine, other)
        ]
        traces = [[jnp.where(surface, o[i], m[i]) for i in range(2)] for m, o in zip(mine, other)]
        for k in range(0, group, 2):
            a, b = rates[k], rates[k + 1]
            firsts.append(jnp.where(lane < half, a, turn(b, half)))
            lasts.append(jnp.where(lane < half, turn(a, half), b))
        strains = jnp.concatenate([jnp.concatenate(firsts, axis=1), jnp.concatenate(lasts, axis=1)], axis=0)
        spot = base * rows + row_ids(group * rows, channels + LANES)
        hot = (spot == wanted).astype(F32).astype(BF16)
        rate = rate + jnp.dot(jnp.concatenate(three(strains), axis=0), hot, preferred_element_type=F32)
        weights, hots = [], []
        for k in range(group):
            for h in range(2):
                along = mine[k][2][h : h + 1]
                mask = (row16 & 3).astype(F32) == mine[k][2][2 + h : 3 + h]
                seen = [traces[k][h][t : t + 1] for t in range(MOMENTS)]
                value = jnp.where(
                    row16 < 8,
                    jnp.where(row16 < 4, seen[0], seen[1]),
                    jnp.where(row16 < 12, seen[2], seen[3]),
                )
                pieces = three(jnp.where(mask, value, 0.0)) + [mask.astype(F32).astype(BF16)]
                weights.append(jnp.concatenate(pieces, axis=0))
                spot = (start + row_ids(LANES, LANES)).astype(F32)
                hots.append((spot == along).astype(F32).astype(BF16))
        image = image + lax.dot_general(
            jnp.concatenate(weights, axis=1),
            jnp.concatenate(hots, axis=1),
            (((1,), (1,)), ((), ())),
            preferred_element_type=F32,
        )
        return rate, image

    carry = jnp.zeros((3 * IMAGE, channels + LANES), F32), jnp.zeros((4 * IMAGE, LANES), F32)
    if tracks == group:
        carry = body(0, carry)
    else:
        carry = lax.fori_loop(0, tracks // group, body, carry)
    rate, image = carry
    return add_up(rate), add_up(image), image[3 * IMAGE :]


def adjoint_kernel(
    tracks, own, got_even, got_odd, media, saved, notes, beside, obs, owner, cell,
    lambda_out, mu_out, residual_out, state, sums, small, numbers, sems,
):
    copies = fetch((obs, owner, cell), (small, numbers.at[0], numbers.at[1]), sems)
    rows = own.shape[2]
    extent = rows + 2 * EDGE
    depth = lax.axis_index("depth")
    load_state(state, own, got_even, got_odd, FORWARD)
    sums[...] = jnp.zeros(sums.shape, F32)
    for copy in copies:
        copy.wait()
    along, row = channel_cells(numbers, rows)
    rate, seen, count = channel_sums(tracks, rows, notes, beside, along)
    channels = along.shape[1]
    at_own = jnp.where((row_ids(IMAGE, channels) & 3) == row, rate[:, :channels], 0.0)
    traces = [
        jnp.sum(at_own[4 * t : 4 * t + 4], axis=0, keepdims=True) - small[t : t + 1, :] for t in range(MOMENTS)
    ]
    residual_out[...] = jnp.where(
        depth == 0, jnp.concatenate(traces[:2], axis=0), jnp.concatenate(traces[2:], axis=0)
    )
    sources = count * rate[:, channels:] - seen
    turned = jnp.concatenate([sources, jnp.zeros((LANES - IMAGE, LANES), F32)], axis=0).T[:extent]
    lane = lane_ids(extent)
    here = (lane >= EDGE) & (lane < EDGE + FIBRE_ROWS) & (depth == 0)

    for step in range(MOMENTS):
        fast, slow = spans(step, rows)
        moment = MOMENTS - 1 - step
        added = jnp.where(here, turn(turned, EDGE - FIBRE_ROWS * moment), 0.0)
        state[2, 0, PAD : PAD + extent, :] += added
        velocities(state, media, fast)

        def gather(p, r, exx, ezz, shear):
            if 0 <= r < rows:
                fxx, fzz, fxz = (saved[moment, k, p, r : r + 8, :] for k in range(3))
                sums[0, p, r : r + 8, :] += (fxx + fzz) * (exx + ezz)
                sums[1, p, r : r + 8, :] += 2.0 * (fxx * exx + fzz * ezz) + fxz * shear

        stresses(state, media, slow, step < MOMENTS - 1, gather)

    for k, out in enumerate((lambda_out, mu_out)):
        first, last = joined([sums[k, p] for p in range(3)])
        out[:, :LANES] = (NEAR * NEAR) * first
        out[:, LANES:] = (NEAR * NEAR) * last


def per_device(
    velocity,
    stress,
    adjoint_velocity,
    adjoint_stress,
    buoyancy,
    lame_lambda,
    shear_modulus,
    observed,
    owner_track,
    fibre_cell,
):
    tracks = lax.axis_size("track")
    rows, depth_cells = buoyancy.shape
    moments, channels = observed.shape
    owner = owner_track.reshape(1, channels)
    cell = fibre_cell.reshape(1, channels)
    pinned = lambda array: pltpu.with_memory_space_constraint(array, pltpu.HBM)
    arrays = (velocity, stress, adjoint_velocity, adjoint_stress, buoyancy, lame_lambda, shear_modulus)
    arrays = tuple(pinned(array) for array in arrays)
    channel_arrays = (pinned(observed), pinned(owner), pinned(cell))
    extent = rows + 2 * EDGE
    block = jax.ShapeDtypeStruct((rows, depth_cells), F32)
    length = EDGE + HALO * FIELDS + EDGE - HALO
    edges = jax.ShapeDtypeStruct((length + (-length) % 8, depth_cells), F32)
    inside = pl.BlockSpec(memory_space=VMEM)
    outside = pl.BlockSpec(memory_space=pltpu.HBM)
    anywhere = pl.BlockSpec(memory_space=pl.ANY)
    held = [VMEM(a.shape, F32) for a in arrays]
    channel_scratch = [
        VMEM((moments, channels), F32),
        VMEM((2, 1, channels), jnp.int32),
        pltpu.SemaphoreType.DMA((3,)),
    ]

    to_depth, *to_track = pl.pallas_call(
        pack_kernel,
        out_shape=(block, edges, edges),
        in_specs=[outside] * 7,
        out_specs=(inside,) * 3,
        scratch_shapes=held + [pltpu.SemaphoreType.DMA((7,))],
        compiler_params=params(),
        cost_estimate=cost(2),
        name="pack",
    )(*arrays)

    depth_swap = [(0, 1), (1, 0)]
    got_depth = lax.ppermute(to_depth, "depth", depth_swap)
    to_track = pl.pallas_call(
        corner_kernel,
        out_shape=(edges, edges),
        in_specs=[anywhere] * 3,
        out_specs=(anywhere,) * 2,
        input_output_aliases={1: 0, 2: 1},
        scratch_shapes=[pltpu.SemaphoreType.DMA((2,))],
        compiler_params=params(),
        name="corners",
    )(got_depth, *to_track)
    swap = lambda k: [pair for i in range(k, tracks - 1, 2) for pair in ((i, i + 1), (i + 1, i))]
    got_odd = lax.ppermute(to_track[1], "track", swap(1))
    got_even = lax.ppermute(to_track[0], "track", swap(0))

    own = pl.pallas_call(
        own_kernel,
        out_shape=jax.ShapeDtypeStruct((FIELDS, 3, rows, LANES), F32),
        in_specs=[outside] * 7 + [inside],
        out_specs=inside,
        scratch_shapes=held + [pltpu.SemaphoreType.DMA((7,))],
        compiler_params=params(),
        cost_estimate=cost(2),
        name="own_planes",
    )(*arrays, got_depth)

    media, saved, velocity_end, note = pl.pallas_call(
        forward_kernel,
        out_shape=(
            jax.ShapeDtypeStruct((4, 3, extent, LANES), F32),
            jax.ShapeDtypeStruct((moments, 3, 3, rows, LANES), F32),
            jax.ShapeDtypeStruct(velocity.shape, F32),
            jax.ShapeDtypeStruct((tracks, 3, 4, LANES), F32),
        ),
        in_specs=[inside] * 3 + [outside] * 3,
        out_specs=(inside,) * 4,
        scratch_shapes=[VMEM((5, 3, extent + 2 * PAD, LANES), F32)] + channel_scratch,
        compiler_params=params(),
        cost_estimate=cost(3),
        name="forward",
    )(own, got_even, got_odd, *channel_arrays)

    notes = lax.all_to_all(note, "track", split_axis=0, concat_axis=0, tiled=True)
    beside = lax.ppermute(notes, "depth", depth_swap)

    gradient_lambda, gradient_mu, residual = pl.pallas_call(
        lambda *refs: adjoint_kernel(tracks, *refs),
        out_shape=(block, block, jax.ShapeDtypeStruct((moments // 2, channels), F32)),
        in_specs=[inside] * 7 + [outside] * 3,
        out_specs=(inside,) * 3,
        scratch_shapes=[
            VMEM((5, 3, extent + 2 * PAD, LANES), F32),
            VMEM((2, 3, rows, LANES), F32),
        ]
        + channel_scratch,
        compiler_params=params(),
        cost_estimate=cost(4),
        name="adjoint",
    )(own, got_even, got_odd, media, saved, notes, beside, *channel_arrays)
    return gradient_lambda, gradient_mu, velocity_end, residual


def solution(mesh):
    return jax.shard_map(
        per_device,
        mesh=mesh,
        in_specs=(
            P("shots", "track", "depth"),
            P("shots", "track", "depth"),
            P("shots", "track", "depth"),
            P("shots", "track", "depth"),
            P("track", "depth"),
            P("track", "depth"),
            P("track", "depth"),
            P("shots", "track"),
            P("track", None),
            P("track"),
        ),
        out_specs=(
            P(("shots", "track"), "depth"),
            P(("shots", "track"), "depth"),
            P("shots", "track", "depth"),
            P(("shots", "depth"), "track"),
        ),
        check_vma=False,
    )
```

```python
import jax
import jax.numpy as jnp
from jax import lax
from jax.experimental import pallas as pl
from jax.experimental.pallas import tpu as pltpu
from jax.sharding import PartitionSpec as P

FIBRE_ROWS = 4
NEAR = 9.0 / 8.0
RATIO = -1.0 / 27.0
HALO = 12
EDGE = 16
LANES = 128
PAD = 8
FORWARD = 8
ADJOINT = 5
FIELDS = FORWARD + ADJOINT
MOMENTS = 4
IMAGE = MOMENTS * FIBRE_ROWS
VMEM = pltpu.VMEM
F32 = jnp.float32
BF16 = jnp.bfloat16


def lane_ids(rows):
    return lax.broadcasted_iota(jnp.int32, (rows, LANES), 1)


def row_ids(rows, columns):
    return lax.broadcasted_iota(jnp.int32, (rows, columns), 0)


def params():
    return pltpu.CompilerParams(vmem_limit_bytes=40 * 1024 * 1024)


def cost(microseconds):
    return pl.CostEstimate(flops=0, bytes_accessed=int(microseconds * 3.5e6), transcendentals=0)


def turn(value, by):
    return pltpu.roll(value, by % LANES, 1)


def is_even():
    return lax.rem(lax.axis_index("track"), 2) == 0


def fetch(sources, targets, sems):
    copies = [pltpu.make_async_copy(s, t, sems.at[i]) for i, (s, t) in enumerate(zip(sources, targets))]
    for copy in copies:
        copy.start()
    return copies


def field_refs(velocity, stress, adj_velocity, adj_stress, buoyancy, lame, shear):
    return (
        [velocity.at[i] for i in range(2)]
        + [stress.at[i] for i in range(3)]
        + [buoyancy, lame, shear]
        + [adj_velocity.at[i] for i in range(2)]
        + [adj_stress.at[i] for i in range(3)]
    )


def pack_kernel(*refs):
    sources, depth_out, edge_outs, held, sems = refs[:7], refs[7], refs[8:10], refs[10:17], refs[17]
    copies = fetch(sources, held, sems)
    depth = lax.axis_index("depth")
    even = is_even()
    fields = field_refs(*held)
    rows = fields[0].shape[0]
    lane = lane_ids(rows)
    tail = EDGE + HALO * FIELDS
    for out in edge_outs:
        out[:EDGE, :] = jnp.zeros((EDGE, 2 * LANES), F32)
        out[tail:, :] = jnp.zeros((out.shape[0] - tail, 2 * LANES), F32)
    for copy in copies:
        copy.wait()
    packed = [jnp.zeros((rows, LANES), F32) for _ in range(2)]
    for f, ref in enumerate(fields):
        first, last = ref[:, :LANES], ref[:, LANES:]
        group, place = divmod(f, FORWARD)
        spot = EDGE * place
        here = (lane >= spot) & (lane < spot + EDGE)
        edge = jnp.where(depth == 0, last, first)
        shift = lax.rem(spot + EDGE * (1 - depth), LANES)
        packed[group] = jnp.where(here, pltpu.roll(edge, shift, 1), packed[group])
        low, high = ref[:HALO, :], ref[rows - HALO :, :]
        at = EDGE + HALO * f
        edge_outs[0][at : at + HALO, :] = jnp.where(even, high, low)
        edge_outs[1][at : at + HALO, :] = jnp.where(even, low, high)
    depth_out[:, :LANES] = packed[0]
    depth_out[:, LANES:] = packed[1]


def corner_kernel(got, even_in, odd_in, even_out, odd_out, sems):
    rows = got.shape[0]
    is_odd = lax.rem(lax.axis_index("track"), 2)
    high, low = (rows - EDGE) * (1 - is_odd), (rows - EDGE) * is_odd
    one = pltpu.make_async_copy(
        got.at[pl.ds(pl.multiple_of(high, EDGE), EDGE), :], even_out.at[pl.ds(0, EDGE), :], sems.at[0]
    )
    two = pltpu.make_async_copy(
        got.at[pl.ds(pl.multiple_of(low, EDGE), EDGE), :], odd_out.at[pl.ds(0, EDGE), :], sems.at[1]
    )
    one.start()
    two.start()
    one.wait()
    two.wait()


def windows(f, first, last, halo):
    depth = lax.axis_index("depth")
    lane = lane_ids(first.shape[0])
    shift = lax.rem(LANES - EDGE * (f % FORWARD) + (LANES - EDGE) * (1 - depth), LANES)
    beside = pltpu.roll(halo, shift, 1)
    return [
        jnp.where(lane >= EDGE, turn(first, EDGE), jnp.where(depth == 1, beside, 0.0)),
        jnp.where(lane < LANES // 2, turn(first, LANES // 2), turn(last, LANES // 2)),
        jnp.where(lane < LANES - EDGE, turn(last, -EDGE), jnp.where(depth == 0, beside, 0.0)),
    ]


def joined(planes):
    lane = lane_ids(planes[0].shape[0])
    middle = turn(planes[1], LANES // 2)
    return (
        jnp.where(lane < 88, turn(planes[0], -EDGE), middle),
        jnp.where(lane < 40, middle, turn(planes[2], EDGE)),
    )


def own_kernel(*refs):
    sources, got_depth, planes_out, held, sems = refs[:7], refs[7], refs[8], refs[9:16], refs[16]
    for copy in fetch(sources, held, sems):
        copy.wait()
    for f, ref in enumerate(field_refs(*held)):
        col = LANES * (f // FORWARD)
        planes = windows(f, ref[:, :LANES], ref[:, LANES:], got_depth[:, col : col + LANES])
        for p in range(3):
            planes_out[f, p] = planes[p]


def halo_windows(f, got_even, got_odd):
    even = is_even()
    high = EDGE + HALO * f
    low = high - (EDGE - HALO)
    col = LANES * (f // FORWARD)
    corner_even, corner_odd = got_even[:EDGE, col : col + LANES], got_odd[:EDGE, col : col + LANES]
    left = jnp.where(even, got_odd[low : low + EDGE, :], got_even[low : low + EDGE, :])
    right = jnp.where(even, got_even[high : high + EDGE, :], got_odd[high : high + EDGE, :])
    left_halo = jnp.where(even, corner_odd, corner_even)
    right_halo = jnp.where(even, corner_even, corner_odd)
    return (
        windows(f, left[:, :LANES], left[:, LANES:], left_halo),
        windows(f, right[:, :LANES], right[:, LANES:], right_halo),
    )


def load_state(state, own, got_even, got_odd, base, planes):
    rows = own.shape[2]
    extent = rows + 2 * EDGE
    for f in range(5):
        below, above = halo_windows(base + f, got_even, got_odd)
        for i, p in enumerate(planes):
            state[f, i, :PAD, :] = jnp.zeros((PAD, LANES), F32)
            state[f, i, PAD : PAD + EDGE, :] = below[p]
            state[f, i, PAD + EDGE : PAD + EDGE + rows, :] = own[base + f, p]
            state[f, i, PAD + EDGE + rows : PAD + extent, :] = above[p]
            state[f, i, PAD + extent :, :] = jnp.zeros((PAD, LANES), F32)


def velocities(state, media, span):
    for r in range(8 * span[0], 8 * span[1], 8):
        for i in range(state.shape[1]):

            def at(f, by=0):
                return state[f, i, r + PAD + by : r + PAD + by + 8, :]

            xx, xz, zz = at(2), at(4), at(3)
            b = media[0, i, r : r + 8, :]
            near = (xx - at(2, -1)) + (xz - turn(xz, 1))
            far = (at(2, 1) - at(2, -2)) + (turn(xz, -1) - turn(xz, 2))
            state[0, i, r + PAD : r + PAD + 8, :] = at(0) + b * (near + RATIO * far)
            near = (at(4, 1) - xz) + (turn(zz, -1) - zz)
            far = (at(4, 2) - at(4, -1)) + (turn(zz, -2) - turn(zz, 1))
            state[1, i, r + PAD : r + PAD + 8, :] = at(1) + b * (near + RATIO * far)


def stresses(state, media, span, update, keep):
    for r in range(8 * span[0], 8 * span[1], 8):
        for i in range(state.shape[1]):

            def at(f, by=0):
                return state[f, i, r + PAD + by : r + PAD + by + 8, :]

            vx, vz = at(0), at(1)
            exx = (at(0, 1) - vx) + RATIO * (at(0, 2) - at(0, -1))
            ezz = (vz - turn(vz, 1)) + RATIO * (turn(vz, -1) - turn(vz, 2))
            near = (turn(vx, -1) - vx) + (vz - at(1, -1))
            far = (turn(vx, -2) - turn(vx, 1)) + (at(1, 1) - at(1, -2))
            shear = near + RATIO * far
            keep(i, r - EDGE, exx, ezz, shear)
            if update:
                whole, lam, mu = (media[k, i, r : r + 8, :] for k in (1, 2, 3))
                state[2, i, r + PAD : r + PAD + 8, :] = at(2) + (whole * exx + lam * ezz)
                state[3, i, r + PAD : r + PAD + 8, :] = at(3) + (lam * exx + whole * ezz)
                state[4, i, r + PAD : r + PAD + 8, :] = at(4) + mu * shear


def spans(step, rows):
    tiles = (rows + 2 * EDGE) // 8
    if step == 0:
        return (0, tiles), (0, tiles)
    inner = (1, tiles - 1)
    return inner, inner if step < MOMENTS - 1 else (EDGE // 8, tiles - EDGE // 8)


def run_forward(own, got_even, got_odd, media, saved, state, planes):
    rows = own.shape[2]
    parts = []
    for f in (5, 6, 7):
        below, above = halo_windows(f, got_even, got_odd)
        parts.append([(below[p], own[f, p], above[p]) for p in planes])
    for i in range(len(planes)):
        for k, at in enumerate((0, EDGE, EDGE + rows)):
            b, lam, mu = (NEAR * parts[m][i][k] for m in range(3))
            span = slice(at, at + b.shape[0])
            media[0, i, span, :] = b
            media[1, i, span, :] = lam + 2.0 * mu
            media[2, i, span, :] = lam
            media[3, i, span, :] = mu
    load_state(state, own, got_even, got_odd, 0, planes)
    for step in range(MOMENTS):
        fast, slow = spans(step, rows)
        velocities(state, media, fast)

        def save(i, r, exx, ezz, shear):
            if 0 <= r < rows:
                saved[step, 0, i, r : r + 8, :] = exx
                saved[step, 1, i, r : r + 8, :] = ezz
                saved[step, 2, i, r : r + 8, :] = shear

        stresses(state, media, slow, step < MOMENTS - 1, save)


def forward_top_kernel(own, got_even, got_odd, media, saved, end_out, image_out, state):
    run_forward(own, got_even, got_odd, media, saved, state, (0,))
    rows = own.shape[2]
    top = PAD + EDGE
    for f in range(2):
        end_out[f] = state[f, 0, top : top + rows, :]
    lane = lane_ids(rows)
    image = jnp.zeros((rows, LANES), F32)
    for step in range(MOMENTS):
        spot = FIBRE_ROWS * step
        here = (lane >= spot) & (lane < spot + FIBRE_ROWS)
        image = jnp.where(here, NEAR * turn(saved[step, 0, 0], spot - EDGE), image)
    turned = image.T
    half = IMAGE // 2
    image_out[...] = jnp.concatenate([turned[:half], turned[half:IMAGE]], axis=1)


def forward_rest_kernel(own, got_even, got_odd, top_end, media, saved, end_out, state):
    run_forward(own, got_even, got_odd, media, saved, state, (1, 2))
    rows = own.shape[2]
    top = PAD + EDGE
    for f in range(2):
        rest = [state[f, i, top : top + rows, :] for i in range(2)]
        first, last = joined([top_end[f]] + rest)
        end_out[f, :, :LANES] = first
        end_out[f, :, LANES:] = last


def note_kernel(rows, image, image_beside, obs, owner, cell, note_out):
    rates = jnp.where(lax.axis_index("depth") == 0, image[...], image_beside[...])
    seen = obs[...]
    along, row = channel_cells(owner, cell, rows)
    cells = jnp.concatenate([along[:, :LANES], along[:, LANES:], row[:, :LANES], row[:, LANES:]], axis=0)
    for i, value in enumerate((rates[:4], rates[4:], seen[:, :LANES], seen[:, LANES:], cells.astype(F32))):
        note_out[:, i] = jnp.broadcast_to(value[None], (note_out.shape[0], 4, LANES))


def channel_cells(owner, cell, rows):
    return owner[...] * rows + lax.shift_right_logical(cell[...], 2), cell[...] & 3


def three(value):
    high = value.astype(BF16)
    rest = value - high.astype(F32)
    middle = rest.astype(BF16)
    low = (rest - middle.astype(F32)).astype(BF16)
    return [high, middle, low]


def add_up(value):
    return (value[2 * IMAGE : 3 * IMAGE] + value[IMAGE : 2 * IMAGE]) + value[:IMAGE]


def channel_sums(tracks, rows, notes, own_along):
    start = lax.axis_index("track") * rows - EDGE
    group = min(8, tracks)
    channels = own_along.shape[1]
    lane = lane_ids(8)
    half = LANES // 2
    wanted = jnp.concatenate([own_along, start + lax.broadcasted_iota(jnp.int32, (1, LANES), 1)], axis=1)
    row16 = row_ids(IMAGE, LANES)

    def body(number, carry):
        rate, image = carry
        base = number * group
        firsts, lasts = [], []
        blocks = [[notes[base + k, i] for i in range(5)] for k in range(group)]
        rates = [jnp.concatenate(block[:2], axis=0) for block in blocks]
        for k in range(0, group, 2):
            a, b = rates[k], rates[k + 1]
            firsts.append(jnp.where(lane < half, a, turn(b, half)))
            lasts.append(jnp.where(lane < half, turn(a, half), b))
        strains = jnp.concatenate([jnp.concatenate(firsts, axis=1), jnp.concatenate(lasts, axis=1)], axis=0)
        spot = base * rows + row_ids(group * rows, channels + LANES)
        hot = (spot == wanted).astype(F32).astype(BF16)
        rate = rate + jnp.dot(jnp.concatenate(three(strains), axis=0), hot, preferred_element_type=F32)
        weights, hots = [], []
        for k in range(group):
            for h in range(2):
                along = blocks[k][4][h : h + 1]
                mask = (row16 & 3).astype(F32) == blocks[k][4][2 + h : 3 + h]
                seen = [blocks[k][2 + h][t : t + 1] for t in range(MOMENTS)]
                value = jnp.where(
                    row16 < 8,
                    jnp.where(row16 < 4, seen[0], seen[1]),
                    jnp.where(row16 < 12, seen[2], seen[3]),
                )
                pieces = three(jnp.where(mask, value, 0.0)) + [mask.astype(F32).astype(BF16)]
                weights.append(jnp.concatenate(pieces, axis=0))
                spot = (start + row_ids(LANES, LANES)).astype(F32)
                hots.append((spot == along).astype(F32).astype(BF16))
        image = image + lax.dot_general(
            jnp.concatenate(weights, axis=1),
            jnp.concatenate(hots, axis=1),
            (((1,), (1,)), ((), ())),
            preferred_element_type=F32,
        )
        return rate, image

    carry = jnp.zeros((3 * IMAGE, channels + LANES), F32), jnp.zeros((4 * IMAGE, LANES), F32)
    if tracks == group:
        carry = body(0, carry)
    else:
        carry = lax.fori_loop(0, tracks // group, body, carry)
    rate, image = carry
    return add_up(rate), add_up(image), image[3 * IMAGE :]


def run_adjoint(media, saved, state, sums, inject=None):
    rows = sums.shape[2]
    sums[...] = jnp.zeros(sums.shape, F32)
    for step in range(MOMENTS):
        fast, slow = spans(step, rows)
        moment = MOMENTS - 1 - step
        if inject is not None:
            inject(moment)
        velocities(state, media, fast)

        def gather(i, r, exx, ezz, shear):
            if 0 <= r < rows:
                fxx, fzz, fxz = (saved[moment, k, i, r : r + 8, :] for k in range(3))
                sums[0, i, r : r + 8, :] += (fxx + fzz) * (exx + ezz)
                sums[1, i, r : r + 8, :] += 2.0 * (fxx * exx + fzz * ezz) + fxz * shear

        stresses(state, media, slow, step < MOMENTS - 1, gather)


def adjoint_rest_kernel(own, got_even, got_odd, media, saved, note, sums, state):
    del note
    load_state(state, own, got_even, got_odd, FORWARD, (1, 2))
    run_adjoint(media, saved, state, sums)


def adjoint_top_kernel(
    tracks, own, got_even, got_odd, media, saved, notes, rest, obs, owner, cell,
    lambda_out, mu_out, residual_out, state, sums,
):
    rows = own.shape[2]
    extent = rows + 2 * EDGE
    depth = lax.axis_index("depth")
    load_state(state, own, got_even, got_odd, FORWARD, (0,))
    along, row = channel_cells(owner, cell, rows)
    rate, seen, count = channel_sums(tracks, rows, notes, along)
    channels = along.shape[1]
    at_own = jnp.where((row_ids(IMAGE, channels) & 3) == row, rate[:, :channels], 0.0)
    traces = [
        jnp.sum(at_own[4 * t : 4 * t + 4], axis=0, keepdims=True) - obs[t : t + 1, :] for t in range(MOMENTS)
    ]
    residual_out[...] = jnp.where(
        depth == 0, jnp.concatenate(traces[:2], axis=0), jnp.concatenate(traces[2:], axis=0)
    )
    sources = count * rate[:, channels:] - seen
    turned = jnp.concatenate([sources, jnp.zeros((LANES - IMAGE, LANES), F32)], axis=0).T[:extent]
    lane = lane_ids(extent)
    here = (lane >= EDGE) & (lane < EDGE + FIBRE_ROWS) & (depth == 0)

    def inject(moment):
        added = jnp.where(here, turn(turned, EDGE - FIBRE_ROWS * moment), 0.0)
        state[2, 0, PAD : PAD + extent, :] += added

    run_adjoint(media, saved, state, sums, inject)
    for k, out in enumerate((lambda_out, mu_out)):
        first, last = joined([sums[k, 0], rest[k, 0], rest[k, 1]])
        out[:, :LANES] = (NEAR * NEAR) * first
        out[:, LANES:] = (NEAR * NEAR) * last


def per_device(
    velocity,
    stress,
    adjoint_velocity,
    adjoint_stress,
    buoyancy,
    lame_lambda,
    shear_modulus,
    observed,
    owner_track,
    fibre_cell,
):
    tracks = lax.axis_size("track")
    rows, depth_cells = buoyancy.shape
    moments, channels = observed.shape
    owner = owner_track.reshape(1, channels)
    cell = fibre_cell.reshape(1, channels)
    pinned = lambda array: pltpu.with_memory_space_constraint(array, pltpu.HBM)
    arrays = (velocity, stress, adjoint_velocity, adjoint_stress, buoyancy, lame_lambda, shear_modulus)
    arrays = tuple(pinned(array) for array in arrays)
    channel_arrays = (observed, owner, cell)
    extent = rows + 2 * EDGE
    block = jax.ShapeDtypeStruct((rows, depth_cells), F32)
    length = EDGE + HALO * FIELDS + EDGE - HALO
    edges = jax.ShapeDtypeStruct((length + (-length) % 8, depth_cells), F32)
    inside = pl.BlockSpec(memory_space=VMEM)
    outside = pl.BlockSpec(memory_space=pltpu.HBM)
    anywhere = pl.BlockSpec(memory_space=pl.ANY)
    held = [VMEM(a.shape, F32) for a in arrays]
    to_depth, *to_track = pl.pallas_call(
        pack_kernel,
        out_shape=(block, edges, edges),
        in_specs=[outside] * 7,
        out_specs=(inside,) * 3,
        scratch_shapes=held + [pltpu.SemaphoreType.DMA((7,))],
        compiler_params=params(),
        cost_estimate=cost(2),
        name="pack",
    )(*arrays)

    depth_swap = [(0, 1), (1, 0)]
    got_depth = lax.ppermute(to_depth, "depth", depth_swap)
    to_track = pl.pallas_call(
        corner_kernel,
        out_shape=(edges, edges),
        in_specs=[anywhere] * 3,
        out_specs=(anywhere,) * 2,
        input_output_aliases={1: 0, 2: 1},
        scratch_shapes=[pltpu.SemaphoreType.DMA((2,))],
        compiler_params=params(),
        name="corners",
    )(got_depth, *to_track)
    swap = lambda k: [pair for i in range(k, tracks - 1, 2) for pair in ((i, i + 1), (i + 1, i))]
    got_odd = lax.ppermute(to_track[1], "track", swap(1))
    got_even = lax.ppermute(to_track[0], "track", swap(0))

    own = pl.pallas_call(
        own_kernel,
        out_shape=jax.ShapeDtypeStruct((FIELDS, 3, rows, LANES), F32),
        in_specs=[outside] * 7 + [inside],
        out_specs=inside,
        scratch_shapes=held + [pltpu.SemaphoreType.DMA((7,))],
        compiler_params=params(),
        cost_estimate=cost(2),
        name="own_planes",
    )(*arrays, got_depth)

    def media_of(planes):
        return jax.ShapeDtypeStruct((4, planes, extent, LANES), F32)

    def saved_of(planes):
        return jax.ShapeDtypeStruct((moments, 3, planes, rows, LANES), F32)

    def state_of(planes):
        return VMEM((5, planes, extent + 2 * PAD, LANES), F32)

    media_top, saved_top, top_end, image = pl.pallas_call(
        forward_top_kernel,
        out_shape=(
            media_of(1),
            saved_of(1),
            jax.ShapeDtypeStruct((2, rows, LANES), F32),
            jax.ShapeDtypeStruct((IMAGE // 2, LANES), F32),
        ),
        in_specs=[inside] * 3,
        out_specs=(inside,) * 4,
        scratch_shapes=[state_of(1)],
        compiler_params=params(),
        cost_estimate=cost(1),
        name="forward_top",
    )(own, got_even, got_odd)
    image_beside = lax.ppermute(image, "depth", depth_swap)
    media_rest, saved_rest, velocity_end = pl.pallas_call(
        forward_rest_kernel,
        out_shape=(media_of(2), saved_of(2), jax.ShapeDtypeStruct(velocity.shape, F32)),
        in_specs=[inside] * 4,
        out_specs=(inside,) * 3,
        scratch_shapes=[state_of(2)],
        compiler_params=params(),
        cost_estimate=cost(2),
        name="forward_rest",
    )(own, got_even, got_odd, top_end)
    note = pl.pallas_call(
        lambda *refs: note_kernel(rows, *refs),
        out_shape=jax.ShapeDtypeStruct((tracks, 5, 4, LANES), F32),
        in_specs=[inside] * 5,
        out_specs=inside,
        compiler_params=params(),
        name="note",
    )(image, image_beside, *channel_arrays)
    notes = lax.all_to_all(note, "track", split_axis=0, concat_axis=0, tiled=True)
    rest = pl.pallas_call(
        adjoint_rest_kernel,
        out_shape=jax.ShapeDtypeStruct((2, 2, rows, LANES), F32),
        in_specs=[inside] * 5 + [anywhere],
        out_specs=inside,
        scratch_shapes=[state_of(2)],
        compiler_params=params(),
        cost_estimate=cost(3),
        name="adjoint_rest",
    )(own, got_even, got_odd, media_rest, saved_rest, note)
    gradient_lambda, gradient_mu, residual = pl.pallas_call(
        lambda *refs: adjoint_top_kernel(tracks, *refs),
        out_shape=(block, block, jax.ShapeDtypeStruct((moments // 2, channels), F32)),
        in_specs=[inside] * 10,
        out_specs=(inside,) * 3,
        scratch_shapes=[state_of(1), VMEM((2, 1, rows, LANES), F32)],
        compiler_params=params(),
        cost_estimate=cost(2),
        name="adjoint_top",
    )(own, got_even, got_odd, media_top, saved_top, notes, rest, *channel_arrays)
    return gradient_lambda, gradient_mu, velocity_end, residual


def solution(mesh):
    return jax.shard_map(
        per_device,
        mesh=mesh,
        in_specs=(
            P("shots", "track", "depth"),
            P("shots", "track", "depth"),
            P("shots", "track", "depth"),
            P("shots", "track", "depth"),
            P("track", "depth"),
            P("track", "depth"),
            P("track", "depth"),
            P("shots", "track"),
            P("track", None),
            P("track"),
        ),
        out_specs=(
            P(("shots", "track"), "depth"),
            P(("shots", "track"), "depth"),
            P("shots", "track", "depth"),
            P(("shots", "depth"), "track"),
        ),
        check_vma=False,
    )
```

```python
import jax
import jax.numpy as jnp
from jax import lax
from jax.experimental import pallas as pl
from jax.experimental.pallas import tpu as pltpu
from jax.sharding import PartitionSpec as P

FIBRE_ROWS = 4
NEAR = 9.0 / 8.0
RATIO = -1.0 / 27.0
HALO = 12
EDGE = 16
LANES = 128
PAD = 8
FORWARD = 8
ADJOINT = 5
FIELDS = FORWARD + ADJOINT
OUTER = EDGE - HALO
INNER = EDGE + HALO * ADJOINT
MOMENTS = 4
IMAGE = MOMENTS * FIBRE_ROWS
VMEM = pltpu.VMEM
F32 = jnp.float32
BF16 = jnp.bfloat16


def lane_ids(rows):
    return lax.broadcasted_iota(jnp.int32, (rows, LANES), 1)


def row_ids(rows, columns):
    return lax.broadcasted_iota(jnp.int32, (rows, columns), 0)


def params():
    return pltpu.CompilerParams(vmem_limit_bytes=40 * 1024 * 1024)


def cost(microseconds):
    return pl.CostEstimate(flops=0, bytes_accessed=int(microseconds * 3.5e6), transcendentals=0)


def turn(value, by):
    return pltpu.roll(value, by % LANES, 1)


def is_even():
    return lax.rem(lax.axis_index("track"), 2) == 0


def fetch(sources, targets, sems):
    copies = [pltpu.make_async_copy(s, t, sems.at[i]) for i, (s, t) in enumerate(zip(sources, targets))]
    for copy in copies:
        copy.start()
    return copies


def field_copies(arrays, held, sems):
    velocity, stress, adj_velocity, adj_stress, buoyancy, lame, shear = arrays
    sources = (velocity, stress, buoyancy, lame, shear, adj_velocity, adj_stress)
    targets = (
        held.at[pl.ds(0, 2)],
        held.at[pl.ds(2, 3)],
        held.at[5],
        held.at[6],
        held.at[7],
        held.at[pl.ds(8, 2)],
        held.at[pl.ds(10, 3)],
    )
    return fetch(sources, targets, sems)


def outer_kernel(velocity, stress, buoyancy, lame, shear, even_out, odd_out, strips, sems):
    depth = lax.axis_index("depth")
    even = is_even()
    rows = buoyancy.shape[0]
    lanes = pl.ds(pl.multiple_of(depth * LANES, LANES), LANES)
    sources, targets = [], []
    for side, row in enumerate((0, rows - EDGE)):
        span = pl.ds(row, EDGE)
        sources += [array.at[:, span, lanes] for array in (velocity, stress)]
        targets += [strips.at[side, pl.ds(0, 2)], strips.at[side, pl.ds(2, 3)]]
        sources += [array.at[span, lanes] for array in (buoyancy, lame, shear)]
        targets += [strips.at[side, f] for f in (5, 6, 7)]
    copies = fetch(sources, targets, sems)
    for out in (even_out, odd_out):
        out[:OUTER, :] = jnp.zeros((OUTER, LANES), F32)
        out[OUTER + HALO * FORWARD :, :] = jnp.zeros((EDGE - HALO, LANES), F32)
    for copy in copies:
        copy.wait()
    for f in range(FORWARD):
        low, high = strips[0, f, :HALO, :], strips[1, f, EDGE - HALO :, :]
        at = OUTER + HALO * f
        even_out[at : at + HALO, :] = jnp.where(even, high, low)
        odd_out[at : at + HALO, :] = jnp.where(even, low, high)


def pack_kernel(*refs):
    arrays, (held, depth_out, even_out, odd_out), sems = refs[:7], refs[8:12], refs[12]
    copies = field_copies(arrays, held, sems)
    depth = lax.axis_index("depth")
    even = is_even()
    rows = held.shape[1]
    lane = lane_ids(rows)
    tail = INNER + HALO * 4
    for out in (even_out, odd_out):
        out[:EDGE, :] = jnp.zeros((EDGE, 2 * LANES), F32)
        out[tail:, :] = jnp.zeros((out.shape[0] - tail, 2 * LANES), F32)
    for copy in copies:
        copy.wait()
    packed = [jnp.zeros((rows, LANES), F32) for _ in range(2)]
    for f in range(FIELDS):
        group, place = divmod(f, FORWARD)
        spot = EDGE * place
        here = (lane >= spot) & (lane < spot + EDGE)
        edge = jnp.where(depth == 0, held[f, :, LANES:], held[f, :, :LANES])
        shift = lax.rem(spot + EDGE * (1 - depth), LANES)
        packed[group] = jnp.where(here, pltpu.roll(edge, shift, 1), packed[group])
        if f < FORWARD:
            low, high = edge[:HALO], edge[rows - HALO :]
            at, lanes = INNER + HALO * (f % 4), slice(LANES * (f // 4), LANES * (f // 4) + LANES)
        else:
            low, high = held[f, :HALO, :], held[f, rows - HALO :, :]
            at, lanes = EDGE + HALO * place, slice(0, 2 * LANES)
        even_out[at : at + HALO, lanes] = jnp.where(even, high, low)
        odd_out[at : at + HALO, lanes] = jnp.where(even, low, high)
    depth_out[:, :LANES] = packed[0]
    depth_out[:, LANES:] = packed[1]


def corner_kernel(got, even_in, odd_in, even_out, odd_out, sems):
    rows = got.shape[0]
    is_odd = lax.rem(lax.axis_index("track"), 2)
    high, low = (rows - EDGE) * (1 - is_odd), (rows - EDGE) * is_odd
    one = pltpu.make_async_copy(
        got.at[pl.ds(pl.multiple_of(high, EDGE), EDGE), :], even_out.at[pl.ds(0, EDGE), :], sems.at[0]
    )
    two = pltpu.make_async_copy(
        got.at[pl.ds(pl.multiple_of(low, EDGE), EDGE), :], odd_out.at[pl.ds(0, EDGE), :], sems.at[1]
    )
    one.start()
    two.start()
    one.wait()
    two.wait()


def window(plane, f, outer, other, halo):
    depth = lax.axis_index("depth")
    surface = depth == 0
    lane = lane_ids(outer.shape[0])
    low = jnp.where(surface, lane, LANES - 1 - lane)
    if plane == 0:
        shift = jnp.where(surface, EDGE, LANES - EDGE)
        return jnp.where(low >= EDGE, pltpu.roll(outer, shift, 1), 0.0)
    if plane == 1:
        return jnp.where(low < LANES // 2, turn(outer, LANES // 2), turn(other, LANES // 2))
    shift = jnp.where(surface, LANES - EDGE, EDGE)
    beside = lax.rem(LANES - EDGE * (f % FORWARD) + (LANES - EDGE) * (1 - depth), LANES)
    return jnp.where(low < LANES - EDGE, pltpu.roll(other, shift, 1), pltpu.roll(halo, beside, 1))


def split(value):
    surface = lax.axis_index("depth") == 0
    first, last = value[:, :LANES], value[:, LANES:]
    return jnp.where(surface, first, last), jnp.where(surface, last, first)


def joined(outer, middle, inner):
    surface = lax.axis_index("depth") == 0
    lane = lane_ids(outer.shape[0])
    first, last = jnp.where(surface, outer, inner), jnp.where(surface, inner, outer)
    middle = turn(middle, LANES // 2)
    return jnp.where(lane < 88, turn(first, -EDGE), middle), jnp.where(lane < 40, middle, turn(last, EDGE))


class Blocks:
    def __init__(self, held, got_depth, outer, bulk):
        self.held, self.got_depth, self.outer, self.bulk = held, got_depth, outer, bulk

    def from_edges(self, pair, side, at, lanes):
        even_got, odd_got = pair
        span = slice(at - (EDGE - HALO), at + HALO) if side == 0 else slice(at, at + EDGE)
        use_odd = is_even() if side == 0 else ~is_even()
        return jnp.where(use_odd, odd_got[span, lanes], even_got[span, lanes])

    def edge_windows(self, f, side, planes):
        whole = slice(0, LANES)
        inner = planes != (0,)
        outer = other = halo = None
        if f < FORWARD:
            outer = self.from_edges(self.outer, side, OUTER + HALO * f, whole)
            if inner:
                lanes = slice(LANES * (f // 4), LANES * (f // 4) + LANES)
                other = self.from_edges(self.bulk, side, INNER + HALO * (f % 4), lanes)
        else:
            at = EDGE + HALO * (f - FORWARD)
            outer, other = split(self.from_edges(self.bulk, side, at, slice(0, 2 * LANES)))
        if inner:
            even_got, odd_got = self.bulk
            lanes = slice(LANES * (f // FORWARD), LANES * (f // FORWARD) + LANES)
            use_odd = is_even() if side == 0 else ~is_even()
            halo = jnp.where(use_odd, odd_got[:EDGE, lanes], even_got[:EDGE, lanes])
        return [window(p, f, outer, other, halo) for p in planes]

    def own_windows(self, f, planes):
        outer, other = split(self.held[f])
        halo = None
        if planes != (0,):
            col = LANES * (f // FORWARD)
            halo = self.got_depth[:, col : col + LANES]
        return [window(p, f, outer, other, halo) for p in planes]

    def windows(self, f, planes):
        rows = self.held.shape[1]
        sets = self.edge_windows(f, 0, planes), self.own_windows(f, planes), self.edge_windows(f, 1, planes)
        return [[(at, part[i]) for at, part in zip((0, EDGE, EDGE + rows), sets)] for i in range(len(planes))]


def load_state(state, blocks, base, planes):
    extent = blocks.held.shape[1] + 2 * EDGE
    for f in range(5):
        for i, parts in enumerate(blocks.windows(base + f, planes)):
            state[f, i, :PAD, :] = jnp.zeros((PAD, LANES), F32)
            state[f, i, PAD + extent :, :] = jnp.zeros((PAD, LANES), F32)
            for at, part in parts:
                state[f, i, PAD + at : PAD + at + part.shape[0], :] = part


def velocities(state, media, span):
    for r in range(8 * span[0], 8 * span[1], 8):
        for i in range(state.shape[1]):

            def at(f, by=0):
                return state[f, i, r + PAD + by : r + PAD + by + 8, :]

            xx, xz, zz = at(2), at(4), at(3)
            b = media[0, i, r : r + 8, :]
            near = (xx - at(2, -1)) + (xz - turn(xz, 1))
            far = (at(2, 1) - at(2, -2)) + (turn(xz, -1) - turn(xz, 2))
            state[0, i, r + PAD : r + PAD + 8, :] = at(0) + b * (near + RATIO * far)
            near = (at(4, 1) - xz) + (turn(zz, -1) - zz)
            far = (at(4, 2) - at(4, -1)) + (turn(zz, -2) - turn(zz, 1))
            state[1, i, r + PAD : r + PAD + 8, :] = at(1) + b * (near + RATIO * far)


def stresses(state, media, span, update, keep):
    for r in range(8 * span[0], 8 * span[1], 8):
        for i in range(state.shape[1]):

            def at(f, by=0):
                return state[f, i, r + PAD + by : r + PAD + by + 8, :]

            vx, vz = at(0), at(1)
            exx = (at(0, 1) - vx) + RATIO * (at(0, 2) - at(0, -1))
            ezz = (vz - turn(vz, 1)) + RATIO * (turn(vz, -1) - turn(vz, 2))
            near = (turn(vx, -1) - vx) + (vz - at(1, -1))
            far = (turn(vx, -2) - turn(vx, 1)) + (at(1, 1) - at(1, -2))
            shear = near + RATIO * far
            keep(i, r - EDGE, exx, ezz, shear)
            if update:
                whole, lam, mu = (media[k, i, r : r + 8, :] for k in (1, 2, 3))
                state[2, i, r + PAD : r + PAD + 8, :] = at(2) + (whole * exx + lam * ezz)
                state[3, i, r + PAD : r + PAD + 8, :] = at(3) + (lam * exx + whole * ezz)
                state[4, i, r + PAD : r + PAD + 8, :] = at(4) + mu * shear


def spans(step, rows):
    tiles = (rows + 2 * EDGE) // 8
    if step == 0:
        return (0, tiles), (0, tiles)
    inner = (1, tiles - 1)
    return inner, inner if step < MOMENTS - 1 else (EDGE // 8, tiles - EDGE // 8)


def run_forward(blocks, media, saved, state, planes):
    rows = blocks.held.shape[1]
    given = [blocks.windows(f, planes) for f in (5, 6, 7)]
    for i in range(len(planes)):
        for k in range(3):
            at = given[0][i][k][0]
            b, lam, mu = (NEAR * given[m][i][k][1] for m in range(3))
            span = slice(at, at + b.shape[0])
            media[0, i, span, :] = b
            media[1, i, span, :] = lam + 2.0 * mu
            media[2, i, span, :] = lam
            media[3, i, span, :] = mu
    load_state(state, blocks, 0, planes)
    for step in range(MOMENTS):
        fast, slow = spans(step, rows)
        velocities(state, media, fast)

        def save(i, r, exx, ezz, shear):
            if 0 <= r < rows:
                saved[step, 0, i, r : r + 8, :] = exx
                saved[step, 1, i, r : r + 8, :] = ezz
                saved[step, 2, i, r : r + 8, :] = shear

        stresses(state, media, slow, step < MOMENTS - 1, save)


def forward_top_kernel(held, outer_even, outer_odd, media, saved, end_out, image_out, state):
    blocks = Blocks(held, None, (outer_even, outer_odd), None)
    run_forward(blocks, media, saved, state, (0,))
    rows = held.shape[1]
    top = PAD + EDGE
    for f in range(2):
        end_out[f] = state[f, 0, top : top + rows, :]
    lane = lane_ids(rows)
    image = jnp.zeros((rows, LANES), F32)
    for step in range(MOMENTS):
        spot = FIBRE_ROWS * step
        here = (lane >= spot) & (lane < spot + FIBRE_ROWS)
        image = jnp.where(here, NEAR * turn(saved[step, 0, 0], spot - EDGE), image)
    turned = image.T
    half = IMAGE // 2
    image_out[...] = jnp.concatenate([turned[:half], turned[half:IMAGE]], axis=1)


def forward_rest_kernel(
    held, got_depth, outer_even, outer_odd, even, odd, top_end, media, saved, end_out, state
):
    blocks = Blocks(held, got_depth, (outer_even, outer_odd), (even, odd))
    run_forward(blocks, media, saved, state, (1, 2))
    rows = held.shape[1]
    top = PAD + EDGE
    for f in range(2):
        first, last = joined(top_end[f], *(state[f, i, top : top + rows, :] for i in range(2)))
        end_out[f, :, :LANES] = first
        end_out[f, :, LANES:] = last


def note_kernel(rows, image, image_beside, obs, owner, cell, note_out):
    rates = jnp.where(lax.axis_index("depth") == 0, image[...], image_beside[...])
    seen = obs[...]
    along, row = channel_cells(owner, cell, rows)
    cells = jnp.concatenate([along[:, :LANES], along[:, LANES:], row[:, :LANES], row[:, LANES:]], axis=0)
    for i, value in enumerate((rates[:4], rates[4:], seen[:, :LANES], seen[:, LANES:], cells.astype(F32))):
        note_out[:, i] = jnp.broadcast_to(value[None], (note_out.shape[0], 4, LANES))


def channel_cells(owner, cell, rows):
    return owner[...] * rows + lax.shift_right_logical(cell[...], 2), cell[...] & 3


def three(value):
    high = value.astype(BF16)
    rest = value - high.astype(F32)
    middle = rest.astype(BF16)
    low = (rest - middle.astype(F32)).astype(BF16)
    return [high, middle, low]


def add_up(value):
    return (value[2 * IMAGE : 3 * IMAGE] + value[IMAGE : 2 * IMAGE]) + value[:IMAGE]


def channel_sums(tracks, rows, notes, own_along):
    start = lax.axis_index("track") * rows - EDGE
    group = min(8, tracks)
    channels = own_along.shape[1]
    lane = lane_ids(8)
    half = LANES // 2
    wanted = jnp.concatenate([own_along, start + lax.broadcasted_iota(jnp.int32, (1, LANES), 1)], axis=1)
    row16 = row_ids(IMAGE, LANES)

    def body(number, carry):
        rate, image = carry
        base = number * group
        firsts, lasts = [], []
        blocks = [[notes[base + k, i] for i in range(5)] for k in range(group)]
        rates = [jnp.concatenate(block[:2], axis=0) for block in blocks]
        for k in range(0, group, 2):
            a, b = rates[k], rates[k + 1]
            firsts.append(jnp.where(lane < half, a, turn(b, half)))
            lasts.append(jnp.where(lane < half, turn(a, half), b))
        strains = jnp.concatenate([jnp.concatenate(firsts, axis=1), jnp.concatenate(lasts, axis=1)], axis=0)
        spot = base * rows + row_ids(group * rows, channels + LANES)
        hot = (spot == wanted).astype(F32).astype(BF16)
        rate = rate + jnp.dot(jnp.concatenate(three(strains), axis=0), hot, preferred_element_type=F32)
        weights, hots = [], []
        for k in range(group):
            for h in range(2):
                along = blocks[k][4][h : h + 1]
                mask = (row16 & 3).astype(F32) == blocks[k][4][2 + h : 3 + h]
                seen = [blocks[k][2 + h][t : t + 1] for t in range(MOMENTS)]
                value = jnp.where(
                    row16 < 8,
                    jnp.where(row16 < 4, seen[0], seen[1]),
                    jnp.where(row16 < 12, seen[2], seen[3]),
                )
                pieces = three(jnp.where(mask, value, 0.0)) + [mask.astype(F32).astype(BF16)]
                weights.append(jnp.concatenate(pieces, axis=0))
                spot = (start + row_ids(LANES, LANES)).astype(F32)
                hots.append((spot == along).astype(F32).astype(BF16))
        image = image + lax.dot_general(
            jnp.concatenate(weights, axis=1),
            jnp.concatenate(hots, axis=1),
            (((1,), (1,)), ((), ())),
            preferred_element_type=F32,
        )
        return rate, image

    carry = jnp.zeros((3 * IMAGE, channels + LANES), F32), jnp.zeros((4 * IMAGE, LANES), F32)
    if tracks == group:
        carry = body(0, carry)
    else:
        carry = lax.fori_loop(0, tracks // group, body, carry)
    rate, image = carry
    return add_up(rate), add_up(image), image[3 * IMAGE :]


def run_adjoint(media, saved, state, sums, inject=None):
    rows = sums.shape[2]
    sums[...] = jnp.zeros(sums.shape, F32)
    for step in range(MOMENTS):
        fast, slow = spans(step, rows)
        moment = MOMENTS - 1 - step
        if inject is not None:
            inject(moment)
        velocities(state, media, fast)

        def gather(i, r, exx, ezz, shear):
            if 0 <= r < rows:
                fxx, fzz, fxz = (saved[moment, k, i, r : r + 8, :] for k in range(3))
                sums[0, i, r : r + 8, :] += (fxx + fzz) * (exx + ezz)
                sums[1, i, r : r + 8, :] += 2.0 * (fxx * exx + fzz * ezz) + fxz * shear

        stresses(state, media, slow, step < MOMENTS - 1, gather)


def adjoint_rest_kernel(held, got_depth, even, odd, media, saved, note, sums, state):
    del note
    load_state(state, Blocks(held, got_depth, None, (even, odd)), FORWARD, (1, 2))
    run_adjoint(media, saved, state, sums)


def adjoint_top_kernel(
    tracks, held, even, odd, media, saved, notes, rest, obs, owner, cell,
    lambda_out, mu_out, residual_out, state, sums,
):
    rows = held.shape[1]
    extent = rows + 2 * EDGE
    depth = lax.axis_index("depth")
    load_state(state, Blocks(held, None, None, (even, odd)), FORWARD, (0,))
    along, row = channel_cells(owner, cell, rows)
    rate, seen, count = channel_sums(tracks, rows, notes, along)
    channels = along.shape[1]
    at_own = jnp.where((row_ids(IMAGE, channels) & 3) == row, rate[:, :channels], 0.0)
    traces = [
        jnp.sum(at_own[4 * t : 4 * t + 4], axis=0, keepdims=True) - obs[t : t + 1, :] for t in range(MOMENTS)
    ]
    residual_out[...] = jnp.where(
        depth == 0, jnp.concatenate(traces[:2], axis=0), jnp.concatenate(traces[2:], axis=0)
    )
    sources = count * rate[:, channels:] - seen
    turned = jnp.concatenate([sources, jnp.zeros((LANES - IMAGE, LANES), F32)], axis=0).T[:extent]
    lane = lane_ids(extent)
    here = (lane >= EDGE) & (lane < EDGE + FIBRE_ROWS) & (depth == 0)

    def inject(moment):
        added = jnp.where(here, turn(turned, EDGE - FIBRE_ROWS * moment), 0.0)
        state[2, 0, PAD : PAD + extent, :] += added

    run_adjoint(media, saved, state, sums, inject)
    for k, out in enumerate((lambda_out, mu_out)):
        first, last = joined(sums[k, 0], rest[k, 0], rest[k, 1])
        out[:, :LANES] = (NEAR * NEAR) * first
        out[:, LANES:] = (NEAR * NEAR) * last


def per_device(
    velocity,
    stress,
    adjoint_velocity,
    adjoint_stress,
    buoyancy,
    lame_lambda,
    shear_modulus,
    observed,
    owner_track,
    fibre_cell,
):
    tracks = lax.axis_size("track")
    rows, depth_cells = buoyancy.shape
    moments, channels = observed.shape
    owner = owner_track.reshape(1, channels)
    cell = fibre_cell.reshape(1, channels)
    pinned = lambda array: pltpu.with_memory_space_constraint(array, pltpu.HBM)
    arrays = (velocity, stress, adjoint_velocity, adjoint_stress, buoyancy, lame_lambda, shear_modulus)
    arrays = tuple(pinned(array) for array in arrays)
    channel_arrays = (observed, owner, cell)
    extent = rows + 2 * EDGE
    block = jax.ShapeDtypeStruct((rows, depth_cells), F32)
    outer_edges = jax.ShapeDtypeStruct((OUTER + HALO * FORWARD + EDGE - HALO, LANES), F32)
    edges = jax.ShapeDtypeStruct((INNER + HALO * 4 + EDGE - HALO, depth_cells), F32)
    inside = pl.BlockSpec(memory_space=VMEM)
    outside = pl.BlockSpec(memory_space=pltpu.HBM)
    anywhere = pl.BlockSpec(memory_space=pl.ANY)
    swap = lambda k: [pair for i in range(k, tracks - 1, 2) for pair in ((i, i + 1), (i + 1, i))]
    to_even, to_odd = pl.pallas_call(
        outer_kernel,
        out_shape=(outer_edges, outer_edges),
        in_specs=[outside] * 5,
        out_specs=(inside,) * 2,
        scratch_shapes=[VMEM((2, FORWARD, EDGE, LANES), F32), pltpu.SemaphoreType.DMA((10,))],
        compiler_params=params(),
        cost_estimate=cost(1),
        name="outer",
    )(*arrays[:2], *arrays[4:])
    outer_odd = lax.ppermute(to_odd, "track", swap(1))
    outer_even = lax.ppermute(to_even, "track", swap(0))

    held, to_depth, to_even, to_odd = pl.pallas_call(
        pack_kernel,
        out_shape=(jax.ShapeDtypeStruct((FIELDS, rows, depth_cells), F32), block, edges, edges),
        in_specs=[outside] * 7 + [anywhere],
        out_specs=(inside,) * 4,
        scratch_shapes=[pltpu.SemaphoreType.DMA((7,))],
        compiler_params=params(),
        cost_estimate=cost(2),
        name="pack",
    )(*arrays, to_even)
    depth_swap = [(0, 1), (1, 0)]
    got_depth = lax.ppermute(to_depth, "depth", depth_swap)
    to_even, to_odd = pl.pallas_call(
        corner_kernel,
        out_shape=(edges, edges),
        in_specs=[anywhere] * 3,
        out_specs=(anywhere,) * 2,
        input_output_aliases={1: 0, 2: 1},
        scratch_shapes=[pltpu.SemaphoreType.DMA((2,))],
        compiler_params=params(),
        name="corners",
    )(got_depth, to_even, to_odd)
    got_odd = lax.ppermute(to_odd, "track", swap(1))
    got_even = lax.ppermute(to_even, "track", swap(0))

    def media_of(planes):
        return jax.ShapeDtypeStruct((4, planes, extent, LANES), F32)

    def saved_of(planes):
        return jax.ShapeDtypeStruct((moments, 3, planes, rows, LANES), F32)

    def state_of(planes):
        return VMEM((5, planes, extent + 2 * PAD, LANES), F32)

    media_top, saved_top, top_end, image = pl.pallas_call(
        forward_top_kernel,
        out_shape=(
            media_of(1),
            saved_of(1),
            jax.ShapeDtypeStruct((2, rows, LANES), F32),
            jax.ShapeDtypeStruct((IMAGE // 2, LANES), F32),
        ),
        in_specs=[inside] * 3,
        out_specs=(inside,) * 4,
        scratch_shapes=[state_of(1)],
        compiler_params=params(),
        cost_estimate=cost(1),
        name="forward_top",
    )(held, outer_even, outer_odd)
    image_beside = lax.ppermute(image, "depth", depth_swap)
    media_rest, saved_rest, velocity_end = pl.pallas_call(
        forward_rest_kernel,
        out_shape=(media_of(2), saved_of(2), jax.ShapeDtypeStruct(velocity.shape, F32)),
        in_specs=[inside] * 7,
        out_specs=(inside,) * 3,
        scratch_shapes=[state_of(2)],
        compiler_params=params(),
        cost_estimate=cost(2),
        name="forward_rest",
    )(held, got_depth, outer_even, outer_odd, got_even, got_odd, top_end)
    note = pl.pallas_call(
        lambda *refs: note_kernel(rows, *refs),
        out_shape=jax.ShapeDtypeStruct((tracks, 5, 4, LANES), F32),
        in_specs=[inside] * 5,
        out_specs=inside,
        compiler_params=params(),
        name="note",
    )(image, image_beside, *channel_arrays)
    notes = lax.all_to_all(note, "track", split_axis=0, concat_axis=0, tiled=True)
    rest = pl.pallas_call(
        adjoint_rest_kernel,
        out_shape=jax.ShapeDtypeStruct((2, 2, rows, LANES), F32),
        in_specs=[inside] * 6 + [anywhere],
        out_specs=inside,
        scratch_shapes=[state_of(2)],
        compiler_params=params(),
        cost_estimate=cost(3),
        name="adjoint_rest",
    )(held, got_depth, got_even, got_odd, media_rest, saved_rest, note)
    gradient_lambda, gradient_mu, residual = pl.pallas_call(
        lambda *refs: adjoint_top_kernel(tracks, *refs),
        out_shape=(block, block, jax.ShapeDtypeStruct((moments // 2, channels), F32)),
        in_specs=[inside] * 10,
        out_specs=(inside,) * 3,
        scratch_shapes=[state_of(1), VMEM((2, 1, rows, LANES), F32)],
        compiler_params=params(),
        cost_estimate=cost(2),
        name="adjoint_top",
    )(held, got_even, got_odd, media_top, saved_top, notes, rest, *channel_arrays)
    return gradient_lambda, gradient_mu, velocity_end, residual


def solution(mesh):
    return jax.shard_map(
        per_device,
        mesh=mesh,
        in_specs=(
            P("shots", "track", "depth"),
            P("shots", "track", "depth"),
            P("shots", "track", "depth"),
            P("shots", "track", "depth"),
            P("track", "depth"),
            P("track", "depth"),
            P("track", "depth"),
            P("shots", "track"),
            P("track", None),
            P("track"),
        ),
        out_specs=(
            P(("shots", "track"), "depth"),
            P(("shots", "track"), "depth"),
            P("shots", "track", "depth"),
            P(("shots", "depth"), "track"),
        ),
        check_vma=False,
    )
```

```python
import jax
import jax.numpy as jnp
from jax import lax
from jax.experimental import pallas as pl
from jax.experimental.pallas import tpu as pltpu
from jax.sharding import PartitionSpec as P

FIBRE_ROWS = 4
NEAR = 9.0 / 8.0
RATIO = -1.0 / 27.0
HALO = 12
EDGE = 16
LANES = 128
PAD = 8
FORWARD = 8
ADJOINT = 5
FIELDS = FORWARD + ADJOINT
OUTER = EDGE - HALO
INNER = EDGE + HALO * ADJOINT
MOMENTS = 4
IMAGE = MOMENTS * FIBRE_ROWS
VMEM = pltpu.VMEM
F32 = jnp.float32
BF16 = jnp.bfloat16


def lane_ids(rows):
    return lax.broadcasted_iota(jnp.int32, (rows, LANES), 1)


def row_ids(rows, columns):
    return lax.broadcasted_iota(jnp.int32, (rows, columns), 0)


def params():
    return pltpu.CompilerParams(vmem_limit_bytes=40 * 1024 * 1024)


def cost(microseconds):
    return pl.CostEstimate(flops=0, bytes_accessed=int(microseconds * 3.5e6), transcendentals=0)


def turn(value, by):
    return pltpu.roll(value, by % LANES, 1)


def is_even():
    return lax.rem(lax.axis_index("track"), 2) == 0


def fetch(sources, targets, sems):
    copies = [pltpu.make_async_copy(s, t, sems.at[i]) for i, (s, t) in enumerate(zip(sources, targets))]
    for copy in copies:
        copy.start()
    return copies


def field_copies(arrays, held, sems):
    velocity, stress, adj_velocity, adj_stress, buoyancy, lame, shear = arrays
    sources = (velocity, stress, buoyancy, lame, shear, adj_velocity, adj_stress)
    targets = (
        held.at[pl.ds(0, 2)],
        held.at[pl.ds(2, 3)],
        held.at[5],
        held.at[6],
        held.at[7],
        held.at[pl.ds(8, 2)],
        held.at[pl.ds(10, 3)],
    )
    return fetch(sources, targets, sems)


def outer_kernel(velocity, stress, buoyancy, lame, shear, even_out, odd_out, strips, sems):
    depth = lax.axis_index("depth")
    even = is_even()
    rows = buoyancy.shape[0]
    lanes = pl.ds(pl.multiple_of(depth * LANES, LANES), LANES)
    sources, targets = [], []
    for side, row in enumerate((0, rows - EDGE)):
        span = pl.ds(row, EDGE)
        sources += [array.at[:, span, lanes] for array in (velocity, stress)]
        targets += [strips.at[side, pl.ds(0, 2)], strips.at[side, pl.ds(2, 3)]]
        sources += [array.at[span, lanes] for array in (buoyancy, lame, shear)]
        targets += [strips.at[side, f] for f in (5, 6, 7)]
    copies = fetch(sources, targets, sems)
    for out in (even_out, odd_out):
        out[:OUTER, :] = jnp.zeros((OUTER, LANES), F32)
        out[OUTER + HALO * FORWARD :, :] = jnp.zeros((EDGE - HALO, LANES), F32)
    for copy in copies:
        copy.wait()
    for f in range(FORWARD):
        low, high = strips[0, f, :HALO, :], strips[1, f, EDGE - HALO :, :]
        at = OUTER + HALO * f
        even_out[at : at + HALO, :] = jnp.where(even, high, low)
        odd_out[at : at + HALO, :] = jnp.where(even, low, high)


def pack_kernel(*refs):
    arrays, channel_arrays = refs[:7], refs[7:10]
    held, depth_out, even_out, odd_out, traces_out, cells_out = refs[11:17]
    numbers, sems = refs[17:]
    copies = field_copies(arrays, held, sems)
    targets = (traces_out, numbers.at[0], numbers.at[1])
    channel_copies = [
        pltpu.make_async_copy(source, target, sems.at[7 + i])
        for i, (source, target) in enumerate(zip(channel_arrays, targets))
    ]
    for copy in channel_copies:
        copy.start()
    depth = lax.axis_index("depth")
    even = is_even()
    rows = held.shape[1]
    lane = lane_ids(rows)
    tail = INNER + HALO * 4
    for out in (even_out, odd_out):
        out[:EDGE, :] = jnp.zeros((EDGE, 2 * LANES), F32)
        out[tail:, :] = jnp.zeros((out.shape[0] - tail, 2 * LANES), F32)
    for copy in copies:
        copy.wait()
    packed = [jnp.zeros((rows, LANES), F32) for _ in range(2)]
    for f in range(FIELDS):
        group, place = divmod(f, FORWARD)
        spot = EDGE * place
        here = (lane >= spot) & (lane < spot + EDGE)
        edge = jnp.where(depth == 0, held[f, :, LANES:], held[f, :, :LANES])
        shift = lax.rem(spot + EDGE * (1 - depth), LANES)
        packed[group] = jnp.where(here, pltpu.roll(edge, shift, 1), packed[group])
        if f < FORWARD:
            low, high = edge[:HALO], edge[rows - HALO :]
            at, lanes = INNER + HALO * (f % 4), slice(LANES * (f // 4), LANES * (f // 4) + LANES)
        else:
            low, high = held[f, :HALO, :], held[f, rows - HALO :, :]
            at, lanes = EDGE + HALO * place, slice(0, 2 * LANES)
        even_out[at : at + HALO, lanes] = jnp.where(even, high, low)
        odd_out[at : at + HALO, lanes] = jnp.where(even, low, high)
    depth_out[:, :LANES] = packed[0]
    depth_out[:, LANES:] = packed[1]
    for copy in channel_copies:
        copy.wait()
    cells_out[0] = numbers[0] * rows + lax.shift_right_logical(numbers[1], 2)
    cells_out[1] = numbers[1] & 3


def corner_kernel(got, even_in, odd_in, even_out, odd_out, sems):
    rows = got.shape[0]
    is_odd = lax.rem(lax.axis_index("track"), 2)
    high, low = (rows - EDGE) * (1 - is_odd), (rows - EDGE) * is_odd
    one = pltpu.make_async_copy(
        got.at[pl.ds(pl.multiple_of(high, EDGE), EDGE), :], even_out.at[pl.ds(0, EDGE), :], sems.at[0]
    )
    two = pltpu.make_async_copy(
        got.at[pl.ds(pl.multiple_of(low, EDGE), EDGE), :], odd_out.at[pl.ds(0, EDGE), :], sems.at[1]
    )
    one.start()
    two.start()
    one.wait()
    two.wait()


def window(plane, f, outer, other, halo):
    depth = lax.axis_index("depth")
    surface = depth == 0
    lane = lane_ids(outer.shape[0])
    low = jnp.where(surface, lane, LANES - 1 - lane)
    if plane == 0:
        shift = jnp.where(surface, EDGE, LANES - EDGE)
        return jnp.where(low >= EDGE, pltpu.roll(outer, shift, 1), 0.0)
    if plane == 1:
        return jnp.where(low < LANES // 2, turn(outer, LANES // 2), turn(other, LANES // 2))
    shift = jnp.where(surface, LANES - EDGE, EDGE)
    beside = lax.rem(LANES - EDGE * (f % FORWARD) + (LANES - EDGE) * (1 - depth), LANES)
    return jnp.where(low < LANES - EDGE, pltpu.roll(other, shift, 1), pltpu.roll(halo, beside, 1))


def split(value):
    surface = lax.axis_index("depth") == 0
    first, last = value[:, :LANES], value[:, LANES:]
    return jnp.where(surface, first, last), jnp.where(surface, last, first)


def joined(outer, middle, inner):
    surface = lax.axis_index("depth") == 0
    lane = lane_ids(outer.shape[0])
    first, last = jnp.where(surface, outer, inner), jnp.where(surface, inner, outer)
    middle = turn(middle, LANES // 2)
    return jnp.where(lane < 88, turn(first, -EDGE), middle), jnp.where(lane < 40, middle, turn(last, EDGE))


class Blocks:
    def __init__(self, held, got_depth, outer, bulk):
        self.held, self.got_depth, self.outer, self.bulk = held, got_depth, outer, bulk

    def from_edges(self, pair, side, at, lanes):
        even_got, odd_got = pair
        span = slice(at - (EDGE - HALO), at + HALO) if side == 0 else slice(at, at + EDGE)
        use_odd = is_even() if side == 0 else ~is_even()
        return jnp.where(use_odd, odd_got[span, lanes], even_got[span, lanes])

    def edge_windows(self, f, side, planes):
        whole = slice(0, LANES)
        inner = planes != (0,)
        outer = other = halo = None
        if f < FORWARD:
            outer = self.from_edges(self.outer, side, OUTER + HALO * f, whole)
            if inner:
                lanes = slice(LANES * (f // 4), LANES * (f // 4) + LANES)
                other = self.from_edges(self.bulk, side, INNER + HALO * (f % 4), lanes)
        else:
            at = EDGE + HALO * (f - FORWARD)
            outer, other = split(self.from_edges(self.bulk, side, at, slice(0, 2 * LANES)))
        if inner:
            even_got, odd_got = self.bulk
            lanes = slice(LANES * (f // FORWARD), LANES * (f // FORWARD) + LANES)
            use_odd = is_even() if side == 0 else ~is_even()
            halo = jnp.where(use_odd, odd_got[:EDGE, lanes], even_got[:EDGE, lanes])
        return [window(p, f, outer, other, halo) for p in planes]

    def own_windows(self, f, planes):
        outer, other = split(self.held[f])
        halo = None
        if planes != (0,):
            col = LANES * (f // FORWARD)
            halo = self.got_depth[:, col : col + LANES]
        return [window(p, f, outer, other, halo) for p in planes]

    def windows(self, f, planes):
        rows = self.held.shape[1]
        sets = self.edge_windows(f, 0, planes), self.own_windows(f, planes), self.edge_windows(f, 1, planes)
        return [[(at, part[i]) for at, part in zip((0, EDGE, EDGE + rows), sets)] for i in range(len(planes))]


def load_state(state, blocks, base, planes):
    extent = blocks.held.shape[1] + 2 * EDGE
    for f in range(5):
        for i, parts in enumerate(blocks.windows(base + f, planes)):
            state[f, i, :PAD, :] = jnp.zeros((PAD, LANES), F32)
            state[f, i, PAD + extent :, :] = jnp.zeros((PAD, LANES), F32)
            for at, part in parts:
                state[f, i, PAD + at : PAD + at + part.shape[0], :] = part


def velocities(state, media, span):
    for r in range(8 * span[0], 8 * span[1], 8):
        for i in range(state.shape[1]):

            def at(f, by=0):
                return state[f, i, r + PAD + by : r + PAD + by + 8, :]

            xx, xz, zz = at(2), at(4), at(3)
            b = media[0, i, r : r + 8, :]
            near = (xx - at(2, -1)) + (xz - turn(xz, 1))
            far = (at(2, 1) - at(2, -2)) + (turn(xz, -1) - turn(xz, 2))
            state[0, i, r + PAD : r + PAD + 8, :] = at(0) + b * (near + RATIO * far)
            near = (at(4, 1) - xz) + (turn(zz, -1) - zz)
            far = (at(4, 2) - at(4, -1)) + (turn(zz, -2) - turn(zz, 1))
            state[1, i, r + PAD : r + PAD + 8, :] = at(1) + b * (near + RATIO * far)


def stresses(state, media, span, update, keep):
    for r in range(8 * span[0], 8 * span[1], 8):
        for i in range(state.shape[1]):

            def at(f, by=0):
                return state[f, i, r + PAD + by : r + PAD + by + 8, :]

            vx, vz = at(0), at(1)
            exx = (at(0, 1) - vx) + RATIO * (at(0, 2) - at(0, -1))
            ezz = (vz - turn(vz, 1)) + RATIO * (turn(vz, -1) - turn(vz, 2))
            near = (turn(vx, -1) - vx) + (vz - at(1, -1))
            far = (turn(vx, -2) - turn(vx, 1)) + (at(1, 1) - at(1, -2))
            shear = near + RATIO * far
            keep(i, r - EDGE, exx, ezz, shear)
            if update:
                whole, lam, mu = (media[k, i, r : r + 8, :] for k in (1, 2, 3))
                state[2, i, r + PAD : r + PAD + 8, :] = at(2) + (whole * exx + lam * ezz)
                state[3, i, r + PAD : r + PAD + 8, :] = at(3) + (lam * exx + whole * ezz)
                state[4, i, r + PAD : r + PAD + 8, :] = at(4) + mu * shear


def spans(step, rows):
    tiles = (rows + 2 * EDGE) // 8
    if step == 0:
        return (0, tiles), (0, tiles)
    inner = (1, tiles - 1)
    return inner, inner if step < MOMENTS - 1 else (EDGE // 8, tiles - EDGE // 8)


def run_forward(blocks, media, saved, state, planes):
    rows = blocks.held.shape[1]
    given = [blocks.windows(f, planes) for f in (5, 6, 7)]
    for i in range(len(planes)):
        for k in range(3):
            at = given[0][i][k][0]
            b, lam, mu = (NEAR * given[m][i][k][1] for m in range(3))
            span = slice(at, at + b.shape[0])
            media[0, i, span, :] = b
            media[1, i, span, :] = lam + 2.0 * mu
            media[2, i, span, :] = lam
            media[3, i, span, :] = mu
    load_state(state, blocks, 0, planes)
    for step in range(MOMENTS):
        fast, slow = spans(step, rows)
        velocities(state, media, fast)

        def save(i, r, exx, ezz, shear):
            if 0 <= r < rows:
                saved[step, 0, i, r : r + 8, :] = exx
                saved[step, 1, i, r : r + 8, :] = ezz
                saved[step, 2, i, r : r + 8, :] = shear

        stresses(state, media, slow, step < MOMENTS - 1, save)


def forward_top_kernel(
    held, outer_even, outer_odd, traces, cells, bulk, media, saved, end_out, note_out, state
):
    del bulk
    blocks = Blocks(held, None, (outer_even, outer_odd), None)
    run_forward(blocks, media, saved, state, (0,))
    rows = held.shape[1]
    top = PAD + EDGE
    for f in range(2):
        end_out[f] = state[f, 0, top : top + rows, :]
    lane = lane_ids(rows)
    image = jnp.zeros((rows, LANES), F32)
    for step in range(MOMENTS):
        spot = FIBRE_ROWS * step
        here = (lane >= spot) & (lane < spot + FIBRE_ROWS)
        image = jnp.where(here, NEAR * turn(saved[step, 0, 0], spot - EDGE), image)
    turned = image.T
    half = IMAGE // 2
    rates = jnp.concatenate([turned[:half], turned[half:IMAGE]], axis=1)
    seen = jnp.concatenate([traces[:, :LANES], traces[:, LANES:]], axis=0)
    mine = jnp.where(lax.axis_index("depth") == 0, rates, seen)
    along, row = cells[0], cells[1]
    places = jnp.concatenate([along[:, :LANES], along[:, LANES:], row[:, :LANES], row[:, LANES:]], axis=0)
    for i, value in enumerate((mine[:4], mine[4:], places.astype(F32))):
        note_out[:, i] = jnp.broadcast_to(value[None], (note_out.shape[0], 4, LANES))


def forward_rest_kernel(
    held, got_depth, outer_even, outer_odd, even, odd, top_end, media, saved, end_out, state
):
    blocks = Blocks(held, got_depth, (outer_even, outer_odd), (even, odd))
    run_forward(blocks, media, saved, state, (1, 2))
    rows = held.shape[1]
    top = PAD + EDGE
    for f in range(2):
        first, last = joined(top_end[f], *(state[f, i, top : top + rows, :] for i in range(2)))
        end_out[f, :, :LANES] = first
        end_out[f, :, LANES:] = last


def three(value):
    high = value.astype(BF16)
    rest = value - high.astype(F32)
    middle = rest.astype(BF16)
    low = (rest - middle.astype(F32)).astype(BF16)
    return [high, middle, low]


def add_up(value):
    return (value[2 * IMAGE : 3 * IMAGE] + value[IMAGE : 2 * IMAGE]) + value[:IMAGE]


def channel_sums(tracks, rows, notes, beside, own_along):
    start = lax.axis_index("track") * rows - EDGE
    surface = lax.axis_index("depth") == 0
    group = min(8, tracks)
    channels = own_along.shape[1]
    lane = lane_ids(8)
    half = LANES // 2
    wanted = jnp.concatenate([own_along, start + lax.broadcasted_iota(jnp.int32, (1, LANES), 1)], axis=1)
    row16 = row_ids(IMAGE, LANES)

    def body(number, carry):
        rate, image = carry
        base = number * group
        firsts, lasts = [], []
        mine = [[notes[base + k, i] for i in range(3)] for k in range(group)]
        other = [[beside[base + k, i] for i in range(3)] for k in range(group)]
        rates = [
            jnp.concatenate([jnp.where(surface, m[i], o[i]) for i in range(2)], axis=0) for m, o in zip(mine, other)
        ]
        traces = [[jnp.where(surface, o[i], m[i]) for i in range(2)] for m, o in zip(mine, other)]
        for k in range(0, group, 2):
            a, b = rates[k], rates[k + 1]
            firsts.append(jnp.where(lane < half, a, turn(b, half)))
            lasts.append(jnp.where(lane < half, turn(a, half), b))
        strains = jnp.concatenate([jnp.concatenate(firsts, axis=1), jnp.concatenate(lasts, axis=1)], axis=0)
        spot = base * rows + row_ids(group * rows, channels + LANES)
        hot = (spot == wanted).astype(F32).astype(BF16)
        rate = rate + jnp.dot(jnp.concatenate(three(strains), axis=0), hot, preferred_element_type=F32)
        weights, hots = [], []
        for k in range(group):
            for h in range(2):
                along = mine[k][2][h : h + 1]
                mask = (row16 & 3).astype(F32) == mine[k][2][2 + h : 3 + h]
                seen = [traces[k][h][t : t + 1] for t in range(MOMENTS)]
                value = jnp.where(
                    row16 < 8,
                    jnp.where(row16 < 4, seen[0], seen[1]),
                    jnp.where(row16 < 12, seen[2], seen[3]),
                )
                pieces = three(jnp.where(mask, value, 0.0)) + [mask.astype(F32).astype(BF16)]
                weights.append(jnp.concatenate(pieces, axis=0))
                spot = (start + row_ids(LANES, LANES)).astype(F32)
                hots.append((spot == along).astype(F32).astype(BF16))
        image = image + lax.dot_general(
            jnp.concatenate(weights, axis=1),
            jnp.concatenate(hots, axis=1),
            (((1,), (1,)), ((), ())),
            preferred_element_type=F32,
        )
        return rate, image

    carry = jnp.zeros((3 * IMAGE, channels + LANES), F32), jnp.zeros((4 * IMAGE, LANES), F32)
    if tracks == group:
        carry = body(0, carry)
    else:
        carry = lax.fori_loop(0, tracks // group, body, carry)
    rate, image = carry
    return add_up(rate), add_up(image), image[3 * IMAGE :]


def run_adjoint(media, saved, state, sums, inject=None):
    rows = sums.shape[2]
    sums[...] = jnp.zeros(sums.shape, F32)
    for step in range(MOMENTS):
        fast, slow = spans(step, rows)
        moment = MOMENTS - 1 - step
        if inject is not None:
            inject(moment)
        velocities(state, media, fast)

        def gather(i, r, exx, ezz, shear):
            if 0 <= r < rows:
                fxx, fzz, fxz = (saved[moment, k, i, r : r + 8, :] for k in range(3))
                sums[0, i, r : r + 8, :] += (fxx + fzz) * (exx + ezz)
                sums[1, i, r : r + 8, :] += 2.0 * (fxx * exx + fzz * ezz) + fxz * shear

        stresses(state, media, slow, step < MOMENTS - 1, gather)


def adjoint_rest_kernel(held, got_depth, even, odd, media, saved, notes, sums, state):
    del notes
    load_state(state, Blocks(held, got_depth, None, (even, odd)), FORWARD, (1, 2))
    run_adjoint(media, saved, state, sums)


def adjoint_top_kernel(
    tracks, held, even, odd, media, saved, notes, beside, rest, obs, cells,
    lambda_out, mu_out, residual_out, state, sums,
):
    rows = held.shape[1]
    extent = rows + 2 * EDGE
    depth = lax.axis_index("depth")
    load_state(state, Blocks(held, None, None, (even, odd)), FORWARD, (0,))
    along, row = cells[0], cells[1]
    rate, seen, count = channel_sums(tracks, rows, notes, beside, along)
    channels = along.shape[1]
    at_own = jnp.where((row_ids(IMAGE, channels) & 3) == row, rate[:, :channels], 0.0)
    traces = [
        jnp.sum(at_own[4 * t : 4 * t + 4], axis=0, keepdims=True) - obs[t : t + 1, :] for t in range(MOMENTS)
    ]
    residual_out[...] = jnp.where(
        depth == 0, jnp.concatenate(traces[:2], axis=0), jnp.concatenate(traces[2:], axis=0)
    )
    sources = count * rate[:, channels:] - seen
    turned = jnp.concatenate([sources, jnp.zeros((LANES - IMAGE, LANES), F32)], axis=0).T[:extent]
    lane = lane_ids(extent)
    here = (lane >= EDGE) & (lane < EDGE + FIBRE_ROWS) & (depth == 0)

    def inject(moment):
        added = jnp.where(here, turn(turned, EDGE - FIBRE_ROWS * moment), 0.0)
        state[2, 0, PAD : PAD + extent, :] += added

    run_adjoint(media, saved, state, sums, inject)
    for k, out in enumerate((lambda_out, mu_out)):
        first, last = joined(sums[k, 0], rest[k, 0], rest[k, 1])
        out[:, :LANES] = (NEAR * NEAR) * first
        out[:, LANES:] = (NEAR * NEAR) * last


def per_device(
    velocity,
    stress,
    adjoint_velocity,
    adjoint_stress,
    buoyancy,
    lame_lambda,
    shear_modulus,
    observed,
    owner_track,
    fibre_cell,
):
    tracks = lax.axis_size("track")
    rows, depth_cells = buoyancy.shape
    moments, channels = observed.shape
    owner = owner_track.reshape(1, channels)
    cell = fibre_cell.reshape(1, channels)
    pinned = lambda array: pltpu.with_memory_space_constraint(array, pltpu.HBM)
    arrays = (velocity, stress, adjoint_velocity, adjoint_stress, buoyancy, lame_lambda, shear_modulus)
    arrays = tuple(pinned(array) for array in arrays)
    channel_arrays = (pinned(observed), pinned(owner), pinned(cell))
    extent = rows + 2 * EDGE
    block = jax.ShapeDtypeStruct((rows, depth_cells), F32)
    outer_edges = jax.ShapeDtypeStruct((OUTER + HALO * FORWARD + EDGE - HALO, LANES), F32)
    edges = jax.ShapeDtypeStruct((INNER + HALO * 4 + EDGE - HALO, depth_cells), F32)
    inside = pl.BlockSpec(memory_space=VMEM)
    outside = pl.BlockSpec(memory_space=pltpu.HBM)
    anywhere = pl.BlockSpec(memory_space=pl.ANY)
    swap = lambda k: [pair for i in range(k, tracks - 1, 2) for pair in ((i, i + 1), (i + 1, i))]
    to_even, to_odd = pl.pallas_call(
        outer_kernel,
        out_shape=(outer_edges, outer_edges),
        in_specs=[outside] * 5,
        out_specs=(inside,) * 2,
        scratch_shapes=[VMEM((2, FORWARD, EDGE, LANES), F32), pltpu.SemaphoreType.DMA((10,))],
        compiler_params=params(),
        cost_estimate=cost(1),
        name="outer",
    )(*arrays[:2], *arrays[4:])
    outer_odd = lax.ppermute(to_odd, "track", swap(1))
    outer_even = lax.ppermute(to_even, "track", swap(0))

    held, to_depth, to_even, to_odd, traces, cells = pl.pallas_call(
        pack_kernel,
        out_shape=(
            jax.ShapeDtypeStruct((FIELDS, rows, depth_cells), F32),
            block,
            edges,
            edges,
            jax.ShapeDtypeStruct((moments, channels), F32),
            jax.ShapeDtypeStruct((2, 1, channels), jnp.int32),
        ),
        in_specs=[outside] * 10 + [anywhere],
        out_specs=(inside,) * 6,
        scratch_shapes=[VMEM((2, 1, channels), jnp.int32), pltpu.SemaphoreType.DMA((10,))],
        compiler_params=params(),
        cost_estimate=cost(2),
        name="pack",
    )(*arrays, *channel_arrays, to_even)
    depth_swap = [(0, 1), (1, 0)]
    got_depth = lax.ppermute(to_depth, "depth", depth_swap)
    to_even, to_odd = pl.pallas_call(
        corner_kernel,
        out_shape=(edges, edges),
        in_specs=[anywhere] * 3,
        out_specs=(anywhere,) * 2,
        input_output_aliases={1: 0, 2: 1},
        scratch_shapes=[pltpu.SemaphoreType.DMA((2,))],
        compiler_params=params(),
        name="corners",
    )(got_depth, to_even, to_odd)
    got_odd = lax.ppermute(to_odd, "track", swap(1))
    got_even = lax.ppermute(to_even, "track", swap(0))

    def media_of(planes):
        return jax.ShapeDtypeStruct((4, planes, extent, LANES), F32)

    def saved_of(planes):
        return jax.ShapeDtypeStruct((moments, 3, planes, rows, LANES), F32)

    def state_of(planes):
        return VMEM((5, planes, extent + 2 * PAD, LANES), F32)

    media_top, saved_top, top_end, note = pl.pallas_call(
        forward_top_kernel,
        out_shape=(
            media_of(1),
            saved_of(1),
            jax.ShapeDtypeStruct((2, rows, LANES), F32),
            jax.ShapeDtypeStruct((tracks, 3, 4, LANES), F32),
        ),
        in_specs=[inside] * 5 + [anywhere],
        out_specs=(inside,) * 4,
        scratch_shapes=[state_of(1)],
        compiler_params=params(),
        cost_estimate=cost(20),
        name="forward_top",
    )(held, outer_even, outer_odd, traces, cells, to_even)
    notes = lax.all_to_all(note, "track", split_axis=0, concat_axis=0, tiled=True)
    beside = lax.ppermute(notes, "depth", depth_swap)
    media_rest, saved_rest, velocity_end = pl.pallas_call(
        forward_rest_kernel,
        out_shape=(media_of(2), saved_of(2), jax.ShapeDtypeStruct(velocity.shape, F32)),
        in_specs=[inside] * 7,
        out_specs=(inside,) * 3,
        scratch_shapes=[state_of(2)],
        compiler_params=params(),
        cost_estimate=cost(20),
        name="forward_rest",
    )(held, got_depth, outer_even, outer_odd, got_even, got_odd, top_end)
    rest = pl.pallas_call(
        adjoint_rest_kernel,
        out_shape=jax.ShapeDtypeStruct((2, 2, rows, LANES), F32),
        in_specs=[inside] * 6 + [anywhere],
        out_specs=inside,
        scratch_shapes=[state_of(2)],
        compiler_params=params(),
        cost_estimate=cost(20),
        name="adjoint_rest",
    )(held, got_depth, got_even, got_odd, media_rest, saved_rest, notes)
    gradient_lambda, gradient_mu, residual = pl.pallas_call(
        lambda *refs: adjoint_top_kernel(tracks, *refs),
        out_shape=(block, block, jax.ShapeDtypeStruct((moments // 2, channels), F32)),
        in_specs=[inside] * 10,
        out_specs=(inside,) * 3,
        scratch_shapes=[state_of(1), VMEM((2, 1, rows, LANES), F32)],
        compiler_params=params(),
        cost_estimate=cost(2),
        name="adjoint_top",
    )(held, got_even, got_odd, media_top, saved_top, notes, beside, rest, traces, cells)
    return gradient_lambda, gradient_mu, velocity_end, residual


def solution(mesh):
    return jax.shard_map(
        per_device,
        mesh=mesh,
        in_specs=(
            P("shots", "track", "depth"),
            P("shots", "track", "depth"),
            P("shots", "track", "depth"),
            P("shots", "track", "depth"),
            P("track", "depth"),
            P("track", "depth"),
            P("track", "depth"),
            P("shots", "track"),
            P("track", None),
            P("track"),
        ),
        out_specs=(
            P(("shots", "track"), "depth"),
            P(("shots", "track"), "depth"),
            P("shots", "track", "depth"),
            P(("shots", "depth"), "track"),
        ),
        check_vma=False,
    )
```

```python
import jax
import jax.numpy as jnp
from jax import lax
from jax.experimental import pallas as pl
from jax.experimental.pallas import tpu as pltpu
from jax.sharding import PartitionSpec as P

FIBRE_ROWS = 4
NEAR = 9.0 / 8.0
RATIO = -1.0 / 27.0
HALO = 12
EDGE = 16
LANES = 128
PAD = 8
FORWARD = 8
ADJOINT = 5
FIELDS = FORWARD + ADJOINT
OUTER = EDGE - HALO
INNER = EDGE + HALO * ADJOINT
MOMENTS = 4
IMAGE = MOMENTS * FIBRE_ROWS
VMEM = pltpu.VMEM
F32 = jnp.float32
BF16 = jnp.bfloat16


def lane_ids(rows):
    return lax.broadcasted_iota(jnp.int32, (rows, LANES), 1)


def row_ids(rows, columns):
    return lax.broadcasted_iota(jnp.int32, (rows, columns), 0)


def params():
    return pltpu.CompilerParams(vmem_limit_bytes=40 * 1024 * 1024)


def cost(microseconds):
    return pl.CostEstimate(flops=0, bytes_accessed=int(microseconds * 3.5e6), transcendentals=0)


def turn(value, by):
    return pltpu.roll(value, by % LANES, 1)


def is_even():
    return lax.rem(lax.axis_index("track"), 2) == 0


def fetch(sources, targets, sems):
    copies = [pltpu.make_async_copy(s, t, sems.at[i]) for i, (s, t) in enumerate(zip(sources, targets))]
    for copy in copies:
        copy.start()
    return copies


def field_copies(arrays, held, sems):
    velocity, stress, adj_velocity, adj_stress, buoyancy, lame, shear = arrays
    sources = (velocity, stress, buoyancy, lame, shear, adj_velocity, adj_stress)
    targets = (
        held.at[pl.ds(0, 2)],
        held.at[pl.ds(2, 3)],
        held.at[5],
        held.at[6],
        held.at[7],
        held.at[pl.ds(8, 2)],
        held.at[pl.ds(10, 3)],
    )
    return fetch(sources, targets, sems)


def outer_kernel(velocity, stress, buoyancy, lame, shear, even_out, odd_out, strips, sems):
    depth = lax.axis_index("depth")
    even = is_even()
    rows = buoyancy.shape[0]
    lanes = pl.ds(pl.multiple_of(depth * LANES, LANES), LANES)
    sources, targets = [], []
    for side, row in enumerate((0, rows - EDGE)):
        span = pl.ds(row, EDGE)
        sources += [array.at[:, span, lanes] for array in (velocity, stress)]
        targets += [strips.at[side, pl.ds(0, 2)], strips.at[side, pl.ds(2, 3)]]
        sources += [array.at[span, lanes] for array in (buoyancy, lame, shear)]
        targets += [strips.at[side, f] for f in (5, 6, 7)]
    copies = fetch(sources, targets, sems)
    for out in (even_out, odd_out):
        out[:OUTER, :] = jnp.zeros((OUTER, LANES), F32)
        out[OUTER + HALO * FORWARD :, :] = jnp.zeros((EDGE - HALO, LANES), F32)
    for copy in copies:
        copy.wait()
    for f in range(FORWARD):
        low, high = strips[0, f, :HALO, :], strips[1, f, EDGE - HALO :, :]
        at = OUTER + HALO * f
        even_out[at : at + HALO, :] = jnp.where(even, high, low)
        odd_out[at : at + HALO, :] = jnp.where(even, low, high)


def pack_kernel(*refs):
    arrays, channel_arrays = refs[:7], refs[7:10]
    held, depth_out, even_out, odd_out, traces_out, cells_out = refs[11:17]
    numbers, sems = refs[17:]
    copies = field_copies(arrays, held, sems)
    targets = (traces_out, numbers.at[0], numbers.at[1])
    channel_copies = [
        pltpu.make_async_copy(source, target, sems.at[7 + i])
        for i, (source, target) in enumerate(zip(channel_arrays, targets))
    ]
    for copy in channel_copies:
        copy.start()
    depth = lax.axis_index("depth")
    even = is_even()
    rows = held.shape[1]
    lane = lane_ids(rows)
    tail = INNER + HALO * 4
    for out in (even_out, odd_out):
        out[:EDGE, :] = jnp.zeros((EDGE, 2 * LANES), F32)
        out[tail:, :] = jnp.zeros((out.shape[0] - tail, 2 * LANES), F32)
    for copy in copies:
        copy.wait()
    packed = [jnp.zeros((rows, LANES), F32) for _ in range(2)]
    for f in range(FIELDS):
        group, place = divmod(f, FORWARD)
        spot = EDGE * place
        here = (lane >= spot) & (lane < spot + EDGE)
        edge = jnp.where(depth == 0, held[f, :, LANES:], held[f, :, :LANES])
        shift = lax.rem(spot + EDGE * (1 - depth), LANES)
        packed[group] = jnp.where(here, pltpu.roll(edge, shift, 1), packed[group])
        if f < FORWARD:
            low, high = edge[:HALO], edge[rows - HALO :]
            at, lanes = INNER + HALO * (f % 4), slice(LANES * (f // 4), LANES * (f // 4) + LANES)
        else:
            low, high = held[f, :HALO, :], held[f, rows - HALO :, :]
            at, lanes = EDGE + HALO * place, slice(0, 2 * LANES)
        even_out[at : at + HALO, lanes] = jnp.where(even, high, low)
        odd_out[at : at + HALO, lanes] = jnp.where(even, low, high)
    depth_out[:, :LANES] = packed[0]
    depth_out[:, LANES:] = packed[1]
    for copy in channel_copies:
        copy.wait()
    cells_out[0] = numbers[0] * rows + lax.shift_right_logical(numbers[1], 2)
    cells_out[1] = numbers[1] & 3


def corner_kernel(got, even_in, odd_in, even_out, odd_out, sems):
    rows = got.shape[0]
    is_odd = lax.rem(lax.axis_index("track"), 2)
    high, low = (rows - EDGE) * (1 - is_odd), (rows - EDGE) * is_odd
    one = pltpu.make_async_copy(
        got.at[pl.ds(pl.multiple_of(high, EDGE), EDGE), :], even_out.at[pl.ds(0, EDGE), :], sems.at[0]
    )
    two = pltpu.make_async_copy(
        got.at[pl.ds(pl.multiple_of(low, EDGE), EDGE), :], odd_out.at[pl.ds(0, EDGE), :], sems.at[1]
    )
    one.start()
    two.start()
    one.wait()
    two.wait()


def window(plane, f, outer, other, halo):
    depth = lax.axis_index("depth")
    surface = depth == 0
    lane = lane_ids(outer.shape[0])
    low = jnp.where(surface, lane, LANES - 1 - lane)
    if plane == 0:
        shift = jnp.where(surface, EDGE, LANES - EDGE)
        return jnp.where(low >= EDGE, pltpu.roll(outer, shift, 1), 0.0)
    if plane == 1:
        return jnp.where(low < LANES // 2, turn(outer, LANES // 2), turn(other, LANES // 2))
    shift = jnp.where(surface, LANES - EDGE, EDGE)
    beside = lax.rem(LANES - EDGE * (f % FORWARD) + (LANES - EDGE) * (1 - depth), LANES)
    return jnp.where(low < LANES - EDGE, pltpu.roll(other, shift, 1), pltpu.roll(halo, beside, 1))


def split(value):
    surface = lax.axis_index("depth") == 0
    first, last = value[:, :LANES], value[:, LANES:]
    return jnp.where(surface, first, last), jnp.where(surface, last, first)


def joined(outer, middle, inner):
    surface = lax.axis_index("depth") == 0
    lane = lane_ids(outer.shape[0])
    first, last = jnp.where(surface, outer, inner), jnp.where(surface, inner, outer)
    middle = turn(middle, LANES // 2)
    return jnp.where(lane < 88, turn(first, -EDGE), middle), jnp.where(lane < 40, middle, turn(last, EDGE))


class Blocks:
    def __init__(self, held, got_depth, outer, bulk):
        self.held, self.got_depth, self.outer, self.bulk = held, got_depth, outer, bulk

    def from_edges(self, pair, side, at, lanes):
        even_got, odd_got = pair
        span = slice(at - (EDGE - HALO), at + HALO) if side == 0 else slice(at, at + EDGE)
        use_odd = is_even() if side == 0 else ~is_even()
        return jnp.where(use_odd, odd_got[span, lanes], even_got[span, lanes])

    def edge_windows(self, f, side, planes):
        whole = slice(0, LANES)
        inner = planes != (0,)
        outer = other = halo = None
        if f < FORWARD:
            outer = self.from_edges(self.outer, side, OUTER + HALO * f, whole)
            if inner:
                lanes = slice(LANES * (f // 4), LANES * (f // 4) + LANES)
                other = self.from_edges(self.bulk, side, INNER + HALO * (f % 4), lanes)
        else:
            at = EDGE + HALO * (f - FORWARD)
            outer, other = split(self.from_edges(self.bulk, side, at, slice(0, 2 * LANES)))
        if inner:
            even_got, odd_got = self.bulk
            lanes = slice(LANES * (f // FORWARD), LANES * (f // FORWARD) + LANES)
            use_odd = is_even() if side == 0 else ~is_even()
            halo = jnp.where(use_odd, odd_got[:EDGE, lanes], even_got[:EDGE, lanes])
        return [window(p, f, outer, other, halo) for p in planes]

    def own_windows(self, f, planes):
        outer, other = split(self.held[f])
        halo = None
        if planes != (0,):
            col = LANES * (f // FORWARD)
            halo = self.got_depth[:, col : col + LANES]
        return [window(p, f, outer, other, halo) for p in planes]

    def windows(self, f, planes):
        rows = self.held.shape[1]
        sets = self.edge_windows(f, 0, planes), self.own_windows(f, planes), self.edge_windows(f, 1, planes)
        return [[(at, part[i]) for at, part in zip((0, EDGE, EDGE + rows), sets)] for i in range(len(planes))]


def load_state(state, blocks, base, planes):
    extent = blocks.held.shape[1] + 2 * EDGE
    for f in range(5):
        for i, parts in enumerate(blocks.windows(base + f, planes)):
            state[f, i, :PAD, :] = jnp.zeros((PAD, LANES), F32)
            state[f, i, PAD + extent :, :] = jnp.zeros((PAD, LANES), F32)
            for at, part in parts:
                state[f, i, PAD + at : PAD + at + part.shape[0], :] = part


def velocities(state, media, span):
    for r in range(8 * span[0], 8 * span[1], 8):
        for i in range(state.shape[1]):

            def at(f, by=0):
                return state[f, i, r + PAD + by : r + PAD + by + 8, :]

            xx, xz, zz = at(2), at(4), at(3)
            b = media[0, i, r : r + 8, :]
            near = (xx - at(2, -1)) + (xz - turn(xz, 1))
            far = (at(2, 1) - at(2, -2)) + (turn(xz, -1) - turn(xz, 2))
            state[0, i, r + PAD : r + PAD + 8, :] = at(0) + b * (near + RATIO * far)
            near = (at(4, 1) - xz) + (turn(zz, -1) - zz)
            far = (at(4, 2) - at(4, -1)) + (turn(zz, -2) - turn(zz, 1))
            state[1, i, r + PAD : r + PAD + 8, :] = at(1) + b * (near + RATIO * far)


def stresses(state, media, span, update, keep):
    for r in range(8 * span[0], 8 * span[1], 8):
        for i in range(state.shape[1]):

            def at(f, by=0):
                return state[f, i, r + PAD + by : r + PAD + by + 8, :]

            vx, vz = at(0), at(1)
            exx = (at(0, 1) - vx) + RATIO * (at(0, 2) - at(0, -1))
            ezz = (vz - turn(vz, 1)) + RATIO * (turn(vz, -1) - turn(vz, 2))
            near = (turn(vx, -1) - vx) + (vz - at(1, -1))
            far = (turn(vx, -2) - turn(vx, 1)) + (at(1, 1) - at(1, -2))
            shear = near + RATIO * far
            keep(i, r - EDGE, exx, ezz, shear)
            if update:
                whole, lam, mu = (media[k, i, r : r + 8, :] for k in (1, 2, 3))
                state[2, i, r + PAD : r + PAD + 8, :] = at(2) + (whole * exx + lam * ezz)
                state[3, i, r + PAD : r + PAD + 8, :] = at(3) + (lam * exx + whole * ezz)
                state[4, i, r + PAD : r + PAD + 8, :] = at(4) + mu * shear


def spans(step, rows):
    tiles = (rows + 2 * EDGE) // 8
    if step == 0:
        return (0, tiles), (0, tiles)
    inner = (1, tiles - 1)
    return inner, inner if step < MOMENTS - 1 else (EDGE // 8, tiles - EDGE // 8)


def run_forward(blocks, media, saved, state, planes):
    rows = blocks.held.shape[1]
    given = [blocks.windows(f, planes) for f in (5, 6, 7)]
    for i in range(len(planes)):
        for k in range(3):
            at = given[0][i][k][0]
            b, lam, mu = (NEAR * given[m][i][k][1] for m in range(3))
            span = slice(at, at + b.shape[0])
            media[0, i, span, :] = b
            media[1, i, span, :] = lam + 2.0 * mu
            media[2, i, span, :] = lam
            media[3, i, span, :] = mu
    load_state(state, blocks, 0, planes)
    for step in range(MOMENTS):
        fast, slow = spans(step, rows)
        velocities(state, media, fast)

        def save(i, r, exx, ezz, shear):
            if 0 <= r < rows:
                saved[step, 0, i, r : r + 8, :] = exx
                saved[step, 1, i, r : r + 8, :] = ezz
                saved[step, 2, i, r : r + 8, :] = shear

        stresses(state, media, slow, step < MOMENTS - 1, save)


def forward_top_kernel(
    held, outer_even, outer_odd, traces, cells, media, saved, end_out, note_out, state
):
    blocks = Blocks(held, None, (outer_even, outer_odd), None)
    run_forward(blocks, media, saved, state, (0,))
    rows = held.shape[1]
    top = PAD + EDGE
    for f in range(2):
        end_out[f] = state[f, 0, top : top + rows, :]
    lane = lane_ids(rows)
    image = jnp.zeros((rows, LANES), F32)
    for step in range(MOMENTS):
        spot = FIBRE_ROWS * step
        here = (lane >= spot) & (lane < spot + FIBRE_ROWS)
        image = jnp.where(here, NEAR * turn(saved[step, 0, 0], spot - EDGE), image)
    turned = image.T
    half = IMAGE // 2
    rates = jnp.concatenate([turned[:half], turned[half:IMAGE]], axis=1)
    seen = jnp.concatenate([traces[:, :LANES], traces[:, LANES:]], axis=0)
    mine = jnp.where(lax.axis_index("depth") == 0, rates, seen)
    along, row = cells[0], cells[1]
    places = jnp.concatenate([along[:, :LANES], along[:, LANES:], row[:, :LANES], row[:, LANES:]], axis=0)
    for i, value in enumerate((mine[:4], mine[4:], places.astype(F32))):
        note_out[:, i] = jnp.broadcast_to(value[None], (note_out.shape[0], 4, LANES))


def forward_rest_kernel(
    held, got_depth, outer_even, outer_odd, even, odd, top_end, media, saved, end_out, state
):
    blocks = Blocks(held, got_depth, (outer_even, outer_odd), (even, odd))
    run_forward(blocks, media, saved, state, (1, 2))
    rows = held.shape[1]
    top = PAD + EDGE
    for f in range(2):
        first, last = joined(top_end[f], *(state[f, i, top : top + rows, :] for i in range(2)))
        end_out[f, :, :LANES] = first
        end_out[f, :, LANES:] = last


def three(value):
    high = value.astype(BF16)
    rest = value - high.astype(F32)
    middle = rest.astype(BF16)
    low = (rest - middle.astype(F32)).astype(BF16)
    return [high, middle, low]


def add_up(value):
    return (value[2 * IMAGE : 3 * IMAGE] + value[IMAGE : 2 * IMAGE]) + value[:IMAGE]


def channel_sums(tracks, rows, notes, beside, own_along):
    start = lax.axis_index("track") * rows - EDGE
    surface = lax.axis_index("depth") == 0
    group = min(8, tracks)
    channels = own_along.shape[1]
    lane = lane_ids(8)
    half = LANES // 2
    wanted = jnp.concatenate([own_along, start + lax.broadcasted_iota(jnp.int32, (1, LANES), 1)], axis=1)
    row16 = row_ids(IMAGE, LANES)

    def body(number, carry):
        rate, image = carry
        base = number * group
        firsts, lasts = [], []
        mine = [[notes[base + k, i] for i in range(3)] for k in range(group)]
        other = [[beside[base + k, i] for i in range(3)] for k in range(group)]
        rates = [
            jnp.concatenate([jnp.where(surface, m[i], o[i]) for i in range(2)], axis=0) for m, o in zip(mine, other)
        ]
        traces = [[jnp.where(surface, o[i], m[i]) for i in range(2)] for m, o in zip(mine, other)]
        for k in range(0, group, 2):
            a, b = rates[k], rates[k + 1]
            firsts.append(jnp.where(lane < half, a, turn(b, half)))
            lasts.append(jnp.where(lane < half, turn(a, half), b))
        strains = jnp.concatenate([jnp.concatenate(firsts, axis=1), jnp.concatenate(lasts, axis=1)], axis=0)
        spot = base * rows + row_ids(group * rows, channels + LANES)
        hot = (spot == wanted).astype(F32).astype(BF16)
        rate = rate + jnp.dot(jnp.concatenate(three(strains), axis=0), hot, preferred_element_type=F32)
        weights, hots = [], []
        for k in range(group):
            for h in range(2):
                along = mine[k][2][h : h + 1]
                mask = (row16 & 3).astype(F32) == mine[k][2][2 + h : 3 + h]
                seen = [traces[k][h][t : t + 1] for t in range(MOMENTS)]
                value = jnp.where(
                    row16 < 8,
                    jnp.where(row16 < 4, seen[0], seen[1]),
                    jnp.where(row16 < 12, seen[2], seen[3]),
                )
                pieces = three(jnp.where(mask, value, 0.0)) + [mask.astype(F32).astype(BF16)]
                weights.append(jnp.concatenate(pieces, axis=0))
                spot = (start + row_ids(LANES, LANES)).astype(F32)
                hots.append((spot == along).astype(F32).astype(BF16))
        image = image + lax.dot_general(
            jnp.concatenate(weights, axis=1),
            jnp.concatenate(hots, axis=1),
            (((1,), (1,)), ((), ())),
            preferred_element_type=F32,
        )
        return rate, image

    carry = jnp.zeros((3 * IMAGE, channels + LANES), F32), jnp.zeros((4 * IMAGE, LANES), F32)
    if tracks == group:
        carry = body(0, carry)
    else:
        carry = lax.fori_loop(0, tracks // group, body, carry)
    rate, image = carry
    return add_up(rate), add_up(image), image[3 * IMAGE :]


def run_adjoint(media, saved, state, sums, inject=None):
    rows = sums.shape[2]
    sums[...] = jnp.zeros(sums.shape, F32)
    for step in range(MOMENTS):
        fast, slow = spans(step, rows)
        moment = MOMENTS - 1 - step
        if inject is not None:
            inject(moment)
        velocities(state, media, fast)

        def gather(i, r, exx, ezz, shear):
            if 0 <= r < rows:
                fxx, fzz, fxz = (saved[moment, k, i, r : r + 8, :] for k in range(3))
                sums[0, i, r : r + 8, :] += (fxx + fzz) * (exx + ezz)
                sums[1, i, r : r + 8, :] += 2.0 * (fxx * exx + fzz * ezz) + fxz * shear

        stresses(state, media, slow, step < MOMENTS - 1, gather)


def adjoint_rest_kernel(held, got_depth, even, odd, media, saved, notes, sums, state):
    del notes
    load_state(state, Blocks(held, got_depth, None, (even, odd)), FORWARD, (1, 2))
    run_adjoint(media, saved, state, sums)


def adjoint_top_kernel(
    tracks, held, even, odd, media, saved, notes, beside, rest, obs, cells,
    lambda_out, mu_out, residual_out, state, sums,
):
    rows = held.shape[1]
    extent = rows + 2 * EDGE
    depth = lax.axis_index("depth")
    load_state(state, Blocks(held, None, None, (even, odd)), FORWARD, (0,))
    along, row = cells[0], cells[1]
    rate, seen, count = channel_sums(tracks, rows, notes, beside, along)
    channels = along.shape[1]
    at_own = jnp.where((row_ids(IMAGE, channels) & 3) == row, rate[:, :channels], 0.0)
    traces = [
        jnp.sum(at_own[4 * t : 4 * t + 4], axis=0, keepdims=True) - obs[t : t + 1, :] for t in range(MOMENTS)
    ]
    residual_out[...] = jnp.where(
        depth == 0, jnp.concatenate(traces[:2], axis=0), jnp.concatenate(traces[2:], axis=0)
    )
    sources = count * rate[:, channels:] - seen
    turned = jnp.concatenate([sources, jnp.zeros((LANES - IMAGE, LANES), F32)], axis=0).T[:extent]
    lane = lane_ids(extent)
    here = (lane >= EDGE) & (lane < EDGE + FIBRE_ROWS) & (depth == 0)

    def inject(moment):
        added = jnp.where(here, turn(turned, EDGE - FIBRE_ROWS * moment), 0.0)
        state[2, 0, PAD : PAD + extent, :] += added

    run_adjoint(media, saved, state, sums, inject)
    for k, out in enumerate((lambda_out, mu_out)):
        first, last = joined(sums[k, 0], rest[k, 0], rest[k, 1])
        out[:, :LANES] = (NEAR * NEAR) * first
        out[:, LANES:] = (NEAR * NEAR) * last


def per_device(
    velocity,
    stress,
    adjoint_velocity,
    adjoint_stress,
    buoyancy,
    lame_lambda,
    shear_modulus,
    observed,
    owner_track,
    fibre_cell,
):
    tracks = lax.axis_size("track")
    rows, depth_cells = buoyancy.shape
    moments, channels = observed.shape
    owner = owner_track.reshape(1, channels)
    cell = fibre_cell.reshape(1, channels)
    pinned = lambda array: pltpu.with_memory_space_constraint(array, pltpu.HBM)
    arrays = (velocity, stress, adjoint_velocity, adjoint_stress, buoyancy, lame_lambda, shear_modulus)
    arrays = tuple(pinned(array) for array in arrays)
    channel_arrays = (pinned(observed), pinned(owner), pinned(cell))
    extent = rows + 2 * EDGE
    block = jax.ShapeDtypeStruct((rows, depth_cells), F32)
    outer_edges = jax.ShapeDtypeStruct((OUTER + HALO * FORWARD + EDGE - HALO, LANES), F32)
    edges = jax.ShapeDtypeStruct((INNER + HALO * 4 + EDGE - HALO, depth_cells), F32)
    inside = pl.BlockSpec(memory_space=VMEM)
    outside = pl.BlockSpec(memory_space=pltpu.HBM)
    anywhere = pl.BlockSpec(memory_space=pl.ANY)
    swap = lambda k: [pair for i in range(k, tracks - 1, 2) for pair in ((i, i + 1), (i + 1, i))]
    to_even, to_odd = pl.pallas_call(
        outer_kernel,
        out_shape=(outer_edges, outer_edges),
        in_specs=[outside] * 5,
        out_specs=(inside,) * 2,
        scratch_shapes=[VMEM((2, FORWARD, EDGE, LANES), F32), pltpu.SemaphoreType.DMA((10,))],
        compiler_params=params(),
        cost_estimate=cost(1),
        name="outer",
    )(*arrays[:2], *arrays[4:])
    outer_odd = lax.ppermute(to_odd, "track", swap(1))
    outer_even = lax.ppermute(to_even, "track", swap(0))

    held, to_depth, to_even, to_odd, traces, cells = pl.pallas_call(
        pack_kernel,
        out_shape=(
            jax.ShapeDtypeStruct((FIELDS, rows, depth_cells), F32),
            block,
            edges,
            edges,
            jax.ShapeDtypeStruct((moments, channels), F32),
            jax.ShapeDtypeStruct((2, 1, channels), jnp.int32),
        ),
        in_specs=[outside] * 10 + [anywhere],
        out_specs=(inside,) * 6,
        scratch_shapes=[VMEM((2, 1, channels), jnp.int32), pltpu.SemaphoreType.DMA((10,))],
        compiler_params=params(),
        cost_estimate=cost(500),
        name="pack",
    )(*arrays, *channel_arrays, to_even)
    depth_swap = [(0, 1), (1, 0)]
    got_depth = lax.ppermute(to_depth, "depth", depth_swap)
    to_even, to_odd = pl.pallas_call(
        corner_kernel,
        out_shape=(edges, edges),
        in_specs=[anywhere] * 3,
        out_specs=(anywhere,) * 2,
        input_output_aliases={1: 0, 2: 1},
        scratch_shapes=[pltpu.SemaphoreType.DMA((2,))],
        compiler_params=params(),
        name="corners",
    )(got_depth, to_even, to_odd)
    got_odd = lax.ppermute(to_odd, "track", swap(1))
    got_even = lax.ppermute(to_even, "track", swap(0))

    def media_of(planes):
        return jax.ShapeDtypeStruct((4, planes, extent, LANES), F32)

    def saved_of(planes):
        return jax.ShapeDtypeStruct((moments, 3, planes, rows, LANES), F32)

    def state_of(planes):
        return VMEM((5, planes, extent + 2 * PAD, LANES), F32)

    media_top, saved_top, top_end, note = pl.pallas_call(
        forward_top_kernel,
        out_shape=(
            media_of(1),
            saved_of(1),
            jax.ShapeDtypeStruct((2, rows, LANES), F32),
            jax.ShapeDtypeStruct((tracks, 3, 4, LANES), F32),
        ),
        in_specs=[inside] * 5,
        out_specs=(inside,) * 4,
        scratch_shapes=[state_of(1)],
        compiler_params=params(),
        cost_estimate=cost(500),
        name="forward_top",
    )(held, outer_even, outer_odd, traces, cells)
    notes = lax.all_to_all(note, "track", split_axis=0, concat_axis=0, tiled=True)
    beside = lax.ppermute(notes, "depth", depth_swap)
    media_rest, saved_rest, velocity_end = pl.pallas_call(
        forward_rest_kernel,
        out_shape=(media_of(2), saved_of(2), jax.ShapeDtypeStruct(velocity.shape, F32)),
        in_specs=[inside] * 7,
        out_specs=(inside,) * 3,
        scratch_shapes=[state_of(2)],
        compiler_params=params(),
        cost_estimate=cost(500),
        name="forward_rest",
    )(held, got_depth, outer_even, outer_odd, got_even, got_odd, top_end)
    rest = pl.pallas_call(
        adjoint_rest_kernel,
        out_shape=jax.ShapeDtypeStruct((2, 2, rows, LANES), F32),
        in_specs=[inside] * 6 + [anywhere],
        out_specs=inside,
        scratch_shapes=[state_of(2)],
        compiler_params=params(),
        cost_estimate=cost(500),
        name="adjoint_rest",
    )(held, got_depth, got_even, got_odd, media_rest, saved_rest, notes)
    gradient_lambda, gradient_mu, residual = pl.pallas_call(
        lambda *refs: adjoint_top_kernel(tracks, *refs),
        out_shape=(block, block, jax.ShapeDtypeStruct((moments // 2, channels), F32)),
        in_specs=[inside] * 10,
        out_specs=(inside,) * 3,
        scratch_shapes=[state_of(1), VMEM((2, 1, rows, LANES), F32)],
        compiler_params=params(),
        cost_estimate=cost(2),
        name="adjoint_top",
    )(held, got_even, got_odd, media_top, saved_top, notes, beside, rest, traces, cells)
    return gradient_lambda, gradient_mu, velocity_end, residual


def solution(mesh):
    return jax.shard_map(
        per_device,
        mesh=mesh,
        in_specs=(
            P("shots", "track", "depth"),
            P("shots", "track", "depth"),
            P("shots", "track", "depth"),
            P("shots", "track", "depth"),
            P("track", "depth"),
            P("track", "depth"),
            P("track", "depth"),
            P("shots", "track"),
            P("track", None),
            P("track"),
        ),
        out_specs=(
            P(("shots", "track"), "depth"),
            P(("shots", "track"), "depth"),
            P("shots", "track", "depth"),
            P(("shots", "depth"), "track"),
        ),
        check_vma=False,
    )
```

```python
import jax
import jax.numpy as jnp
from jax import lax
from jax.experimental import pallas as pl
from jax.experimental.pallas import tpu as pltpu
from jax.sharding import PartitionSpec as P

FIBRE_ROWS = 4
NEAR = 9.0 / 8.0
RATIO = -1.0 / 27.0
HALO = 12
EDGE = 16
LANES = 128
PAD = 8
FORWARD = 8
ADJOINT = 5
FIELDS = FORWARD + ADJOINT
OUTER = EDGE - HALO
INNER = EDGE + HALO * ADJOINT
MOMENTS = 4
IMAGE = MOMENTS * FIBRE_ROWS
VMEM = pltpu.VMEM
F32 = jnp.float32
BF16 = jnp.bfloat16


def lane_ids(rows):
    return lax.broadcasted_iota(jnp.int32, (rows, LANES), 1)


def row_ids(rows, columns):
    return lax.broadcasted_iota(jnp.int32, (rows, columns), 0)


def params():
    return pltpu.CompilerParams(vmem_limit_bytes=40 * 1024 * 1024)


def cost(microseconds):
    return pl.CostEstimate(flops=0, bytes_accessed=int(microseconds * 3.5e6), transcendentals=0)


def turn(value, by):
    return pltpu.roll(value, by % LANES, 1)


def is_even():
    return lax.rem(lax.axis_index("track"), 2) == 0


def fetch(sources, targets, sems):
    copies = [pltpu.make_async_copy(s, t, sems.at[i]) for i, (s, t) in enumerate(zip(sources, targets))]
    for copy in copies:
        copy.start()
    return copies


def field_copies(arrays, held, sems):
    velocity, stress, adj_velocity, adj_stress, buoyancy, lame, shear = arrays
    sources = (velocity, stress, buoyancy, lame, shear, adj_velocity, adj_stress)
    targets = (
        held.at[pl.ds(0, 2)],
        held.at[pl.ds(2, 3)],
        held.at[5],
        held.at[6],
        held.at[7],
        held.at[pl.ds(8, 2)],
        held.at[pl.ds(10, 3)],
    )
    return fetch(sources, targets, sems)


def outer_kernel(velocity, stress, buoyancy, lame, shear, even_out, odd_out, strips, sems):
    depth = lax.axis_index("depth")
    even = is_even()
    rows = buoyancy.shape[0]
    lanes = pl.ds(pl.multiple_of(depth * LANES, LANES), LANES)
    sources, targets = [], []
    for side, row in enumerate((0, rows - EDGE)):
        span = pl.ds(row, EDGE)
        sources += [array.at[:, span, lanes] for array in (velocity, stress)]
        targets += [strips.at[side, pl.ds(0, 2)], strips.at[side, pl.ds(2, 3)]]
        sources += [array.at[span, lanes] for array in (buoyancy, lame, shear)]
        targets += [strips.at[side, f] for f in (5, 6, 7)]
    copies = fetch(sources, targets, sems)
    for out in (even_out, odd_out):
        out[:OUTER, :] = jnp.zeros((OUTER, LANES), F32)
        out[OUTER + HALO * FORWARD :, :] = jnp.zeros((EDGE - HALO, LANES), F32)
    for copy in copies:
        copy.wait()
    for f in range(FORWARD):
        low, high = strips[0, f, :HALO, :], strips[1, f, EDGE - HALO :, :]
        at = OUTER + HALO * f
        even_out[at : at + HALO, :] = jnp.where(even, high, low)
        odd_out[at : at + HALO, :] = jnp.where(even, low, high)


def pack_kernel(*refs):
    arrays, channel_arrays = refs[:7], refs[7:10]
    held, depth_out, even_out, odd_out, traces_out, cells_out = refs[11:17]
    numbers, sems = refs[17:]
    copies = field_copies(arrays, held, sems)
    targets = (traces_out, numbers.at[0], numbers.at[1])
    channel_copies = [
        pltpu.make_async_copy(source, target, sems.at[7 + i])
        for i, (source, target) in enumerate(zip(channel_arrays, targets))
    ]
    for copy in channel_copies:
        copy.start()
    depth = lax.axis_index("depth")
    even = is_even()
    rows = held.shape[1]
    lane = lane_ids(rows)
    tail = INNER + HALO * 4
    for out in (even_out, odd_out):
        out[:EDGE, :] = jnp.zeros((EDGE, 2 * LANES), F32)
        out[tail:, :] = jnp.zeros((out.shape[0] - tail, 2 * LANES), F32)
    for copy in copies:
        copy.wait()
    packed = [jnp.zeros((rows, LANES), F32) for _ in range(2)]
    for f in range(FIELDS):
        group, place = divmod(f, FORWARD)
        spot = EDGE * place
        here = (lane >= spot) & (lane < spot + EDGE)
        edge = jnp.where(depth == 0, held[f, :, LANES:], held[f, :, :LANES])
        shift = lax.rem(spot + EDGE * (1 - depth), LANES)
        packed[group] = jnp.where(here, pltpu.roll(edge, shift, 1), packed[group])
        if f < FORWARD:
            low, high = edge[:HALO], edge[rows - HALO :]
            at, lanes = INNER + HALO * (f % 4), slice(LANES * (f // 4), LANES * (f // 4) + LANES)
        else:
            low, high = held[f, :HALO, :], held[f, rows - HALO :, :]
            at, lanes = EDGE + HALO * place, slice(0, 2 * LANES)
        even_out[at : at + HALO, lanes] = jnp.where(even, high, low)
        odd_out[at : at + HALO, lanes] = jnp.where(even, low, high)
    depth_out[:, :LANES] = packed[0]
    depth_out[:, LANES:] = packed[1]
    for copy in channel_copies:
        copy.wait()
    cells_out[0] = numbers[0] * rows + lax.shift_right_logical(numbers[1], 2)
    cells_out[1] = numbers[1] & 3


def corner_kernel(got, even_in, odd_in, even_out, odd_out, sems):
    rows = got.shape[0]
    is_odd = lax.rem(lax.axis_index("track"), 2)
    high, low = (rows - EDGE) * (1 - is_odd), (rows - EDGE) * is_odd
    one = pltpu.make_async_copy(
        got.at[pl.ds(pl.multiple_of(high, EDGE), EDGE), :], even_out.at[pl.ds(0, EDGE), :], sems.at[0]
    )
    two = pltpu.make_async_copy(
        got.at[pl.ds(pl.multiple_of(low, EDGE), EDGE), :], odd_out.at[pl.ds(0, EDGE), :], sems.at[1]
    )
    one.start()
    two.start()
    one.wait()
    two.wait()


def window(plane, f, outer, other, halo):
    depth = lax.axis_index("depth")
    surface = depth == 0
    lane = lane_ids(outer.shape[0])
    low = jnp.where(surface, lane, LANES - 1 - lane)
    if plane == 0:
        shift = jnp.where(surface, EDGE, LANES - EDGE)
        return jnp.where(low >= EDGE, pltpu.roll(outer, shift, 1), 0.0)
    if plane == 1:
        return jnp.where(low < LANES // 2, turn(outer, LANES // 2), turn(other, LANES // 2))
    shift = jnp.where(surface, LANES - EDGE, EDGE)
    beside = lax.rem(LANES - EDGE * (f % FORWARD) + (LANES - EDGE) * (1 - depth), LANES)
    return jnp.where(low < LANES - EDGE, pltpu.roll(other, shift, 1), pltpu.roll(halo, beside, 1))


def split(value):
    surface = lax.axis_index("depth") == 0
    first, last = value[:, :LANES], value[:, LANES:]
    return jnp.where(surface, first, last), jnp.where(surface, last, first)


def joined(outer, middle, inner):
    surface = lax.axis_index("depth") == 0
    lane = lane_ids(outer.shape[0])
    first, last = jnp.where(surface, outer, inner), jnp.where(surface, inner, outer)
    middle = turn(middle, LANES // 2)
    return jnp.where(lane < 88, turn(first, -EDGE), middle), jnp.where(lane < 40, middle, turn(last, EDGE))


class Blocks:
    def __init__(self, held, got_depth, outer, bulk):
        self.held, self.got_depth, self.outer, self.bulk = held, got_depth, outer, bulk

    def from_edges(self, pair, side, at, lanes):
        even_got, odd_got = pair
        span = slice(at - (EDGE - HALO), at + HALO) if side == 0 else slice(at, at + EDGE)
        use_odd = is_even() if side == 0 else ~is_even()
        return jnp.where(use_odd, odd_got[span, lanes], even_got[span, lanes])

    def edge_windows(self, f, side, planes):
        whole = slice(0, LANES)
        inner = planes != (0,)
        outer = other = halo = None
        if f < FORWARD:
            outer = self.from_edges(self.outer, side, OUTER + HALO * f, whole)
            if inner:
                lanes = slice(LANES * (f // 4), LANES * (f // 4) + LANES)
                other = self.from_edges(self.bulk, side, INNER + HALO * (f % 4), lanes)
        else:
            at = EDGE + HALO * (f - FORWARD)
            outer, other = split(self.from_edges(self.bulk, side, at, slice(0, 2 * LANES)))
        if inner:
            even_got, odd_got = self.bulk
            lanes = slice(LANES * (f // FORWARD), LANES * (f // FORWARD) + LANES)
            use_odd = is_even() if side == 0 else ~is_even()
            halo = jnp.where(use_odd, odd_got[:EDGE, lanes], even_got[:EDGE, lanes])
        return [window(p, f, outer, other, halo) for p in planes]

    def own_windows(self, f, planes):
        outer, other = split(self.held[f])
        halo = None
        if planes != (0,):
            col = LANES * (f // FORWARD)
            halo = self.got_depth[:, col : col + LANES]
        return [window(p, f, outer, other, halo) for p in planes]

    def windows(self, f, planes):
        rows = self.held.shape[1]
        sets = self.edge_windows(f, 0, planes), self.own_windows(f, planes), self.edge_windows(f, 1, planes)
        return [[(at, part[i]) for at, part in zip((0, EDGE, EDGE + rows), sets)] for i in range(len(planes))]


def load_state(state, blocks, base, planes):
    extent = blocks.held.shape[1] + 2 * EDGE
    for f in range(5):
        for i, parts in enumerate(blocks.windows(base + f, planes)):
            state[f, i, :PAD, :] = jnp.zeros((PAD, LANES), F32)
            state[f, i, PAD + extent :, :] = jnp.zeros((PAD, LANES), F32)
            for at, part in parts:
                state[f, i, PAD + at : PAD + at + part.shape[0], :] = part


def velocities(state, media, span):
    for r in range(8 * span[0], 8 * span[1], 8):
        for i in range(state.shape[1]):

            def at(f, by=0):
                return state[f, i, r + PAD + by : r + PAD + by + 8, :]

            xx, xz, zz = at(2), at(4), at(3)
            b = media[0, i, r : r + 8, :]
            near = (xx - at(2, -1)) + (xz - turn(xz, 1))
            far = (at(2, 1) - at(2, -2)) + (turn(xz, -1) - turn(xz, 2))
            state[0, i, r + PAD : r + PAD + 8, :] = at(0) + b * (near + RATIO * far)
            near = (at(4, 1) - xz) + (turn(zz, -1) - zz)
            far = (at(4, 2) - at(4, -1)) + (turn(zz, -2) - turn(zz, 1))
            state[1, i, r + PAD : r + PAD + 8, :] = at(1) + b * (near + RATIO * far)


def stresses(state, media, span, update, keep):
    for r in range(8 * span[0], 8 * span[1], 8):
        for i in range(state.shape[1]):

            def at(f, by=0):
                return state[f, i, r + PAD + by : r + PAD + by + 8, :]

            vx, vz = at(0), at(1)
            exx = (at(0, 1) - vx) + RATIO * (at(0, 2) - at(0, -1))
            ezz = (vz - turn(vz, 1)) + RATIO * (turn(vz, -1) - turn(vz, 2))
            near = (turn(vx, -1) - vx) + (vz - at(1, -1))
            far = (turn(vx, -2) - turn(vx, 1)) + (at(1, 1) - at(1, -2))
            shear = near + RATIO * far
            keep(i, r - EDGE, exx, ezz, shear)
            if update:
                whole, lam, mu = (media[k, i, r : r + 8, :] for k in (1, 2, 3))
                state[2, i, r + PAD : r + PAD + 8, :] = at(2) + (whole * exx + lam * ezz)
                state[3, i, r + PAD : r + PAD + 8, :] = at(3) + (lam * exx + whole * ezz)
                state[4, i, r + PAD : r + PAD + 8, :] = at(4) + mu * shear


def spans(step, rows):
    tiles = (rows + 2 * EDGE) // 8
    if step == 0:
        return (0, tiles), (0, tiles)
    inner = (1, tiles - 1)
    return inner, inner if step < MOMENTS - 1 else (EDGE // 8, tiles - EDGE // 8)


def run_forward(blocks, media, saved, state, planes):
    rows = blocks.held.shape[1]
    given = [blocks.windows(f, planes) for f in (5, 6, 7)]
    for i in range(len(planes)):
        for k in range(3):
            at = given[0][i][k][0]
            b, lam, mu = (NEAR * given[m][i][k][1] for m in range(3))
            span = slice(at, at + b.shape[0])
            media[0, i, span, :] = b
            media[1, i, span, :] = lam + 2.0 * mu
            media[2, i, span, :] = lam
            media[3, i, span, :] = mu
    load_state(state, blocks, 0, planes)
    for step in range(MOMENTS):
        fast, slow = spans(step, rows)
        velocities(state, media, fast)

        def save(i, r, exx, ezz, shear):
            if 0 <= r < rows:
                saved[step, 0, i, r : r + 8, :] = exx
                saved[step, 1, i, r : r + 8, :] = ezz
                saved[step, 2, i, r : r + 8, :] = shear

        stresses(state, media, slow, step < MOMENTS - 1, save)


def forward_top_kernel(held, outer_even, outer_odd, media, saved, end_out, image_out, state):
    blocks = Blocks(held, None, (outer_even, outer_odd), None)
    run_forward(blocks, media, saved, state, (0,))
    rows = held.shape[1]
    top = PAD + EDGE
    for f in range(2):
        end_out[f] = state[f, 0, top : top + rows, :]
    lane = lane_ids(rows)
    image = jnp.zeros((rows, LANES), F32)
    for step in range(MOMENTS):
        spot = FIBRE_ROWS * step
        here = (lane >= spot) & (lane < spot + FIBRE_ROWS)
        image = jnp.where(here, NEAR * turn(saved[step, 0, 0], spot - EDGE), image)
    turned = image.T
    half = IMAGE // 2
    image_out[...] = jnp.concatenate([turned[:half], turned[half:IMAGE]], axis=1)


def forward_rest_kernel(
    held, got_depth, outer_even, outer_odd, even, odd, top_end, media, saved, end_out, state
):
    blocks = Blocks(held, got_depth, (outer_even, outer_odd), (even, odd))
    run_forward(blocks, media, saved, state, (1, 2))
    rows = held.shape[1]
    top = PAD + EDGE
    for f in range(2):
        first, last = joined(top_end[f], *(state[f, i, top : top + rows, :] for i in range(2)))
        end_out[f, :, :LANES] = first
        end_out[f, :, LANES:] = last


def note_kernel(image, image_beside, obs, cells, note_out):
    rates = jnp.where(lax.axis_index("depth") == 0, image[...], image_beside[...])
    seen = obs[...]
    along, row = cells[0], cells[1]
    places = jnp.concatenate([along[:, :LANES], along[:, LANES:], row[:, :LANES], row[:, LANES:]], axis=0)
    for i, value in enumerate((rates[:4], rates[4:], seen[:, :LANES], seen[:, LANES:], places.astype(F32))):
        note_out[:, i] = jnp.broadcast_to(value[None], (note_out.shape[0], 4, LANES))


def three(value):
    high = value.astype(BF16)
    rest = value - high.astype(F32)
    middle = rest.astype(BF16)
    low = (rest - middle.astype(F32)).astype(BF16)
    return [high, middle, low]


def add_up(value):
    return (value[2 * IMAGE : 3 * IMAGE] + value[IMAGE : 2 * IMAGE]) + value[:IMAGE]


def channel_sums(tracks, rows, notes, own_along):
    start = lax.axis_index("track") * rows - EDGE
    group = min(8, tracks)
    channels = own_along.shape[1]
    lane = lane_ids(8)
    half = LANES // 2
    wanted = jnp.concatenate([own_along, start + lax.broadcasted_iota(jnp.int32, (1, LANES), 1)], axis=1)
    row16 = row_ids(IMAGE, LANES)

    def body(number, carry):
        rate, image = carry
        base = number * group
        firsts, lasts = [], []
        blocks = [[notes[base + k, i] for i in range(5)] for k in range(group)]
        rates = [jnp.concatenate(block[:2], axis=0) for block in blocks]
        for k in range(0, group, 2):
            a, b = rates[k], rates[k + 1]
            firsts.append(jnp.where(lane < half, a, turn(b, half)))
            lasts.append(jnp.where(lane < half, turn(a, half), b))
        strains = jnp.concatenate([jnp.concatenate(firsts, axis=1), jnp.concatenate(lasts, axis=1)], axis=0)
        spot = base * rows + row_ids(group * rows, channels + LANES)
        hot = (spot == wanted).astype(F32).astype(BF16)
        rate = rate + jnp.dot(jnp.concatenate(three(strains), axis=0), hot, preferred_element_type=F32)
        weights, hots = [], []
        for k in range(group):
            for h in range(2):
                along = blocks[k][4][h : h + 1]
                mask = (row16 & 3).astype(F32) == blocks[k][4][2 + h : 3 + h]
                seen = [blocks[k][2 + h][t : t + 1] for t in range(MOMENTS)]
                value = jnp.where(
                    row16 < 8,
                    jnp.where(row16 < 4, seen[0], seen[1]),
                    jnp.where(row16 < 12, seen[2], seen[3]),
                )
                pieces = three(jnp.where(mask, value, 0.0)) + [mask.astype(F32).astype(BF16)]
                weights.append(jnp.concatenate(pieces, axis=0))
                spot = (start + row_ids(LANES, LANES)).astype(F32)
                hots.append((spot == along).astype(F32).astype(BF16))
        image = image + lax.dot_general(
            jnp.concatenate(weights, axis=1),
            jnp.concatenate(hots, axis=1),
            (((1,), (1,)), ((), ())),
            preferred_element_type=F32,
        )
        return rate, image

    carry = jnp.zeros((3 * IMAGE, channels + LANES), F32), jnp.zeros((4 * IMAGE, LANES), F32)
    if tracks == group:
        carry = body(0, carry)
    else:
        carry = lax.fori_loop(0, tracks // group, body, carry)
    rate, image = carry
    return add_up(rate), add_up(image), image[3 * IMAGE :]


def run_adjoint(media, saved, state, sums, inject=None):
    rows = sums.shape[2]
    sums[...] = jnp.zeros(sums.shape, F32)
    for step in range(MOMENTS):
        fast, slow = spans(step, rows)
        moment = MOMENTS - 1 - step
        if inject is not None:
            inject(moment)
        velocities(state, media, fast)

        def gather(i, r, exx, ezz, shear):
            if 0 <= r < rows:
                fxx, fzz, fxz = (saved[moment, k, i, r : r + 8, :] for k in range(3))
                sums[0, i, r : r + 8, :] += (fxx + fzz) * (exx + ezz)
                sums[1, i, r : r + 8, :] += 2.0 * (fxx * exx + fzz * ezz) + fxz * shear

        stresses(state, media, slow, step < MOMENTS - 1, gather)


def adjoint_rest_kernel(held, got_depth, even, odd, media, saved, note, sums, state):
    del note
    load_state(state, Blocks(held, got_depth, None, (even, odd)), FORWARD, (1, 2))
    run_adjoint(media, saved, state, sums)


def adjoint_top_kernel(
    tracks, held, even, odd, media, saved, notes, rest, obs, cells,
    lambda_out, mu_out, residual_out, state, sums,
):
    rows = held.shape[1]
    extent = rows + 2 * EDGE
    depth = lax.axis_index("depth")
    load_state(state, Blocks(held, None, None, (even, odd)), FORWARD, (0,))
    along, row = cells[0], cells[1]
    rate, seen, count = channel_sums(tracks, rows, notes, along)
    channels = along.shape[1]
    at_own = jnp.where((row_ids(IMAGE, channels) & 3) == row, rate[:, :channels], 0.0)
    traces = [
        jnp.sum(at_own[4 * t : 4 * t + 4], axis=0, keepdims=True) - obs[t : t + 1, :] for t in range(MOMENTS)
    ]
    residual_out[...] = jnp.where(
        depth == 0, jnp.concatenate(traces[:2], axis=0), jnp.concatenate(traces[2:], axis=0)
    )
    sources = count * rate[:, channels:] - seen
    turned = jnp.concatenate([sources, jnp.zeros((LANES - IMAGE, LANES), F32)], axis=0).T[:extent]
    lane = lane_ids(extent)
    here = (lane >= EDGE) & (lane < EDGE + FIBRE_ROWS) & (depth == 0)

    def inject(moment):
        added = jnp.where(here, turn(turned, EDGE - FIBRE_ROWS * moment), 0.0)
        state[2, 0, PAD : PAD + extent, :] += added

    run_adjoint(media, saved, state, sums, inject)
    for k, out in enumerate((lambda_out, mu_out)):
        first, last = joined(sums[k, 0], rest[k, 0], rest[k, 1])
        out[:, :LANES] = (NEAR * NEAR) * first
        out[:, LANES:] = (NEAR * NEAR) * last


def per_device(
    velocity,
    stress,
    adjoint_velocity,
    adjoint_stress,
    buoyancy,
    lame_lambda,
    shear_modulus,
    observed,
    owner_track,
    fibre_cell,
):
    tracks = lax.axis_size("track")
    rows, depth_cells = buoyancy.shape
    moments, channels = observed.shape
    owner = owner_track.reshape(1, channels)
    cell = fibre_cell.reshape(1, channels)
    pinned = lambda array: pltpu.with_memory_space_constraint(array, pltpu.HBM)
    arrays = (velocity, stress, adjoint_velocity, adjoint_stress, buoyancy, lame_lambda, shear_modulus)
    arrays = tuple(pinned(array) for array in arrays)
    channel_arrays = (pinned(observed), pinned(owner), pinned(cell))
    extent = rows + 2 * EDGE
    block = jax.ShapeDtypeStruct((rows, depth_cells), F32)
    outer_edges = jax.ShapeDtypeStruct((OUTER + HALO * FORWARD + EDGE - HALO, LANES), F32)
    edges = jax.ShapeDtypeStruct((INNER + HALO * 4 + EDGE - HALO, depth_cells), F32)
    inside = pl.BlockSpec(memory_space=VMEM)
    outside = pl.BlockSpec(memory_space=pltpu.HBM)
    anywhere = pl.BlockSpec(memory_space=pl.ANY)
    swap = lambda k: [pair for i in range(k, tracks - 1, 2) for pair in ((i, i + 1), (i + 1, i))]
    to_even, to_odd = pl.pallas_call(
        outer_kernel,
        out_shape=(outer_edges, outer_edges),
        in_specs=[outside] * 5,
        out_specs=(inside,) * 2,
        scratch_shapes=[VMEM((2, FORWARD, EDGE, LANES), F32), pltpu.SemaphoreType.DMA((10,))],
        compiler_params=params(),
        cost_estimate=cost(1),
        name="outer",
    )(*arrays[:2], *arrays[4:])
    outer_odd = lax.ppermute(to_odd, "track", swap(1))
    outer_even = lax.ppermute(to_even, "track", swap(0))

    held, to_depth, to_even, to_odd, traces, cells = pl.pallas_call(
        pack_kernel,
        out_shape=(
            jax.ShapeDtypeStruct((FIELDS, rows, depth_cells), F32),
            block,
            edges,
            edges,
            jax.ShapeDtypeStruct((moments, channels), F32),
            jax.ShapeDtypeStruct((2, 1, channels), jnp.int32),
        ),
        in_specs=[outside] * 10 + [anywhere],
        out_specs=(inside,) * 6,
        scratch_shapes=[VMEM((2, 1, channels), jnp.int32), pltpu.SemaphoreType.DMA((10,))],
        compiler_params=params(),
        cost_estimate=cost(2),
        name="pack",
    )(*arrays, *channel_arrays, to_even)
    depth_swap = [(0, 1), (1, 0)]
    got_depth = lax.ppermute(to_depth, "depth", depth_swap)
    to_even, to_odd = pl.pallas_call(
        corner_kernel,
        out_shape=(edges, edges),
        in_specs=[anywhere] * 3,
        out_specs=(anywhere,) * 2,
        input_output_aliases={1: 0, 2: 1},
        scratch_shapes=[pltpu.SemaphoreType.DMA((2,))],
        compiler_params=params(),
        name="corners",
    )(got_depth, to_even, to_odd)
    got_odd = lax.ppermute(to_odd, "track", swap(1))
    got_even = lax.ppermute(to_even, "track", swap(0))

    def media_of(planes):
        return jax.ShapeDtypeStruct((4, planes, extent, LANES), F32)

    def saved_of(planes):
        return jax.ShapeDtypeStruct((moments, 3, planes, rows, LANES), F32)

    def state_of(planes):
        return VMEM((5, planes, extent + 2 * PAD, LANES), F32)

    media_top, saved_top, top_end, image = pl.pallas_call(
        forward_top_kernel,
        out_shape=(
            media_of(1),
            saved_of(1),
            jax.ShapeDtypeStruct((2, rows, LANES), F32),
            jax.ShapeDtypeStruct((IMAGE // 2, LANES), F32),
        ),
        in_specs=[inside] * 3,
        out_specs=(inside,) * 4,
        scratch_shapes=[state_of(1)],
        compiler_params=params(),
        cost_estimate=cost(500),
        name="forward_top",
    )(held, outer_even, outer_odd)
    image_beside = lax.ppermute(image, "depth", depth_swap)
    media_rest, saved_rest, velocity_end = pl.pallas_call(
        forward_rest_kernel,
        out_shape=(media_of(2), saved_of(2), jax.ShapeDtypeStruct(velocity.shape, F32)),
        in_specs=[inside] * 7,
        out_specs=(inside,) * 3,
        scratch_shapes=[state_of(2)],
        compiler_params=params(),
        cost_estimate=cost(500),
        name="forward_rest",
    )(held, got_depth, outer_even, outer_odd, got_even, got_odd, top_end)
    note = pl.pallas_call(
        note_kernel,
        out_shape=jax.ShapeDtypeStruct((tracks, 5, 4, LANES), F32),
        in_specs=[inside] * 4,
        out_specs=inside,
        compiler_params=params(),
        name="note",
    )(image, image_beside, traces, cells)
    notes = lax.all_to_all(note, "track", split_axis=0, concat_axis=0, tiled=True)
    rest = pl.pallas_call(
        adjoint_rest_kernel,
        out_shape=jax.ShapeDtypeStruct((2, 2, rows, LANES), F32),
        in_specs=[inside] * 6 + [anywhere],
        out_specs=inside,
        scratch_shapes=[state_of(2)],
        compiler_params=params(),
        cost_estimate=cost(500),
        name="adjoint_rest",
    )(held, got_depth, got_even, got_odd, media_rest, saved_rest, note)
    gradient_lambda, gradient_mu, residual = pl.pallas_call(
        lambda *refs: adjoint_top_kernel(tracks, *refs),
        out_shape=(block, block, jax.ShapeDtypeStruct((moments // 2, channels), F32)),
        in_specs=[inside] * 9,
        out_specs=(inside,) * 3,
        scratch_shapes=[state_of(1), VMEM((2, 1, rows, LANES), F32)],
        compiler_params=params(),
        cost_estimate=cost(2),
        name="adjoint_top",
    )(held, got_even, got_odd, media_top, saved_top, notes, rest, traces, cells)
    return gradient_lambda, gradient_mu, velocity_end, residual


def solution(mesh):
    return jax.shard_map(
        per_device,
        mesh=mesh,
        in_specs=(
            P("shots", "track", "depth"),
            P("shots", "track", "depth"),
            P("shots", "track", "depth"),
            P("shots", "track", "depth"),
            P("track", "depth"),
            P("track", "depth"),
            P("track", "depth"),
            P("shots", "track"),
            P("track", None),
            P("track"),
        ),
        out_specs=(
            P(("shots", "track"), "depth"),
            P(("shots", "track"), "depth"),
            P("shots", "track", "depth"),
            P(("shots", "depth"), "track"),
        ),
        check_vma=False,
    )
```

```python
import jax
import jax.numpy as jnp
from jax import lax
from jax.experimental import pallas as pl
from jax.experimental.pallas import tpu as pltpu
from jax.sharding import PartitionSpec as P

FIBRE_ROWS = 4
NEAR = 9.0 / 8.0
RATIO = -1.0 / 27.0
HALO = 12
EDGE = 16
LANES = 128
PAD = 8
FORWARD = 8
ADJOINT = 5
FIELDS = FORWARD + ADJOINT
STRIP = 16
MOMENTS = 4
IMAGE = MOMENTS * FIBRE_ROWS
VMEM = pltpu.VMEM
F32 = jnp.float32
BF16 = jnp.bfloat16


def lane_ids(rows):
    return lax.broadcasted_iota(jnp.int32, (rows, LANES), 1)


def row_ids(rows, columns):
    return lax.broadcasted_iota(jnp.int32, (rows, columns), 0)


def params():
    return pltpu.CompilerParams(vmem_limit_bytes=40 * 1024 * 1024)


def cost(microseconds):
    return pl.CostEstimate(flops=int(microseconds * 1e9), bytes_accessed=1 << 20, transcendentals=0)


def turn(value, by):
    return pltpu.roll(value, by % LANES, 1)


def is_even():
    return lax.rem(lax.axis_index("track"), 2) == 0


def fetch(sources, targets, sems):
    copies = [pltpu.make_async_copy(s, t, sems.at[i]) for i, (s, t) in enumerate(zip(sources, targets))]
    for copy in copies:
        copy.start()
    return copies


def field_refs(velocity, stress, adj_velocity, adj_stress, buoyancy, lame, shear):
    return (
        [velocity.at[i] for i in range(2)]
        + [stress.at[i] for i in range(3)]
        + [buoyancy, lame, shear]
        + [adj_velocity.at[i] for i in range(2)]
        + [adj_stress.at[i] for i in range(3)]
    )


def pack_kernel(*refs):
    sources, channel_arrays = refs[:7], refs[7:10]
    depth_out, edge_outs, strip_out, traces_out, cells_out = refs[10], refs[11:13], *refs[13:16]
    held, numbers, sems = refs[16:23], refs[23], refs[24]
    targets = (*held, traces_out, numbers.at[0], numbers.at[1])
    copies = fetch((*sources, *channel_arrays), targets, sems)
    depth = lax.axis_index("depth")
    even = is_even()
    fields = field_refs(*held)
    rows = fields[0].shape[0]
    lane = lane_ids(rows)
    tail = EDGE + HALO * FIELDS
    for out in edge_outs:
        out[:EDGE, :] = jnp.zeros((EDGE, 2 * LANES), F32)
        out[tail:, :] = jnp.zeros((out.shape[0] - tail, 2 * LANES), F32)
    for copy in copies:
        copy.wait()
    packed = [jnp.zeros((rows, LANES), F32) for _ in range(2)]
    strip = jnp.zeros((rows, LANES), F32)
    for f, ref in enumerate(fields):
        first, last = ref[:, :LANES], ref[:, LANES:]
        group, place = divmod(f, FORWARD)
        spot = EDGE * place
        here = (lane >= spot) & (lane < spot + EDGE)
        edge = jnp.where(depth == 0, last, first)
        shift = lax.rem(spot + EDGE * (1 - depth), LANES)
        packed[group] = jnp.where(here, pltpu.roll(edge, shift, 1), packed[group])
        if f < FORWARD:
            strip = jnp.where(here, turn(first, spot), strip)
        low, high = ref[:HALO, :], ref[rows - HALO :, :]
        at = EDGE + HALO * f
        edge_outs[0][at : at + HALO, :] = jnp.where(even, high, low)
        edge_outs[1][at : at + HALO, :] = jnp.where(even, low, high)
    depth_out[:rows, :LANES] = packed[0]
    depth_out[:rows, LANES:] = packed[1]
    turned = strip.T
    strip_out[:, :rows] = turned[: 2 * STRIP]
    strip_out[:, rows:] = turned[2 * STRIP : 4 * STRIP]
    depth_out[rows:, :rows] = turned[4 * STRIP : 5 * STRIP]
    depth_out[rows:, rows : 2 * rows] = turned[6 * STRIP : 7 * STRIP]
    depth_out[rows:, 2 * rows : 3 * rows] = turned[5 * STRIP : 6 * STRIP]
    depth_out[rows:, 3 * rows :] = turned[7 * STRIP :]
    cells_out[0] = numbers[0] * rows + lax.shift_right_logical(numbers[1], 2)
    cells_out[1] = numbers[1] & 3


def corner_kernel(got, even_in, odd_in, even_out, odd_out, sems):
    rows = got.shape[0] - STRIP
    is_odd = lax.rem(lax.axis_index("track"), 2)
    high, low = (rows - EDGE) * (1 - is_odd), (rows - EDGE) * is_odd
    one = pltpu.make_async_copy(
        got.at[pl.ds(pl.multiple_of(high, EDGE), EDGE), :], even_out.at[pl.ds(0, EDGE), :], sems.at[0]
    )
    two = pltpu.make_async_copy(
        got.at[pl.ds(pl.multiple_of(low, EDGE), EDGE), :], odd_out.at[pl.ds(0, EDGE), :], sems.at[1]
    )
    one.start()
    two.start()
    one.wait()
    two.wait()


def windows(f, first, last, halo):
    depth = lax.axis_index("depth")
    lane = lane_ids(first.shape[0])
    shift = lax.rem(LANES - EDGE * (f % FORWARD) + (LANES - EDGE) * (1 - depth), LANES)
    beside = pltpu.roll(halo, shift, 1)
    return [
        jnp.where(lane >= EDGE, turn(first, EDGE), jnp.where(depth == 1, beside, 0.0)),
        jnp.where(lane < LANES // 2, turn(first, LANES // 2), turn(last, LANES // 2)),
        jnp.where(lane < LANES - EDGE, turn(last, -EDGE), jnp.where(depth == 0, beside, 0.0)),
    ]


def joined(planes):
    lane = lane_ids(planes[0].shape[0])
    middle = turn(planes[1], LANES // 2)
    return (
        jnp.where(lane < 88, turn(planes[0], -EDGE), middle),
        jnp.where(lane < 40, middle, turn(planes[2], EDGE)),
    )


def own_kernel(*refs):
    sources, got_depth, planes_out, held, sems = refs[:7], refs[7], refs[8], refs[9:16], refs[16]
    for copy in fetch(sources, held, sems):
        copy.wait()
    for f, ref in enumerate(field_refs(*held)):
        col = LANES * (f // FORWARD)
        planes = windows(f, ref[:, :LANES], ref[:, LANES:], got_depth[: ref.shape[0], col : col + LANES])
        for p in range(3):
            planes_out[f, p] = planes[p]


def halo_windows(f, got_even, got_odd):
    even = is_even()
    high = EDGE + HALO * f
    low = high - (EDGE - HALO)
    col = LANES * (f // FORWARD)
    corner_even, corner_odd = got_even[:EDGE, col : col + LANES], got_odd[:EDGE, col : col + LANES]
    left = jnp.where(even, got_odd[low : low + EDGE, :], got_even[low : low + EDGE, :])
    right = jnp.where(even, got_even[high : high + EDGE, :], got_odd[high : high + EDGE, :])
    left_halo = jnp.where(even, corner_odd, corner_even)
    right_halo = jnp.where(even, corner_even, corner_odd)
    return (
        windows(f, left[:, :LANES], left[:, LANES:], left_halo),
        windows(f, right[:, :LANES], right[:, LANES:], right_halo),
    )


def load_state(state, own, got_even, got_odd, base, planes):
    rows = own.shape[2]
    extent = rows + 2 * EDGE
    for f in range(5):
        below, above = halo_windows(base + f, got_even, got_odd)
        for i, p in enumerate(planes):
            state[f, i, :PAD, :] = jnp.zeros((PAD, LANES), F32)
            state[f, i, PAD : PAD + EDGE, :] = below[p]
            state[f, i, PAD + EDGE : PAD + EDGE + rows, :] = own[base + f, p]
            state[f, i, PAD + EDGE + rows : PAD + extent, :] = above[p]
            state[f, i, PAD + extent :, :] = jnp.zeros((PAD, LANES), F32)


def velocities(state, media, span):
    for r in range(8 * span[0], 8 * span[1], 8):
        for i in range(state.shape[1]):

            def at(f, by=0):
                return state[f, i, r + PAD + by : r + PAD + by + 8, :]

            xx, xz, zz = at(2), at(4), at(3)
            b = media[0, i, r : r + 8, :]
            near = (xx - at(2, -1)) + (xz - turn(xz, 1))
            far = (at(2, 1) - at(2, -2)) + (turn(xz, -1) - turn(xz, 2))
            state[0, i, r + PAD : r + PAD + 8, :] = at(0) + b * (near + RATIO * far)
            near = (at(4, 1) - xz) + (turn(zz, -1) - zz)
            far = (at(4, 2) - at(4, -1)) + (turn(zz, -2) - turn(zz, 1))
            state[1, i, r + PAD : r + PAD + 8, :] = at(1) + b * (near + RATIO * far)


def stresses(state, media, span, update, keep):
    for r in range(8 * span[0], 8 * span[1], 8):
        for i in range(state.shape[1]):

            def at(f, by=0):
                return state[f, i, r + PAD + by : r + PAD + by + 8, :]

            vx, vz = at(0), at(1)
            exx = (at(0, 1) - vx) + RATIO * (at(0, 2) - at(0, -1))
            ezz = (vz - turn(vz, 1)) + RATIO * (turn(vz, -1) - turn(vz, 2))
            near = (turn(vx, -1) - vx) + (vz - at(1, -1))
            far = (turn(vx, -2) - turn(vx, 1)) + (at(1, 1) - at(1, -2))
            shear = near + RATIO * far
            keep(i, r - EDGE, exx, ezz, shear)
            if update:
                whole, lam, mu = (media[k, i, r : r + 8, :] for k in (1, 2, 3))
                state[2, i, r + PAD : r + PAD + 8, :] = at(2) + (whole * exx + lam * ezz)
                state[3, i, r + PAD : r + PAD + 8, :] = at(3) + (lam * exx + whole * ezz)
                state[4, i, r + PAD : r + PAD + 8, :] = at(4) + mu * shear


def spans(step, rows):
    tiles = (rows + 2 * EDGE) // 8
    if step == 0:
        return (0, tiles), (0, tiles)
    inner = (1, tiles - 1)
    return inner, inner if step < MOMENTS - 1 else (EDGE // 8, tiles - EDGE // 8)


def run_forward(own, got_even, got_odd, media, saved, state, planes):
    rows = own.shape[2]
    parts = []
    for f in (5, 6, 7):
        below, above = halo_windows(f, got_even, got_odd)
        parts.append([(below[p], own[f, p], above[p]) for p in planes])
    for i in range(len(planes)):
        for k, at in enumerate((0, EDGE, EDGE + rows)):
            b, lam, mu = (NEAR * parts[m][i][k] for m in range(3))
            span = slice(at, at + b.shape[0])
            media[0, i, span, :] = b
            media[1, i, span, :] = lam + 2.0 * mu
            media[2, i, span, :] = lam
            media[3, i, span, :] = mu
    load_state(state, own, got_even, got_odd, 0, planes)
    for step in range(MOMENTS):
        fast, slow = spans(step, rows)
        velocities(state, media, fast)

        def save(i, r, exx, ezz, shear):
            if 0 <= r < rows:
                saved[step, 0, i, r : r + 8, :] = exx
                saved[step, 1, i, r : r + 8, :] = ezz
                saved[step, 2, i, r : r + 8, :] = shear

        stresses(state, media, slow, step < MOMENTS - 1, save)


def forward_kernel(own, got_even, got_odd, media, saved, end_out, state):
    run_forward(own, got_even, got_odd, media, saved, state, (0, 1, 2))
    rows = own.shape[2]
    top = PAD + EDGE
    for f in range(2):
        first, last = joined([state[f, i, top : top + rows, :] for i in range(3)])
        end_out[f, :, :LANES] = first
        end_out[f, :, LANES:] = last


def note_kernel(strip, got_depth, traces, cells, note_out):
    first = lax.axis_index("depth") == 0
    beside = got_depth[got_depth.shape[0] - STRIP :, :]
    beside = jnp.concatenate([beside[:, :LANES], beside[:, LANES:]], axis=0)
    seen = jnp.concatenate([traces[:, :LANES], traces[:, LANES:]], axis=0)
    along, row = cells[0], cells[1]
    places = jnp.concatenate([along[:, :LANES], along[:, LANES:], row[:, :LANES], row[:, LANES:]] * 2, axis=0)
    block = jnp.concatenate(
        [jnp.where(first, strip[...], beside), jnp.where(first, seen, places.astype(F32))], axis=0
    )
    for k in range(note_out.shape[0]):
        note_out[k] = block


def relay_kernel(notes, saved, notes_out):
    del saved
    notes_out[...] = notes[...]


def three(value):
    high = value.astype(BF16)
    rest = value - high.astype(F32)
    middle = rest.astype(BF16)
    low = (rest - middle.astype(F32)).astype(BF16)
    return [high, middle, low]


def add_up(value, count):
    return (value[2 * count : 3 * count] + value[count : 2 * count]) + value[:count]


BATCH = 5
OWN = LANES - 2 * HALO


def fill_strip(state, media, low, high, first, tracks, columns):
    lane = lane_ids(STRIP)
    state[...] = jnp.zeros(state.shape, F32)
    for w in range(BATCH):
        begin = (first + w) * OWN - HALO
        base = (begin + columns) // columns - 1
        offset = begin - base * columns
        part = lax.div(offset + lane, columns)
        inside = (begin + lane >= 0) & (begin + lane < tracks * columns)
        values = []
        for f in range(FORWARD):
            source, q = (low, high)[f // 4], f % 4
            value = jnp.zeros((STRIP, LANES), F32)
            for step in range(3):
                who = jnp.clip(base + step, 0, tracks - 1)
                block = source[who, STRIP * (q % 2) : STRIP * (q % 2 + 1), :]
                shift = (4 * LANES - offset + columns * step - columns * (q // 2)) % LANES
                value = jnp.where(part == step, pltpu.roll(block, shift, 1), value)
            values.append(jnp.where(inside, value, 0.0))
        for f in range(5):
            state[f, w, PAD : PAD + STRIP, :] = values[f]
        buoyancy, lame, shear = (NEAR * value for value in values[5:])
        media[0, w] = buoyancy
        media[1, w] = lame + 2.0 * shear
        media[2, w] = lame
        media[3, w] = shear


def strip_steps(state, media):
    def at(f, w, r, by=0):
        return state[f, w, PAD + r + by : PAD + r + by + 8, :]

    strains = [[] for _ in range(BATCH)]
    for moment in range(MOMENTS):
        last = moment == MOMENTS - 1
        for r in (0, 8) if moment < 2 else (0,):
            for w in range(BATCH):
                here = slice(PAD + r, PAD + r + 8)
                xx, xz, zz = at(2, w, r), at(4, w, r), at(3, w, r)
                b = media[0, w, r : r + 8, :]
                near = (xx - turn(xx, 1)) + (xz - at(4, w, r, -1))
                far = (turn(xx, -1) - turn(xx, 2)) + (at(4, w, r, 1) - at(4, w, r, -2))
                state[0, w, here, :] = at(0, w, r) + b * (near + RATIO * far)
                if not last:
                    near = (turn(xz, -1) - xz) + (at(3, w, r, 1) - zz)
                    far = (turn(xz, -2) - turn(xz, 1)) + (at(3, w, r, 2) - at(3, w, r, -1))
                    state[1, w, here, :] = at(1, w, r) + b * (near + RATIO * far)
        for r in (0, 8) if moment < 1 else (0,):
            for w in range(BATCH):
                here = slice(PAD + r, PAD + r + 8)
                vx, vz = at(0, w, r), at(1, w, r)
                exx = (turn(vx, -1) - vx) + RATIO * (turn(vx, -2) - turn(vx, 1))
                if r == 0:
                    strains[w].append(NEAR * exx)
                if not last:
                    ezz = (vz - at(1, w, r, -1)) + RATIO * (at(1, w, r, 1) - at(1, w, r, -2))
                    near = (at(0, w, r, 1) - vx) + (vz - turn(vz, 1))
                    far = (at(0, w, r, 2) - at(0, w, r, -1)) + (turn(vz, -1) - turn(vz, 2))
                    whole, lam, mu = (media[k, w, r : r + 8, :] for k in (1, 2, 3))
                    state[2, w, here, :] = at(2, w, r) + (whole * exx + lam * ezz)
                    state[3, w, here, :] = at(3, w, r) + (lam * exx + whole * ezz)
                    state[4, w, here, :] = at(4, w, r) + mu * (near + RATIO * far)
    return [jnp.concatenate(parts, axis=0) for parts in strains]


def recorded_rates(state, media, low, high, wanted, tracks, columns):
    lane = lane_ids(8 * MOMENTS)
    mine = (lane >= HALO) & (lane < HALO + OWN)

    def body(number, rate):
        first = number * BATCH
        fill_strip(state, media, low, high, first, tracks, columns)
        images = [three(jnp.where(mine, image, 0.0)) for image in strip_steps(state, media)]
        parts = [jnp.concatenate([image[i] for image in images], axis=1) for i in range(3)]
        spots = [
            (first + w) * OWN - HALO + row_ids(LANES, wanted.shape[1]) for w in range(BATCH)
        ]
        hot = (jnp.concatenate(spots, axis=0) == wanted).astype(F32).astype(BF16)
        return rate + jnp.dot(jnp.concatenate(parts, axis=0), hot, preferred_element_type=F32)

    rate = jnp.zeros((3 * 8 * MOMENTS, wanted.shape[1]), F32)
    batches = -(-(-(-tracks * columns // OWN)) // BATCH)
    rate = body(0, rate) if batches == 1 else lax.fori_loop(0, batches, body, rate)
    return add_up(rate, 8 * MOMENTS)


def window_sums(low, high, start, tracks):
    group = min(8, tracks)
    row16 = row_ids(IMAGE, LANES)

    def body(number, image):
        weights, hots = [], []
        for k in range(group):
            who = number * group + k
            traces = low[who, 2 * STRIP :, :]
            places = high[who, 2 * STRIP :, :]
            for h in range(2):
                mask = (row16 & 3).astype(F32) == places[2 + h : 3 + h]
                seen = [traces[4 * h + t : 4 * h + t + 1] for t in range(MOMENTS)]
                value = jnp.where(
                    row16 < 8,
                    jnp.where(row16 < 4, seen[0], seen[1]),
                    jnp.where(row16 < 12, seen[2], seen[3]),
                )
                pieces = three(jnp.where(mask, value, 0.0)) + [mask.astype(F32).astype(BF16)]
                weights.append(jnp.concatenate(pieces, axis=0))
                spot = (start + row_ids(LANES, LANES)).astype(F32)
                hots.append((spot == places[h : h + 1]).astype(F32).astype(BF16))
        return image + lax.dot_general(
            jnp.concatenate(weights, axis=1),
            jnp.concatenate(hots, axis=1),
            (((1,), (1,)), ((), ())),
            preferred_element_type=F32,
        )

    image = jnp.zeros((4 * IMAGE, LANES), F32)
    image = body(0, image) if tracks == group else lax.fori_loop(0, tracks // group, body, image)
    return add_up(image, IMAGE), image[3 * IMAGE :]


def surface_kernel(tracks, columns, notes, beside, obs, cells, inject_out, residual_out, state, media, low, high):
    depth = lax.axis_index("depth")
    low[...] = jnp.where(depth == 0, notes[...], beside[...])
    high[...] = jnp.where(depth == 0, beside[...], notes[...])
    start = lax.axis_index("track") * columns - EDGE
    along, row = cells[0], cells[1]
    channels = along.shape[1]
    wanted = jnp.concatenate([along, start + lax.broadcasted_iota(jnp.int32, (1, LANES), 1)], axis=1)
    seen, count = window_sums(low, high, start, tracks)
    rate = recorded_rates(state, media, low, high, wanted, tracks, columns)
    mask = row_ids(8, channels) == row
    traces = [
        jnp.sum(jnp.where(mask, rate[8 * t : 8 * t + 8, :channels], 0.0), axis=0, keepdims=True)
        - obs[t : t + 1, :]
        for t in range(MOMENTS)
    ]
    residual_out[...] = jnp.where(
        depth == 0, jnp.concatenate(traces[:2], axis=0), jnp.concatenate(traces[2:], axis=0)
    )
    near = jnp.concatenate([rate[8 * t : 8 * t + 4, channels:] for t in range(MOMENTS)], axis=0)
    sources = jnp.where(depth == 0, count * near - seen, 0.0)
    turned = jnp.concatenate([sources, jnp.zeros((LANES - IMAGE, LANES), F32)], axis=0).T
    inject_out[...] = turned[: inject_out.shape[0]]


def run_adjoint(media, saved, state, sums, inject=None):
    rows = sums.shape[2]
    sums[...] = jnp.zeros(sums.shape, F32)
    for step in range(MOMENTS):
        fast, slow = spans(step, rows)
        moment = MOMENTS - 1 - step
        if inject is not None:
            inject(moment)
        velocities(state, media, fast)

        def gather(i, r, exx, ezz, shear):
            if 0 <= r < rows:
                fxx, fzz, fxz = (saved[moment, k, i, r : r + 8, :] for k in range(3))
                sums[0, i, r : r + 8, :] += (fxx + fzz) * (exx + ezz)
                sums[1, i, r : r + 8, :] += 2.0 * (fxx * exx + fzz * ezz) + fxz * shear

        stresses(state, media, slow, step < MOMENTS - 1, gather)


def adjoint_rest_kernel(own, got_even, got_odd, media, saved, notes, sums, state):
    del notes
    load_state(state, own, got_even, got_odd, FORWARD, (1, 2))
    run_adjoint(media.at[:, pl.ds(1, 2)], saved.at[:, :, pl.ds(1, 2)], state, sums)


def adjoint_top_kernel(own, got_even, got_odd, media, saved, rest, inject, lambda_out, mu_out, state, sums):
    rows = own.shape[2]
    extent = rows + 2 * EDGE
    load_state(state, own, got_even, got_odd, FORWARD, (0,))
    lane = lane_ids(extent)
    here = (lane >= EDGE) & (lane < EDGE + FIBRE_ROWS)

    def add(moment):
        added = jnp.where(here, turn(inject[...], EDGE - FIBRE_ROWS * moment), 0.0)
        state[2, 0, PAD : PAD + extent, :] += added

    run_adjoint(media.at[:, pl.ds(0, 1)], saved.at[:, :, pl.ds(0, 1)], state, sums, add)
    for k, out in enumerate((lambda_out, mu_out)):
        first, last = joined([sums[k, 0], rest[k, 0], rest[k, 1]])
        out[:, :LANES] = (NEAR * NEAR) * first
        out[:, LANES:] = (NEAR * NEAR) * last


def per_device(
    velocity,
    stress,
    adjoint_velocity,
    adjoint_stress,
    buoyancy,
    lame_lambda,
    shear_modulus,
    observed,
    owner_track,
    fibre_cell,
):
    tracks = lax.axis_size("track")
    rows, depth_cells = buoyancy.shape
    moments, channels = observed.shape
    owner = owner_track.reshape(1, channels)
    cell = fibre_cell.reshape(1, channels)
    pinned = lambda array: pltpu.with_memory_space_constraint(array, pltpu.HBM)
    arrays = (velocity, stress, adjoint_velocity, adjoint_stress, buoyancy, lame_lambda, shear_modulus)
    arrays = tuple(pinned(array) for array in arrays)
    channel_arrays = (pinned(observed), pinned(owner), pinned(cell))
    extent = rows + 2 * EDGE
    block = jax.ShapeDtypeStruct((rows, depth_cells), F32)
    length = EDGE + HALO * FIELDS + EDGE - HALO
    edges = jax.ShapeDtypeStruct((length + (-length) % 8, depth_cells), F32)
    inside = pl.BlockSpec(memory_space=VMEM)
    outside = pl.BlockSpec(memory_space=pltpu.HBM)
    anywhere = pl.BlockSpec(memory_space=pl.ANY)
    held = [VMEM(a.shape, F32) for a in arrays]
    to_depth, to_even, to_odd, strip, traces, cells = pl.pallas_call(
        pack_kernel,
        out_shape=(
            jax.ShapeDtypeStruct((rows + STRIP, depth_cells), F32),
            edges,
            edges,
            jax.ShapeDtypeStruct((2 * STRIP, LANES), F32),
            jax.ShapeDtypeStruct((moments, channels), F32),
            jax.ShapeDtypeStruct((2, 1, channels), jnp.int32),
        ),
        in_specs=[outside] * 10,
        out_specs=(inside,) * 6,
        scratch_shapes=held + [VMEM((2, 1, channels), jnp.int32), pltpu.SemaphoreType.DMA((10,))],
        compiler_params=params(),
        cost_estimate=cost(5),
        name="pack",
    )(*arrays, *channel_arrays)
    to_track = (to_even, to_odd)

    depth_swap = [(0, 1), (1, 0)]
    got_depth = lax.ppermute(to_depth, "depth", depth_swap)
    to_track = pl.pallas_call(
        corner_kernel,
        out_shape=(edges, edges),
        in_specs=[anywhere] * 3,
        out_specs=(anywhere,) * 2,
        input_output_aliases={1: 0, 2: 1},
        scratch_shapes=[pltpu.SemaphoreType.DMA((2,))],
        compiler_params=params(),
        name="corners",
    )(got_depth, *to_track)
    swap = lambda k: [pair for i in range(k, tracks - 1, 2) for pair in ((i, i + 1), (i + 1, i))]
    got_odd = lax.ppermute(to_track[1], "track", swap(1))
    got_even = lax.ppermute(to_track[0], "track", swap(0))

    own = pl.pallas_call(
        own_kernel,
        out_shape=jax.ShapeDtypeStruct((FIELDS, 3, rows, LANES), F32),
        in_specs=[outside] * 7 + [inside],
        out_specs=inside,
        scratch_shapes=held + [pltpu.SemaphoreType.DMA((7,))],
        compiler_params=params(),
        cost_estimate=cost(20),
        name="own_planes",
    )(*arrays, got_depth)

    def state_of(planes):
        return VMEM((5, planes, extent + 2 * PAD, LANES), F32)

    note = pl.pallas_call(
        note_kernel,
        out_shape=jax.ShapeDtypeStruct((tracks, 2 * STRIP + 8, LANES), F32),
        in_specs=[inside] * 4,
        out_specs=inside,
        compiler_params=params(),
        cost_estimate=cost(1),
        name="note",
    )(strip, got_depth, traces, cells)
    notes = lax.all_to_all(note, "track", split_axis=0, concat_axis=0, tiled=True)

    media, saved, velocity_end = pl.pallas_call(
        forward_kernel,
        out_shape=(
            jax.ShapeDtypeStruct((4, 3, extent, LANES), F32),
            jax.ShapeDtypeStruct((moments, 3, 3, rows, LANES), F32),
            jax.ShapeDtypeStruct(velocity.shape, F32),
        ),
        in_specs=[inside] * 3,
        out_specs=(inside,) * 3,
        scratch_shapes=[state_of(3)],
        compiler_params=params(),
        cost_estimate=cost(60),
        name="forward",
    )(own, got_even, got_odd)

    mine = pl.pallas_call(
        relay_kernel,
        out_shape=jax.ShapeDtypeStruct(note.shape, F32),
        in_specs=[inside, anywhere],
        out_specs=inside,
        compiler_params=params(),
        cost_estimate=cost(1),
        name="relay",
    )(notes, saved)
    beside = lax.ppermute(mine, "depth", depth_swap)

    rest = pl.pallas_call(
        adjoint_rest_kernel,
        out_shape=jax.ShapeDtypeStruct((2, 2, rows, LANES), F32),
        in_specs=[inside] * 5 + [anywhere],
        out_specs=inside,
        scratch_shapes=[state_of(2)],
        compiler_params=params(),
        cost_estimate=cost(60),
        name="adjoint_rest",
    )(own, got_even, got_odd, media, saved, mine)

    inject, residual = pl.pallas_call(
        lambda *refs: surface_kernel(tracks, rows, *refs),
        out_shape=(
            jax.ShapeDtypeStruct((extent, LANES), F32),
            jax.ShapeDtypeStruct((moments // 2, channels), F32),
        ),
        in_specs=[inside] * 4,
        out_specs=(inside,) * 2,
        scratch_shapes=[
            VMEM((5, BATCH, 2 * PAD + STRIP, LANES), F32),
            VMEM((4, BATCH, STRIP, LANES), F32),
            VMEM(note.shape, F32),
            VMEM(note.shape, F32),
        ],
        compiler_params=params(),
        cost_estimate=cost(2),
        name="surface",
    )(mine, beside, traces, cells)

    gradient_lambda, gradient_mu = pl.pallas_call(
        adjoint_top_kernel,
        out_shape=(block, block),
        in_specs=[inside] * 7,
        out_specs=(inside,) * 2,
        scratch_shapes=[state_of(1), VMEM((2, 1, rows, LANES), F32)],
        compiler_params=params(),
        cost_estimate=cost(2),
        name="adjoint_top",
    )(own, got_even, got_odd, media, saved, rest, inject)
    return gradient_lambda, gradient_mu, velocity_end, residual


def solution(mesh):
    return jax.shard_map(
        per_device,
        mesh=mesh,
        in_specs=(
            P("shots", "track", "depth"),
            P("shots", "track", "depth"),
            P("shots", "track", "depth"),
            P("shots", "track", "depth"),
            P("track", "depth"),
            P("track", "depth"),
            P("track", "depth"),
            P("shots", "track"),
            P("track", None),
            P("track"),
        ),
        out_specs=(
            P(("shots", "track"), "depth"),
            P(("shots", "track"), "depth"),
            P("shots", "track", "depth"),
            P(("shots", "depth"), "track"),
        ),
        check_vma=False,
    )
```

```python
import jax
import jax.numpy as jnp
from jax import lax
from jax.experimental import pallas as pl
from jax.experimental.pallas import tpu as pltpu
from jax.sharding import PartitionSpec as P

FIBRE_ROWS = 4
NEAR = 9.0 / 8.0
RATIO = -1.0 / 27.0
HALO = 12
EDGE = 16
LANES = 128
PAD = 8
FORWARD = 8
ADJOINT = 5
FIELDS = FORWARD + ADJOINT
STRIP = 16
MOMENTS = 4
IMAGE = MOMENTS * FIBRE_ROWS
VMEM = pltpu.VMEM
F32 = jnp.float32
BF16 = jnp.bfloat16


def lane_ids(rows):
    return lax.broadcasted_iota(jnp.int32, (rows, LANES), 1)


def row_ids(rows, columns):
    return lax.broadcasted_iota(jnp.int32, (rows, columns), 0)


def params():
    return pltpu.CompilerParams(vmem_limit_bytes=16 * 1024 * 1024)


def cost(microseconds):
    return pl.CostEstimate(flops=int(microseconds * 1e9), bytes_accessed=1 << 20, transcendentals=0)


def turn(value, by):
    return pltpu.roll(value, by % LANES, 1)


def is_even():
    return lax.rem(lax.axis_index("track"), 2) == 0


def fetch(sources, targets, sems):
    copies = [pltpu.make_async_copy(s, t, sems.at[i]) for i, (s, t) in enumerate(zip(sources, targets))]
    for copy in copies:
        copy.start()
    return copies


def pack_kernel(*refs):
    sources, channel_arrays = refs[:7], refs[7:10]
    held, depth_out, edge_outs, strip_out, traces_out, cells_out = refs[10], refs[11], refs[12:14], *refs[14:17]
    numbers, sems = refs[17:]
    targets = (
        held.at[pl.ds(0, 2)],
        held.at[pl.ds(2, 3)],
        held.at[5],
        held.at[6],
        held.at[7],
        held.at[pl.ds(8, 2)],
        held.at[pl.ds(10, 3)],
        traces_out,
        numbers.at[0],
        numbers.at[1],
    )
    copies = fetch((*sources[:2], *sources[4:], *sources[2:4], *channel_arrays), targets, sems)
    arriving = {0: copies[0], 2: copies[1], 5: copies[2], 6: copies[3], 7: copies[4], 8: copies[5], 10: copies[6]}
    depth = lax.axis_index("depth")
    even = is_even()
    rows = held.shape[1]
    lane = lane_ids(rows)
    tail = EDGE + HALO * FIELDS
    for out in edge_outs:
        out[:EDGE, :] = jnp.zeros((EDGE, 2 * LANES), F32)
        out[tail:, :] = jnp.zeros((out.shape[0] - tail, 2 * LANES), F32)
    packed = [jnp.zeros((rows, LANES), F32) for _ in range(2)]
    strip = jnp.zeros((rows, LANES), F32)
    for f in range(FIELDS):
        if f in arriving:
            arriving[f].wait()
        first, last = held[f, :, :LANES], held[f, :, LANES:]
        group, place = divmod(f, FORWARD)
        spot = EDGE * place
        here = (lane >= spot) & (lane < spot + EDGE)
        edge = jnp.where(depth == 0, last, first)
        shift = lax.rem(spot + EDGE * (1 - depth), LANES)
        packed[group] = jnp.where(here, pltpu.roll(edge, shift, 1), packed[group])
        if f < FORWARD:
            strip = jnp.where(here, turn(first, spot), strip)
        low, high = held[f, :HALO, :], held[f, rows - HALO :, :]
        at = EDGE + HALO * f
        edge_outs[0][at : at + HALO, :] = jnp.where(even, high, low)
        edge_outs[1][at : at + HALO, :] = jnp.where(even, low, high)
    depth_out[:rows, :LANES] = packed[0]
    depth_out[:rows, LANES:] = packed[1]
    turned = strip.T
    strip_out[:, :rows] = turned[: 2 * STRIP]
    strip_out[:, rows:] = turned[2 * STRIP : 4 * STRIP]
    depth_out[rows:, :rows] = turned[4 * STRIP : 5 * STRIP]
    depth_out[rows:, rows : 2 * rows] = turned[6 * STRIP : 7 * STRIP]
    depth_out[rows:, 2 * rows : 3 * rows] = turned[5 * STRIP : 6 * STRIP]
    depth_out[rows:, 3 * rows :] = turned[7 * STRIP :]
    for copy in copies[7:]:
        copy.wait()
    cells_out[0] = numbers[0] * rows + lax.shift_right_logical(numbers[1], 2)
    cells_out[1] = numbers[1] & 3


def corner_kernel(got, even_in, odd_in, even_out, odd_out, sems):
    rows = got.shape[0] - STRIP
    is_odd = lax.rem(lax.axis_index("track"), 2)
    high, low = (rows - EDGE) * (1 - is_odd), (rows - EDGE) * is_odd
    one = pltpu.make_async_copy(
        got.at[pl.ds(pl.multiple_of(high, EDGE), EDGE), :], even_out.at[pl.ds(0, EDGE), :], sems.at[0]
    )
    two = pltpu.make_async_copy(
        got.at[pl.ds(pl.multiple_of(low, EDGE), EDGE), :], odd_out.at[pl.ds(0, EDGE), :], sems.at[1]
    )
    one.start()
    two.start()
    one.wait()
    two.wait()


def windows(f, first, last, halo):
    depth = lax.axis_index("depth")
    lane = lane_ids(first.shape[0])
    shift = lax.rem(LANES - EDGE * (f % FORWARD) + (LANES - EDGE) * (1 - depth), LANES)
    beside = pltpu.roll(halo, shift, 1)
    return [
        jnp.where(lane >= EDGE, turn(first, EDGE), jnp.where(depth == 1, beside, 0.0)),
        jnp.where(lane < LANES // 2, turn(first, LANES // 2), turn(last, LANES // 2)),
        jnp.where(lane < LANES - EDGE, turn(last, -EDGE), jnp.where(depth == 0, beside, 0.0)),
    ]


def joined(planes):
    lane = lane_ids(planes[0].shape[0])
    middle = turn(planes[1], LANES // 2)
    return (
        jnp.where(lane < 88, turn(planes[0], -EDGE), middle),
        jnp.where(lane < 40, middle, turn(planes[2], EDGE)),
    )


def own_windows(f, held, got_depth):
    col = LANES * (f // FORWARD)
    return windows(f, held[f, :, :LANES], held[f, :, LANES:], got_depth[: held.shape[1], col : col + LANES])


def halo_windows(f, got_even, got_odd):
    even = is_even()
    high = EDGE + HALO * f
    low = high - (EDGE - HALO)
    col = LANES * (f // FORWARD)
    corner_even, corner_odd = got_even[:EDGE, col : col + LANES], got_odd[:EDGE, col : col + LANES]
    left = jnp.where(even, got_odd[low : low + EDGE, :], got_even[low : low + EDGE, :])
    right = jnp.where(even, got_even[high : high + EDGE, :], got_odd[high : high + EDGE, :])
    left_halo = jnp.where(even, corner_odd, corner_even)
    right_halo = jnp.where(even, corner_even, corner_odd)
    return (
        windows(f, left[:, :LANES], left[:, LANES:], left_halo),
        windows(f, right[:, :LANES], right[:, LANES:], right_halo),
    )


def load_state(state, held, got_depth, got_even, got_odd, base, planes):
    rows = held.shape[1]
    extent = rows + 2 * EDGE
    for f in range(5):
        below, above = halo_windows(base + f, got_even, got_odd)
        own = own_windows(base + f, held, got_depth)
        for i, p in enumerate(planes):
            state[f, i, :PAD, :] = jnp.zeros((PAD, LANES), F32)
            state[f, i, PAD : PAD + EDGE, :] = below[p]
            state[f, i, PAD + EDGE : PAD + EDGE + rows, :] = own[p]
            state[f, i, PAD + EDGE + rows : PAD + extent, :] = above[p]
            state[f, i, PAD + extent :, :] = jnp.zeros((PAD, LANES), F32)


def velocities(state, media, span):
    for r in range(8 * span[0], 8 * span[1], 8):
        for i in range(state.shape[1]):

            def at(f, by=0):
                return state[f, i, r + PAD + by : r + PAD + by + 8, :]

            xx, xz, zz = at(2), at(4), at(3)
            b = media[0, i, r : r + 8, :]
            near = (xx - at(2, -1)) + (xz - turn(xz, 1))
            far = (at(2, 1) - at(2, -2)) + (turn(xz, -1) - turn(xz, 2))
            state[0, i, r + PAD : r + PAD + 8, :] = at(0) + b * (near + RATIO * far)
            near = (at(4, 1) - xz) + (turn(zz, -1) - zz)
            far = (at(4, 2) - at(4, -1)) + (turn(zz, -2) - turn(zz, 1))
            state[1, i, r + PAD : r + PAD + 8, :] = at(1) + b * (near + RATIO * far)


def stresses(state, media, span, update, keep):
    for r in range(8 * span[0], 8 * span[1], 8):
        for i in range(state.shape[1]):

            def at(f, by=0):
                return state[f, i, r + PAD + by : r + PAD + by + 8, :]

            vx, vz = at(0), at(1)
            exx = (at(0, 1) - vx) + RATIO * (at(0, 2) - at(0, -1))
            ezz = (vz - turn(vz, 1)) + RATIO * (turn(vz, -1) - turn(vz, 2))
            near = (turn(vx, -1) - vx) + (vz - at(1, -1))
            far = (turn(vx, -2) - turn(vx, 1)) + (at(1, 1) - at(1, -2))
            shear = near + RATIO * far
            keep(i, r - EDGE, exx, ezz, shear)
            if update:
                whole, lam, mu = (media[k, i, r : r + 8, :] for k in (1, 2, 3))
                state[2, i, r + PAD : r + PAD + 8, :] = at(2) + (whole * exx + lam * ezz)
                state[3, i, r + PAD : r + PAD + 8, :] = at(3) + (lam * exx + whole * ezz)
                state[4, i, r + PAD : r + PAD + 8, :] = at(4) + mu * shear


def spans(step, rows):
    tiles = (rows + 2 * EDGE) // 8
    if step == 0:
        return (0, tiles), (0, tiles)
    inner = (1, tiles - 1)
    return inner, inner if step < MOMENTS - 1 else (EDGE // 8, tiles - EDGE // 8)


def run_forward(held, got_depth, got_even, got_odd, media, saved, state, planes):
    rows = held.shape[1]
    parts = []
    for f in (5, 6, 7):
        below, above = halo_windows(f, got_even, got_odd)
        own = own_windows(f, held, got_depth)
        parts.append([(below[p], own[p], above[p]) for p in planes])
    for i in range(len(planes)):
        for k, at in enumerate((0, EDGE, EDGE + rows)):
            b, lam, mu = (NEAR * parts[m][i][k] for m in range(3))
            span = slice(at, at + b.shape[0])
            media[0, i, span, :] = b
            media[1, i, span, :] = lam + 2.0 * mu
            media[2, i, span, :] = lam
            media[3, i, span, :] = mu
    load_state(state, held, got_depth, got_even, got_odd, 0, planes)
    for step in range(MOMENTS):
        fast, slow = spans(step, rows)
        velocities(state, media, fast)

        def save(i, r, exx, ezz, shear):
            if 0 <= r < rows:
                saved[step, 0, i, r : r + 8, :] = exx
                saved[step, 1, i, r : r + 8, :] = ezz
                saved[step, 2, i, r : r + 8, :] = shear

        stresses(state, media, slow, step < MOMENTS - 1, save)


def forward_kernel(held, got_depth, got_even, got_odd, media, saved, end_out, state):
    run_forward(held, got_depth, got_even, got_odd, media, saved, state, (0, 1, 2))
    rows = held.shape[1]
    top = PAD + EDGE
    for f in range(2):
        first, last = joined([state[f, i, top : top + rows, :] for i in range(3)])
        end_out[f, :, :LANES] = first
        end_out[f, :, LANES:] = last


def note_kernel(strip, got_depth, traces, cells, note_out):
    first = lax.axis_index("depth") == 0
    beside = got_depth[got_depth.shape[0] - STRIP :, :]
    beside = jnp.concatenate([beside[:, :LANES], beside[:, LANES:]], axis=0)
    seen = jnp.concatenate([traces[:, :LANES], traces[:, LANES:]], axis=0)
    along, row = cells[0], cells[1]
    places = jnp.concatenate([along[:, :LANES], along[:, LANES:], row[:, :LANES], row[:, LANES:]] * 2, axis=0)
    block = jnp.concatenate(
        [jnp.where(first, strip[...], beside), jnp.where(first, seen, places.astype(F32))], axis=0
    )
    for k in range(note_out.shape[0]):
        note_out[k] = block


def relay_kernel(notes, saved, notes_out):
    del saved
    notes_out[...] = notes[...]


def three(value):
    high = value.astype(BF16)
    rest = value - high.astype(F32)
    middle = rest.astype(BF16)
    low = (rest - middle.astype(F32)).astype(BF16)
    return [high, middle, low]


def add_up(value, count):
    return (value[2 * count : 3 * count] + value[count : 2 * count]) + value[:count]


BATCH = 5
OWN = LANES - 2 * HALO


def fill_strip(state, media, low, high, first, tracks, columns):
    lane = lane_ids(STRIP)
    state[...] = jnp.zeros(state.shape, F32)
    for w in range(BATCH):
        begin = (first + w) * OWN - HALO
        base = (begin + columns) // columns - 1
        offset = begin - base * columns
        part = lax.div(offset + lane, columns)
        inside = (begin + lane >= 0) & (begin + lane < tracks * columns)
        values = []
        for f in range(FORWARD):
            source, q = (low, high)[f // 4], f % 4
            value = jnp.zeros((STRIP, LANES), F32)
            for step in range(3):
                who = jnp.clip(base + step, 0, tracks - 1)
                block = source[who, STRIP * (q % 2) : STRIP * (q % 2 + 1), :]
                shift = (4 * LANES - offset + columns * step - columns * (q // 2)) % LANES
                value = jnp.where(part == step, pltpu.roll(block, shift, 1), value)
            values.append(jnp.where(inside, value, 0.0))
        for f in range(5):
            state[f, w, PAD : PAD + STRIP, :] = values[f]
        buoyancy, lame, shear = (NEAR * value for value in values[5:])
        media[0, w] = buoyancy
        media[1, w] = lame + 2.0 * shear
        media[2, w] = lame
        media[3, w] = shear


def strip_steps(state, media):
    def at(f, w, r, by=0):
        return state[f, w, PAD + r + by : PAD + r + by + 8, :]

    strains = [[] for _ in range(BATCH)]
    for moment in range(MOMENTS):
        last = moment == MOMENTS - 1
        for r in (0, 8) if moment < 2 else (0,):
            for w in range(BATCH):
                here = slice(PAD + r, PAD + r + 8)
                xx, xz, zz = at(2, w, r), at(4, w, r), at(3, w, r)
                b = media[0, w, r : r + 8, :]
                near = (xx - turn(xx, 1)) + (xz - at(4, w, r, -1))
                far = (turn(xx, -1) - turn(xx, 2)) + (at(4, w, r, 1) - at(4, w, r, -2))
                state[0, w, here, :] = at(0, w, r) + b * (near + RATIO * far)
                if not last:
                    near = (turn(xz, -1) - xz) + (at(3, w, r, 1) - zz)
                    far = (turn(xz, -2) - turn(xz, 1)) + (at(3, w, r, 2) - at(3, w, r, -1))
                    state[1, w, here, :] = at(1, w, r) + b * (near + RATIO * far)
        for r in (0, 8) if moment < 1 else (0,):
            for w in range(BATCH):
                here = slice(PAD + r, PAD + r + 8)
                vx, vz = at(0, w, r), at(1, w, r)
                exx = (turn(vx, -1) - vx) + RATIO * (turn(vx, -2) - turn(vx, 1))
                if r == 0:
                    strains[w].append(NEAR * exx)
                if not last:
                    ezz = (vz - at(1, w, r, -1)) + RATIO * (at(1, w, r, 1) - at(1, w, r, -2))
                    near = (at(0, w, r, 1) - vx) + (vz - turn(vz, 1))
                    far = (at(0, w, r, 2) - at(0, w, r, -1)) + (turn(vz, -1) - turn(vz, 2))
                    whole, lam, mu = (media[k, w, r : r + 8, :] for k in (1, 2, 3))
                    state[2, w, here, :] = at(2, w, r) + (whole * exx + lam * ezz)
                    state[3, w, here, :] = at(3, w, r) + (lam * exx + whole * ezz)
                    state[4, w, here, :] = at(4, w, r) + mu * (near + RATIO * far)
    return [jnp.concatenate(parts, axis=0) for parts in strains]


def recorded_rates(state, media, low, high, wanted, tracks, columns):
    lane = lane_ids(8 * MOMENTS)
    mine = (lane >= HALO) & (lane < HALO + OWN)

    def body(number, rate):
        first = number * BATCH
        fill_strip(state, media, low, high, first, tracks, columns)
        images = [three(jnp.where(mine, image, 0.0)) for image in strip_steps(state, media)]
        parts = [jnp.concatenate([image[i] for image in images], axis=1) for i in range(3)]
        spots = [
            (first + w) * OWN - HALO + row_ids(LANES, wanted.shape[1]) for w in range(BATCH)
        ]
        hot = (jnp.concatenate(spots, axis=0) == wanted).astype(F32).astype(BF16)
        return rate + jnp.dot(jnp.concatenate(parts, axis=0), hot, preferred_element_type=F32)

    rate = jnp.zeros((3 * 8 * MOMENTS, wanted.shape[1]), F32)
    batches = -(-(-(-tracks * columns // OWN)) // BATCH)
    rate = body(0, rate) if batches == 1 else lax.fori_loop(0, batches, body, rate)
    return add_up(rate, 8 * MOMENTS)


def window_sums(low, high, start, tracks):
    group = min(8, tracks)
    row16 = row_ids(IMAGE, LANES)

    def body(number, image):
        weights, hots = [], []
        for k in range(group):
            who = number * group + k
            traces = low[who, 2 * STRIP :, :]
            places = high[who, 2 * STRIP :, :]
            for h in range(2):
                mask = (row16 & 3).astype(F32) == places[2 + h : 3 + h]
                seen = [traces[4 * h + t : 4 * h + t + 1] for t in range(MOMENTS)]
                value = jnp.where(
                    row16 < 8,
                    jnp.where(row16 < 4, seen[0], seen[1]),
                    jnp.where(row16 < 12, seen[2], seen[3]),
                )
                pieces = three(jnp.where(mask, value, 0.0)) + [mask.astype(F32).astype(BF16)]
                weights.append(jnp.concatenate(pieces, axis=0))
                spot = (start + row_ids(LANES, LANES)).astype(F32)
                hots.append((spot == places[h : h + 1]).astype(F32).astype(BF16))
        return image + lax.dot_general(
            jnp.concatenate(weights, axis=1),
            jnp.concatenate(hots, axis=1),
            (((1,), (1,)), ((), ())),
            preferred_element_type=F32,
        )

    image = jnp.zeros((4 * IMAGE, LANES), F32)
    image = body(0, image) if tracks == group else lax.fori_loop(0, tracks // group, body, image)
    return add_up(image, IMAGE), image[3 * IMAGE :]


def surface_kernel(tracks, columns, notes, beside, obs, cells, inject_out, residual_out, state, media, low, high):
    depth = lax.axis_index("depth")
    low[...] = jnp.where(depth == 0, notes[...], beside[...])
    high[...] = jnp.where(depth == 0, beside[...], notes[...])
    start = lax.axis_index("track") * columns - EDGE
    along, row = cells[0], cells[1]
    channels = along.shape[1]
    wanted = jnp.concatenate([along, start + lax.broadcasted_iota(jnp.int32, (1, LANES), 1)], axis=1)
    seen, count = window_sums(low, high, start, tracks)
    rate = recorded_rates(state, media, low, high, wanted, tracks, columns)
    mask = row_ids(8, channels) == row
    traces = [
        jnp.sum(jnp.where(mask, rate[8 * t : 8 * t + 8, :channels], 0.0), axis=0, keepdims=True)
        - obs[t : t + 1, :]
        for t in range(MOMENTS)
    ]
    residual_out[...] = jnp.where(
        depth == 0, jnp.concatenate(traces[:2], axis=0), jnp.concatenate(traces[2:], axis=0)
    )
    near = jnp.concatenate([rate[8 * t : 8 * t + 4, channels:] for t in range(MOMENTS)], axis=0)
    sources = jnp.where(depth == 0, count * near - seen, 0.0)
    turned = jnp.concatenate([sources, jnp.zeros((LANES - IMAGE, LANES), F32)], axis=0).T
    inject_out[...] = turned[: inject_out.shape[0]]


def run_adjoint(media, saved, state, sums, inject=None):
    rows = sums.shape[2]
    sums[...] = jnp.zeros(sums.shape, F32)
    for step in range(MOMENTS):
        fast, slow = spans(step, rows)
        moment = MOMENTS - 1 - step
        if inject is not None:
            inject(moment)
        velocities(state, media, fast)

        def gather(i, r, exx, ezz, shear):
            if 0 <= r < rows:
                fxx, fzz, fxz = (saved[moment, k, i, r : r + 8, :] for k in range(3))
                sums[0, i, r : r + 8, :] += (fxx + fzz) * (exx + ezz)
                sums[1, i, r : r + 8, :] += 2.0 * (fxx * exx + fzz * ezz) + fxz * shear

        stresses(state, media, slow, step < MOMENTS - 1, gather)


def adjoint_rest_kernel(held, got_depth, got_even, got_odd, media, saved, notes, sums, state):
    del notes
    load_state(state, held, got_depth, got_even, got_odd, FORWARD, (1, 2))
    run_adjoint(media.at[:, pl.ds(1, 2)], saved.at[:, :, pl.ds(1, 2)], state, sums)


def adjoint_top_kernel(
    held, got_depth, got_even, got_odd, media, saved, rest, inject, end, residual,
    lambda_out, mu_out, end_out, residual_out, state, sums, sems,
):
    copies = fetch((end, residual), (end_out, residual_out), sems)
    rows = held.shape[1]
    extent = rows + 2 * EDGE
    load_state(state, held, got_depth, got_even, got_odd, FORWARD, (0,))
    lane = lane_ids(extent)
    here = (lane >= EDGE) & (lane < EDGE + FIBRE_ROWS)

    def add(moment):
        added = jnp.where(here, turn(inject[...], EDGE - FIBRE_ROWS * moment), 0.0)
        state[2, 0, PAD : PAD + extent, :] += added

    run_adjoint(media.at[:, pl.ds(0, 1)], saved.at[:, :, pl.ds(0, 1)], state, sums, add)
    for k, out in enumerate((lambda_out, mu_out)):
        first, last = joined([sums[k, 0], rest[k, 0], rest[k, 1]])
        out[:, :LANES] = (NEAR * NEAR) * first
        out[:, LANES:] = (NEAR * NEAR) * last
    for copy in copies:
        copy.wait()


def per_device(
    velocity,
    stress,
    adjoint_velocity,
    adjoint_stress,
    buoyancy,
    lame_lambda,
    shear_modulus,
    observed,
    owner_track,
    fibre_cell,
):
    tracks = lax.axis_size("track")
    rows, depth_cells = buoyancy.shape
    moments, channels = observed.shape
    owner = owner_track.reshape(1, channels)
    cell = fibre_cell.reshape(1, channels)
    pinned = lambda array: pltpu.with_memory_space_constraint(array, pltpu.HBM)
    arrays = (velocity, stress, adjoint_velocity, adjoint_stress, buoyancy, lame_lambda, shear_modulus)
    arrays = tuple(pinned(array) for array in arrays)
    channel_arrays = (pinned(observed), pinned(owner), pinned(cell))
    extent = rows + 2 * EDGE
    block = jax.ShapeDtypeStruct((rows, depth_cells), F32)
    length = EDGE + HALO * FIELDS + EDGE - HALO
    edges = jax.ShapeDtypeStruct((length + (-length) % 8, depth_cells), F32)
    inside = pl.BlockSpec(memory_space=VMEM)
    outside = pl.BlockSpec(memory_space=pltpu.HBM)
    anywhere = pl.BlockSpec(memory_space=pl.ANY)
    held, to_depth, to_even, to_odd, strip, traces, cells = pl.pallas_call(
        pack_kernel,
        out_shape=(
            jax.ShapeDtypeStruct((FIELDS, rows, depth_cells), F32),
            jax.ShapeDtypeStruct((rows + STRIP, depth_cells), F32),
            edges,
            edges,
            jax.ShapeDtypeStruct((2 * STRIP, LANES), F32),
            jax.ShapeDtypeStruct((moments, channels), F32),
            jax.ShapeDtypeStruct((2, 1, channels), jnp.int32),
        ),
        in_specs=[outside] * 10,
        out_specs=(inside,) * 7,
        scratch_shapes=[VMEM((2, 1, channels), jnp.int32), pltpu.SemaphoreType.DMA((10,))],
        compiler_params=params(),
        cost_estimate=cost(5),
        name="pack",
    )(*arrays, *channel_arrays)
    to_track = (to_even, to_odd)

    depth_swap = [(0, 1), (1, 0)]
    got_depth = lax.ppermute(to_depth, "depth", depth_swap)
    to_track = pl.pallas_call(
        corner_kernel,
        out_shape=(edges, edges),
        in_specs=[anywhere] * 3,
        out_specs=(anywhere,) * 2,
        input_output_aliases={1: 0, 2: 1},
        scratch_shapes=[pltpu.SemaphoreType.DMA((2,))],
        compiler_params=params(),
        name="corners",
    )(got_depth, *to_track)
    swap = lambda k: [pair for i in range(k, tracks - 1, 2) for pair in ((i, i + 1), (i + 1, i))]
    got_odd = lax.ppermute(to_track[1], "track", swap(1))
    got_even = lax.ppermute(to_track[0], "track", swap(0))

    def state_of(planes):
        return VMEM((5, planes, extent + 2 * PAD, LANES), F32)

    note = pl.pallas_call(
        note_kernel,
        out_shape=jax.ShapeDtypeStruct((tracks, 2 * STRIP + 8, LANES), F32),
        in_specs=[inside] * 4,
        out_specs=inside,
        compiler_params=params(),
        cost_estimate=cost(1),
        name="note",
    )(strip, got_depth, traces, cells)
    notes = lax.all_to_all(note, "track", split_axis=0, concat_axis=0, tiled=True)

    media, saved, end = pl.pallas_call(
        forward_kernel,
        out_shape=(
            jax.ShapeDtypeStruct((4, 3, extent, LANES), F32),
            jax.ShapeDtypeStruct((moments, 3, 3, rows, LANES), F32),
            jax.ShapeDtypeStruct(velocity.shape, F32),
        ),
        in_specs=[inside] * 4,
        out_specs=(inside,) * 3,
        scratch_shapes=[state_of(3)],
        compiler_params=params(),
        cost_estimate=cost(20),
        name="forward",
    )(held, got_depth, got_even, got_odd)

    mine = pl.pallas_call(
        relay_kernel,
        out_shape=jax.ShapeDtypeStruct(note.shape, F32),
        in_specs=[inside, anywhere],
        out_specs=inside,
        compiler_params=params(),
        cost_estimate=cost(1),
        name="relay",
    )(notes, saved)
    beside = lax.ppermute(mine, "depth", depth_swap)

    rest = pl.pallas_call(
        adjoint_rest_kernel,
        out_shape=jax.ShapeDtypeStruct((2, 2, rows, LANES), F32),
        in_specs=[inside] * 6 + [anywhere],
        out_specs=inside,
        scratch_shapes=[state_of(2)],
        compiler_params=params(),
        cost_estimate=cost(20),
        name="adjoint_rest",
    )(held, got_depth, got_even, got_odd, media, saved, mine)

    inject, residual = pl.pallas_call(
        lambda *refs: surface_kernel(tracks, rows, *refs),
        out_shape=(
            jax.ShapeDtypeStruct((extent, LANES), F32),
            jax.ShapeDtypeStruct((moments // 2, channels), F32),
        ),
        in_specs=[inside] * 4,
        out_specs=(inside,) * 2,
        scratch_shapes=[
            VMEM((5, BATCH, 2 * PAD + STRIP, LANES), F32),
            VMEM((4, BATCH, STRIP, LANES), F32),
            VMEM(note.shape, F32),
            VMEM(note.shape, F32),
        ],
        compiler_params=params(),
        cost_estimate=cost(2),
        name="surface",
    )(mine, beside, traces, cells)

    gradient_lambda, gradient_mu, velocity_end, residual = pl.pallas_call(
        adjoint_top_kernel,
        out_shape=(
            block,
            block,
            jax.ShapeDtypeStruct(velocity.shape, F32),
            jax.ShapeDtypeStruct((moments // 2, channels), F32),
        ),
        in_specs=[inside] * 10,
        out_specs=(inside, inside, outside, outside),
        scratch_shapes=[state_of(1), VMEM((2, 1, rows, LANES), F32), pltpu.SemaphoreType.DMA((2,))],
        compiler_params=params(),
        cost_estimate=cost(2),
        name="adjoint_top",
    )(held, got_depth, got_even, got_odd, media, saved, rest, inject, end, residual)
    return gradient_lambda, gradient_mu, velocity_end, residual


def solution(mesh):
    return jax.shard_map(
        per_device,
        mesh=mesh,
        in_specs=(
            P("shots", "track", "depth"),
            P("shots", "track", "depth"),
            P("shots", "track", "depth"),
            P("shots", "track", "depth"),
            P("track", "depth"),
            P("track", "depth"),
            P("track", "depth"),
            P("shots", "track"),
            P("track", None),
            P("track"),
        ),
        out_specs=(
            P(("shots", "track"), "depth"),
            P(("shots", "track"), "depth"),
            P("shots", "track", "depth"),
            P(("shots", "depth"), "track"),
        ),
        check_vma=False,
    )
```

```python
import jax
import jax.numpy as jnp
from jax import lax
from jax.experimental import pallas as pl
from jax.experimental.pallas import tpu as pltpu
from jax.sharding import PartitionSpec as P

FIBRE_ROWS = 4
NEAR = 9.0 / 8.0
RATIO = -1.0 / 27.0
HALO = 12
EDGE = 16
LANES = 128
PAD = 8
FORWARD = 8
ADJOINT = 5
FIELDS = FORWARD + ADJOINT
STRIP = 16
BASE = EDGE - HALO
MOMENTS = 4
IMAGE = MOMENTS * FIBRE_ROWS
VMEM = pltpu.VMEM
F32 = jnp.float32
BF16 = jnp.bfloat16


def lane_ids(rows):
    return lax.broadcasted_iota(jnp.int32, (rows, LANES), 1)


def row_ids(rows, columns):
    return lax.broadcasted_iota(jnp.int32, (rows, columns), 0)


def params():
    return pltpu.CompilerParams(vmem_limit_bytes=16 * 1024 * 1024)


def cost(microseconds):
    return pl.CostEstimate(flops=int(microseconds * 1e9), bytes_accessed=1 << 20, transcendentals=0)


def turn(value, by):
    return pltpu.roll(value, by % LANES, 1)


def is_even():
    return lax.rem(lax.axis_index("track"), 2) == 0


def fetch(sources, targets, sems):
    copies = [pltpu.make_async_copy(s, t, sems.at[i]) for i, (s, t) in enumerate(zip(sources, targets))]
    for copy in copies:
        copy.start()
    return copies


def pack_kernel(*refs):
    sources, channel_arrays = refs[:7], refs[7:10]
    held, held_adj, depth_out, edge_outs, strip_out, traces_out, cells_out = *refs[10:13], refs[13:15], *refs[15:18]
    numbers, sems = refs[18:]
    targets = (
        held.at[pl.ds(0, 2)],
        held.at[pl.ds(2, 3)],
        held.at[5],
        held.at[6],
        held.at[7],
        held_adj.at[pl.ds(0, 2)],
        held_adj.at[pl.ds(2, 3)],
        traces_out,
        numbers.at[0],
        numbers.at[1],
    )
    copies = fetch((*sources[:2], *sources[4:], *sources[2:4], *channel_arrays), targets, sems)
    arriving = {0: copies[0], 2: copies[1], 5: copies[2], 6: copies[3], 7: copies[4], 8: copies[5], 10: copies[6]}
    depth = lax.axis_index("depth")
    even = is_even()
    rows = held.shape[1]
    lane = lane_ids(rows)
    tail = BASE + HALO * FIELDS
    for out in edge_outs:
        out[:BASE, :] = jnp.zeros((BASE, 2 * LANES), F32)
        out[tail:, :] = jnp.zeros((out.shape[0] - tail, 2 * LANES), F32)
    packed = [jnp.zeros((rows, LANES), F32) for _ in range(2)]
    strip = jnp.zeros((rows, LANES), F32)
    for f in range(FIELDS):
        if f in arriving:
            arriving[f].wait()
        ref = held.at[f] if f < FORWARD else held_adj.at[f - FORWARD]
        first, last = ref[:, :LANES], ref[:, LANES:]
        group, place = divmod(f, FORWARD)
        spot = EDGE * place
        here = (lane >= spot) & (lane < spot + EDGE)
        edge = jnp.where(depth == 0, last, first)
        shift = lax.rem(spot + EDGE * (1 - depth), LANES)
        packed[group] = jnp.where(here, pltpu.roll(edge, shift, 1), packed[group])
        if f < FORWARD:
            strip = jnp.where(here, turn(first, spot), strip)
        low, high = ref[:HALO, :], ref[rows - HALO :, :]
        at = BASE + HALO * f
        edge_outs[0][at : at + HALO, :] = jnp.where(even, high, low)
        edge_outs[1][at : at + HALO, :] = jnp.where(even, low, high)
    depth_out[:rows, :LANES] = packed[0]
    depth_out[:rows, LANES:] = packed[1]
    turned = strip.T
    strip_out[:, :rows] = turned[: 2 * STRIP]
    strip_out[:, rows:] = turned[2 * STRIP : 4 * STRIP]
    depth_out[rows:, :rows] = turned[4 * STRIP : 5 * STRIP]
    depth_out[rows:, rows : 2 * rows] = turned[6 * STRIP : 7 * STRIP]
    depth_out[rows:, 2 * rows : 3 * rows] = turned[5 * STRIP : 6 * STRIP]
    depth_out[rows:, 3 * rows :] = turned[7 * STRIP :]
    for copy in copies[7:]:
        copy.wait()
    cells_out[0] = numbers[0] * rows + lax.shift_right_logical(numbers[1], 2)
    cells_out[1] = numbers[1] & 3


def edge_rows(f, side, got_even, got_odd):
    at = BASE + HALO * f
    span = slice(at - BASE, at + HALO) if side == 0 else slice(at, at + EDGE)
    use_odd = is_even() if side == 0 else ~is_even()
    return jnp.where(use_odd, got_odd[span, :], got_even[span, :])


def corner_kernel(got_even, got_odd, corner_out):
    depth = lax.axis_index("depth")
    lane = lane_ids(EDGE)
    for side in range(2):
        packed = [jnp.zeros((EDGE, LANES), F32) for _ in range(2)]
        for f in range(FIELDS):
            group, place = divmod(f, FORWARD)
            spot = EDGE * place
            value = edge_rows(f, side, got_even, got_odd)
            edge = jnp.where(depth == 0, value[:, LANES:], value[:, :LANES])
            shift = lax.rem(spot + EDGE * (1 - depth), LANES)
            here = (lane >= spot) & (lane < spot + EDGE)
            packed[group] = jnp.where(here, pltpu.roll(edge, shift, 1), packed[group])
        corner_out[EDGE * side : EDGE * (side + 1), :LANES] = packed[0]
        corner_out[EDGE * side : EDGE * (side + 1), LANES:] = packed[1]


def window(plane, f, value, halo):
    depth = lax.axis_index("depth")
    surface = depth == 0
    first, last = value[:, :LANES], value[:, LANES:]
    lane = lane_ids(first.shape[0])
    low = jnp.where(surface, lane, LANES - 1 - lane)
    if plane == 0:
        shift = jnp.where(surface, EDGE, LANES - EDGE)
        return jnp.where(low >= EDGE, pltpu.roll(jnp.where(surface, first, last), shift, 1), 0.0)
    if plane == 1:
        return jnp.where(lane < LANES // 2, turn(first, LANES // 2), turn(last, LANES // 2))
    shift = jnp.where(surface, LANES - EDGE, EDGE)
    beside = lax.rem(LANES - EDGE * (f % FORWARD) + (LANES - EDGE) * (1 - depth), LANES)
    own = pltpu.roll(jnp.where(surface, last, first), shift, 1)
    return jnp.where(low < LANES - EDGE, own, pltpu.roll(halo, beside, 1))


def field_windows(f, planes, held, got_even, got_odd, got_depth=None, corner=None):
    rows = held.shape[1]
    col = LANES * (f // FORWARD)
    blocks = (
        (0, edge_rows(f, 0, got_even, got_odd), corner, 0),
        (EDGE, held[f % FORWARD], got_depth, 0),
        (EDGE + rows, edge_rows(f, 1, got_even, got_odd), corner, EDGE),
    )
    found = [[] for _ in planes]
    for at, value, halo, start in blocks:
        if halo is not None:
            halo = halo[start : start + value.shape[0], col : col + LANES]
        for parts, p in zip(found, planes):
            parts.append((at, window(p, f, value, halo)))
    return found


def joined(outer, middle, inner):
    surface = lax.axis_index("depth") == 0
    lane = lane_ids(outer.shape[0])
    first, last = jnp.where(surface, outer, inner), jnp.where(surface, inner, outer)
    middle = turn(middle, LANES // 2)
    return jnp.where(lane < 88, turn(first, -EDGE), middle), jnp.where(lane < 40, middle, turn(last, EDGE))


def load_state(states, base, planes, held, *got):
    extent = held.shape[1] + 2 * EDGE
    for f in range(5):
        for state, parts in zip(states, field_windows(base + f, planes, held, *got)):
            state[f, :PAD, :] = jnp.zeros((PAD, LANES), F32)
            state[f, PAD + extent :, :] = jnp.zeros((PAD, LANES), F32)
            for at, part in parts:
                state[f, PAD + at : PAD + at + part.shape[0], :] = part


def velocities(states, medias, span):
    for r in range(8 * span[0], 8 * span[1], 8):
        for state, media in zip(states, medias):

            def at(f, by=0):
                return state[f, r + PAD + by : r + PAD + by + 8, :]

            xx, xz, zz = at(2), at(4), at(3)
            b = media[0, r : r + 8, :]
            near = (xx - at(2, -1)) + (xz - turn(xz, 1))
            far = (at(2, 1) - at(2, -2)) + (turn(xz, -1) - turn(xz, 2))
            state[0, r + PAD : r + PAD + 8, :] = at(0) + b * (near + RATIO * far)
            near = (at(4, 1) - xz) + (turn(zz, -1) - zz)
            far = (at(4, 2) - at(4, -1)) + (turn(zz, -2) - turn(zz, 1))
            state[1, r + PAD : r + PAD + 8, :] = at(1) + b * (near + RATIO * far)


def stresses(states, medias, span, update, keep):
    for r in range(8 * span[0], 8 * span[1], 8):
        for i, (state, media) in enumerate(zip(states, medias)):

            def at(f, by=0):
                return state[f, r + PAD + by : r + PAD + by + 8, :]

            vx, vz = at(0), at(1)
            exx = (at(0, 1) - vx) + RATIO * (at(0, 2) - at(0, -1))
            ezz = (vz - turn(vz, 1)) + RATIO * (turn(vz, -1) - turn(vz, 2))
            near = (turn(vx, -1) - vx) + (vz - at(1, -1))
            far = (turn(vx, -2) - turn(vx, 1)) + (at(1, 1) - at(1, -2))
            shear = near + RATIO * far
            keep(i, r - EDGE, exx, ezz, shear)
            if update:
                whole, lam, mu = (media[k, r : r + 8, :] for k in (1, 2, 3))
                state[2, r + PAD : r + PAD + 8, :] = at(2) + (whole * exx + lam * ezz)
                state[3, r + PAD : r + PAD + 8, :] = at(3) + (lam * exx + whole * ezz)
                state[4, r + PAD : r + PAD + 8, :] = at(4) + mu * shear


def spans(step, rows):
    tiles = (rows + 2 * EDGE) // 8
    if step == 0:
        return (0, tiles), (0, tiles)
    inner = (1, tiles - 1)
    return inner, inner if step < MOMENTS - 1 else (EDGE // 8, tiles - EDGE // 8)


def run_forward(states, medias, saveds, planes, held, *got):
    rows = held.shape[1]
    given = [field_windows(f, planes, held, *got) for f in (5, 6, 7)]
    for i, media in enumerate(medias):
        for k in range(3):
            at = given[0][i][k][0]
            b, lam, mu = (NEAR * given[m][i][k][1] for m in range(3))
            span = slice(at, at + b.shape[0])
            media[0, span, :] = b
            media[1, span, :] = lam + 2.0 * mu
            media[2, span, :] = lam
            media[3, span, :] = mu
    load_state(states, 0, planes, held, *got)
    for step in range(MOMENTS):
        fast, slow = spans(step, rows)
        velocities(states, medias, fast)

        def save(i, r, exx, ezz, shear):
            if 0 <= r < rows:
                saveds[i][step, 0, r : r + 8, :] = exx
                saveds[i][step, 1, r : r + 8, :] = ezz
                saveds[i][step, 2, r : r + 8, :] = shear

        stresses(states, medias, slow, step < MOMENTS - 1, save)


def each(ref, count, axis):
    return [ref.at[(slice(None),) * axis + (i,)] for i in range(count)]


def forward_kernel(held, got_even, got_odd, media, saved, end_out, state):
    states = each(state, 2, 1)
    run_forward(states, each(media, 2, 1), each(saved, 2, 2), (0, 1), held, got_even, got_odd)
    top, rows = PAD + EDGE, held.shape[1]
    for f in range(2):
        for i in range(2):
            end_out[f, i] = states[i][f, top : top + rows, :]


def forward_inner_kernel(held, got_even, got_odd, got_depth, corner, end, media, saved, end_out, state):
    states = each(state, 1, 1)
    run_forward(
        states, each(media, 1, 1), each(saved, 1, 2), (2,), held, got_even, got_odd, got_depth, corner
    )
    top, rows = PAD + EDGE, held.shape[1]
    for f in range(2):
        first, last = joined(end[f, 0], end[f, 1], states[0][f, top : top + rows, :])
        end_out[f, :, :LANES] = first
        end_out[f, :, LANES:] = last


def note_kernel(strip, got_depth, traces, cells, note_out):
    first = lax.axis_index("depth") == 0
    beside = got_depth[got_depth.shape[0] - STRIP :, :]
    beside = jnp.concatenate([beside[:, :LANES], beside[:, LANES:]], axis=0)
    seen = jnp.concatenate([traces[:, :LANES], traces[:, LANES:]], axis=0)
    along, row = cells[0], cells[1]
    places = jnp.concatenate([along[:, :LANES], along[:, LANES:], row[:, :LANES], row[:, LANES:]] * 2, axis=0)
    block = jnp.concatenate(
        [jnp.where(first, strip[...], beside), jnp.where(first, seen, places.astype(F32))], axis=0
    )
    for k in range(note_out.shape[0]):
        note_out[k] = block


def relay_kernel(notes, rest, notes_out):
    del rest
    notes_out[...] = notes[...]


def three(value):
    high = value.astype(BF16)
    rest = value - high.astype(F32)
    middle = rest.astype(BF16)
    low = (rest - middle.astype(F32)).astype(BF16)
    return [high, middle, low]


def add_up(value, count):
    return (value[2 * count : 3 * count] + value[count : 2 * count]) + value[:count]


BATCH = 5
OWN = LANES - 2 * HALO


def fill_strip(state, media, low, high, first, tracks, columns):
    lane = lane_ids(STRIP)
    state[...] = jnp.zeros(state.shape, F32)
    for w in range(BATCH):
        begin = (first + w) * OWN - HALO
        base = (begin + columns) // columns - 1
        offset = begin - base * columns
        part = lax.div(offset + lane, columns)
        inside = (begin + lane >= 0) & (begin + lane < tracks * columns)
        values = []
        for f in range(FORWARD):
            source, q = (low, high)[f // 4], f % 4
            value = jnp.zeros((STRIP, LANES), F32)
            for step in range(3):
                who = jnp.clip(base + step, 0, tracks - 1)
                block = source[who, STRIP * (q % 2) : STRIP * (q % 2 + 1), :]
                shift = (4 * LANES - offset + columns * step - columns * (q // 2)) % LANES
                value = jnp.where(part == step, pltpu.roll(block, shift, 1), value)
            values.append(jnp.where(inside, value, 0.0))
        for f in range(5):
            state[f, w, PAD : PAD + STRIP, :] = values[f]
        buoyancy, lame, shear = (NEAR * value for value in values[5:])
        media[0, w] = buoyancy
        media[1, w] = lame + 2.0 * shear
        media[2, w] = lame
        media[3, w] = shear


def strip_steps(state, media):
    def at(f, w, r, by=0):
        return state[f, w, PAD + r + by : PAD + r + by + 8, :]

    strains = [[] for _ in range(BATCH)]
    for moment in range(MOMENTS):
        last = moment == MOMENTS - 1
        for r in (0, 8) if moment < 2 else (0,):
            for w in range(BATCH):
                here = slice(PAD + r, PAD + r + 8)
                xx, xz, zz = at(2, w, r), at(4, w, r), at(3, w, r)
                b = media[0, w, r : r + 8, :]
                near = (xx - turn(xx, 1)) + (xz - at(4, w, r, -1))
                far = (turn(xx, -1) - turn(xx, 2)) + (at(4, w, r, 1) - at(4, w, r, -2))
                state[0, w, here, :] = at(0, w, r) + b * (near + RATIO * far)
                if not last:
                    near = (turn(xz, -1) - xz) + (at(3, w, r, 1) - zz)
                    far = (turn(xz, -2) - turn(xz, 1)) + (at(3, w, r, 2) - at(3, w, r, -1))
                    state[1, w, here, :] = at(1, w, r) + b * (near + RATIO * far)
        for r in (0, 8) if moment < 1 else (0,):
            for w in range(BATCH):
                here = slice(PAD + r, PAD + r + 8)
                vx, vz = at(0, w, r), at(1, w, r)
                exx = (turn(vx, -1) - vx) + RATIO * (turn(vx, -2) - turn(vx, 1))
                if r == 0:
                    strains[w].append(NEAR * exx)
                if not last:
                    ezz = (vz - at(1, w, r, -1)) + RATIO * (at(1, w, r, 1) - at(1, w, r, -2))
                    near = (at(0, w, r, 1) - vx) + (vz - turn(vz, 1))
                    far = (at(0, w, r, 2) - at(0, w, r, -1)) + (turn(vz, -1) - turn(vz, 2))
                    whole, lam, mu = (media[k, w, r : r + 8, :] for k in (1, 2, 3))
                    state[2, w, here, :] = at(2, w, r) + (whole * exx + lam * ezz)
                    state[3, w, here, :] = at(3, w, r) + (lam * exx + whole * ezz)
                    state[4, w, here, :] = at(4, w, r) + mu * (near + RATIO * far)
    return [jnp.concatenate(parts, axis=0) for parts in strains]


def recorded_rates(state, media, low, high, wanted, tracks, columns):
    lane = lane_ids(8 * MOMENTS)
    mine = (lane >= HALO) & (lane < HALO + OWN)

    def body(number, rate):
        first = number * BATCH
        fill_strip(state, media, low, high, first, tracks, columns)
        images = [three(jnp.where(mine, image, 0.0)) for image in strip_steps(state, media)]
        parts = [jnp.concatenate([image[i] for image in images], axis=1) for i in range(3)]
        spots = [
            (first + w) * OWN - HALO + row_ids(LANES, wanted.shape[1]) for w in range(BATCH)
        ]
        hot = (jnp.concatenate(spots, axis=0) == wanted).astype(F32).astype(BF16)
        return rate + jnp.dot(jnp.concatenate(parts, axis=0), hot, preferred_element_type=F32)

    rate = jnp.zeros((3 * 8 * MOMENTS, wanted.shape[1]), F32)
    batches = -(-(-(-tracks * columns // OWN)) // BATCH)
    rate = body(0, rate) if batches == 1 else lax.fori_loop(0, batches, body, rate)
    return add_up(rate, 8 * MOMENTS)


def window_sums(low, high, start, tracks):
    group = min(8, tracks)
    row16 = row_ids(IMAGE, LANES)

    def body(number, image):
        weights, hots = [], []
        for k in range(group):
            who = number * group + k
            traces = low[who, 2 * STRIP :, :]
            places = high[who, 2 * STRIP :, :]
            for h in range(2):
                mask = (row16 & 3).astype(F32) == places[2 + h : 3 + h]
                seen = [traces[4 * h + t : 4 * h + t + 1] for t in range(MOMENTS)]
                value = jnp.where(
                    row16 < 8,
                    jnp.where(row16 < 4, seen[0], seen[1]),
                    jnp.where(row16 < 12, seen[2], seen[3]),
                )
                pieces = three(jnp.where(mask, value, 0.0)) + [mask.astype(F32).astype(BF16)]
                weights.append(jnp.concatenate(pieces, axis=0))
                spot = (start + row_ids(LANES, LANES)).astype(F32)
                hots.append((spot == places[h : h + 1]).astype(F32).astype(BF16))
        return image + lax.dot_general(
            jnp.concatenate(weights, axis=1),
            jnp.concatenate(hots, axis=1),
            (((1,), (1,)), ((), ())),
            preferred_element_type=F32,
        )

    image = jnp.zeros((4 * IMAGE, LANES), F32)
    image = body(0, image) if tracks == group else lax.fori_loop(0, tracks // group, body, image)
    return add_up(image, IMAGE), image[3 * IMAGE :]


def surface_kernel(tracks, columns, notes, beside, obs, cells, inject_out, residual_out, state, media, low, high):
    depth = lax.axis_index("depth")
    low[...] = jnp.where(depth == 0, notes[...], beside[...])
    high[...] = jnp.where(depth == 0, beside[...], notes[...])
    start = lax.axis_index("track") * columns - EDGE
    along, row = cells[0], cells[1]
    channels = along.shape[1]
    wanted = jnp.concatenate([along, start + lax.broadcasted_iota(jnp.int32, (1, LANES), 1)], axis=1)
    seen, count = window_sums(low, high, start, tracks)
    rate = recorded_rates(state, media, low, high, wanted, tracks, columns)
    mask = row_ids(8, channels) == row
    traces = [
        jnp.sum(jnp.where(mask, rate[8 * t : 8 * t + 8, :channels], 0.0), axis=0, keepdims=True)
        - obs[t : t + 1, :]
        for t in range(MOMENTS)
    ]
    residual_out[...] = jnp.where(
        depth == 0, jnp.concatenate(traces[:2], axis=0), jnp.concatenate(traces[2:], axis=0)
    )
    near = jnp.concatenate([rate[8 * t : 8 * t + 4, channels:] for t in range(MOMENTS)], axis=0)
    sources = jnp.where(depth == 0, count * near - seen, 0.0)
    turned = jnp.concatenate([sources, jnp.zeros((LANES - IMAGE, LANES), F32)], axis=0).T
    inject_out[...] = turned[: inject_out.shape[0]]


def run_adjoint(states, medias, saveds, sums, inject=None):
    rows = sums[0].shape[1]
    for total in sums:
        total[...] = jnp.zeros(total.shape, F32)
    for step in range(MOMENTS):
        fast, slow = spans(step, rows)
        moment = MOMENTS - 1 - step
        if inject is not None:
            inject(moment)
        velocities(states, medias, fast)

        def gather(i, r, exx, ezz, shear):
            if 0 <= r < rows:
                fxx, fzz, fxz = (saveds[i][moment, k, r : r + 8, :] for k in range(3))
                sums[i][0, r : r + 8, :] += (fxx + fzz) * (exx + ezz)
                sums[i][1, r : r + 8, :] += 2.0 * (fxx * exx + fzz * ezz) + fxz * shear

        stresses(states, medias, slow, step < MOMENTS - 1, gather)


def adjoint_rest_kernel(
    held, got_even, got_odd, got_depth, corner, media, saved, inner_media, inner_saved, sums, state
):
    states = each(state, 2, 1)
    load_state(states, FORWARD, (1, 2), held, got_even, got_odd, got_depth, corner)
    medias = [media.at[:, 1], inner_media.at[:, 0]]
    saveds = [saved.at[:, :, 1], inner_saved.at[:, :, 0]]
    run_adjoint(states, medias, saveds, each(sums, 2, 1))


def adjoint_top_kernel(
    held, got_even, got_odd, media, saved, rest, inject, end, residual,
    lambda_out, mu_out, end_out, residual_out, state, sums, sems,
):
    copies = fetch((end, residual), (end_out, residual_out), sems)
    rows = held.shape[1]
    extent = rows + 2 * EDGE
    states = each(state, 1, 1)
    load_state(states, FORWARD, (0,), held, got_even, got_odd)
    lane = lane_ids(extent)
    here = (lane >= EDGE) & (lane < EDGE + FIBRE_ROWS)

    def add(moment):
        added = jnp.where(here, turn(inject[...], EDGE - FIBRE_ROWS * moment), 0.0)
        states[0][2, PAD : PAD + extent, :] += added

    run_adjoint(states, [media.at[:, 0]], [saved.at[:, :, 0]], each(sums, 1, 1), add)
    for k, out in enumerate((lambda_out, mu_out)):
        first, last = joined(sums[k, 0], rest[k, 0], rest[k, 1])
        out[:, :LANES] = (NEAR * NEAR) * first
        out[:, LANES:] = (NEAR * NEAR) * last
    for copy in copies:
        copy.wait()


def per_device(
    velocity,
    stress,
    adjoint_velocity,
    adjoint_stress,
    buoyancy,
    lame_lambda,
    shear_modulus,
    observed,
    owner_track,
    fibre_cell,
):
    tracks = lax.axis_size("track")
    rows, depth_cells = buoyancy.shape
    moments, channels = observed.shape
    owner = owner_track.reshape(1, channels)
    cell = fibre_cell.reshape(1, channels)
    pinned = lambda array: pltpu.with_memory_space_constraint(array, pltpu.HBM)
    arrays = (velocity, stress, adjoint_velocity, adjoint_stress, buoyancy, lame_lambda, shear_modulus)
    arrays = tuple(pinned(array) for array in arrays)
    channel_arrays = (pinned(observed), pinned(owner), pinned(cell))
    extent = rows + 2 * EDGE
    block = jax.ShapeDtypeStruct((rows, depth_cells), F32)
    length = BASE + HALO * FIELDS + BASE
    edges = jax.ShapeDtypeStruct((length + (-length) % 8, depth_cells), F32)
    inside = pl.BlockSpec(memory_space=VMEM)
    outside = pl.BlockSpec(memory_space=pltpu.HBM)
    anywhere = pl.BlockSpec(memory_space=pl.ANY)
    held, held_adj, to_depth, to_even, to_odd, strip, traces, cells = pl.pallas_call(
        pack_kernel,
        out_shape=(
            jax.ShapeDtypeStruct((FORWARD, rows, depth_cells), F32),
            jax.ShapeDtypeStruct((ADJOINT, rows, depth_cells), F32),
            jax.ShapeDtypeStruct((rows + STRIP, depth_cells), F32),
            edges,
            edges,
            jax.ShapeDtypeStruct((2 * STRIP, LANES), F32),
            jax.ShapeDtypeStruct((moments, channels), F32),
            jax.ShapeDtypeStruct((2, 1, channels), jnp.int32),
        ),
        in_specs=[outside] * 10,
        out_specs=(inside,) * 8,
        scratch_shapes=[VMEM((2, 1, channels), jnp.int32), pltpu.SemaphoreType.DMA((10,))],
        compiler_params=params(),
        cost_estimate=cost(5),
        name="pack",
    )(*arrays, *channel_arrays)
    depth_swap = [(0, 1), (1, 0)]
    got_depth = lax.ppermute(to_depth, "depth", depth_swap)
    swap = lambda k: [pair for i in range(k, tracks - 1, 2) for pair in ((i, i + 1), (i + 1, i))]
    got_odd = lax.ppermute(to_odd, "track", swap(1))
    got_even = lax.ppermute(to_even, "track", swap(0))

    def state_of(planes):
        return VMEM((5, planes, extent + 2 * PAD, LANES), F32)

    note = pl.pallas_call(
        note_kernel,
        out_shape=jax.ShapeDtypeStruct((tracks, 2 * STRIP + 8, LANES), F32),
        in_specs=[inside] * 4,
        out_specs=inside,
        compiler_params=params(),
        cost_estimate=cost(1),
        name="note",
    )(strip, got_depth, traces, cells)
    notes = lax.all_to_all(note, "track", split_axis=0, concat_axis=0, tiled=True)

    corner = pl.pallas_call(
        corner_kernel,
        out_shape=jax.ShapeDtypeStruct((2 * EDGE, depth_cells), F32),
        in_specs=[inside] * 2,
        out_specs=inside,
        compiler_params=params(),
        cost_estimate=cost(1),
        name="corners",
    )(got_even, got_odd)
    got_corner = lax.ppermute(corner, "depth", depth_swap)

    def media_of(planes):
        return jax.ShapeDtypeStruct((4, planes, extent, LANES), F32)

    def saved_of(planes):
        return jax.ShapeDtypeStruct((moments, 3, planes, rows, LANES), F32)

    media, saved, end = pl.pallas_call(
        forward_kernel,
        out_shape=(media_of(2), saved_of(2), jax.ShapeDtypeStruct((2, 2, rows, LANES), F32)),
        in_specs=[inside] * 3,
        out_specs=(inside,) * 3,
        scratch_shapes=[state_of(2)],
        compiler_params=params(),
        cost_estimate=cost(20),
        name="forward",
    )(held, got_even, got_odd)

    inner_media, inner_saved, end = pl.pallas_call(
        forward_inner_kernel,
        out_shape=(media_of(1), saved_of(1), jax.ShapeDtypeStruct(velocity.shape, F32)),
        in_specs=[inside] * 6,
        out_specs=(inside,) * 3,
        scratch_shapes=[state_of(1)],
        compiler_params=params(),
        cost_estimate=cost(20),
        name="forward_inner",
    )(held, got_even, got_odd, got_depth, got_corner, end)

    rest = pl.pallas_call(
        adjoint_rest_kernel,
        out_shape=jax.ShapeDtypeStruct((2, 2, rows, LANES), F32),
        in_specs=[inside] * 9,
        out_specs=inside,
        scratch_shapes=[state_of(2)],
        compiler_params=params(),
        cost_estimate=cost(20),
        name="adjoint_rest",
    )(held_adj, got_even, got_odd, got_depth, got_corner, media, saved, inner_media, inner_saved)

    mine = pl.pallas_call(
        relay_kernel,
        out_shape=jax.ShapeDtypeStruct(note.shape, F32),
        in_specs=[inside, anywhere],
        out_specs=inside,
        compiler_params=params(),
        cost_estimate=cost(1),
        name="relay",
    )(notes, rest)
    beside = lax.ppermute(mine, "depth", depth_swap)

    inject, residual = pl.pallas_call(
        lambda *refs: surface_kernel(tracks, rows, *refs),
        out_shape=(
            jax.ShapeDtypeStruct((extent, LANES), F32),
            jax.ShapeDtypeStruct((moments // 2, channels), F32),
        ),
        in_specs=[inside] * 4,
        out_specs=(inside,) * 2,
        scratch_shapes=[
            VMEM((5, BATCH, 2 * PAD + STRIP, LANES), F32),
            VMEM((4, BATCH, STRIP, LANES), F32),
            VMEM(note.shape, F32),
            VMEM(note.shape, F32),
        ],
        compiler_params=params(),
        cost_estimate=cost(2),
        name="surface",
    )(mine, beside, traces, cells)

    gradient_lambda, gradient_mu, velocity_end, residual = pl.pallas_call(
        adjoint_top_kernel,
        out_shape=(
            block,
            block,
            jax.ShapeDtypeStruct(velocity.shape, F32),
            jax.ShapeDtypeStruct((moments // 2, channels), F32),
        ),
        in_specs=[inside] * 9,
        out_specs=(inside, inside, outside, outside),
        scratch_shapes=[state_of(1), VMEM((2, 1, rows, LANES), F32), pltpu.SemaphoreType.DMA((2,))],
        compiler_params=params(),
        cost_estimate=cost(2),
        name="adjoint_top",
    )(held_adj, got_even, got_odd, media, saved, rest, inject, end, residual)
    return gradient_lambda, gradient_mu, velocity_end, residual


def solution(mesh):
    return jax.shard_map(
        per_device,
        mesh=mesh,
        in_specs=(
            P("shots", "track", "depth"),
            P("shots", "track", "depth"),
            P("shots", "track", "depth"),
            P("shots", "track", "depth"),
            P("track", "depth"),
            P("track", "depth"),
            P("track", "depth"),
            P("shots", "track"),
            P("track", None),
            P("track"),
        ),
        out_specs=(
            P(("shots", "track"), "depth"),
            P(("shots", "track"), "depth"),
            P("shots", "track", "depth"),
            P(("shots", "depth"), "track"),
        ),
        check_vma=False,
    )
```

```python
import jax
import jax.numpy as jnp
from jax import lax
from jax.experimental import pallas as pl
from jax.experimental.pallas import tpu as pltpu
from jax.sharding import PartitionSpec as P

FIBRE_ROWS = 4
NEAR = 9.0 / 8.0
RATIO = -1.0 / 27.0
HALO = 12
EDGE = 16
LANES = 128
PAD = 8
FORWARD = 8
ADJOINT = 5
FIELDS = FORWARD + ADJOINT
STRIP = 16
LAYERS = (11, 11, 12, 11, 12, 11, 9, 9, 11, 11, 12, 11, 12)
PLACES = tuple(5 + sum(LAYERS[:f]) for f in range(FIELDS))
EDGE_ROWS = 5 + sum(LAYERS) + 4
MOMENTS = 4
IMAGE = MOMENTS * FIBRE_ROWS
VMEM = pltpu.VMEM
F32 = jnp.float32
BF16 = jnp.bfloat16


def lane_ids(rows):
    return lax.broadcasted_iota(jnp.int32, (rows, LANES), 1)


def row_ids(rows, columns):
    return lax.broadcasted_iota(jnp.int32, (rows, columns), 0)


def params():
    return pltpu.CompilerParams(vmem_limit_bytes=16 * 1024 * 1024)


def cost(microseconds):
    return pl.CostEstimate(flops=int(microseconds * 1e9), bytes_accessed=1 << 20, transcendentals=0)


def turn(value, by):
    return pltpu.roll(value, by % LANES, 1)


def is_even():
    return lax.rem(lax.axis_index("track"), 2) == 0


def fetch(sources, targets, sems):
    copies = [pltpu.make_async_copy(s, t, sems.at[i]) for i, (s, t) in enumerate(zip(sources, targets))]
    for copy in copies:
        copy.start()
    return copies


def pack_kernel(*refs):
    sources, channel_arrays = refs[:7], refs[7:10]
    held, held_adj, depth_out, edge_outs, strip_out, traces_out, cells_out = *refs[10:13], refs[13:15], *refs[15:18]
    numbers, sems = refs[18:]
    velocity, stress, adj_velocity, adj_stress, buoyancy, lame, shear = sources
    fields = [velocity.at[i] for i in range(2)] + [stress.at[i] for i in range(3)] + [buoyancy, lame, shear]
    fields += [adj_velocity.at[i] for i in range(2)] + [adj_stress.at[i] for i in range(3)]
    targets = [held.at[f] for f in range(FORWARD)] + [held_adj.at[f] for f in range(ADJOINT)]
    targets += [traces_out, numbers.at[0], numbers.at[1]]
    copies = fetch((*fields, *channel_arrays), targets, sems)
    depth = lax.axis_index("depth")
    even = is_even()
    rows = held.shape[1]
    lane = lane_ids(rows)
    tail = PLACES[-1] + LAYERS[-1]
    for out in edge_outs:
        out[: PLACES[0], :] = jnp.zeros((PLACES[0], 2 * LANES), F32)
        out[tail:, :] = jnp.zeros((out.shape[0] - tail, 2 * LANES), F32)
    packed = [jnp.zeros((rows, LANES), F32) for _ in range(2)]
    strip = jnp.zeros((rows, LANES), F32)
    for f in range(FIELDS):
        copies[f].wait()
        ref = held.at[f] if f < FORWARD else held_adj.at[f - FORWARD]
        first, last = ref[:, :LANES], ref[:, LANES:]
        group, place = divmod(f, FORWARD)
        spot = EDGE * place
        here = (lane >= spot) & (lane < spot + EDGE)
        edge = jnp.where(depth == 0, last, first)
        shift = lax.rem(spot + EDGE * (1 - depth), LANES)
        packed[group] = jnp.where(here, pltpu.roll(edge, shift, 1), packed[group])
        if f < FORWARD:
            strip = jnp.where(here, turn(first, spot), strip)
        count, at = LAYERS[f], PLACES[f]
        low, high = ref[:count, :], ref[rows - count :, :]
        edge_outs[0][at : at + count, :] = jnp.where(even, high, low)
        edge_outs[1][at : at + count, :] = jnp.where(even, low, high)
    depth_out[:rows, :LANES] = packed[0]
    depth_out[:rows, LANES:] = packed[1]
    turned = strip.T
    strip_out[:, :rows] = turned[: 2 * STRIP]
    strip_out[:, rows:] = turned[2 * STRIP : 4 * STRIP]
    depth_out[rows:, :rows] = turned[4 * STRIP : 5 * STRIP]
    depth_out[rows:, rows : 2 * rows] = turned[6 * STRIP : 7 * STRIP]
    depth_out[rows:, 2 * rows : 3 * rows] = turned[5 * STRIP : 6 * STRIP]
    depth_out[rows:, 3 * rows :] = turned[7 * STRIP :]
    for copy in copies[FIELDS:]:
        copy.wait()
    cells_out[0] = numbers[0] * rows + lax.shift_right_logical(numbers[1], 2)
    cells_out[1] = numbers[1] & 3


def edge_rows(f, side, got_even, got_odd):
    at = PLACES[f]
    span = slice(at + LAYERS[f] - EDGE, at + LAYERS[f]) if side == 0 else slice(at, at + EDGE)
    use_odd = is_even() if side == 0 else ~is_even()
    return jnp.where(use_odd, got_odd[span, :], got_even[span, :])


def corner_kernel(got_even, got_odd, corner_out):
    depth = lax.axis_index("depth")
    lane = lane_ids(EDGE)
    for side in range(2):
        packed = [jnp.zeros((EDGE, LANES), F32) for _ in range(2)]
        for f in range(FIELDS):
            group, place = divmod(f, FORWARD)
            spot = EDGE * place
            value = edge_rows(f, side, got_even, got_odd)
            edge = jnp.where(depth == 0, value[:, LANES:], value[:, :LANES])
            shift = lax.rem(spot + EDGE * (1 - depth), LANES)
            here = (lane >= spot) & (lane < spot + EDGE)
            packed[group] = jnp.where(here, pltpu.roll(edge, shift, 1), packed[group])
        corner_out[EDGE * side : EDGE * (side + 1), :LANES] = packed[0]
        corner_out[EDGE * side : EDGE * (side + 1), LANES:] = packed[1]


def window(plane, f, value, halo):
    depth = lax.axis_index("depth")
    surface = depth == 0
    first, last = value[:, :LANES], value[:, LANES:]
    lane = lane_ids(first.shape[0])
    low = jnp.where(surface, lane, LANES - 1 - lane)
    if plane == 0:
        shift = jnp.where(surface, EDGE, LANES - EDGE)
        return jnp.where(low >= EDGE, pltpu.roll(jnp.where(surface, first, last), shift, 1), 0.0)
    if plane == 1:
        return jnp.where(lane < LANES // 2, turn(first, LANES // 2), turn(last, LANES // 2))
    shift = jnp.where(surface, LANES - EDGE, EDGE)
    beside = lax.rem(LANES - EDGE * (f % FORWARD) + (LANES - EDGE) * (1 - depth), LANES)
    own = pltpu.roll(jnp.where(surface, last, first), shift, 1)
    return jnp.where(low < LANES - EDGE, own, pltpu.roll(halo, beside, 1))


def field_windows(f, planes, held, got_even, got_odd, got_depth=None, corner=None):
    rows = held.shape[1]
    col = LANES * (f // FORWARD)
    blocks = (
        (0, edge_rows(f, 0, got_even, got_odd), corner, 0),
        (EDGE, held[f % FORWARD], got_depth, 0),
        (EDGE + rows, edge_rows(f, 1, got_even, got_odd), corner, EDGE),
    )
    found = [[] for _ in planes]
    for at, value, halo, start in blocks:
        if halo is not None:
            halo = halo[start : start + value.shape[0], col : col + LANES]
        for parts, p in zip(found, planes):
            parts.append((at, window(p, f, value, halo)))
    return found


def joined(outer, middle, inner):
    surface = lax.axis_index("depth") == 0
    lane = lane_ids(outer.shape[0])
    first, last = jnp.where(surface, outer, inner), jnp.where(surface, inner, outer)
    middle = turn(middle, LANES // 2)
    return jnp.where(lane < 88, turn(first, -EDGE), middle), jnp.where(lane < 40, middle, turn(last, EDGE))


def load_state(states, base, planes, held, *got):
    extent = held.shape[1] + 2 * EDGE
    for f in range(5):
        for state, parts in zip(states, field_windows(base + f, planes, held, *got)):
            state[f, :PAD, :] = jnp.zeros((PAD, LANES), F32)
            state[f, PAD + extent :, :] = jnp.zeros((PAD, LANES), F32)
            for at, part in parts:
                state[f, PAD + at : PAD + at + part.shape[0], :] = part


def velocities(states, medias, span):
    for r in range(8 * span[0], 8 * span[1], 8):
        for state, media in zip(states, medias):

            def at(f, by=0):
                return state[f, r + PAD + by : r + PAD + by + 8, :]

            xx, xz, zz = at(2), at(4), at(3)
            b = media[0, r : r + 8, :]
            near = (xx - at(2, -1)) + (xz - turn(xz, 1))
            far = (at(2, 1) - at(2, -2)) + (turn(xz, -1) - turn(xz, 2))
            state[0, r + PAD : r + PAD + 8, :] = at(0) + b * (near + RATIO * far)
            near = (at(4, 1) - xz) + (turn(zz, -1) - zz)
            far = (at(4, 2) - at(4, -1)) + (turn(zz, -2) - turn(zz, 1))
            state[1, r + PAD : r + PAD + 8, :] = at(1) + b * (near + RATIO * far)


def stresses(states, medias, span, update, keep):
    for r in range(8 * span[0], 8 * span[1], 8):
        for i, (state, media) in enumerate(zip(states, medias)):

            def at(f, by=0):
                return state[f, r + PAD + by : r + PAD + by + 8, :]

            vx, vz = at(0), at(1)
            exx = (at(0, 1) - vx) + RATIO * (at(0, 2) - at(0, -1))
            ezz = (vz - turn(vz, 1)) + RATIO * (turn(vz, -1) - turn(vz, 2))
            near = (turn(vx, -1) - vx) + (vz - at(1, -1))
            far = (turn(vx, -2) - turn(vx, 1)) + (at(1, 1) - at(1, -2))
            shear = near + RATIO * far
            keep(i, r - EDGE, exx, ezz, shear)
            if update:
                whole, lam, mu = (media[k, r : r + 8, :] for k in (1, 2, 3))
                state[2, r + PAD : r + PAD + 8, :] = at(2) + (whole * exx + lam * ezz)
                state[3, r + PAD : r + PAD + 8, :] = at(3) + (lam * exx + whole * ezz)
                state[4, r + PAD : r + PAD + 8, :] = at(4) + mu * shear


def spans(step, rows):
    tiles = (rows + 2 * EDGE) // 8
    if step == 0:
        return (0, tiles), (0, tiles)
    inner = (1, tiles - 1)
    return inner, inner if step < MOMENTS - 1 else (EDGE // 8, tiles - EDGE // 8)


def run_forward(states, medias, saveds, planes, held, *got):
    rows = held.shape[1]
    given = [field_windows(f, planes, held, *got) for f in (5, 6, 7)]
    for i, media in enumerate(medias):
        for k in range(3):
            at = given[0][i][k][0]
            b, lam, mu = (NEAR * given[m][i][k][1] for m in range(3))
            span = slice(at, at + b.shape[0])
            media[0, span, :] = b
            media[1, span, :] = lam + 2.0 * mu
            media[2, span, :] = lam
            media[3, span, :] = mu
    load_state(states, 0, planes, held, *got)
    for step in range(MOMENTS):
        fast, slow = spans(step, rows)
        velocities(states, medias, fast)

        def save(i, r, exx, ezz, shear):
            if 0 <= r < rows:
                saveds[i][step, 0, r : r + 8, :] = exx
                saveds[i][step, 1, r : r + 8, :] = ezz
                saveds[i][step, 2, r : r + 8, :] = shear

        stresses(states, medias, slow, step < MOMENTS - 1, save)


def each(ref, count, axis):
    return [ref.at[(slice(None),) * axis + (i,)] for i in range(count)]


def forward_kernel(held, got_even, got_odd, media, saved, end_out, state):
    states = each(state, 2, 1)
    run_forward(states, each(media, 2, 1), each(saved, 2, 2), (0, 1), held, got_even, got_odd)
    top, rows = PAD + EDGE, held.shape[1]
    for f in range(2):
        for i in range(2):
            end_out[f, i] = states[i][f, top : top + rows, :]


def forward_inner_kernel(held, got_even, got_odd, got_depth, corner, end, media, saved, end_out, state):
    states = each(state, 1, 1)
    run_forward(
        states, each(media, 1, 1), each(saved, 1, 2), (2,), held, got_even, got_odd, got_depth, corner
    )
    top, rows = PAD + EDGE, held.shape[1]
    for f in range(2):
        first, last = joined(end[f, 0], end[f, 1], states[0][f, top : top + rows, :])
        end_out[f, :, :LANES] = first
        end_out[f, :, LANES:] = last


def note_kernel(strip, got_depth, traces, cells, note_out, block, sems):
    first = lax.axis_index("depth") == 0
    beside = got_depth[got_depth.shape[0] - STRIP :, :]
    beside = jnp.concatenate([beside[:, :LANES], beside[:, LANES:]], axis=0)
    seen = jnp.concatenate([traces[:, :LANES], traces[:, LANES:]], axis=0)
    along, row = cells[0], cells[1]
    places = jnp.concatenate([along[:, :LANES], along[:, LANES:], row[:, :LANES], row[:, LANES:]] * 2, axis=0)
    block[: 2 * STRIP, :] = jnp.where(first, strip[...], beside)
    block[2 * STRIP :, :] = jnp.where(first, seen, places.astype(F32))
    count = note_out.shape[0]
    for copy in fetch([block] * count, [note_out.at[k] for k in range(count)], sems):
        copy.wait()


def relay_kernel(notes, rest, notes_out):
    del rest
    notes_out[...] = notes[...]


def three(value):
    high = value.astype(BF16)
    rest = value - high.astype(F32)
    middle = rest.astype(BF16)
    low = (rest - middle.astype(F32)).astype(BF16)
    return [high, middle, low]


def add_up(value, count):
    return (value[2 * count : 3 * count] + value[count : 2 * count]) + value[:count]


BATCH = 5
OWN = LANES - 2 * HALO


def fill_strip(state, media, low, high, first, tracks, columns):
    lane = lane_ids(STRIP)
    state[...] = jnp.zeros(state.shape, F32)
    for w in range(BATCH):
        begin = (first + w) * OWN - HALO
        base = (begin + columns) // columns - 1
        offset = begin - base * columns
        part = lax.div(offset + lane, columns)
        inside = (begin + lane >= 0) & (begin + lane < tracks * columns)
        values = []
        for f in range(FORWARD):
            source, q = (low, high)[f // 4], f % 4
            value = jnp.zeros((STRIP, LANES), F32)
            for step in range(3):
                who = jnp.clip(base + step, 0, tracks - 1)
                block = source[who, STRIP * (q % 2) : STRIP * (q % 2 + 1), :]
                shift = (4 * LANES - offset + columns * step - columns * (q // 2)) % LANES
                value = jnp.where(part == step, pltpu.roll(block, shift, 1), value)
            values.append(jnp.where(inside, value, 0.0))
        for f in range(5):
            state[f, w, PAD : PAD + STRIP, :] = values[f]
        buoyancy, lame, shear = (NEAR * value for value in values[5:])
        media[0, w] = buoyancy
        media[1, w] = lame + 2.0 * shear
        media[2, w] = lame
        media[3, w] = shear


def strip_steps(state, media):
    def at(f, w, r, by=0):
        return state[f, w, PAD + r + by : PAD + r + by + 8, :]

    strains = [[] for _ in range(BATCH)]
    for moment in range(MOMENTS):
        last = moment == MOMENTS - 1
        for r in (0, 8) if moment < 2 else (0,):
            for w in range(BATCH):
                here = slice(PAD + r, PAD + r + 8)
                xx, xz, zz = at(2, w, r), at(4, w, r), at(3, w, r)
                b = media[0, w, r : r + 8, :]
                near = (xx - turn(xx, 1)) + (xz - at(4, w, r, -1))
                far = (turn(xx, -1) - turn(xx, 2)) + (at(4, w, r, 1) - at(4, w, r, -2))
                state[0, w, here, :] = at(0, w, r) + b * (near + RATIO * far)
                if not last:
                    near = (turn(xz, -1) - xz) + (at(3, w, r, 1) - zz)
                    far = (turn(xz, -2) - turn(xz, 1)) + (at(3, w, r, 2) - at(3, w, r, -1))
                    state[1, w, here, :] = at(1, w, r) + b * (near + RATIO * far)
        for r in (0, 8) if moment < 1 else (0,):
            for w in range(BATCH):
                here = slice(PAD + r, PAD + r + 8)
                vx, vz = at(0, w, r), at(1, w, r)
                exx = (turn(vx, -1) - vx) + RATIO * (turn(vx, -2) - turn(vx, 1))
                if r == 0:
                    strains[w].append(NEAR * exx)
                if not last:
                    ezz = (vz - at(1, w, r, -1)) + RATIO * (at(1, w, r, 1) - at(1, w, r, -2))
                    near = (at(0, w, r, 1) - vx) + (vz - turn(vz, 1))
                    far = (at(0, w, r, 2) - at(0, w, r, -1)) + (turn(vz, -1) - turn(vz, 2))
                    whole, lam, mu = (media[k, w, r : r + 8, :] for k in (1, 2, 3))
                    state[2, w, here, :] = at(2, w, r) + (whole * exx + lam * ezz)
                    state[3, w, here, :] = at(3, w, r) + (lam * exx + whole * ezz)
                    state[4, w, here, :] = at(4, w, r) + mu * (near + RATIO * far)
    return [jnp.concatenate(parts, axis=0) for parts in strains]


def recorded_rates(state, media, low, high, wanted, tracks, columns):
    lane = lane_ids(8 * MOMENTS)
    mine = (lane >= HALO) & (lane < HALO + OWN)

    def body(number, rate):
        first = number * BATCH
        fill_strip(state, media, low, high, first, tracks, columns)
        images = [three(jnp.where(mine, image, 0.0)) for image in strip_steps(state, media)]
        parts = [jnp.concatenate([image[i] for image in images], axis=1) for i in range(3)]
        spots = [
            (first + w) * OWN - HALO + row_ids(LANES, wanted.shape[1]) for w in range(BATCH)
        ]
        hot = (jnp.concatenate(spots, axis=0) == wanted).astype(F32).astype(BF16)
        return rate + jnp.dot(jnp.concatenate(parts, axis=0), hot, preferred_element_type=F32)

    rate = jnp.zeros((3 * 8 * MOMENTS, wanted.shape[1]), F32)
    batches = -(-(-(-tracks * columns // OWN)) // BATCH)
    rate = body(0, rate) if batches == 1 else lax.fori_loop(0, batches, body, rate)
    return add_up(rate, 8 * MOMENTS)


def window_sums(low, high, start, tracks):
    group = min(8, tracks)
    row16 = row_ids(IMAGE, LANES)

    def body(number, image):
        weights, hots = [], []
        for k in range(group):
            who = number * group + k
            traces = low[who, 2 * STRIP :, :]
            places = high[who, 2 * STRIP :, :]
            for h in range(2):
                mask = (row16 & 3).astype(F32) == places[2 + h : 3 + h]
                seen = [traces[4 * h + t : 4 * h + t + 1] for t in range(MOMENTS)]
                value = jnp.where(
                    row16 < 8,
                    jnp.where(row16 < 4, seen[0], seen[1]),
                    jnp.where(row16 < 12, seen[2], seen[3]),
                )
                pieces = three(jnp.where(mask, value, 0.0)) + [mask.astype(F32).astype(BF16)]
                weights.append(jnp.concatenate(pieces, axis=0))
                spot = (start + row_ids(LANES, LANES)).astype(F32)
                hots.append((spot == places[h : h + 1]).astype(F32).astype(BF16))
        return image + lax.dot_general(
            jnp.concatenate(weights, axis=1),
            jnp.concatenate(hots, axis=1),
            (((1,), (1,)), ((), ())),
            preferred_element_type=F32,
        )

    image = jnp.zeros((4 * IMAGE, LANES), F32)
    image = body(0, image) if tracks == group else lax.fori_loop(0, tracks // group, body, image)
    return add_up(image, IMAGE), image[3 * IMAGE :]


def surface_kernel(tracks, columns, notes, beside, obs, cells, inject_out, residual_out, state, media, low, high):
    depth = lax.axis_index("depth")
    low[...] = jnp.where(depth == 0, notes[...], beside[...])
    high[...] = jnp.where(depth == 0, beside[...], notes[...])
    start = lax.axis_index("track") * columns - EDGE
    along, row = cells[0], cells[1]
    channels = along.shape[1]
    wanted = jnp.concatenate([along, start + lax.broadcasted_iota(jnp.int32, (1, LANES), 1)], axis=1)
    seen, count = window_sums(low, high, start, tracks)
    rate = recorded_rates(state, media, low, high, wanted, tracks, columns)
    mask = row_ids(8, channels) == row
    traces = [
        jnp.sum(jnp.where(mask, rate[8 * t : 8 * t + 8, :channels], 0.0), axis=0, keepdims=True)
        - obs[t : t + 1, :]
        for t in range(MOMENTS)
    ]
    residual_out[...] = jnp.where(
        depth == 0, jnp.concatenate(traces[:2], axis=0), jnp.concatenate(traces[2:], axis=0)
    )
    near = jnp.concatenate([rate[8 * t : 8 * t + 4, channels:] for t in range(MOMENTS)], axis=0)
    sources = jnp.where(depth == 0, count * near - seen, 0.0)
    turned = jnp.concatenate([sources, jnp.zeros((LANES - IMAGE, LANES), F32)], axis=0).T
    inject_out[...] = turned[: inject_out.shape[0]]


def run_adjoint(states, medias, saveds, sums, inject=None):
    rows = sums[0].shape[1]
    for total in sums:
        total[...] = jnp.zeros(total.shape, F32)
    for step in range(MOMENTS):
        fast, slow = spans(step, rows)
        moment = MOMENTS - 1 - step
        if inject is not None:
            inject(moment)
        velocities(states, medias, fast)

        def gather(i, r, exx, ezz, shear):
            if 0 <= r < rows:
                fxx, fzz, fxz = (saveds[i][moment, k, r : r + 8, :] for k in range(3))
                sums[i][0, r : r + 8, :] += (fxx + fzz) * (exx + ezz)
                sums[i][1, r : r + 8, :] += 2.0 * (fxx * exx + fzz * ezz) + fxz * shear

        stresses(states, medias, slow, step < MOMENTS - 1, gather)


def adjoint_rest_kernel(
    held, got_even, got_odd, got_depth, corner, media, saved, inner_media, inner_saved, sums, state
):
    states = each(state, 2, 1)
    load_state(states, FORWARD, (1, 2), held, got_even, got_odd, got_depth, corner)
    medias = [media.at[:, 1], inner_media.at[:, 0]]
    saveds = [saved.at[:, :, 1], inner_saved.at[:, :, 0]]
    run_adjoint(states, medias, saveds, each(sums, 2, 1))


def adjoint_top_kernel(
    held, got_even, got_odd, media, saved, rest, inject, end, residual,
    lambda_out, mu_out, end_out, residual_out, state, sums, sems,
):
    copies = fetch((end, residual), (end_out, residual_out), sems)
    rows = held.shape[1]
    extent = rows + 2 * EDGE
    states = each(state, 1, 1)
    load_state(states, FORWARD, (0,), held, got_even, got_odd)
    lane = lane_ids(extent)
    here = (lane >= EDGE) & (lane < EDGE + FIBRE_ROWS)

    def add(moment):
        added = jnp.where(here, turn(inject[...], EDGE - FIBRE_ROWS * moment), 0.0)
        states[0][2, PAD : PAD + extent, :] += added

    run_adjoint(states, [media.at[:, 0]], [saved.at[:, :, 0]], each(sums, 1, 1), add)
    for k, out in enumerate((lambda_out, mu_out)):
        first, last = joined(sums[k, 0], rest[k, 0], rest[k, 1])
        out[:, :LANES] = (NEAR * NEAR) * first
        out[:, LANES:] = (NEAR * NEAR) * last
    for copy in copies:
        copy.wait()


def per_device(
    velocity,
    stress,
    adjoint_velocity,
    adjoint_stress,
    buoyancy,
    lame_lambda,
    shear_modulus,
    observed,
    owner_track,
    fibre_cell,
):
    tracks = lax.axis_size("track")
    rows, depth_cells = buoyancy.shape
    moments, channels = observed.shape
    owner = owner_track.reshape(1, channels)
    cell = fibre_cell.reshape(1, channels)
    pinned = lambda array: pltpu.with_memory_space_constraint(array, pltpu.HBM)
    arrays = (velocity, stress, adjoint_velocity, adjoint_stress, buoyancy, lame_lambda, shear_modulus)
    arrays = tuple(pinned(array) for array in arrays)
    channel_arrays = (pinned(observed), pinned(owner), pinned(cell))
    extent = rows + 2 * EDGE
    block = jax.ShapeDtypeStruct((rows, depth_cells), F32)
    edges = jax.ShapeDtypeStruct((EDGE_ROWS, depth_cells), F32)
    inside = pl.BlockSpec(memory_space=VMEM)
    outside = pl.BlockSpec(memory_space=pltpu.HBM)
    anywhere = pl.BlockSpec(memory_space=pl.ANY)
    held, held_adj, to_depth, to_even, to_odd, strip, traces, cells = pl.pallas_call(
        pack_kernel,
        out_shape=(
            jax.ShapeDtypeStruct((FORWARD, rows, depth_cells), F32),
            jax.ShapeDtypeStruct((ADJOINT, rows, depth_cells), F32),
            jax.ShapeDtypeStruct((rows + STRIP, depth_cells), F32),
            edges,
            edges,
            jax.ShapeDtypeStruct((2 * STRIP, LANES), F32),
            jax.ShapeDtypeStruct((moments, channels), F32),
            jax.ShapeDtypeStruct((2, 1, channels), jnp.int32),
        ),
        in_specs=[outside] * 10,
        out_specs=(inside,) * 8,
        scratch_shapes=[VMEM((2, 1, channels), jnp.int32), pltpu.SemaphoreType.DMA((FIELDS + 3,))],
        compiler_params=params(),
        cost_estimate=cost(5),
        name="pack",
    )(*arrays, *channel_arrays)
    depth_swap = [(0, 1), (1, 0)]
    got_depth = lax.ppermute(to_depth, "depth", depth_swap)
    swap = lambda k: [pair for i in range(k, tracks - 1, 2) for pair in ((i, i + 1), (i + 1, i))]
    got_odd = lax.ppermute(to_odd, "track", swap(1))
    got_even = lax.ppermute(to_even, "track", swap(0))

    def state_of(planes):
        return VMEM((5, planes, extent + 2 * PAD, LANES), F32)

    note = pl.pallas_call(
        note_kernel,
        out_shape=jax.ShapeDtypeStruct((tracks, 2 * STRIP + 8, LANES), F32),
        in_specs=[inside] * 4,
        out_specs=outside,
        scratch_shapes=[VMEM((2 * STRIP + 8, LANES), F32), pltpu.SemaphoreType.DMA((tracks,))],
        compiler_params=params(),
        cost_estimate=cost(1),
        name="note",
    )(strip, got_depth, traces, cells)
    notes = lax.all_to_all(note, "track", split_axis=0, concat_axis=0, tiled=True)

    corner = pl.pallas_call(
        corner_kernel,
        out_shape=jax.ShapeDtypeStruct((2 * EDGE, depth_cells), F32),
        in_specs=[inside] * 2,
        out_specs=inside,
        compiler_params=params(),
        cost_estimate=cost(1),
        name="corners",
    )(got_even, got_odd)
    got_corner = lax.ppermute(corner, "depth", depth_swap)

    def media_of(planes):
        return jax.ShapeDtypeStruct((4, planes, extent, LANES), F32)

    def saved_of(planes):
        return jax.ShapeDtypeStruct((moments, 3, planes, rows, LANES), F32)

    media, saved, end = pl.pallas_call(
        forward_kernel,
        out_shape=(media_of(2), saved_of(2), jax.ShapeDtypeStruct((2, 2, rows, LANES), F32)),
        in_specs=[inside] * 3,
        out_specs=(inside,) * 3,
        scratch_shapes=[state_of(2)],
        compiler_params=params(),
        cost_estimate=cost(20),
        name="forward",
    )(held, got_even, got_odd)

    inner_media, inner_saved, end = pl.pallas_call(
        forward_inner_kernel,
        out_shape=(media_of(1), saved_of(1), jax.ShapeDtypeStruct(velocity.shape, F32)),
        in_specs=[inside] * 6,
        out_specs=(inside,) * 3,
        scratch_shapes=[state_of(1)],
        compiler_params=params(),
        cost_estimate=cost(20),
        name="forward_inner",
    )(held, got_even, got_odd, got_depth, got_corner, end)

    rest = pl.pallas_call(
        adjoint_rest_kernel,
        out_shape=jax.ShapeDtypeStruct((2, 2, rows, LANES), F32),
        in_specs=[inside] * 9,
        out_specs=inside,
        scratch_shapes=[state_of(2)],
        compiler_params=params(),
        cost_estimate=cost(20),
        name="adjoint_rest",
    )(held_adj, got_even, got_odd, got_depth, got_corner, media, saved, inner_media, inner_saved)

    mine = pl.pallas_call(
        relay_kernel,
        out_shape=jax.ShapeDtypeStruct(note.shape, F32),
        in_specs=[inside, anywhere],
        out_specs=inside,
        compiler_params=params(),
        cost_estimate=cost(1),
        name="relay",
    )(notes, rest)
    beside = lax.ppermute(mine, "depth", depth_swap)

    inject, residual = pl.pallas_call(
        lambda *refs: surface_kernel(tracks, rows, *refs),
        out_shape=(
            jax.ShapeDtypeStruct((extent, LANES), F32),
            jax.ShapeDtypeStruct((moments // 2, channels), F32),
        ),
        in_specs=[inside] * 4,
        out_specs=(inside,) * 2,
        scratch_shapes=[
            VMEM((5, BATCH, 2 * PAD + STRIP, LANES), F32),
            VMEM((4, BATCH, STRIP, LANES), F32),
            VMEM(note.shape, F32),
            VMEM(note.shape, F32),
        ],
        compiler_params=params(),
        cost_estimate=cost(2),
        name="surface",
    )(mine, beside, traces, cells)

    gradient_lambda, gradient_mu, velocity_end, residual = pl.pallas_call(
        adjoint_top_kernel,
        out_shape=(
            block,
            block,
            jax.ShapeDtypeStruct(velocity.shape, F32),
            jax.ShapeDtypeStruct((moments // 2, channels), F32),
        ),
        in_specs=[inside] * 9,
        out_specs=(inside, inside, outside, outside),
        scratch_shapes=[state_of(1), VMEM((2, 1, rows, LANES), F32), pltpu.SemaphoreType.DMA((2,))],
        compiler_params=params(),
        cost_estimate=cost(2),
        name="adjoint_top",
    )(held_adj, got_even, got_odd, media, saved, rest, inject, end, residual)
    return gradient_lambda, gradient_mu, velocity_end, residual


def solution(mesh):
    return jax.shard_map(
        per_device,
        mesh=mesh,
        in_specs=(
            P("shots", "track", "depth"),
            P("shots", "track", "depth"),
            P("shots", "track", "depth"),
            P("shots", "track", "depth"),
            P("track", "depth"),
            P("track", "depth"),
            P("track", "depth"),
            P("shots", "track"),
            P("track", None),
            P("track"),
        ),
        out_specs=(
            P(("shots", "track"), "depth"),
            P(("shots", "track"), "depth"),
            P("shots", "track", "depth"),
            P(("shots", "depth"), "track"),
        ),
        check_vma=False,
    )
```

```python
import jax
import jax.numpy as jnp
from jax import lax
from jax.experimental import pallas as pl
from jax.experimental.pallas import tpu as pltpu
from jax.sharding import PartitionSpec as P

FIBRE_ROWS = 4
NEAR = 9.0 / 8.0
RATIO = -1.0 / 27.0
HALO = 12
EDGE = 16
LANES = 128
PAD = 8
FORWARD = 8
ADJOINT = 5
FIELDS = FORWARD + ADJOINT
STRIP = 16
BASE = EDGE - HALO
MOMENTS = 4
IMAGE = MOMENTS * FIBRE_ROWS
VMEM = pltpu.VMEM
F32 = jnp.float32
BF16 = jnp.bfloat16


def lane_ids(rows):
    return lax.broadcasted_iota(jnp.int32, (rows, LANES), 1)


def row_ids(rows, columns):
    return lax.broadcasted_iota(jnp.int32, (rows, columns), 0)


def params():
    return pltpu.CompilerParams(vmem_limit_bytes=16 * 1024 * 1024)


def cost(microseconds):
    return pl.CostEstimate(flops=int(microseconds * 1e9), bytes_accessed=1 << 20, transcendentals=0)


def turn(value, by):
    return pltpu.roll(value, by % LANES, 1)


def is_even():
    return lax.rem(lax.axis_index("track"), 2) == 0


def fetch(sources, targets, sems):
    copies = [pltpu.make_async_copy(s, t, sems.at[i]) for i, (s, t) in enumerate(zip(sources, targets))]
    for copy in copies:
        copy.start()
    return copies


def pack_kernel(*refs):
    sources, channel_arrays = refs[:7], refs[7:10]
    held, held_adj, depth_out, edge_outs, strip_out, traces_out, cells_out = *refs[10:13], refs[13:15], *refs[15:18]
    numbers, sems = refs[18:]
    targets = (
        held.at[pl.ds(0, 2)],
        held.at[pl.ds(2, 3)],
        held.at[5],
        held.at[6],
        held.at[7],
        held_adj.at[pl.ds(0, 2)],
        held_adj.at[pl.ds(2, 3)],
        traces_out,
        numbers.at[0],
        numbers.at[1],
    )
    copies = fetch((*sources[:2], *sources[4:], *sources[2:4], *channel_arrays), targets, sems)
    arriving = {0: copies[0], 2: copies[1], 5: copies[2], 6: copies[3], 7: copies[4], 8: copies[5], 10: copies[6]}
    depth = lax.axis_index("depth")
    even = is_even()
    rows = held.shape[1]
    lane = lane_ids(rows)
    tail = BASE + HALO * FIELDS
    for out in edge_outs:
        out[:BASE, :] = jnp.zeros((BASE, 2 * LANES), F32)
        out[tail:, :] = jnp.zeros((out.shape[0] - tail, 2 * LANES), F32)
    packed = [jnp.zeros((rows, LANES), F32) for _ in range(2)]
    strip = jnp.zeros((rows, LANES), F32)
    for f in range(FIELDS):
        if f in arriving:
            arriving[f].wait()
        ref = held.at[f] if f < FORWARD else held_adj.at[f - FORWARD]
        first, last = ref[:, :LANES], ref[:, LANES:]
        group, place = divmod(f, FORWARD)
        spot = EDGE * place
        here = (lane >= spot) & (lane < spot + EDGE)
        edge = jnp.where(depth == 0, last, first)
        shift = lax.rem(spot + EDGE * (1 - depth), LANES)
        packed[group] = jnp.where(here, pltpu.roll(edge, shift, 1), packed[group])
        if f < FORWARD:
            strip = jnp.where(here, turn(first, spot), strip)
        low, high = ref[:HALO, :], ref[rows - HALO :, :]
        at = BASE + HALO * f
        edge_outs[0][at : at + HALO, :] = jnp.where(even, high, low)
        edge_outs[1][at : at + HALO, :] = jnp.where(even, low, high)
    depth_out[:rows, :LANES] = packed[0]
    depth_out[:rows, LANES:] = packed[1]
    turned = strip.T
    strip_out[:, :rows] = turned[: 2 * STRIP]
    strip_out[:, rows:] = turned[2 * STRIP : 4 * STRIP]
    depth_out[rows:, :rows] = turned[4 * STRIP : 5 * STRIP]
    depth_out[rows:, rows : 2 * rows] = turned[6 * STRIP : 7 * STRIP]
    depth_out[rows:, 2 * rows : 3 * rows] = turned[5 * STRIP : 6 * STRIP]
    depth_out[rows:, 3 * rows :] = turned[7 * STRIP :]
    for copy in copies[7:]:
        copy.wait()
    cells_out[0] = numbers[0] * rows + lax.shift_right_logical(numbers[1], 2)
    cells_out[1] = numbers[1] & 3


def edge_rows(f, side, got_even, got_odd):
    at = BASE + HALO * f
    span = slice(at - BASE, at + HALO) if side == 0 else slice(at, at + EDGE)
    use_odd = is_even() if side == 0 else ~is_even()
    return jnp.where(use_odd, got_odd[span, :], got_even[span, :])


def corner_kernel(got_even, got_odd, corner_out):
    depth = lax.axis_index("depth")
    lane = lane_ids(EDGE)
    for side in range(2):
        packed = [jnp.zeros((EDGE, LANES), F32) for _ in range(2)]
        for f in range(FIELDS):
            group, place = divmod(f, FORWARD)
            spot = EDGE * place
            value = edge_rows(f, side, got_even, got_odd)
            edge = jnp.where(depth == 0, value[:, LANES:], value[:, :LANES])
            shift = lax.rem(spot + EDGE * (1 - depth), LANES)
            here = (lane >= spot) & (lane < spot + EDGE)
            packed[group] = jnp.where(here, pltpu.roll(edge, shift, 1), packed[group])
        corner_out[EDGE * side : EDGE * (side + 1), :LANES] = packed[0]
        corner_out[EDGE * side : EDGE * (side + 1), LANES:] = packed[1]


def window(plane, f, value, halo):
    depth = lax.axis_index("depth")
    surface = depth == 0
    first, last = value[:, :LANES], value[:, LANES:]
    lane = lane_ids(first.shape[0])
    low = jnp.where(surface, lane, LANES - 1 - lane)
    if plane == 0:
        shift = jnp.where(surface, EDGE, LANES - EDGE)
        return jnp.where(low >= EDGE, pltpu.roll(jnp.where(surface, first, last), shift, 1), 0.0)
    if plane == 1:
        return jnp.where(lane < LANES // 2, turn(first, LANES // 2), turn(last, LANES // 2))
    shift = jnp.where(surface, LANES - EDGE, EDGE)
    beside = lax.rem(LANES - EDGE * (f % FORWARD) + (LANES - EDGE) * (1 - depth), LANES)
    own = pltpu.roll(jnp.where(surface, last, first), shift, 1)
    return jnp.where(low < LANES - EDGE, own, pltpu.roll(halo, beside, 1))


def field_windows(f, planes, held, got_even, got_odd, got_depth=None, corner=None):
    rows = held.shape[1]
    col = LANES * (f // FORWARD)
    blocks = (
        (0, edge_rows(f, 0, got_even, got_odd), corner, 0),
        (EDGE, held[f % FORWARD], got_depth, 0),
        (EDGE + rows, edge_rows(f, 1, got_even, got_odd), corner, EDGE),
    )
    found = [[] for _ in planes]
    for at, value, halo, start in blocks:
        if halo is not None:
            halo = halo[start : start + value.shape[0], col : col + LANES]
        for parts, p in zip(found, planes):
            parts.append((at, window(p, f, value, halo)))
    return found


def joined(outer, middle, inner):
    surface = lax.axis_index("depth") == 0
    lane = lane_ids(outer.shape[0])
    first, last = jnp.where(surface, outer, inner), jnp.where(surface, inner, outer)
    middle = turn(middle, LANES // 2)
    return jnp.where(lane < 88, turn(first, -EDGE), middle), jnp.where(lane < 40, middle, turn(last, EDGE))


def load_state(states, base, planes, held, *got):
    extent = held.shape[1] + 2 * EDGE
    for f in range(5):
        for state, parts in zip(states, field_windows(base + f, planes, held, *got)):
            state[f, :PAD, :] = jnp.zeros((PAD, LANES), F32)
            state[f, PAD + extent :, :] = jnp.zeros((PAD, LANES), F32)
            for at, part in parts:
                state[f, PAD + at : PAD + at + part.shape[0], :] = part


def velocities(states, medias, span):
    for r in range(8 * span[0], 8 * span[1], 8):
        for state, media in zip(states, medias):

            def at(f, by=0):
                return state[f, r + PAD + by : r + PAD + by + 8, :]

            xx, xz, zz = at(2), at(4), at(3)
            b = media[0, r : r + 8, :]
            near = (xx - at(2, -1)) + (xz - turn(xz, 1))
            far = (at(2, 1) - at(2, -2)) + (turn(xz, -1) - turn(xz, 2))
            state[0, r + PAD : r + PAD + 8, :] = at(0) + b * (near + RATIO * far)
            near = (at(4, 1) - xz) + (turn(zz, -1) - zz)
            far = (at(4, 2) - at(4, -1)) + (turn(zz, -2) - turn(zz, 1))
            state[1, r + PAD : r + PAD + 8, :] = at(1) + b * (near + RATIO * far)


def stresses(states, medias, span, update, keep):
    for r in range(8 * span[0], 8 * span[1], 8):
        for i, (state, media) in enumerate(zip(states, medias)):

            def at(f, by=0):
                return state[f, r + PAD + by : r + PAD + by + 8, :]

            vx, vz = at(0), at(1)
            exx = (at(0, 1) - vx) + RATIO * (at(0, 2) - at(0, -1))
            ezz = (vz - turn(vz, 1)) + RATIO * (turn(vz, -1) - turn(vz, 2))
            near = (turn(vx, -1) - vx) + (vz - at(1, -1))
            far = (turn(vx, -2) - turn(vx, 1)) + (at(1, 1) - at(1, -2))
            shear = near + RATIO * far
            keep(i, r - EDGE, exx, ezz, shear)
            if update:
                whole, lam, mu = (media[k, r : r + 8, :] for k in (1, 2, 3))
                state[2, r + PAD : r + PAD + 8, :] = at(2) + (whole * exx + lam * ezz)
                state[3, r + PAD : r + PAD + 8, :] = at(3) + (lam * exx + whole * ezz)
                state[4, r + PAD : r + PAD + 8, :] = at(4) + mu * shear


def spans(step, rows):
    tiles = (rows + 2 * EDGE) // 8
    if step == 0:
        return (0, tiles), (0, tiles)
    inner = (1, tiles - 1)
    return inner, inner if step < MOMENTS - 1 else (EDGE // 8, tiles - EDGE // 8)


def run_forward(states, medias, saveds, planes, held, *got):
    rows = held.shape[1]
    given = [field_windows(f, planes, held, *got) for f in (5, 6, 7)]
    for i, media in enumerate(medias):
        for k in range(3):
            at = given[0][i][k][0]
            b, lam, mu = (NEAR * given[m][i][k][1] for m in range(3))
            span = slice(at, at + b.shape[0])
            media[0, span, :] = b
            media[1, span, :] = lam + 2.0 * mu
            media[2, span, :] = lam
            media[3, span, :] = mu
    load_state(states, 0, planes, held, *got)
    for step in range(MOMENTS):
        fast, slow = spans(step, rows)
        velocities(states, medias, fast)

        def save(i, r, exx, ezz, shear):
            if 0 <= r < rows:
                saveds[i][step, 0, r : r + 8, :] = exx
                saveds[i][step, 1, r : r + 8, :] = ezz
                saveds[i][step, 2, r : r + 8, :] = shear

        stresses(states, medias, slow, step < MOMENTS - 1, save)


def each(ref, count, axis):
    return [ref.at[(slice(None),) * axis + (i,)] for i in range(count)]


def forward_kernel(held, got_even, got_odd, media, saved, end_out, state):
    states = each(state, 2, 1)
    run_forward(states, each(media, 2, 1), each(saved, 2, 2), (0, 1), held, got_even, got_odd)
    top, rows = PAD + EDGE, held.shape[1]
    for f in range(2):
        for i in range(2):
            end_out[f, i] = states[i][f, top : top + rows, :]


def forward_inner_kernel(held, got_even, got_odd, got_depth, corner, end, media, saved, end_out, state):
    states = each(state, 1, 1)
    run_forward(
        states, each(media, 1, 1), each(saved, 1, 2), (2,), held, got_even, got_odd, got_depth, corner
    )
    top, rows = PAD + EDGE, held.shape[1]
    for f in range(2):
        first, last = joined(end[f, 0], end[f, 1], states[0][f, top : top + rows, :])
        end_out[f, :, :LANES] = first
        end_out[f, :, LANES:] = last


def note_kernel(strip, got_depth, traces, cells, note_out):
    first = lax.axis_index("depth") == 0
    beside = got_depth[got_depth.shape[0] - STRIP :, :]
    beside = jnp.concatenate([beside[:, :LANES], beside[:, LANES:]], axis=0)
    seen = jnp.concatenate([traces[:, :LANES], traces[:, LANES:]], axis=0)
    along, row = cells[0], cells[1]
    places = jnp.concatenate([along[:, :LANES], along[:, LANES:], row[:, :LANES], row[:, LANES:]] * 2, axis=0)
    block = jnp.concatenate(
        [jnp.where(first, strip[...], beside), jnp.where(first, seen, places.astype(F32))], axis=0
    )
    for k in range(note_out.shape[0]):
        note_out[k] = block


def relay_kernel(notes, rest, notes_out):
    del rest
    notes_out[...] = notes[...]


def three(value):
    high = value.astype(BF16)
    rest = value - high.astype(F32)
    middle = rest.astype(BF16)
    low = (rest - middle.astype(F32)).astype(BF16)
    return [high, middle, low]


def add_up(value, count):
    return (value[2 * count : 3 * count] + value[count : 2 * count]) + value[:count]


BATCH = 5
OWN = LANES - 2 * HALO


def strip_window(f, low, high, base, offset, tracks, columns):
    lane = lane_ids(STRIP)
    part = lax.div(offset + lane, columns)
    spot = base * columns + offset + lane
    source, q = (low, high)[f // 4], f % 4
    value = jnp.zeros((STRIP, LANES), F32)
    for step in range(3):
        who = jnp.clip(base + step, 0, tracks - 1)
        block = source[who, STRIP * (q % 2) : STRIP * (q % 2 + 1), :]
        shift = (4 * LANES - offset + columns * step - columns * (q // 2)) % LANES
        value = jnp.where(part == step, pltpu.roll(block, shift, 1), value)
    return jnp.where((spot >= 0) & (spot < tracks * columns), value, 0.0)


def fill_strip(state, media, low, high, first, tracks, columns):
    state[...] = jnp.zeros(state.shape, F32)
    for w in range(BATCH):
        begin = (first + w) * OWN - HALO
        base = (begin + columns) // columns - 1
        offset = begin - base * columns
        values = [strip_window(f, low, high, base, offset, tracks, columns) for f in range(FORWARD)]
        for f in range(5):
            state[f, w, PAD : PAD + STRIP, :] = values[f]
        buoyancy, lame, shear = (NEAR * value for value in values[5:])
        media[0, w] = buoyancy
        media[1, w] = lame + 2.0 * shear
        media[2, w] = lame
        media[3, w] = shear


def strip_steps(state, media):
    def at(f, w, r, by=0):
        return state[f, w, PAD + r + by : PAD + r + by + 8, :]

    strains = [[] for _ in range(BATCH)]
    for moment in range(MOMENTS):
        last = moment == MOMENTS - 1
        for r in (0, 8) if moment < 2 else (0,):
            for w in range(BATCH):
                here = slice(PAD + r, PAD + r + 8)
                xx, xz, zz = at(2, w, r), at(4, w, r), at(3, w, r)
                b = media[0, w, r : r + 8, :]
                near = (xx - turn(xx, 1)) + (xz - at(4, w, r, -1))
                far = (turn(xx, -1) - turn(xx, 2)) + (at(4, w, r, 1) - at(4, w, r, -2))
                state[0, w, here, :] = at(0, w, r) + b * (near + RATIO * far)
                if not last:
                    near = (turn(xz, -1) - xz) + (at(3, w, r, 1) - zz)
                    far = (turn(xz, -2) - turn(xz, 1)) + (at(3, w, r, 2) - at(3, w, r, -1))
                    state[1, w, here, :] = at(1, w, r) + b * (near + RATIO * far)
        for r in (0, 8) if moment < 1 else (0,):
            for w in range(BATCH):
                here = slice(PAD + r, PAD + r + 8)
                vx, vz = at(0, w, r), at(1, w, r)
                exx = (turn(vx, -1) - vx) + RATIO * (turn(vx, -2) - turn(vx, 1))
                if r == 0:
                    strains[w].append(NEAR * exx)
                if not last:
                    ezz = (vz - at(1, w, r, -1)) + RATIO * (at(1, w, r, 1) - at(1, w, r, -2))
                    near = (at(0, w, r, 1) - vx) + (vz - turn(vz, 1))
                    far = (at(0, w, r, 2) - at(0, w, r, -1)) + (turn(vz, -1) - turn(vz, 2))
                    whole, lam, mu = (media[k, w, r : r + 8, :] for k in (1, 2, 3))
                    state[2, w, here, :] = at(2, w, r) + (whole * exx + lam * ezz)
                    state[3, w, here, :] = at(3, w, r) + (lam * exx + whole * ezz)
                    state[4, w, here, :] = at(4, w, r) + mu * (near + RATIO * far)
    return [jnp.concatenate(parts, axis=0) for parts in strains]


def recorded_rates(state, media, low, high, wanted, tracks, columns):
    lane = lane_ids(8 * MOMENTS)
    mine = (lane >= HALO) & (lane < HALO + OWN)

    def body(number, rate):
        first = number * BATCH
        fill_strip(state, media, low, high, first, tracks, columns)
        images = [three(jnp.where(mine, image, 0.0)) for image in strip_steps(state, media)]
        parts = [jnp.concatenate([image[i] for image in images], axis=1) for i in range(3)]
        spots = [
            (first + w) * OWN - HALO + row_ids(LANES, wanted.shape[1]) for w in range(BATCH)
        ]
        hot = (jnp.concatenate(spots, axis=0) == wanted).astype(F32).astype(BF16)
        return rate + jnp.dot(jnp.concatenate(parts, axis=0), hot, preferred_element_type=F32)

    rate = jnp.zeros((3 * 8 * MOMENTS, wanted.shape[1]), F32)
    batches = -(-(-(-tracks * columns // OWN)) // BATCH)
    rate = body(0, rate) if batches == 1 else lax.fori_loop(0, batches, body, rate)
    return add_up(rate, 8 * MOMENTS)


def window_sums(low, high, start, tracks):
    group = min(8, tracks)
    row16 = row_ids(IMAGE, LANES)

    def body(number, image):
        weights, hots = [], []
        for k in range(group):
            who = number * group + k
            traces = low[who, 2 * STRIP :, :]
            places = high[who, 2 * STRIP :, :]
            for h in range(2):
                mask = (row16 & 3).astype(F32) == places[2 + h : 3 + h]
                seen = [traces[4 * h + t : 4 * h + t + 1] for t in range(MOMENTS)]
                value = jnp.where(
                    row16 < 8,
                    jnp.where(row16 < 4, seen[0], seen[1]),
                    jnp.where(row16 < 12, seen[2], seen[3]),
                )
                pieces = three(jnp.where(mask, value, 0.0)) + [mask.astype(F32).astype(BF16)]
                weights.append(jnp.concatenate(pieces, axis=0))
                spot = (start + row_ids(LANES, LANES)).astype(F32)
                hots.append((spot == places[h : h + 1]).astype(F32).astype(BF16))
        return image + lax.dot_general(
            jnp.concatenate(weights, axis=1),
            jnp.concatenate(hots, axis=1),
            (((1,), (1,)), ((), ())),
            preferred_element_type=F32,
        )

    image = jnp.zeros((4 * IMAGE, LANES), F32)
    image = body(0, image) if tracks == group else lax.fori_loop(0, tracks // group, body, image)
    return add_up(image, IMAGE), image[3 * IMAGE :]


def response(state, media, sources, strains):
    state[...] = jnp.zeros(state.shape, F32)
    tiles = (0, 8)
    sums = [[jnp.zeros((8, LANES), F32) for _ in tiles] for _ in range(2)]

    def at(f, r, by=0):
        return state[f, PAD + r + by : PAD + r + by + 8, :]

    def put(f, r, value):
        state[f, PAD + r : PAD + r + 8, :] = value

    for moment in reversed(range(MOMENTS)):
        put(2, 0, at(2, 0) + sources[moment])
        for r in tiles:
            xx, xz, zz = at(2, r), at(4, r), at(3, r)
            b = media[0, r : r + 8, :]
            near = (xx - turn(xx, 1)) + (xz - at(4, r, -1))
            far = (turn(xx, -1) - turn(xx, 2)) + (at(4, r, 1) - at(4, r, -2))
            put(0, r, at(0, r) + b * (near + RATIO * far))
            near = (turn(xz, -1) - xz) + (at(3, r, 1) - zz)
            far = (turn(xz, -2) - turn(xz, 1)) + (at(3, r, 2) - at(3, r, -1))
            put(1, r, at(1, r) + b * (near + RATIO * far))
        for i, r in enumerate(tiles):
            vx, vz = at(0, r), at(1, r)
            exx = (turn(vx, -1) - vx) + RATIO * (turn(vx, -2) - turn(vx, 1))
            ezz = (vz - at(1, r, -1)) + RATIO * (at(1, r, 1) - at(1, r, -2))
            near = (at(0, r, 1) - vx) + (vz - turn(vz, 1))
            far = (at(0, r, 2) - at(0, r, -1)) + (turn(vz, -1) - turn(vz, 2))
            shear = near + RATIO * far
            fxx, fzz, fxz = (
                strains[j // 8, STRIP * (j % 8) + r : STRIP * (j % 8) + r + 8, :]
                for j in range(3 * moment, 3 * moment + 3)
            )
            sums[0][i] += (fxx + fzz) * (exx + ezz)
            sums[1][i] += 2.0 * (fxx * exx + fzz * ezz) + fxz * shear
            if moment > 0:
                whole, lam, mu = (media[k, r : r + 8, :] for k in (1, 2, 3))
                put(2, r, at(2, r) + (whole * exx + lam * ezz))
                put(3, r, at(3, r) + (lam * exx + whole * ezz))
                put(4, r, at(4, r) + mu * shear)
    return sums[0] + sums[1]


def finish_kernel(
    tracks, columns, notes, beside, obs, cells, base, strains, end,
    lambda_out, mu_out, residual_out, end_out, state, media, low, high, sems,
):
    copy = pltpu.make_async_copy(end, end_out, sems.at[0])
    copy.start()
    depth = lax.axis_index("depth")
    low[...] = jnp.where(depth == 0, notes[...], beside[...])
    high[...] = jnp.where(depth == 0, beside[...], notes[...])
    track = lax.axis_index("track")
    start = track * columns - EDGE
    along, row = cells[0], cells[1]
    channels = along.shape[1]
    wanted = jnp.concatenate([along, start + lax.broadcasted_iota(jnp.int32, (1, LANES), 1)], axis=1)
    seen, count = window_sums(low, high, start, tracks)
    rate = recorded_rates(state, media, low, high, wanted, tracks, columns)
    mask = row_ids(8, channels) == row
    traces = [
        jnp.sum(jnp.where(mask, rate[8 * t : 8 * t + 8, :channels], 0.0), axis=0, keepdims=True)
        - obs[t : t + 1, :]
        for t in range(MOMENTS)
    ]
    residual_out[...] = jnp.where(
        depth == 0, jnp.concatenate(traces[:2], axis=0), jnp.concatenate(traces[2:], axis=0)
    )
    near = jnp.concatenate([rate[8 * t : 8 * t + 4, channels:] for t in range(MOMENTS)], axis=0)
    found = jnp.where(depth == 0, count * near - seen, 0.0)
    nothing = jnp.zeros((8 - FIBRE_ROWS, LANES), F32)
    sources = [
        jnp.concatenate([found[FIBRE_ROWS * t : FIBRE_ROWS * (t + 1)], nothing], axis=0) for t in range(MOMENTS)
    ]
    own = [
        NEAR * strip_window(f, low, high, track - 1, columns - EDGE, tracks, columns) for f in (5, 6, 7)
    ]
    media[0, 0] = own[0]
    media[1, 0] = own[1] + 2.0 * own[2]
    media[2, 0] = own[1]
    media[3, 0] = own[2]
    added = response(state.at[:, 0], media.at[:, 0], sources, strains)
    rows = base.shape[1]
    added = jnp.concatenate(added + [jnp.zeros((LANES - 32, LANES), F32)], axis=0).T[EDGE : EDGE + rows]
    lane = lane_ids(rows)
    for k, out in enumerate((lambda_out, mu_out)):
        more = jnp.where(lane < STRIP, turn(added, -STRIP * k), 0.0)
        out[:, :LANES] = (NEAR * NEAR) * (base[k, :, :LANES] + more)
        out[:, LANES:] = (NEAR * NEAR) * base[k, :, LANES:]
    copy.wait()


def adjoint_kernel(
    held, got_even, got_odd, got_depth, corner, media, saved, inner_media, inner_saved,
    base_out, strains_out, state, sums,
):
    states, totals = each(state, 3, 1), each(sums, 3, 1)
    rows = held.shape[1]
    load_state(states, FORWARD, (0, 1, 2), held, got_even, got_odd, got_depth, corner)
    medias = each(media, 2, 1) + each(inner_media, 1, 1)
    saveds = each(saved, 2, 2) + each(inner_saved, 1, 2)
    sums[...] = jnp.zeros(sums.shape, F32)
    for step in range(MOMENTS):
        fast, slow = spans(step, rows)
        moment = MOMENTS - 1 - step
        velocities(states, medias, fast)

        def gather(i, r, exx, ezz, shear):
            if 0 <= r < rows:
                fxx, fzz, fxz = (saveds[i][moment, k, r : r + 8, :] for k in range(3))
                totals[i][0, r : r + 8, :] += (fxx + fzz) * (exx + ezz)
                totals[i][1, r : r + 8, :] += 2.0 * (fxx * exx + fzz * ezz) + fxz * shear

        stresses(states, medias, slow, step < MOMENTS - 1, gather)
    for k in range(2):
        first, last = joined(*(total[k] for total in totals))
        base_out[k, :, :LANES] = first
        base_out[k, :, LANES:] = last
    lane = lane_ids(rows)
    for group in range(2):
        packed = jnp.zeros((rows, LANES), F32)
        for j in range(8 * group, min(8 * group + 8, 3 * MOMENTS)):
            spot = STRIP * (j % 8)
            here = (lane >= spot) & (lane < spot + STRIP)
            packed = jnp.where(here, turn(saveds[0][j // 3, j % 3], spot - EDGE), packed)
        turned = packed.T
        strains_out[group] = turn(jnp.concatenate([turned, jnp.zeros_like(turned)], axis=1), EDGE)


def per_device(
    velocity,
    stress,
    adjoint_velocity,
    adjoint_stress,
    buoyancy,
    lame_lambda,
    shear_modulus,
    observed,
    owner_track,
    fibre_cell,
):
    tracks = lax.axis_size("track")
    rows, depth_cells = buoyancy.shape
    moments, channels = observed.shape
    owner = owner_track.reshape(1, channels)
    cell = fibre_cell.reshape(1, channels)
    pinned = lambda array: pltpu.with_memory_space_constraint(array, pltpu.HBM)
    arrays = (velocity, stress, adjoint_velocity, adjoint_stress, buoyancy, lame_lambda, shear_modulus)
    arrays = tuple(pinned(array) for array in arrays)
    channel_arrays = (pinned(observed), pinned(owner), pinned(cell))
    extent = rows + 2 * EDGE
    block = jax.ShapeDtypeStruct((rows, depth_cells), F32)
    length = BASE + HALO * FIELDS + BASE
    edges = jax.ShapeDtypeStruct((length + (-length) % 8, depth_cells), F32)
    inside = pl.BlockSpec(memory_space=VMEM)
    outside = pl.BlockSpec(memory_space=pltpu.HBM)
    anywhere = pl.BlockSpec(memory_space=pl.ANY)
    held, held_adj, to_depth, to_even, to_odd, strip, traces, cells = pl.pallas_call(
        pack_kernel,
        out_shape=(
            jax.ShapeDtypeStruct((FORWARD, rows, depth_cells), F32),
            jax.ShapeDtypeStruct((ADJOINT, rows, depth_cells), F32),
            jax.ShapeDtypeStruct((rows + STRIP, depth_cells), F32),
            edges,
            edges,
            jax.ShapeDtypeStruct((2 * STRIP, LANES), F32),
            jax.ShapeDtypeStruct((moments, channels), F32),
            jax.ShapeDtypeStruct((2, 1, channels), jnp.int32),
        ),
        in_specs=[outside] * 10,
        out_specs=(inside,) * 8,
        scratch_shapes=[VMEM((2, 1, channels), jnp.int32), pltpu.SemaphoreType.DMA((10,))],
        compiler_params=params(),
        cost_estimate=cost(5),
        name="pack",
    )(*arrays, *channel_arrays)
    depth_swap = [(0, 1), (1, 0)]
    got_depth = lax.ppermute(to_depth, "depth", depth_swap)
    swap = lambda k: [pair for i in range(k, tracks - 1, 2) for pair in ((i, i + 1), (i + 1, i))]
    got_odd = lax.ppermute(to_odd, "track", swap(1))
    got_even = lax.ppermute(to_even, "track", swap(0))

    def state_of(planes):
        return VMEM((5, planes, extent + 2 * PAD, LANES), F32)

    note = pl.pallas_call(
        note_kernel,
        out_shape=jax.ShapeDtypeStruct((tracks, 2 * STRIP + 8, LANES), F32),
        in_specs=[inside] * 4,
        out_specs=inside,
        compiler_params=params(),
        cost_estimate=cost(1),
        name="note",
    )(strip, got_depth, traces, cells)
    notes = lax.all_to_all(note, "track", split_axis=0, concat_axis=0, tiled=True)

    corner = pl.pallas_call(
        corner_kernel,
        out_shape=jax.ShapeDtypeStruct((2 * EDGE, depth_cells), F32),
        in_specs=[inside] * 2,
        out_specs=inside,
        compiler_params=params(),
        cost_estimate=cost(1),
        name="corners",
    )(got_even, got_odd)
    got_corner = lax.ppermute(corner, "depth", depth_swap)

    def media_of(planes):
        return jax.ShapeDtypeStruct((4, planes, extent, LANES), F32)

    def saved_of(planes):
        return jax.ShapeDtypeStruct((moments, 3, planes, rows, LANES), F32)

    media, saved, end = pl.pallas_call(
        forward_kernel,
        out_shape=(media_of(2), saved_of(2), jax.ShapeDtypeStruct((2, 2, rows, LANES), F32)),
        in_specs=[inside] * 3,
        out_specs=(inside,) * 3,
        scratch_shapes=[state_of(2)],
        compiler_params=params(),
        cost_estimate=cost(20),
        name="forward",
    )(held, got_even, got_odd)

    inner_media, inner_saved, end = pl.pallas_call(
        forward_inner_kernel,
        out_shape=(media_of(1), saved_of(1), jax.ShapeDtypeStruct(velocity.shape, F32)),
        in_specs=[inside] * 6,
        out_specs=(inside,) * 3,
        scratch_shapes=[state_of(1)],
        compiler_params=params(),
        cost_estimate=cost(20),
        name="forward_inner",
    )(held, got_even, got_odd, got_depth, got_corner, end)

    base, strains = pl.pallas_call(
        adjoint_kernel,
        out_shape=(
            jax.ShapeDtypeStruct((2, rows, depth_cells), F32),
            jax.ShapeDtypeStruct((2, LANES, LANES), F32),
        ),
        in_specs=[inside] * 9,
        out_specs=(inside,) * 2,
        scratch_shapes=[state_of(3), VMEM((2, 3, rows, LANES), F32)],
        compiler_params=params(),
        cost_estimate=cost(20),
        name="adjoint",
    )(held_adj, got_even, got_odd, got_depth, got_corner, media, saved, inner_media, inner_saved)

    mine = pl.pallas_call(
        relay_kernel,
        out_shape=jax.ShapeDtypeStruct(note.shape, F32),
        in_specs=[inside, anywhere],
        out_specs=inside,
        compiler_params=params(),
        cost_estimate=cost(1),
        name="relay",
    )(notes, base)
    beside = lax.ppermute(mine, "depth", depth_swap)

    gradient_lambda, gradient_mu, residual, velocity_end = pl.pallas_call(
        lambda *refs: finish_kernel(tracks, rows, *refs),
        out_shape=(
            block,
            block,
            jax.ShapeDtypeStruct((moments // 2, channels), F32),
            jax.ShapeDtypeStruct(velocity.shape, F32),
        ),
        in_specs=[inside] * 7,
        out_specs=(inside, inside, inside, outside),
        scratch_shapes=[
            VMEM((5, BATCH, 2 * PAD + STRIP, LANES), F32),
            VMEM((4, BATCH, STRIP, LANES), F32),
            VMEM(note.shape, F32),
            VMEM(note.shape, F32),
            pltpu.SemaphoreType.DMA((1,)),
        ],
        compiler_params=params(),
        cost_estimate=cost(2),
        name="finish",
    )(mine, beside, traces, cells, base, strains, end)
    return gradient_lambda, gradient_mu, velocity_end, residual


def solution(mesh):
    return jax.shard_map(
        per_device,
        mesh=mesh,
        in_specs=(
            P("shots", "track", "depth"),
            P("shots", "track", "depth"),
            P("shots", "track", "depth"),
            P("shots", "track", "depth"),
            P("track", "depth"),
            P("track", "depth"),
            P("track", "depth"),
            P("shots", "track"),
            P("track", None),
            P("track"),
        ),
        out_specs=(
            P(("shots", "track"), "depth"),
            P(("shots", "track"), "depth"),
            P("shots", "track", "depth"),
            P(("shots", "depth"), "track"),
        ),
        check_vma=False,
    )
```

```python
import jax
import jax.numpy as jnp
from jax import lax
from jax.experimental import pallas as pl
from jax.experimental.pallas import tpu as pltpu
from jax.sharding import PartitionSpec as P

FIBRE_ROWS = 4
NEAR = 9.0 / 8.0
RATIO = -1.0 / 27.0
HALO = 12
EDGE = 16
LANES = 128
PAD = 8
FORWARD = 8
ADJOINT = 5
FIELDS = FORWARD + ADJOINT
STRIP = 16
BASE = EDGE - HALO
MOMENTS = 4
IMAGE = MOMENTS * FIBRE_ROWS
VMEM = pltpu.VMEM
F32 = jnp.float32
BF16 = jnp.bfloat16


def lane_ids(rows):
    return lax.broadcasted_iota(jnp.int32, (rows, LANES), 1)


def row_ids(rows, columns):
    return lax.broadcasted_iota(jnp.int32, (rows, columns), 0)


def params():
    return pltpu.CompilerParams(vmem_limit_bytes=16 * 1024 * 1024)


def cost(microseconds):
    return pl.CostEstimate(flops=int(microseconds * 1e9), bytes_accessed=1 << 20, transcendentals=0)


def turn(value, by):
    return pltpu.roll(value, by % LANES, 1)


def is_lower():
    return lax.rem(lax.axis_index("track"), 2) == 1


def fetch(sources, targets, sems):
    copies = [pltpu.make_async_copy(s, t, sems.at[i]) for i, (s, t) in enumerate(zip(sources, targets))]
    for copy in copies:
        copy.start()
    return copies


def pack_kernel(*refs):
    sources, channel_arrays = refs[:7], refs[7:10]
    held, held_adj, depth_out, edge_outs, strip_out, traces_out, cells_out = *refs[10:13], refs[13:15], *refs[15:18]
    numbers, sems = refs[18:]
    targets = (
        held.at[pl.ds(0, 2)],
        held.at[pl.ds(2, 3)],
        held.at[5],
        held.at[6],
        held.at[7],
        held_adj.at[pl.ds(0, 2)],
        held_adj.at[pl.ds(2, 3)],
        traces_out,
        numbers.at[0],
        numbers.at[1],
    )
    copies = fetch((*sources[:2], *sources[4:], *sources[2:4], *channel_arrays), targets, sems)
    arriving = {0: copies[0], 2: copies[1], 5: copies[2], 6: copies[3], 7: copies[4], 8: copies[5], 10: copies[6]}
    depth = lax.axis_index("depth")
    lower = is_lower()
    rows = held.shape[1]
    lane = lane_ids(rows)
    tail = BASE + HALO * FIELDS
    for out in edge_outs:
        out[:BASE, :] = jnp.zeros((BASE, 2 * LANES), F32)
        out[tail:, :] = jnp.zeros((out.shape[0] - tail, 2 * LANES), F32)
    packed = [jnp.zeros((rows, LANES), F32) for _ in range(2)]
    strip = jnp.zeros((rows, LANES), F32)
    for f in range(FIELDS):
        if f in arriving:
            arriving[f].wait()
        ref = held.at[f] if f < FORWARD else held_adj.at[f - FORWARD]
        first, last = ref[:, :LANES], ref[:, LANES:]
        group, place = divmod(f, FORWARD)
        spot = EDGE * place
        here = (lane >= spot) & (lane < spot + EDGE)
        edge = jnp.where(depth == 0, last, first)
        shift = lax.rem(spot + EDGE * (1 - depth), LANES)
        packed[group] = jnp.where(here, pltpu.roll(edge, shift, 1), packed[group])
        if f < FORWARD:
            strip = jnp.where(here, turn(first, spot), strip)
        low, high = ref[:HALO, :], ref[rows - HALO :, :]
        at = BASE + HALO * f
        edge_outs[0][at : at + HALO, :] = jnp.where(lower, high, low)
        edge_outs[1][at : at + HALO, :] = jnp.where(lower, low, high)
    depth_out[:rows, :LANES] = packed[0]
    depth_out[:rows, LANES:] = packed[1]
    turned = strip.T
    strip_out[:, :rows] = turned[: 2 * STRIP]
    strip_out[:, rows:] = turned[2 * STRIP : 4 * STRIP]
    depth_out[rows:, :rows] = turned[4 * STRIP : 5 * STRIP]
    depth_out[rows:, rows : 2 * rows] = turned[6 * STRIP : 7 * STRIP]
    depth_out[rows:, 2 * rows : 3 * rows] = turned[5 * STRIP : 6 * STRIP]
    depth_out[rows:, 3 * rows :] = turned[7 * STRIP :]
    for copy in copies[7:]:
        copy.wait()
    cells_out[0] = numbers[0] * rows + lax.shift_right_logical(numbers[1], 2)
    cells_out[1] = numbers[1] & 3


def edge_rows(f, side, got_first, got_second):
    at = BASE + HALO * f
    span = slice(at - BASE, at + HALO) if side == 0 else slice(at, at + EDGE)
    use_second = is_lower() if side == 0 else ~is_lower()
    return jnp.where(use_second, got_second[span, :], got_first[span, :])


def corner_kernel(got_first, got_second, corner_out):
    depth = lax.axis_index("depth")
    lane = lane_ids(EDGE)
    for side in range(2):
        packed = [jnp.zeros((EDGE, LANES), F32) for _ in range(2)]
        for f in range(FIELDS):
            group, place = divmod(f, FORWARD)
            spot = EDGE * place
            value = edge_rows(f, side, got_first, got_second)
            edge = jnp.where(depth == 0, value[:, LANES:], value[:, :LANES])
            shift = lax.rem(spot + EDGE * (1 - depth), LANES)
            here = (lane >= spot) & (lane < spot + EDGE)
            packed[group] = jnp.where(here, pltpu.roll(edge, shift, 1), packed[group])
        corner_out[EDGE * side : EDGE * (side + 1), :LANES] = packed[0]
        corner_out[EDGE * side : EDGE * (side + 1), LANES:] = packed[1]


def window(plane, f, value, halo):
    depth = lax.axis_index("depth")
    surface = depth == 0
    first, last = value[:, :LANES], value[:, LANES:]
    lane = lane_ids(first.shape[0])
    low = jnp.where(surface, lane, LANES - 1 - lane)
    if plane == 0:
        shift = jnp.where(surface, EDGE, LANES - EDGE)
        return jnp.where(low >= EDGE, pltpu.roll(jnp.where(surface, first, last), shift, 1), 0.0)
    if plane == 1:
        return jnp.where(lane < LANES // 2, turn(first, LANES // 2), turn(last, LANES // 2))
    shift = jnp.where(surface, LANES - EDGE, EDGE)
    beside = lax.rem(LANES - EDGE * (f % FORWARD) + (LANES - EDGE) * (1 - depth), LANES)
    own = pltpu.roll(jnp.where(surface, last, first), shift, 1)
    return jnp.where(low < LANES - EDGE, own, pltpu.roll(halo, beside, 1))


def field_windows(f, planes, held, got_first, got_second, got_depth=None, corner=None):
    rows = held.shape[1]
    col = LANES * (f // FORWARD)
    blocks = (
        (0, edge_rows(f, 0, got_first, got_second), corner, 0),
        (EDGE, held[f % FORWARD], got_depth, 0),
        (EDGE + rows, edge_rows(f, 1, got_first, got_second), corner, EDGE),
    )
    found = [[] for _ in planes]
    for at, value, halo, start in blocks:
        if halo is not None:
            halo = halo[start : start + value.shape[0], col : col + LANES]
        for parts, p in zip(found, planes):
            parts.append((at, window(p, f, value, halo)))
    return found


def joined(outer, middle, inner):
    surface = lax.axis_index("depth") == 0
    lane = lane_ids(outer.shape[0])
    first, last = jnp.where(surface, outer, inner), jnp.where(surface, inner, outer)
    middle = turn(middle, LANES // 2)
    return jnp.where(lane < 88, turn(first, -EDGE), middle), jnp.where(lane < 40, middle, turn(last, EDGE))


def load_state(states, base, planes, held, *got):
    extent = held.shape[1] + 2 * EDGE
    for f in range(5):
        for state, parts in zip(states, field_windows(base + f, planes, held, *got)):
            state[f, :PAD, :] = jnp.zeros((PAD, LANES), F32)
            state[f, PAD + extent :, :] = jnp.zeros((PAD, LANES), F32)
            for at, part in parts:
                state[f, PAD + at : PAD + at + part.shape[0], :] = part


def velocities(states, medias, span):
    for r in range(8 * span[0], 8 * span[1], 8):
        for state, media in zip(states, medias):

            def at(f, by=0):
                return state[f, r + PAD + by : r + PAD + by + 8, :]

            xx, xz, zz = at(2), at(4), at(3)
            b = media[0, r : r + 8, :]
            near = (xx - at(2, -1)) + (xz - turn(xz, 1))
            far = (at(2, 1) - at(2, -2)) + (turn(xz, -1) - turn(xz, 2))
            state[0, r + PAD : r + PAD + 8, :] = at(0) + b * (near + RATIO * far)
            near = (at(4, 1) - xz) + (turn(zz, -1) - zz)
            far = (at(4, 2) - at(4, -1)) + (turn(zz, -2) - turn(zz, 1))
            state[1, r + PAD : r + PAD + 8, :] = at(1) + b * (near + RATIO * far)


def stresses(states, medias, span, update, keep):
    for r in range(8 * span[0], 8 * span[1], 8):
        for i, (state, media) in enumerate(zip(states, medias)):

            def at(f, by=0):
                return state[f, r + PAD + by : r + PAD + by + 8, :]

            vx, vz = at(0), at(1)
            exx = (at(0, 1) - vx) + RATIO * (at(0, 2) - at(0, -1))
            ezz = (vz - turn(vz, 1)) + RATIO * (turn(vz, -1) - turn(vz, 2))
            near = (turn(vx, -1) - vx) + (vz - at(1, -1))
            far = (turn(vx, -2) - turn(vx, 1)) + (at(1, 1) - at(1, -2))
            shear = near + RATIO * far
            keep(i, r - EDGE, exx, ezz, shear)
            if update:
                whole, lam, mu = (media[k, r : r + 8, :] for k in (1, 2, 3))
                state[2, r + PAD : r + PAD + 8, :] = at(2) + (whole * exx + lam * ezz)
                state[3, r + PAD : r + PAD + 8, :] = at(3) + (lam * exx + whole * ezz)
                state[4, r + PAD : r + PAD + 8, :] = at(4) + mu * shear


def spans(step, rows):
    tiles = (rows + 2 * EDGE) // 8
    if step == 0:
        return (0, tiles), (0, tiles)
    inner = (1, tiles - 1)
    return inner, inner if step < MOMENTS - 1 else (EDGE // 8, tiles - EDGE // 8)


def run_forward(states, medias, saveds, planes, held, *got):
    rows = held.shape[1]
    given = [field_windows(f, planes, held, *got) for f in (5, 6, 7)]
    for i, media in enumerate(medias):
        for k in range(3):
            at = given[0][i][k][0]
            b, lam, mu = (NEAR * given[m][i][k][1] for m in range(3))
            span = slice(at, at + b.shape[0])
            media[0, span, :] = b
            media[1, span, :] = lam + 2.0 * mu
            media[2, span, :] = lam
            media[3, span, :] = mu
    load_state(states, 0, planes, held, *got)
    for step in range(MOMENTS):
        fast, slow = spans(step, rows)
        velocities(states, medias, fast)

        def save(i, r, exx, ezz, shear):
            if 0 <= r < rows:
                saveds[i][step, 0, r : r + 8, :] = exx
                saveds[i][step, 1, r : r + 8, :] = ezz
                saveds[i][step, 2, r : r + 8, :] = shear

        stresses(states, medias, slow, step < MOMENTS - 1, save)


def each(ref, count, axis):
    return [ref.at[(slice(None),) * axis + (i,)] for i in range(count)]


def forward_kernel(held, got_first, got_second, media, saved, end_out, state):
    states = each(state, 2, 1)
    run_forward(states, each(media, 2, 1), each(saved, 2, 2), (0, 1), held, got_first, got_second)
    top, rows = PAD + EDGE, held.shape[1]
    for f in range(2):
        for i in range(2):
            end_out[f, i] = states[i][f, top : top + rows, :]


def forward_inner_kernel(held, got_first, got_second, got_depth, corner, end, media, saved, end_out, state):
    states = each(state, 1, 1)
    run_forward(
        states, each(media, 1, 1), each(saved, 1, 2), (2,), held, got_first, got_second, got_depth, corner
    )
    top, rows = PAD + EDGE, held.shape[1]
    for f in range(2):
        first, last = joined(end[f, 0], end[f, 1], states[0][f, top : top + rows, :])
        end_out[f, :, :LANES] = first
        end_out[f, :, LANES:] = last


def note_kernel(strip, got_depth, traces, cells, note_out):
    first = lax.axis_index("depth") == 0
    beside = got_depth[got_depth.shape[0] - STRIP :, :]
    beside = jnp.concatenate([beside[:, :LANES], beside[:, LANES:]], axis=0)
    seen = jnp.concatenate([traces[:, :LANES], traces[:, LANES:]], axis=0)
    along, row = cells[0], cells[1]
    places = jnp.concatenate([along[:, :LANES], along[:, LANES:], row[:, :LANES], row[:, LANES:]] * 2, axis=0)
    block = jnp.concatenate(
        [jnp.where(first, strip[...], beside), jnp.where(first, seen, places.astype(F32))], axis=0
    )
    for k in range(note_out.shape[0]):
        note_out[k] = block


def relay_kernel(notes, rest, notes_out):
    del rest
    notes_out[...] = notes[...]


def three(value):
    high = value.astype(BF16)
    rest = value - high.astype(F32)
    middle = rest.astype(BF16)
    low = (rest - middle.astype(F32)).astype(BF16)
    return [high, middle, low]


def add_up(value, count):
    return (value[2 * count : 3 * count] + value[count : 2 * count]) + value[:count]


BATCH = 5
OWN = LANES - 2 * HALO


def strip_window(f, low, high, base, offset, tracks, columns):
    lane = lane_ids(STRIP)
    part = lax.div(offset + lane, columns)
    spot = base * columns + offset + lane
    source, q = (low, high)[f // 4], f % 4
    value = jnp.zeros((STRIP, LANES), F32)
    for step in range(3):
        who = jnp.clip(base + step, 0, tracks - 1)
        block = source[who, STRIP * (q % 2) : STRIP * (q % 2 + 1), :]
        shift = (4 * LANES - offset + columns * step - columns * (q // 2)) % LANES
        value = jnp.where(part == step, pltpu.roll(block, shift, 1), value)
    return jnp.where((spot >= 0) & (spot < tracks * columns), value, 0.0)


def fill_strip(state, media, low, high, first, tracks, columns):
    state[...] = jnp.zeros(state.shape, F32)
    for w in range(BATCH):
        begin = (first + w) * OWN - HALO
        base = (begin + columns) // columns - 1
        offset = begin - base * columns
        values = [strip_window(f, low, high, base, offset, tracks, columns) for f in range(FORWARD)]
        for f in range(5):
            state[f, w, PAD : PAD + STRIP, :] = values[f]
        buoyancy, lame, shear = (NEAR * value for value in values[5:])
        media[0, w] = buoyancy
        media[1, w] = lame + 2.0 * shear
        media[2, w] = lame
        media[3, w] = shear


def strip_steps(state, media):
    def at(f, w, r, by=0):
        return state[f, w, PAD + r + by : PAD + r + by + 8, :]

    strains = [[] for _ in range(BATCH)]
    for moment in range(MOMENTS):
        last = moment == MOMENTS - 1
        for r in (0, 8) if moment < 2 else (0,):
            for w in range(BATCH):
                here = slice(PAD + r, PAD + r + 8)
                xx, xz, zz = at(2, w, r), at(4, w, r), at(3, w, r)
                b = media[0, w, r : r + 8, :]
                near = (xx - turn(xx, 1)) + (xz - at(4, w, r, -1))
                far = (turn(xx, -1) - turn(xx, 2)) + (at(4, w, r, 1) - at(4, w, r, -2))
                state[0, w, here, :] = at(0, w, r) + b * (near + RATIO * far)
                if not last:
                    near = (turn(xz, -1) - xz) + (at(3, w, r, 1) - zz)
                    far = (turn(xz, -2) - turn(xz, 1)) + (at(3, w, r, 2) - at(3, w, r, -1))
                    state[1, w, here, :] = at(1, w, r) + b * (near + RATIO * far)
        for r in (0, 8) if moment < 1 else (0,):
            for w in range(BATCH):
                here = slice(PAD + r, PAD + r + 8)
                vx, vz = at(0, w, r), at(1, w, r)
                exx = (turn(vx, -1) - vx) + RATIO * (turn(vx, -2) - turn(vx, 1))
                if r == 0:
                    strains[w].append(NEAR * exx)
                if not last:
                    ezz = (vz - at(1, w, r, -1)) + RATIO * (at(1, w, r, 1) - at(1, w, r, -2))
                    near = (at(0, w, r, 1) - vx) + (vz - turn(vz, 1))
                    far = (at(0, w, r, 2) - at(0, w, r, -1)) + (turn(vz, -1) - turn(vz, 2))
                    whole, lam, mu = (media[k, w, r : r + 8, :] for k in (1, 2, 3))
                    state[2, w, here, :] = at(2, w, r) + (whole * exx + lam * ezz)
                    state[3, w, here, :] = at(3, w, r) + (lam * exx + whole * ezz)
                    state[4, w, here, :] = at(4, w, r) + mu * (near + RATIO * far)
    return [jnp.concatenate(parts, axis=0) for parts in strains]


def recorded_rates(state, media, low, high, wanted, tracks, columns):
    lane = lane_ids(8 * MOMENTS)
    mine = (lane >= HALO) & (lane < HALO + OWN)

    def body(number, rate):
        first = number * BATCH
        fill_strip(state, media, low, high, first, tracks, columns)
        images = [three(jnp.where(mine, image, 0.0)) for image in strip_steps(state, media)]
        parts = [jnp.concatenate([image[i] for image in images], axis=1) for i in range(3)]
        spots = [
            (first + w) * OWN - HALO + row_ids(LANES, wanted.shape[1]) for w in range(BATCH)
        ]
        hot = (jnp.concatenate(spots, axis=0) == wanted).astype(F32).astype(BF16)
        return rate + jnp.dot(jnp.concatenate(parts, axis=0), hot, preferred_element_type=F32)

    rate = jnp.zeros((3 * 8 * MOMENTS, wanted.shape[1]), F32)
    batches = -(-(-(-tracks * columns // OWN)) // BATCH)
    rate = body(0, rate) if batches == 1 else lax.fori_loop(0, batches, body, rate)
    return add_up(rate, 8 * MOMENTS)


def window_sums(low, high, start, tracks):
    group = min(8, tracks)
    row16 = row_ids(IMAGE, LANES)

    def body(number, image):
        weights, hots = [], []
        for k in range(group):
            who = number * group + k
            traces = low[who, 2 * STRIP :, :]
            places = high[who, 2 * STRIP :, :]
            for h in range(2):
                mask = (row16 & 3).astype(F32) == places[2 + h : 3 + h]
                seen = [traces[4 * h + t : 4 * h + t + 1] for t in range(MOMENTS)]
                value = jnp.where(
                    row16 < 8,
                    jnp.where(row16 < 4, seen[0], seen[1]),
                    jnp.where(row16 < 12, seen[2], seen[3]),
                )
                pieces = three(jnp.where(mask, value, 0.0)) + [mask.astype(F32).astype(BF16)]
                weights.append(jnp.concatenate(pieces, axis=0))
                spot = (start + row_ids(LANES, LANES)).astype(F32)
                hots.append((spot == places[h : h + 1]).astype(F32).astype(BF16))
        return image + lax.dot_general(
            jnp.concatenate(weights, axis=1),
            jnp.concatenate(hots, axis=1),
            (((1,), (1,)), ((), ())),
            preferred_element_type=F32,
        )

    image = jnp.zeros((4 * IMAGE, LANES), F32)
    image = body(0, image) if tracks == group else lax.fori_loop(0, tracks // group, body, image)
    return add_up(image, IMAGE), image[3 * IMAGE :]


def response(state, media, sources, strains):
    state[...] = jnp.zeros(state.shape, F32)
    tiles = (0, 8)
    sums = [[jnp.zeros((8, LANES), F32) for _ in tiles] for _ in range(2)]

    def at(f, r, by=0):
        return state[f, PAD + r + by : PAD + r + by + 8, :]

    def put(f, r, value):
        state[f, PAD + r : PAD + r + 8, :] = value

    for moment in reversed(range(MOMENTS)):
        put(2, 0, at(2, 0) + sources[moment])
        for r in tiles:
            xx, xz, zz = at(2, r), at(4, r), at(3, r)
            b = media[0, r : r + 8, :]
            near = (xx - turn(xx, 1)) + (xz - at(4, r, -1))
            far = (turn(xx, -1) - turn(xx, 2)) + (at(4, r, 1) - at(4, r, -2))
            put(0, r, at(0, r) + b * (near + RATIO * far))
            near = (turn(xz, -1) - xz) + (at(3, r, 1) - zz)
            far = (turn(xz, -2) - turn(xz, 1)) + (at(3, r, 2) - at(3, r, -1))
            put(1, r, at(1, r) + b * (near + RATIO * far))
        for i, r in enumerate(tiles):
            vx, vz = at(0, r), at(1, r)
            exx = (turn(vx, -1) - vx) + RATIO * (turn(vx, -2) - turn(vx, 1))
            ezz = (vz - at(1, r, -1)) + RATIO * (at(1, r, 1) - at(1, r, -2))
            near = (at(0, r, 1) - vx) + (vz - turn(vz, 1))
            far = (at(0, r, 2) - at(0, r, -1)) + (turn(vz, -1) - turn(vz, 2))
            shear = near + RATIO * far
            fxx, fzz, fxz = (
                strains[j // 8, STRIP * (j % 8) + r : STRIP * (j % 8) + r + 8, :]
                for j in range(3 * moment, 3 * moment + 3)
            )
            sums[0][i] += (fxx + fzz) * (exx + ezz)
            sums[1][i] += 2.0 * (fxx * exx + fzz * ezz) + fxz * shear
            if moment > 0:
                whole, lam, mu = (media[k, r : r + 8, :] for k in (1, 2, 3))
                put(2, r, at(2, r) + (whole * exx + lam * ezz))
                put(3, r, at(3, r) + (lam * exx + whole * ezz))
                put(4, r, at(4, r) + mu * shear)
    return sums[0] + sums[1]


def finish_kernel(
    tracks, columns, notes, beside, obs, cells, base, strains, end,
    lambda_out, mu_out, residual_out, end_out, state, media, low, high, sems,
):
    copy = pltpu.make_async_copy(end, end_out, sems.at[0])
    copy.start()
    depth = lax.axis_index("depth")
    low[...] = jnp.where(depth == 0, notes[...], beside[...])
    high[...] = jnp.where(depth == 0, beside[...], notes[...])
    track = lax.axis_index("track")
    start = track * columns - EDGE
    along, row = cells[0], cells[1]
    channels = along.shape[1]
    wanted = jnp.concatenate([along, start + lax.broadcasted_iota(jnp.int32, (1, LANES), 1)], axis=1)
    seen, count = window_sums(low, high, start, tracks)
    rate = recorded_rates(state, media, low, high, wanted, tracks, columns)
    mask = row_ids(8, channels) == row
    traces = [
        jnp.sum(jnp.where(mask, rate[8 * t : 8 * t + 8, :channels], 0.0), axis=0, keepdims=True)
        - obs[t : t + 1, :]
        for t in range(MOMENTS)
    ]
    residual_out[...] = jnp.where(
        depth == 0, jnp.concatenate(traces[:2], axis=0), jnp.concatenate(traces[2:], axis=0)
    )
    near = jnp.concatenate([rate[8 * t : 8 * t + 4, channels:] for t in range(MOMENTS)], axis=0)
    found = jnp.where(depth == 0, count * near - seen, 0.0)
    nothing = jnp.zeros((8 - FIBRE_ROWS, LANES), F32)
    sources = [
        jnp.concatenate([found[FIBRE_ROWS * t : FIBRE_ROWS * (t + 1)], nothing], axis=0) for t in range(MOMENTS)
    ]
    own = [
        NEAR * strip_window(f, low, high, track - 1, columns - EDGE, tracks, columns) for f in (5, 6, 7)
    ]
    media[0, 0] = own[0]
    media[1, 0] = own[1] + 2.0 * own[2]
    media[2, 0] = own[1]
    media[3, 0] = own[2]
    added = response(state.at[:, 0], media.at[:, 0], sources, strains)
    rows = base.shape[1]
    added = jnp.concatenate(added + [jnp.zeros((LANES - 32, LANES), F32)], axis=0).T[EDGE : EDGE + rows]
    lane = lane_ids(rows)
    for k, out in enumerate((lambda_out, mu_out)):
        more = jnp.where(lane < STRIP, turn(added, -STRIP * k), 0.0)
        out[:, :LANES] = (NEAR * NEAR) * (base[k, :, :LANES] + more)
        out[:, LANES:] = (NEAR * NEAR) * base[k, :, LANES:]
    copy.wait()


def adjoint_kernel(
    held, got_first, got_second, got_depth, corner, media, saved, inner_media, inner_saved,
    base_out, strains_out, state, sums,
):
    states, totals = each(state, 3, 1), each(sums, 3, 1)
    rows = held.shape[1]
    load_state(states, FORWARD, (0, 1, 2), held, got_first, got_second, got_depth, corner)
    medias = each(media, 2, 1) + each(inner_media, 1, 1)
    saveds = each(saved, 2, 2) + each(inner_saved, 1, 2)
    sums[...] = jnp.zeros(sums.shape, F32)
    for step in range(MOMENTS):
        fast, slow = spans(step, rows)
        moment = MOMENTS - 1 - step
        velocities(states, medias, fast)

        def gather(i, r, exx, ezz, shear):
            if 0 <= r < rows:
                fxx, fzz, fxz = (saveds[i][moment, k, r : r + 8, :] for k in range(3))
                totals[i][0, r : r + 8, :] += (fxx + fzz) * (exx + ezz)
                totals[i][1, r : r + 8, :] += 2.0 * (fxx * exx + fzz * ezz) + fxz * shear

        stresses(states, medias, slow, step < MOMENTS - 1, gather)
    for k in range(2):
        first, last = joined(*(total[k] for total in totals))
        base_out[k, :, :LANES] = first
        base_out[k, :, LANES:] = last
    lane = lane_ids(rows)
    for group in range(2):
        packed = jnp.zeros((rows, LANES), F32)
        for j in range(8 * group, min(8 * group + 8, 3 * MOMENTS)):
            spot = STRIP * (j % 8)
            here = (lane >= spot) & (lane < spot + STRIP)
            packed = jnp.where(here, turn(saveds[0][j // 3, j % 3], spot - EDGE), packed)
        turned = packed.T
        strains_out[group] = turn(jnp.concatenate([turned, jnp.zeros_like(turned)], axis=1), EDGE)


def per_device(
    velocity,
    stress,
    adjoint_velocity,
    adjoint_stress,
    buoyancy,
    lame_lambda,
    shear_modulus,
    observed,
    owner_track,
    fibre_cell,
):
    tracks = lax.axis_size("track")
    rows, depth_cells = buoyancy.shape
    moments, channels = observed.shape
    owner = owner_track.reshape(1, channels)
    cell = fibre_cell.reshape(1, channels)
    pinned = lambda array: pltpu.with_memory_space_constraint(array, pltpu.HBM)
    arrays = (velocity, stress, adjoint_velocity, adjoint_stress, buoyancy, lame_lambda, shear_modulus)
    arrays = tuple(pinned(array) for array in arrays)
    channel_arrays = (pinned(observed), pinned(owner), pinned(cell))
    extent = rows + 2 * EDGE
    block = jax.ShapeDtypeStruct((rows, depth_cells), F32)
    length = BASE + HALO * FIELDS + BASE
    edges = jax.ShapeDtypeStruct((length + (-length) % 8, depth_cells), F32)
    inside = pl.BlockSpec(memory_space=VMEM)
    outside = pl.BlockSpec(memory_space=pltpu.HBM)
    anywhere = pl.BlockSpec(memory_space=pl.ANY)
    held, held_adj, to_depth, to_first, to_second, strip, traces, cells = pl.pallas_call(
        pack_kernel,
        out_shape=(
            jax.ShapeDtypeStruct((FORWARD, rows, depth_cells), F32),
            jax.ShapeDtypeStruct((ADJOINT, rows, depth_cells), F32),
            jax.ShapeDtypeStruct((rows + STRIP, depth_cells), F32),
            edges,
            edges,
            jax.ShapeDtypeStruct((2 * STRIP, LANES), F32),
            jax.ShapeDtypeStruct((moments, channels), F32),
            jax.ShapeDtypeStruct((2, 1, channels), jnp.int32),
        ),
        in_specs=[outside] * 10,
        out_specs=(inside,) * 8,
        scratch_shapes=[VMEM((2, 1, channels), jnp.int32), pltpu.SemaphoreType.DMA((10,))],
        compiler_params=params(),
        cost_estimate=cost(5),
        name="pack",
    )(*arrays, *channel_arrays)
    depth_swap = [(0, 1), (1, 0)]
    got_depth = lax.ppermute(to_depth, "depth", depth_swap)
    swap = lambda k: [pair for i in range(k, tracks - 1, 2) for pair in ((i, i + 1), (i + 1, i))]
    got_first = lax.ppermute(to_first, "track", swap(1))
    got_second = lax.ppermute(to_second, "track", swap(0))

    def state_of(planes):
        return VMEM((5, planes, extent + 2 * PAD, LANES), F32)

    note = pl.pallas_call(
        note_kernel,
        out_shape=jax.ShapeDtypeStruct((tracks, 2 * STRIP + 8, LANES), F32),
        in_specs=[inside] * 4,
        out_specs=inside,
        compiler_params=params(),
        cost_estimate=cost(1),
        name="note",
    )(strip, got_depth, traces, cells)
    notes = lax.all_to_all(note, "track", split_axis=0, concat_axis=0, tiled=True)

    corner = pl.pallas_call(
        corner_kernel,
        out_shape=jax.ShapeDtypeStruct((2 * EDGE, depth_cells), F32),
        in_specs=[inside] * 2,
        out_specs=inside,
        compiler_params=params(),
        cost_estimate=cost(1),
        name="corners",
    )(got_first, got_second)
    got_corner = lax.ppermute(corner, "depth", depth_swap)

    def media_of(planes):
        return jax.ShapeDtypeStruct((4, planes, extent, LANES), F32)

    def saved_of(planes):
        return jax.ShapeDtypeStruct((moments, 3, planes, rows, LANES), F32)

    media, saved, end = pl.pallas_call(
        forward_kernel,
        out_shape=(media_of(2), saved_of(2), jax.ShapeDtypeStruct((2, 2, rows, LANES), F32)),
        in_specs=[inside] * 3,
        out_specs=(inside,) * 3,
        scratch_shapes=[state_of(2)],
        compiler_params=params(),
        cost_estimate=cost(20),
        name="forward",
    )(held, got_first, got_second)

    inner_media, inner_saved, end = pl.pallas_call(
        forward_inner_kernel,
        out_shape=(media_of(1), saved_of(1), jax.ShapeDtypeStruct(velocity.shape, F32)),
        in_specs=[inside] * 6,
        out_specs=(inside,) * 3,
        scratch_shapes=[state_of(1)],
        compiler_params=params(),
        cost_estimate=cost(20),
        name="forward_inner",
    )(held, got_first, got_second, got_depth, got_corner, end)

    base, strains = pl.pallas_call(
        adjoint_kernel,
        out_shape=(
            jax.ShapeDtypeStruct((2, rows, depth_cells), F32),
            jax.ShapeDtypeStruct((2, LANES, LANES), F32),
        ),
        in_specs=[inside] * 9,
        out_specs=(inside,) * 2,
        scratch_shapes=[state_of(3), VMEM((2, 3, rows, LANES), F32)],
        compiler_params=params(),
        cost_estimate=cost(20),
        name="adjoint",
    )(held_adj, got_first, got_second, got_depth, got_corner, media, saved, inner_media, inner_saved)

    mine = pl.pallas_call(
        relay_kernel,
        out_shape=jax.ShapeDtypeStruct(note.shape, F32),
        in_specs=[inside, anywhere],
        out_specs=inside,
        compiler_params=params(),
        cost_estimate=cost(1),
        name="relay",
    )(notes, base)
    beside = lax.ppermute(mine, "depth", depth_swap)

    gradient_lambda, gradient_mu, residual, velocity_end = pl.pallas_call(
        lambda *refs: finish_kernel(tracks, rows, *refs),
        out_shape=(
            block,
            block,
            jax.ShapeDtypeStruct((moments // 2, channels), F32),
            jax.ShapeDtypeStruct(velocity.shape, F32),
        ),
        in_specs=[inside] * 7,
        out_specs=(inside, inside, inside, outside),
        scratch_shapes=[
            VMEM((5, BATCH, 2 * PAD + STRIP, LANES), F32),
            VMEM((4, BATCH, STRIP, LANES), F32),
            VMEM(note.shape, F32),
            VMEM(note.shape, F32),
            pltpu.SemaphoreType.DMA((1,)),
        ],
        compiler_params=params(),
        cost_estimate=cost(2),
        name="finish",
    )(mine, beside, traces, cells, base, strains, end)
    return gradient_lambda, gradient_mu, velocity_end, residual


def solution(mesh):
    return jax.shard_map(
        per_device,
        mesh=mesh,
        in_specs=(
            P("shots", "track", "depth"),
            P("shots", "track", "depth"),
            P("shots", "track", "depth"),
            P("shots", "track", "depth"),
            P("track", "depth"),
            P("track", "depth"),
            P("track", "depth"),
            P("shots", "track"),
            P("track", None),
            P("track"),
        ),
        out_specs=(
            P(("shots", "track"), "depth"),
            P(("shots", "track"), "depth"),
            P("shots", "track", "depth"),
            P(("shots", "depth"), "track"),
        ),
        check_vma=False,
    )
```

```python
import jax
import jax.numpy as jnp
from jax import lax
from jax.experimental import pallas as pl
from jax.experimental.pallas import tpu as pltpu
from jax.sharding import PartitionSpec as P

FIBRE_ROWS = 4
NEAR = 9.0 / 8.0
RATIO = -1.0 / 27.0
HALO = 12
EDGE = 16
LANES = 128
PAD = 8
FORWARD = 8
ADJOINT = 5
FIELDS = FORWARD + ADJOINT
STRIP = 16
CELL_ROWS = (14, 15, 30, 31)
BASE = EDGE - HALO
MOMENTS = 4
IMAGE = MOMENTS * FIBRE_ROWS
VMEM = pltpu.VMEM
F32 = jnp.float32
BF16 = jnp.bfloat16


def lane_ids(rows):
    return lax.broadcasted_iota(jnp.int32, (rows, LANES), 1)


def row_ids(rows, columns):
    return lax.broadcasted_iota(jnp.int32, (rows, columns), 0)


def params():
    return pltpu.CompilerParams(vmem_limit_bytes=16 * 1024 * 1024)


def cost(microseconds):
    return pl.CostEstimate(flops=int(microseconds * 1e9), bytes_accessed=1 << 20, transcendentals=0)


def turn(value, by):
    return pltpu.roll(value, by % LANES, 1)


def is_even():
    return lax.rem(lax.axis_index("track"), 2) == 0


def fetch(sources, targets, sems):
    copies = [pltpu.make_async_copy(s, t, sems.at[i]) for i, (s, t) in enumerate(zip(sources, targets))]
    for copy in copies:
        copy.start()
    return copies


def pack_kernel(*refs):
    sources, channel_arrays = refs[:7], refs[7:10]
    held, held_adj, depth_out, edge_outs, strip_out, traces_out, cells_out = *refs[10:13], refs[13:15], *refs[15:18]
    numbers, sems = refs[18:]
    targets = (
        held.at[pl.ds(0, 2)],
        held.at[pl.ds(2, 3)],
        held.at[5],
        held.at[6],
        held.at[7],
        held_adj.at[pl.ds(0, 2)],
        held_adj.at[pl.ds(2, 3)],
        traces_out,
        numbers.at[0],
        numbers.at[1],
    )
    copies = fetch((*sources[:2], *sources[4:], *sources[2:4], *channel_arrays), targets, sems)
    depth = lax.axis_index("depth")
    even = is_even()
    rows = held.shape[1]
    lane = lane_ids(rows)
    tail = BASE + HALO * FIELDS
    for out in edge_outs:
        out[:BASE, :] = jnp.zeros((BASE, 2 * LANES), F32)
        out[tail:, :] = jnp.zeros((out.shape[0] - tail, 2 * LANES), F32)
    for copy in copies:
        copy.wait()
    packed = [jnp.zeros((rows, LANES), F32) for _ in range(2)]
    strip = jnp.zeros((rows, LANES), F32)
    for f in range(FIELDS):
        ref = held.at[f] if f < FORWARD else held_adj.at[f - FORWARD]
        first, last = ref[:, :LANES], ref[:, LANES:]
        group, place = divmod(f, FORWARD)
        spot = EDGE * place
        here = (lane >= spot) & (lane < spot + EDGE)
        edge = jnp.where(depth == 0, last, first)
        shift = lax.rem(spot + EDGE * (1 - depth), LANES)
        packed[group] = jnp.where(here, pltpu.roll(edge, shift, 1), packed[group])
        if f < FORWARD:
            strip = jnp.where(here, turn(first, spot), strip)
        low, high = ref[:HALO, :], ref[rows - HALO :, :]
        at = BASE + HALO * f
        edge_outs[0][at : at + HALO, :] = jnp.where(even, high, low)
        edge_outs[1][at : at + HALO, :] = jnp.where(even, low, high)
    depth_out[:rows, :LANES] = packed[0]
    depth_out[:rows, LANES:] = packed[1]
    turned = strip.T
    strip_out[:, :rows] = turned[: 2 * STRIP]
    strip_out[:, rows:] = turned[2 * STRIP : 4 * STRIP]
    depth_out[rows:, :rows] = turned[4 * STRIP : 5 * STRIP]
    depth_out[rows:, rows : 2 * rows] = turned[6 * STRIP : 7 * STRIP]
    depth_out[rows:, 2 * rows : 3 * rows] = turned[5 * STRIP : 6 * STRIP]
    depth_out[rows:, 3 * rows :] = turned[7 * STRIP :]
    cells_out[0] = numbers[0] * rows + lax.shift_right_logical(numbers[1], 2)
    cells_out[1] = numbers[1] & 3


def edge_rows(f, side, got_even, got_odd):
    at = BASE + HALO * f
    span = slice(at - BASE, at + HALO) if side == 0 else slice(at, at + EDGE)
    use_odd = is_even() if side == 0 else ~is_even()
    return jnp.where(use_odd, got_odd[span, :], got_even[span, :])


def corner_kernel(got_even, got_odd, corner_out):
    depth = lax.axis_index("depth")
    lane = lane_ids(EDGE)
    for side in range(2):
        packed = [jnp.zeros((EDGE, LANES), F32) for _ in range(2)]
        for f in range(FIELDS):
            group, place = divmod(f, FORWARD)
            spot = EDGE * place
            value = edge_rows(f, side, got_even, got_odd)
            edge = jnp.where(depth == 0, value[:, LANES:], value[:, :LANES])
            shift = lax.rem(spot + EDGE * (1 - depth), LANES)
            here = (lane >= spot) & (lane < spot + EDGE)
            packed[group] = jnp.where(here, pltpu.roll(edge, shift, 1), packed[group])
        corner_out[EDGE * side : EDGE * (side + 1), :LANES] = packed[0]
        corner_out[EDGE * side : EDGE * (side + 1), LANES:] = packed[1]


def window(plane, f, value, halo):
    depth = lax.axis_index("depth")
    surface = depth == 0
    first, last = value[:, :LANES], value[:, LANES:]
    lane = lane_ids(first.shape[0])
    low = jnp.where(surface, lane, LANES - 1 - lane)
    if plane == 0:
        shift = jnp.where(surface, EDGE, LANES - EDGE)
        return jnp.where(low >= EDGE, pltpu.roll(jnp.where(surface, first, last), shift, 1), 0.0)
    if plane == 1:
        return jnp.where(lane < LANES // 2, turn(first, LANES // 2), turn(last, LANES // 2))
    shift = jnp.where(surface, LANES - EDGE, EDGE)
    beside = lax.rem(LANES - EDGE * (f % FORWARD) + (LANES - EDGE) * (1 - depth), LANES)
    own = pltpu.roll(jnp.where(surface, last, first), shift, 1)
    return jnp.where(low < LANES - EDGE, own, pltpu.roll(halo, beside, 1))


def field_windows(f, planes, held, got_even, got_odd, got_depth=None, corner=None):
    rows = held.shape[1]
    col = LANES * (f // FORWARD)
    blocks = (
        (0, edge_rows(f, 0, got_even, got_odd), corner, 0),
        (EDGE, held[f % FORWARD], got_depth, 0),
        (EDGE + rows, edge_rows(f, 1, got_even, got_odd), corner, EDGE),
    )
    found = [[] for _ in planes]
    for at, value, halo, start in blocks:
        if halo is not None:
            halo = halo[start : start + value.shape[0], col : col + LANES]
        for parts, p in zip(found, planes):
            parts.append((at, window(p, f, value, halo)))
    return found


def joined(outer, middle, inner):
    surface = lax.axis_index("depth") == 0
    lane = lane_ids(outer.shape[0])
    first, last = jnp.where(surface, outer, inner), jnp.where(surface, inner, outer)
    middle = turn(middle, LANES // 2)
    return jnp.where(lane < 88, turn(first, -EDGE), middle), jnp.where(lane < 40, middle, turn(last, EDGE))


def load_state(states, base, planes, held, *got):
    extent = held.shape[1] + 2 * EDGE
    for f in range(5):
        for state, parts in zip(states, field_windows(base + f, planes, held, *got)):
            state[f, :PAD, :] = jnp.zeros((PAD, LANES), F32)
            state[f, PAD + extent :, :] = jnp.zeros((PAD, LANES), F32)
            for at, part in parts:
                state[f, PAD + at : PAD + at + part.shape[0], :] = part


def velocities(states, medias, span):
    for r in range(8 * span[0], 8 * span[1], 8):
        for state, media in zip(states, medias):

            def at(f, by=0):
                return state[f, r + PAD + by : r + PAD + by + 8, :]

            xx, xz, zz = at(2), at(4), at(3)
            b = media[0, r : r + 8, :]
            near = (xx - at(2, -1)) + (xz - turn(xz, 1))
            far = (at(2, 1) - at(2, -2)) + (turn(xz, -1) - turn(xz, 2))
            state[0, r + PAD : r + PAD + 8, :] = at(0) + b * (near + RATIO * far)
            near = (at(4, 1) - xz) + (turn(zz, -1) - zz)
            far = (at(4, 2) - at(4, -1)) + (turn(zz, -2) - turn(zz, 1))
            state[1, r + PAD : r + PAD + 8, :] = at(1) + b * (near + RATIO * far)


def stresses(states, medias, span, update, keep):
    for r in range(8 * span[0], 8 * span[1], 8):
        for i, (state, media) in enumerate(zip(states, medias)):

            def at(f, by=0):
                return state[f, r + PAD + by : r + PAD + by + 8, :]

            vx, vz = at(0), at(1)
            exx = (at(0, 1) - vx) + RATIO * (at(0, 2) - at(0, -1))
            ezz = (vz - turn(vz, 1)) + RATIO * (turn(vz, -1) - turn(vz, 2))
            near = (turn(vx, -1) - vx) + (vz - at(1, -1))
            far = (turn(vx, -2) - turn(vx, 1)) + (at(1, 1) - at(1, -2))
            shear = near + RATIO * far
            keep(i, r - EDGE, exx, ezz, shear)
            if update:
                whole, lam, mu = (media[k, r : r + 8, :] for k in (1, 2, 3))
                state[2, r + PAD : r + PAD + 8, :] = at(2) + (whole * exx + lam * ezz)
                state[3, r + PAD : r + PAD + 8, :] = at(3) + (lam * exx + whole * ezz)
                state[4, r + PAD : r + PAD + 8, :] = at(4) + mu * shear


def spans(step, rows):
    tiles = (rows + 2 * EDGE) // 8
    if step == 0:
        return (0, tiles), (0, tiles)
    inner = (1, tiles - 1)
    return inner, inner if step < MOMENTS - 1 else (EDGE // 8, tiles - EDGE // 8)


def run_forward(states, medias, saveds, planes, held, *got):
    rows = held.shape[1]
    given = [field_windows(f, planes, held, *got) for f in (5, 6, 7)]
    for i, media in enumerate(medias):
        for k in range(3):
            at = given[0][i][k][0]
            b, lam, mu = (NEAR * given[m][i][k][1] for m in range(3))
            span = slice(at, at + b.shape[0])
            media[0, span, :] = b
            media[1, span, :] = lam + 2.0 * mu
            media[2, span, :] = lam
            media[3, span, :] = mu
    load_state(states, 0, planes, held, *got)
    for step in range(MOMENTS):
        fast, slow = spans(step, rows)
        velocities(states, medias, fast)

        def save(i, r, exx, ezz, shear):
            if 0 <= r < rows:
                saveds[i][step, 0, r : r + 8, :] = exx
                saveds[i][step, 1, r : r + 8, :] = ezz
                saveds[i][step, 2, r : r + 8, :] = shear

        stresses(states, medias, slow, step < MOMENTS - 1, save)


def each(ref, count, axis):
    return [ref.at[(slice(None),) * axis + (i,)] for i in range(count)]


def forward_kernel(held, got_even, got_odd, media, saved, end_out, state):
    states = each(state, 2, 1)
    run_forward(states, each(media, 2, 1), each(saved, 2, 2), (0, 1), held, got_even, got_odd)
    top, rows = PAD + EDGE, held.shape[1]
    for f in range(2):
        for i in range(2):
            end_out[f, i] = states[i][f, top : top + rows, :]


def forward_inner_kernel(held, got_even, got_odd, got_depth, corner, end, media, saved, end_out, state):
    states = each(state, 1, 1)
    run_forward(
        states, each(media, 1, 1), each(saved, 1, 2), (2,), held, got_even, got_odd, got_depth, corner
    )
    top, rows = PAD + EDGE, held.shape[1]
    for f in range(2):
        first, last = joined(end[f, 0], end[f, 1], states[0][f, top : top + rows, :])
        end_out[f, :, :LANES] = first
        end_out[f, :, LANES:] = last


def note_kernel(strip, got_depth, traces, cells, note_out):
    first = lax.axis_index("depth") == 0
    beside = got_depth[got_depth.shape[0] - STRIP :, :]
    beside = jnp.concatenate([beside[:, :LANES], beside[:, LANES:]], axis=0)
    seen = jnp.concatenate([traces[:, :LANES], traces[:, LANES:]], axis=0)
    value = jnp.where(first, strip[...], beside)
    row = row_ids(2 * STRIP, LANES)
    for i, place in enumerate(CELL_ROWS):
        cell = cells[i // 2][:, LANES * (i % 2) : LANES * (i % 2 + 1)].astype(F32)
        value = jnp.where((row == place) & first, cell, value)
    block = jnp.concatenate([value, seen], axis=0)
    for k in range(note_out.shape[0]):
        note_out[k] = block


def relay_kernel(notes, rest, notes_out):
    del rest
    notes_out[...] = notes[...]


def three(value):
    high = value.astype(BF16)
    rest = value - high.astype(F32)
    middle = rest.astype(BF16)
    low = (rest - middle.astype(F32)).astype(BF16)
    return [high, middle, low]


def add_up(value, count):
    return (value[2 * count : 3 * count] + value[count : 2 * count]) + value[:count]


BATCH = 5
OWN = LANES - 2 * HALO


def strip_window(f, low, high, base, offset, tracks, columns):
    lane = lane_ids(STRIP)
    part = lax.div(offset + lane, columns)
    spot = base * columns + offset + lane
    source, q = (low, high)[f // 4], f % 4
    value = jnp.zeros((STRIP, LANES), F32)
    for step in range(3):
        who = jnp.clip(base + step, 0, tracks - 1)
        block = source[who, STRIP * (q % 2) : STRIP * (q % 2 + 1), :]
        shift = (4 * LANES - offset + columns * step - columns * (q // 2)) % LANES
        value = jnp.where(part == step, pltpu.roll(block, shift, 1), value)
    return jnp.where((spot >= 0) & (spot < tracks * columns), value, 0.0)


def fill_strip(state, media, low, high, first, tracks, columns):
    state[...] = jnp.zeros(state.shape, F32)
    for w in range(BATCH):
        begin = (first + w) * OWN - HALO
        base = (begin + columns) // columns - 1
        offset = begin - base * columns
        values = [strip_window(f, low, high, base, offset, tracks, columns) for f in range(FORWARD)]
        for f in range(5):
            state[f, w, PAD : PAD + STRIP, :] = values[f]
        buoyancy, lame, shear = (NEAR * value for value in values[5:])
        media[0, w] = buoyancy
        media[1, w] = lame + 2.0 * shear
        media[2, w] = lame
        media[3, w] = shear


def strip_steps(state, media):
    def at(f, w, r, by=0):
        return state[f, w, PAD + r + by : PAD + r + by + 8, :]

    strains = [[] for _ in range(BATCH)]
    for moment in range(MOMENTS):
        last = moment == MOMENTS - 1
        for r in (0, 8) if moment < 2 else (0,):
            for w in range(BATCH):
                here = slice(PAD + r, PAD + r + 8)
                xx, xz, zz = at(2, w, r), at(4, w, r), at(3, w, r)
                b = media[0, w, r : r + 8, :]
                near = (xx - turn(xx, 1)) + (xz - at(4, w, r, -1))
                far = (turn(xx, -1) - turn(xx, 2)) + (at(4, w, r, 1) - at(4, w, r, -2))
                state[0, w, here, :] = at(0, w, r) + b * (near + RATIO * far)
                if not last:
                    near = (turn(xz, -1) - xz) + (at(3, w, r, 1) - zz)
                    far = (turn(xz, -2) - turn(xz, 1)) + (at(3, w, r, 2) - at(3, w, r, -1))
                    state[1, w, here, :] = at(1, w, r) + b * (near + RATIO * far)
        for r in (0, 8) if moment < 1 else (0,):
            for w in range(BATCH):
                here = slice(PAD + r, PAD + r + 8)
                vx, vz = at(0, w, r), at(1, w, r)
                exx = (turn(vx, -1) - vx) + RATIO * (turn(vx, -2) - turn(vx, 1))
                if r == 0:
                    strains[w].append(NEAR * exx)
                if not last:
                    ezz = (vz - at(1, w, r, -1)) + RATIO * (at(1, w, r, 1) - at(1, w, r, -2))
                    near = (at(0, w, r, 1) - vx) + (vz - turn(vz, 1))
                    far = (at(0, w, r, 2) - at(0, w, r, -1)) + (turn(vz, -1) - turn(vz, 2))
                    whole, lam, mu = (media[k, w, r : r + 8, :] for k in (1, 2, 3))
                    state[2, w, here, :] = at(2, w, r) + (whole * exx + lam * ezz)
                    state[3, w, here, :] = at(3, w, r) + (lam * exx + whole * ezz)
                    state[4, w, here, :] = at(4, w, r) + mu * (near + RATIO * far)
    return [jnp.concatenate(parts, axis=0) for parts in strains]


def recorded_rates(state, media, low, high, wanted, tracks, columns):
    lane = lane_ids(8 * MOMENTS)
    mine = (lane >= HALO) & (lane < HALO + OWN)

    def body(number, rate):
        first = number * BATCH
        fill_strip(state, media, low, high, first, tracks, columns)
        images = [three(jnp.where(mine, image, 0.0)) for image in strip_steps(state, media)]
        parts = [jnp.concatenate([image[i] for image in images], axis=1) for i in range(3)]
        spots = [
            (first + w) * OWN - HALO + row_ids(LANES, wanted.shape[1]) for w in range(BATCH)
        ]
        hot = (jnp.concatenate(spots, axis=0) == wanted).astype(F32).astype(BF16)
        return rate + jnp.dot(jnp.concatenate(parts, axis=0), hot, preferred_element_type=F32)

    rate = jnp.zeros((3 * 8 * MOMENTS, wanted.shape[1]), F32)
    batches = -(-(-(-tracks * columns // OWN)) // BATCH)
    rate = body(0, rate) if batches == 1 else lax.fori_loop(0, batches, body, rate)
    return add_up(rate, 8 * MOMENTS)


def sums_kernel(tracks, columns, notes, sums_out):
    start = lax.axis_index("track") * columns - EDGE
    group = min(8, tracks)
    row16 = row_ids(IMAGE, LANES)

    def body(number, image):
        weights, hots = [], []
        for k in range(group):
            who = number * group + k
            traces = notes[who, 2 * STRIP :, :]
            places = [notes[who, place : place + 1, :] for place in CELL_ROWS]
            for h in range(2):
                mask = (row16 & 3).astype(F32) == places[2 + h]
                seen = [traces[4 * h + t : 4 * h + t + 1] for t in range(MOMENTS)]
                value = jnp.where(
                    row16 < 8,
                    jnp.where(row16 < 4, seen[0], seen[1]),
                    jnp.where(row16 < 12, seen[2], seen[3]),
                )
                pieces = three(jnp.where(mask, value, 0.0)) + [mask.astype(F32).astype(BF16)]
                weights.append(jnp.concatenate(pieces, axis=0))
                spot = (start + row_ids(LANES, LANES)).astype(F32)
                hots.append((spot == places[h]).astype(F32).astype(BF16))
        return image + lax.dot_general(
            jnp.concatenate(weights, axis=1),
            jnp.concatenate(hots, axis=1),
            (((1,), (1,)), ((), ())),
            preferred_element_type=F32,
        )

    image = jnp.zeros((4 * IMAGE, LANES), F32)
    image = body(0, image) if tracks == group else lax.fori_loop(0, tracks // group, body, image)
    sums_out[:IMAGE, :] = add_up(image, IMAGE)
    sums_out[IMAGE:, :] = image[3 * IMAGE :]


def response(state, media, sources, strains):
    state[...] = jnp.zeros(state.shape, F32)
    tiles = (0, 8)
    sums = [[jnp.zeros((8, LANES), F32) for _ in tiles] for _ in range(2)]

    def at(f, r, by=0):
        return state[f, PAD + r + by : PAD + r + by + 8, :]

    def put(f, r, value):
        state[f, PAD + r : PAD + r + 8, :] = value

    for moment in reversed(range(MOMENTS)):
        put(2, 0, at(2, 0) + sources[moment])
        for r in tiles:
            xx, xz, zz = at(2, r), at(4, r), at(3, r)
            b = media[0, r : r + 8, :]
            near = (xx - turn(xx, 1)) + (xz - at(4, r, -1))
            far = (turn(xx, -1) - turn(xx, 2)) + (at(4, r, 1) - at(4, r, -2))
            put(0, r, at(0, r) + b * (near + RATIO * far))
            near = (turn(xz, -1) - xz) + (at(3, r, 1) - zz)
            far = (turn(xz, -2) - turn(xz, 1)) + (at(3, r, 2) - at(3, r, -1))
            put(1, r, at(1, r) + b * (near + RATIO * far))
        for i, r in enumerate(tiles):
            vx, vz = at(0, r), at(1, r)
            exx = (turn(vx, -1) - vx) + RATIO * (turn(vx, -2) - turn(vx, 1))
            ezz = (vz - at(1, r, -1)) + RATIO * (at(1, r, 1) - at(1, r, -2))
            near = (at(0, r, 1) - vx) + (vz - turn(vz, 1))
            far = (at(0, r, 2) - at(0, r, -1)) + (turn(vz, -1) - turn(vz, 2))
            shear = near + RATIO * far
            fxx, fzz, fxz = (
                strains[j // 8, STRIP * (j % 8) + r : STRIP * (j % 8) + r + 8, :]
                for j in range(3 * moment, 3 * moment + 3)
            )
            sums[0][i] += (fxx + fzz) * (exx + ezz)
            sums[1][i] += 2.0 * (fxx * exx + fzz * ezz) + fxz * shear
            if moment > 0:
                whole, lam, mu = (media[k, r : r + 8, :] for k in (1, 2, 3))
                put(2, r, at(2, r) + (whole * exx + lam * ezz))
                put(3, r, at(3, r) + (lam * exx + whole * ezz))
                put(4, r, at(4, r) + mu * shear)
    return sums[0] + sums[1]


def finish_kernel(
    tracks, columns, notes, beside, sums, obs, cells, base, strains, end,
    lambda_out, mu_out, residual_out, end_out, state, media, low, high, sems,
):
    copy = pltpu.make_async_copy(end, end_out, sems.at[0])
    copy.start()
    depth = lax.axis_index("depth")
    low[...] = jnp.where(depth == 0, notes[...], beside[...])
    high[...] = jnp.where(depth == 0, beside[...], notes[...])
    track = lax.axis_index("track")
    start = track * columns - EDGE
    along, row = cells[0], cells[1]
    channels = along.shape[1]
    wanted = jnp.concatenate([along, start + lax.broadcasted_iota(jnp.int32, (1, LANES), 1)], axis=1)
    seen, count = sums[:IMAGE, :], sums[IMAGE:, :]
    rate = recorded_rates(state, media, low, high, wanted, tracks, columns)
    mask = row_ids(8, channels) == row
    traces = [
        jnp.sum(jnp.where(mask, rate[8 * t : 8 * t + 8, :channels], 0.0), axis=0, keepdims=True)
        - obs[t : t + 1, :]
        for t in range(MOMENTS)
    ]
    residual_out[...] = jnp.where(
        depth == 0, jnp.concatenate(traces[:2], axis=0), jnp.concatenate(traces[2:], axis=0)
    )
    near = jnp.concatenate([rate[8 * t : 8 * t + 4, channels:] for t in range(MOMENTS)], axis=0)
    found = jnp.where(depth == 0, count * near - seen, 0.0)
    nothing = jnp.zeros((8 - FIBRE_ROWS, LANES), F32)
    sources = [
        jnp.concatenate([found[FIBRE_ROWS * t : FIBRE_ROWS * (t + 1)], nothing], axis=0) for t in range(MOMENTS)
    ]
    own = [
        NEAR * strip_window(f, low, high, track - 1, columns - EDGE, tracks, columns) for f in (5, 6, 7)
    ]
    media[0, 0] = own[0]
    media[1, 0] = own[1] + 2.0 * own[2]
    media[2, 0] = own[1]
    media[3, 0] = own[2]
    added = response(state.at[:, 0], media.at[:, 0], sources, strains)
    rows = base.shape[1]
    added = jnp.concatenate(added + [jnp.zeros((LANES - 32, LANES), F32)], axis=0).T[EDGE : EDGE + rows]
    lane = lane_ids(rows)
    for k, out in enumerate((lambda_out, mu_out)):
        more = jnp.where(lane < STRIP, turn(added, -STRIP * k), 0.0)
        out[:, :LANES] = (NEAR * NEAR) * (base[k, :, :LANES] + more)
        out[:, LANES:] = (NEAR * NEAR) * base[k, :, LANES:]
    copy.wait()


def adjoint_kernel(
    held, got_even, got_odd, got_depth, corner, media, saved, inner_media, inner_saved,
    base_out, strains_out, state, sums,
):
    states, totals = each(state, 3, 1), each(sums, 3, 1)
    rows = held.shape[1]
    load_state(states, FORWARD, (0, 1, 2), held, got_even, got_odd, got_depth, corner)
    medias = each(media, 2, 1) + each(inner_media, 1, 1)
    saveds = each(saved, 2, 2) + each(inner_saved, 1, 2)
    sums[...] = jnp.zeros(sums.shape, F32)
    for step in range(MOMENTS):
        fast, slow = spans(step, rows)
        moment = MOMENTS - 1 - step
        velocities(states, medias, fast)

        def gather(i, r, exx, ezz, shear):
            if 0 <= r < rows:
                fxx, fzz, fxz = (saveds[i][moment, k, r : r + 8, :] for k in range(3))
                totals[i][0, r : r + 8, :] += (fxx + fzz) * (exx + ezz)
                totals[i][1, r : r + 8, :] += 2.0 * (fxx * exx + fzz * ezz) + fxz * shear

        stresses(states, medias, slow, step < MOMENTS - 1, gather)
    for k in range(2):
        first, last = joined(*(total[k] for total in totals))
        base_out[k, :, :LANES] = first
        base_out[k, :, LANES:] = last
    lane = lane_ids(rows)
    for group in range(2):
        packed = jnp.zeros((rows, LANES), F32)
        for j in range(8 * group, min(8 * group + 8, 3 * MOMENTS)):
            spot = STRIP * (j % 8)
            here = (lane >= spot) & (lane < spot + STRIP)
            packed = jnp.where(here, turn(saveds[0][j // 3, j % 3], spot - EDGE), packed)
        turned = packed.T
        strains_out[group] = turn(jnp.concatenate([turned, jnp.zeros_like(turned)], axis=1), EDGE)


def per_device(
    velocity,
    stress,
    adjoint_velocity,
    adjoint_stress,
    buoyancy,
    lame_lambda,
    shear_modulus,
    observed,
    owner_track,
    fibre_cell,
):
    tracks = lax.axis_size("track")
    rows, depth_cells = buoyancy.shape
    moments, channels = observed.shape
    owner = owner_track.reshape(1, channels)
    cell = fibre_cell.reshape(1, channels)
    pinned = lambda array: pltpu.with_memory_space_constraint(array, pltpu.HBM)
    arrays = (velocity, stress, adjoint_velocity, adjoint_stress, buoyancy, lame_lambda, shear_modulus)
    arrays = tuple(pinned(array) for array in arrays)
    channel_arrays = (pinned(observed), pinned(owner), pinned(cell))
    extent = rows + 2 * EDGE
    block = jax.ShapeDtypeStruct((rows, depth_cells), F32)
    length = BASE + HALO * FIELDS + BASE
    edges = jax.ShapeDtypeStruct((length + (-length) % 8, depth_cells), F32)
    inside = pl.BlockSpec(memory_space=VMEM)
    outside = pl.BlockSpec(memory_space=pltpu.HBM)
    anywhere = pl.BlockSpec(memory_space=pl.ANY)
    held, held_adj, to_depth, to_even, to_odd, strip, traces, cells = pl.pallas_call(
        pack_kernel,
        out_shape=(
            jax.ShapeDtypeStruct((FORWARD, rows, depth_cells), F32),
            jax.ShapeDtypeStruct((ADJOINT, rows, depth_cells), F32),
            jax.ShapeDtypeStruct((rows + STRIP, depth_cells), F32),
            edges,
            edges,
            jax.ShapeDtypeStruct((2 * STRIP, LANES), F32),
            jax.ShapeDtypeStruct((moments, channels), F32),
            jax.ShapeDtypeStruct((2, 1, channels), jnp.int32),
        ),
        in_specs=[outside] * 10,
        out_specs=(inside,) * 8,
        scratch_shapes=[VMEM((2, 1, channels), jnp.int32), pltpu.SemaphoreType.DMA((10,))],
        compiler_params=params(),
        cost_estimate=cost(5),
        name="pack",
    )(*arrays, *channel_arrays)
    depth_swap = [(0, 1), (1, 0)]
    got_depth = lax.ppermute(to_depth, "depth", depth_swap)
    swap = lambda k: [pair for i in range(k, tracks - 1, 2) for pair in ((i, i + 1), (i + 1, i))]
    got_odd = lax.ppermute(to_odd, "track", swap(1))
    got_even = lax.ppermute(to_even, "track", swap(0))

    def state_of(planes):
        return VMEM((5, planes, extent + 2 * PAD, LANES), F32)

    note = pl.pallas_call(
        note_kernel,
        out_shape=jax.ShapeDtypeStruct((tracks, 2 * STRIP + 8, LANES), F32),
        in_specs=[inside] * 4,
        out_specs=inside,
        compiler_params=params(),
        cost_estimate=cost(1),
        name="note",
    )(strip, got_depth, traces, cells)
    notes = lax.all_to_all(note, "track", split_axis=0, concat_axis=0, tiled=True)

    corner = pl.pallas_call(
        corner_kernel,
        out_shape=jax.ShapeDtypeStruct((2 * EDGE, depth_cells), F32),
        in_specs=[inside] * 2,
        out_specs=inside,
        compiler_params=params(),
        cost_estimate=cost(1),
        name="corners",
    )(got_even, got_odd)
    got_corner = lax.ppermute(corner, "depth", depth_swap)

    def media_of(planes):
        return jax.ShapeDtypeStruct((4, planes, extent, LANES), F32)

    def saved_of(planes):
        return jax.ShapeDtypeStruct((moments, 3, planes, rows, LANES), F32)

    media, saved, end = pl.pallas_call(
        forward_kernel,
        out_shape=(media_of(2), saved_of(2), jax.ShapeDtypeStruct((2, 2, rows, LANES), F32)),
        in_specs=[inside] * 3,
        out_specs=(inside,) * 3,
        scratch_shapes=[state_of(2)],
        compiler_params=params(),
        cost_estimate=cost(20),
        name="forward",
    )(held, got_even, got_odd)

    inner_media, inner_saved, end = pl.pallas_call(
        forward_inner_kernel,
        out_shape=(media_of(1), saved_of(1), jax.ShapeDtypeStruct(velocity.shape, F32)),
        in_specs=[inside] * 6,
        out_specs=(inside,) * 3,
        scratch_shapes=[state_of(1)],
        compiler_params=params(),
        cost_estimate=cost(20),
        name="forward_inner",
    )(held, got_even, got_odd, got_depth, got_corner, end)

    base, strains = pl.pallas_call(
        adjoint_kernel,
        out_shape=(
            jax.ShapeDtypeStruct((2, rows, depth_cells), F32),
            jax.ShapeDtypeStruct((2, LANES, LANES), F32),
        ),
        in_specs=[inside] * 9,
        out_specs=(inside,) * 2,
        scratch_shapes=[state_of(3), VMEM((2, 3, rows, LANES), F32)],
        compiler_params=params(),
        cost_estimate=cost(20),
        name="adjoint",
    )(held_adj, got_even, got_odd, got_depth, got_corner, media, saved, inner_media, inner_saved)

    mine = pl.pallas_call(
        relay_kernel,
        out_shape=jax.ShapeDtypeStruct(note.shape, F32),
        in_specs=[inside, anywhere],
        out_specs=inside,
        compiler_params=params(),
        cost_estimate=cost(1),
        name="relay",
    )(notes, base)
    beside = lax.ppermute(mine, "depth", depth_swap)

    sums = pl.pallas_call(
        lambda *refs: sums_kernel(tracks, rows, *refs),
        out_shape=jax.ShapeDtypeStruct((2 * IMAGE, LANES), F32),
        in_specs=[inside],
        out_specs=inside,
        compiler_params=params(),
        cost_estimate=cost(20),
        name="sums",
    )(mine)

    gradient_lambda, gradient_mu, residual, velocity_end = pl.pallas_call(
        lambda *refs: finish_kernel(tracks, rows, *refs),
        out_shape=(
            block,
            block,
            jax.ShapeDtypeStruct((moments // 2, channels), F32),
            jax.ShapeDtypeStruct(velocity.shape, F32),
        ),
        in_specs=[inside] * 8,
        out_specs=(inside, inside, inside, outside),
        scratch_shapes=[
            VMEM((5, BATCH, 2 * PAD + STRIP, LANES), F32),
            VMEM((4, BATCH, STRIP, LANES), F32),
            VMEM(note.shape, F32),
            VMEM(note.shape, F32),
            pltpu.SemaphoreType.DMA((1,)),
        ],
        compiler_params=params(),
        cost_estimate=cost(2),
        name="finish",
    )(mine, beside, sums, traces, cells, base, strains, end)
    return gradient_lambda, gradient_mu, velocity_end, residual


def solution(mesh):
    return jax.shard_map(
        per_device,
        mesh=mesh,
        in_specs=(
            P("shots", "track", "depth"),
            P("shots", "track", "depth"),
            P("shots", "track", "depth"),
            P("shots", "track", "depth"),
            P("track", "depth"),
            P("track", "depth"),
            P("track", "depth"),
            P("shots", "track"),
            P("track", None),
            P("track"),
        ),
        out_specs=(
            P(("shots", "track"), "depth"),
            P(("shots", "track"), "depth"),
            P("shots", "track", "depth"),
            P(("shots", "depth"), "track"),
        ),
        check_vma=False,
    )
```

```python
import jax
import jax.numpy as jnp
from jax import lax
from jax.experimental import pallas as pl
from jax.experimental.pallas import tpu as pltpu
from jax.sharding import PartitionSpec as P

FIBRE_ROWS = 4
NEAR = 9.0 / 8.0
RATIO = -1.0 / 27.0
HALO = 12
EDGE = 16
LANES = 128
PAD = 8
FORWARD = 8
ADJOINT = 5
FIELDS = FORWARD + ADJOINT
STRIP = 16
CELL_ROWS = (14, 15, 30, 31)
EXTRA = 168
BASE = EDGE - HALO
MOMENTS = 4
IMAGE = MOMENTS * FIBRE_ROWS
VMEM = pltpu.VMEM
F32 = jnp.float32
BF16 = jnp.bfloat16


def lane_ids(rows):
    return lax.broadcasted_iota(jnp.int32, (rows, LANES), 1)


def row_ids(rows, columns):
    return lax.broadcasted_iota(jnp.int32, (rows, columns), 0)


def params():
    return pltpu.CompilerParams(vmem_limit_bytes=16 * 1024 * 1024)


def cost(microseconds):
    return pl.CostEstimate(flops=int(microseconds * 1e9), bytes_accessed=1 << 20, transcendentals=0)


def turn(value, by):
    return pltpu.roll(value, by % LANES, 1)


def is_even():
    return lax.rem(lax.axis_index("track"), 2) == 0


def fetch(sources, targets, sems):
    copies = [pltpu.make_async_copy(s, t, sems.at[i]) for i, (s, t) in enumerate(zip(sources, targets))]
    for copy in copies:
        copy.start()
    return copies


def pack_kernel(*refs):
    sources, channel_arrays = refs[:7], refs[7:10]
    held, held_adj, depth_out, edge_outs, strip_out, traces_out, cells_out = *refs[10:13], refs[13:15], *refs[15:18]
    rows_out, numbers, sems = refs[18:]
    targets = (
        held.at[pl.ds(0, 2)],
        held.at[pl.ds(2, 3)],
        held.at[5],
        held.at[6],
        held.at[7],
        held_adj.at[pl.ds(0, 2)],
        held_adj.at[pl.ds(2, 3)],
        traces_out,
        numbers.at[0],
        numbers.at[1],
    )
    copies = fetch((*sources[:2], *sources[4:], *sources[2:4], *channel_arrays), targets, sems)
    depth = lax.axis_index("depth")
    even = is_even()
    rows = held.shape[1]
    lane = lane_ids(rows)
    tail = BASE + HALO * FIELDS
    for out in edge_outs:
        out[:BASE, :] = jnp.zeros((BASE, 2 * LANES), F32)
        out[tail:, :] = jnp.zeros((out.shape[0] - tail, 2 * LANES), F32)
    for copy in copies:
        copy.wait()
    packed = [jnp.zeros((rows, LANES), F32) for _ in range(2)]
    strip = jnp.zeros((rows, LANES), F32)
    for f in range(FIELDS):
        ref = held.at[f] if f < FORWARD else held_adj.at[f - FORWARD]
        first, last = ref[:, :LANES], ref[:, LANES:]
        group, place = divmod(f, FORWARD)
        spot = EDGE * place
        here = (lane >= spot) & (lane < spot + EDGE)
        edge = jnp.where(depth == 0, last, first)
        shift = lax.rem(spot + EDGE * (1 - depth), LANES)
        packed[group] = jnp.where(here, pltpu.roll(edge, shift, 1), packed[group])
        if f < FORWARD:
            strip = jnp.where(here, turn(first, spot), strip)
        low, high = ref[:HALO, :], ref[rows - HALO :, :]
        at = BASE + HALO * f
        edge_outs[0][at : at + HALO, :] = jnp.where(even, high, low)
        edge_outs[1][at : at + HALO, :] = jnp.where(even, low, high)
    depth_out[:rows, :LANES] = packed[0]
    depth_out[:rows, LANES:] = packed[1]
    rows_out[...] = strip
    low, high = strip[HALO : 2 * HALO], strip[rows - 2 * HALO : rows - HALO]
    edge_outs[0][EXTRA : EXTRA + HALO, :LANES] = jnp.where(even, high, low)
    edge_outs[1][EXTRA : EXTRA + HALO, :LANES] = jnp.where(even, low, high)
    turned = strip.T
    strip_out[:, :rows] = turned[: 2 * STRIP]
    strip_out[:, rows:] = turned[2 * STRIP : 4 * STRIP]
    depth_out[rows:, :rows] = turned[4 * STRIP : 5 * STRIP]
    depth_out[rows:, rows : 2 * rows] = turned[6 * STRIP : 7 * STRIP]
    depth_out[rows:, 2 * rows : 3 * rows] = turned[5 * STRIP : 6 * STRIP]
    depth_out[rows:, 3 * rows :] = turned[7 * STRIP :]
    cells_out[0] = numbers[0] * rows + lax.shift_right_logical(numbers[1], 2)
    cells_out[1] = numbers[1] & 3


def edge_rows(f, side, got_even, got_odd):
    at = BASE + HALO * f
    span = slice(at - BASE, at + HALO) if side == 0 else slice(at, at + EDGE)
    use_odd = is_even() if side == 0 else ~is_even()
    return jnp.where(use_odd, got_odd[span, :], got_even[span, :])


def corner_kernel(got_even, got_odd, corner_out):
    depth = lax.axis_index("depth")
    lane = lane_ids(EDGE)
    for side in range(2):
        packed = [jnp.zeros((EDGE, LANES), F32) for _ in range(2)]
        for f in range(FIELDS):
            group, place = divmod(f, FORWARD)
            spot = EDGE * place
            value = edge_rows(f, side, got_even, got_odd)
            edge = jnp.where(depth == 0, value[:, LANES:], value[:, :LANES])
            shift = lax.rem(spot + EDGE * (1 - depth), LANES)
            here = (lane >= spot) & (lane < spot + EDGE)
            packed[group] = jnp.where(here, pltpu.roll(edge, shift, 1), packed[group])
        corner_out[EDGE * side : EDGE * (side + 1), :LANES] = packed[0]
        corner_out[EDGE * side : EDGE * (side + 1), LANES:] = packed[1]


def window(plane, f, value, halo):
    depth = lax.axis_index("depth")
    surface = depth == 0
    first, last = value[:, :LANES], value[:, LANES:]
    lane = lane_ids(first.shape[0])
    low = jnp.where(surface, lane, LANES - 1 - lane)
    if plane == 0:
        shift = jnp.where(surface, EDGE, LANES - EDGE)
        return jnp.where(low >= EDGE, pltpu.roll(jnp.where(surface, first, last), shift, 1), 0.0)
    if plane == 1:
        return jnp.where(lane < LANES // 2, turn(first, LANES // 2), turn(last, LANES // 2))
    shift = jnp.where(surface, LANES - EDGE, EDGE)
    beside = lax.rem(LANES - EDGE * (f % FORWARD) + (LANES - EDGE) * (1 - depth), LANES)
    own = pltpu.roll(jnp.where(surface, last, first), shift, 1)
    return jnp.where(low < LANES - EDGE, own, pltpu.roll(halo, beside, 1))


def field_windows(f, planes, held, got_even, got_odd, got_depth=None, corner=None):
    rows = held.shape[1]
    col = LANES * (f // FORWARD)
    blocks = (
        (0, edge_rows(f, 0, got_even, got_odd), corner, 0),
        (EDGE, held[f % FORWARD], got_depth, 0),
        (EDGE + rows, edge_rows(f, 1, got_even, got_odd), corner, EDGE),
    )
    found = [[] for _ in planes]
    for at, value, halo, start in blocks:
        if halo is not None:
            halo = halo[start : start + value.shape[0], col : col + LANES]
        for parts, p in zip(found, planes):
            parts.append((at, window(p, f, value, halo)))
    return found


def joined(outer, middle, inner):
    surface = lax.axis_index("depth") == 0
    lane = lane_ids(outer.shape[0])
    first, last = jnp.where(surface, outer, inner), jnp.where(surface, inner, outer)
    middle = turn(middle, LANES // 2)
    return jnp.where(lane < 88, turn(first, -EDGE), middle), jnp.where(lane < 40, middle, turn(last, EDGE))


def load_state(states, base, planes, held, *got):
    extent = held.shape[1] + 2 * EDGE
    for f in range(5):
        for state, parts in zip(states, field_windows(base + f, planes, held, *got)):
            state[f, :PAD, :] = jnp.zeros((PAD, LANES), F32)
            state[f, PAD + extent :, :] = jnp.zeros((PAD, LANES), F32)
            for at, part in parts:
                state[f, PAD + at : PAD + at + part.shape[0], :] = part


def velocities(states, medias, span):
    for r in range(8 * span[0], 8 * span[1], 8):
        for state, media in zip(states, medias):

            def at(f, by=0):
                return state[f, r + PAD + by : r + PAD + by + 8, :]

            xx, xz, zz = at(2), at(4), at(3)
            b = media[0, r : r + 8, :]
            near = (xx - at(2, -1)) + (xz - turn(xz, 1))
            far = (at(2, 1) - at(2, -2)) + (turn(xz, -1) - turn(xz, 2))
            state[0, r + PAD : r + PAD + 8, :] = at(0) + b * (near + RATIO * far)
            near = (at(4, 1) - xz) + (turn(zz, -1) - zz)
            far = (at(4, 2) - at(4, -1)) + (turn(zz, -2) - turn(zz, 1))
            state[1, r + PAD : r + PAD + 8, :] = at(1) + b * (near + RATIO * far)


def stresses(states, medias, span, update, keep):
    for r in range(8 * span[0], 8 * span[1], 8):
        for i, (state, media) in enumerate(zip(states, medias)):

            def at(f, by=0):
                return state[f, r + PAD + by : r + PAD + by + 8, :]

            vx, vz = at(0), at(1)
            exx = (at(0, 1) - vx) + RATIO * (at(0, 2) - at(0, -1))
            ezz = (vz - turn(vz, 1)) + RATIO * (turn(vz, -1) - turn(vz, 2))
            near = (turn(vx, -1) - vx) + (vz - at(1, -1))
            far = (turn(vx, -2) - turn(vx, 1)) + (at(1, 1) - at(1, -2))
            shear = near + RATIO * far
            keep(i, r - EDGE, exx, ezz, shear)
            if update:
                whole, lam, mu = (media[k, r : r + 8, :] for k in (1, 2, 3))
                state[2, r + PAD : r + PAD + 8, :] = at(2) + (whole * exx + lam * ezz)
                state[3, r + PAD : r + PAD + 8, :] = at(3) + (lam * exx + whole * ezz)
                state[4, r + PAD : r + PAD + 8, :] = at(4) + mu * shear


def spans(step, rows):
    tiles = (rows + 2 * EDGE) // 8
    if step == 0:
        return (0, tiles), (0, tiles)
    inner = (1, tiles - 1)
    return inner, inner if step < MOMENTS - 1 else (EDGE // 8, tiles - EDGE // 8)


def run_forward(states, medias, saveds, planes, held, *got):
    rows = held.shape[1]
    given = [field_windows(f, planes, held, *got) for f in (5, 6, 7)]
    for i, media in enumerate(medias):
        for k in range(3):
            at = given[0][i][k][0]
            b, lam, mu = (NEAR * given[m][i][k][1] for m in range(3))
            span = slice(at, at + b.shape[0])
            media[0, span, :] = b
            media[1, span, :] = lam + 2.0 * mu
            media[2, span, :] = lam
            media[3, span, :] = mu
    load_state(states, 0, planes, held, *got)
    for step in range(MOMENTS):
        fast, slow = spans(step, rows)
        velocities(states, medias, fast)

        def save(i, r, exx, ezz, shear):
            if 0 <= r < rows:
                saveds[i][step, 0, r : r + 8, :] = exx
                saveds[i][step, 1, r : r + 8, :] = ezz
                saveds[i][step, 2, r : r + 8, :] = shear

        stresses(states, medias, slow, step < MOMENTS - 1, save)


def each(ref, count, axis):
    return [ref.at[(slice(None),) * axis + (i,)] for i in range(count)]


def forward_kernel(held, got_even, got_odd, media, saved, end_out, state):
    states = each(state, 2, 1)
    run_forward(states, each(media, 2, 1), each(saved, 2, 2), (0, 1), held, got_even, got_odd)
    top, rows = PAD + EDGE, held.shape[1]
    for f in range(2):
        for i in range(2):
            end_out[f, i] = states[i][f, top : top + rows, :]


def forward_inner_kernel(held, got_even, got_odd, got_depth, corner, end, media, saved, end_out, state):
    states = each(state, 1, 1)
    run_forward(
        states, each(media, 1, 1), each(saved, 1, 2), (2,), held, got_even, got_odd, got_depth, corner
    )
    top, rows = PAD + EDGE, held.shape[1]
    for f in range(2):
        first, last = joined(end[f, 0], end[f, 1], states[0][f, top : top + rows, :])
        end_out[f, :, :LANES] = first
        end_out[f, :, LANES:] = last


def note_kernel(strip, got_depth, traces, cells, note_out):
    first = lax.axis_index("depth") == 0
    beside = got_depth[got_depth.shape[0] - STRIP :, :]
    beside = jnp.concatenate([beside[:, :LANES], beside[:, LANES:]], axis=0)
    seen = jnp.concatenate([traces[:, :LANES], traces[:, LANES:]], axis=0)
    value = jnp.where(first, strip[...], beside)
    row = row_ids(2 * STRIP, LANES)
    for i, place in enumerate(CELL_ROWS):
        cell = cells[i // 2][:, LANES * (i % 2) : LANES * (i % 2 + 1)].astype(F32)
        value = jnp.where((row == place) & first, cell, value)
    block = jnp.concatenate([value, seen], axis=0)
    for k in range(note_out.shape[0]):
        note_out[k] = block


def relay_kernel(notes, base, rates, notes_out):
    del base, rates
    notes_out[...] = notes[...]


def three(value):
    high = value.astype(BF16)
    rest = value - high.astype(F32)
    middle = rest.astype(BF16)
    low = (rest - middle.astype(F32)).astype(BF16)
    return [high, middle, low]


def add_up(value, count):
    return (value[2 * count : 3 * count] + value[count : 2 * count]) + value[:count]


BATCH = 5
OWN = LANES - 2 * HALO


def strip_window(f, low, high, base, offset, tracks, columns):
    lane = lane_ids(STRIP)
    part = lax.div(offset + lane, columns)
    spot = base * columns + offset + lane
    source, q = (low, high)[f // 4], f % 4
    value = jnp.zeros((STRIP, LANES), F32)
    for step in range(3):
        who = jnp.clip(base + step, 0, tracks - 1)
        block = source[who, STRIP * (q % 2) : STRIP * (q % 2 + 1), :]
        shift = (4 * LANES - offset + columns * step - columns * (q // 2)) % LANES
        value = jnp.where(part == step, pltpu.roll(block, shift, 1), value)
    return jnp.where((spot >= 0) & (spot < tracks * columns), value, 0.0)


def fill_strip(state, media, low, high, first, tracks, columns):
    state[...] = jnp.zeros(state.shape, F32)
    for w in range(BATCH):
        begin = (first + w) * OWN - HALO
        base = (begin + columns) // columns - 1
        offset = begin - base * columns
        values = [strip_window(f, low, high, base, offset, tracks, columns) for f in range(FORWARD)]
        for f in range(5):
            state[f, w, PAD : PAD + STRIP, :] = values[f]
        buoyancy, lame, shear = (NEAR * value for value in values[5:])
        media[0, w] = buoyancy
        media[1, w] = lame + 2.0 * shear
        media[2, w] = lame
        media[3, w] = shear


def strip_steps(state, media):
    def at(f, w, r, by=0):
        return state[f, w, PAD + r + by : PAD + r + by + 8, :]

    count = state.shape[1]
    strains = [[] for _ in range(count)]
    for moment in range(MOMENTS):
        last = moment == MOMENTS - 1
        for r in (0, 8) if moment < 2 else (0,):
            for w in range(count):
                here = slice(PAD + r, PAD + r + 8)
                xx, xz, zz = at(2, w, r), at(4, w, r), at(3, w, r)
                b = media[0, w, r : r + 8, :]
                near = (xx - turn(xx, 1)) + (xz - at(4, w, r, -1))
                far = (turn(xx, -1) - turn(xx, 2)) + (at(4, w, r, 1) - at(4, w, r, -2))
                state[0, w, here, :] = at(0, w, r) + b * (near + RATIO * far)
                if not last:
                    near = (turn(xz, -1) - xz) + (at(3, w, r, 1) - zz)
                    far = (turn(xz, -2) - turn(xz, 1)) + (at(3, w, r, 2) - at(3, w, r, -1))
                    state[1, w, here, :] = at(1, w, r) + b * (near + RATIO * far)
        for r in (0, 8) if moment < 1 else (0,):
            for w in range(count):
                here = slice(PAD + r, PAD + r + 8)
                vx, vz = at(0, w, r), at(1, w, r)
                exx = (turn(vx, -1) - vx) + RATIO * (turn(vx, -2) - turn(vx, 1))
                if r == 0:
                    strains[w].append(NEAR * exx)
                if not last:
                    ezz = (vz - at(1, w, r, -1)) + RATIO * (at(1, w, r, 1) - at(1, w, r, -2))
                    near = (at(0, w, r, 1) - vx) + (vz - turn(vz, 1))
                    far = (at(0, w, r, 2) - at(0, w, r, -1)) + (turn(vz, -1) - turn(vz, 2))
                    whole, lam, mu = (media[k, w, r : r + 8, :] for k in (1, 2, 3))
                    state[2, w, here, :] = at(2, w, r) + (whole * exx + lam * ezz)
                    state[3, w, here, :] = at(3, w, r) + (lam * exx + whole * ezz)
                    state[4, w, here, :] = at(4, w, r) + mu * (near + RATIO * far)
    return [jnp.concatenate(parts, axis=0) for parts in strains]


def recorded_rates(state, media, low, high, wanted, tracks, columns):
    lane = lane_ids(8 * MOMENTS)
    mine = (lane >= HALO) & (lane < HALO + OWN)

    def body(number, rate):
        first = number * BATCH
        fill_strip(state, media, low, high, first, tracks, columns)
        images = [three(jnp.where(mine, image, 0.0)) for image in strip_steps(state, media)]
        parts = [jnp.concatenate([image[i] for image in images], axis=1) for i in range(3)]
        spots = [
            (first + w) * OWN - HALO + row_ids(LANES, wanted.shape[1]) for w in range(BATCH)
        ]
        hot = (jnp.concatenate(spots, axis=0) == wanted).astype(F32).astype(BF16)
        return rate + jnp.dot(jnp.concatenate(parts, axis=0), hot, preferred_element_type=F32)

    rate = jnp.zeros((3 * 8 * MOMENTS, wanted.shape[1]), F32)
    batches = -(-(-(-tracks * columns // OWN)) // BATCH)
    rate = body(0, rate) if batches == 1 else lax.fori_loop(0, batches, body, rate)
    return add_up(rate, 8 * MOMENTS)


def sums_kernel(tracks, columns, notes, sums_out):
    start = lax.axis_index("track") * columns - EDGE
    group = min(8, tracks)
    row16 = row_ids(IMAGE, LANES)

    def body(number, image):
        weights, hots = [], []
        for k in range(group):
            who = number * group + k
            traces = notes[who, 2 * STRIP :, :]
            places = [notes[who, place : place + 1, :] for place in CELL_ROWS]
            for h in range(2):
                mask = (row16 & 3).astype(F32) == places[2 + h]
                seen = [traces[4 * h + t : 4 * h + t + 1] for t in range(MOMENTS)]
                value = jnp.where(
                    row16 < 8,
                    jnp.where(row16 < 4, seen[0], seen[1]),
                    jnp.where(row16 < 12, seen[2], seen[3]),
                )
                pieces = three(jnp.where(mask, value, 0.0)) + [mask.astype(F32).astype(BF16)]
                weights.append(jnp.concatenate(pieces, axis=0))
                spot = (start + row_ids(LANES, LANES)).astype(F32)
                hots.append((spot == places[h]).astype(F32).astype(BF16))
        return image + lax.dot_general(
            jnp.concatenate(weights, axis=1),
            jnp.concatenate(hots, axis=1),
            (((1,), (1,)), ((), ())),
            preferred_element_type=F32,
        )

    image = jnp.zeros((4 * IMAGE, LANES), F32)
    image = body(0, image) if tracks == group else lax.fori_loop(0, tracks // group, body, image)
    sums_out[:IMAGE, :] = add_up(image, IMAGE)
    sums_out[IMAGE:, :] = image[3 * IMAGE :]


def response(state, media, sources, strains):
    state[...] = jnp.zeros(state.shape, F32)
    tiles = (0, 8)
    sums = [[jnp.zeros((8, LANES), F32) for _ in tiles] for _ in range(2)]

    def at(f, r, by=0):
        return state[f, PAD + r + by : PAD + r + by + 8, :]

    def put(f, r, value):
        state[f, PAD + r : PAD + r + 8, :] = value

    for moment in reversed(range(MOMENTS)):
        put(2, 0, at(2, 0) + sources[moment])
        for r in tiles:
            xx, xz, zz = at(2, r), at(4, r), at(3, r)
            b = media[0, r : r + 8, :]
            near = (xx - turn(xx, 1)) + (xz - at(4, r, -1))
            far = (turn(xx, -1) - turn(xx, 2)) + (at(4, r, 1) - at(4, r, -2))
            put(0, r, at(0, r) + b * (near + RATIO * far))
            near = (turn(xz, -1) - xz) + (at(3, r, 1) - zz)
            far = (turn(xz, -2) - turn(xz, 1)) + (at(3, r, 2) - at(3, r, -1))
            put(1, r, at(1, r) + b * (near + RATIO * far))
        for i, r in enumerate(tiles):
            vx, vz = at(0, r), at(1, r)
            exx = (turn(vx, -1) - vx) + RATIO * (turn(vx, -2) - turn(vx, 1))
            ezz = (vz - at(1, r, -1)) + RATIO * (at(1, r, 1) - at(1, r, -2))
            near = (at(0, r, 1) - vx) + (vz - turn(vz, 1))
            far = (at(0, r, 2) - at(0, r, -1)) + (turn(vz, -1) - turn(vz, 2))
            shear = near + RATIO * far
            fxx, fzz, fxz = (
                strains[j // 8, STRIP * (j % 8) + r : STRIP * (j % 8) + r + 8, :]
                for j in range(3 * moment, 3 * moment + 3)
            )
            sums[0][i] += (fxx + fzz) * (exx + ezz)
            sums[1][i] += 2.0 * (fxx * exx + fzz * ezz) + fxz * shear
            if moment > 0:
                whole, lam, mu = (media[k, r : r + 8, :] for k in (1, 2, 3))
                put(2, r, at(2, r) + (whole * exx + lam * ezz))
                put(3, r, at(3, r) + (lam * exx + whole * ezz))
                put(4, r, at(4, r) + mu * shear)
    return sums[0] + sums[1]


def fibre_kernel(strip, got_even, got_odd, rates_out, media_out, state, media, rows_in):
    rows = strip.shape[0]
    rows_in[...] = jnp.zeros(rows_in.shape, F32)
    rows_in[EDGE : EDGE + rows, :] = strip[...]
    lane = lane_ids(HALO)
    for side in range(2):
        use_odd = is_even() if side == 0 else ~is_even()
        near = jnp.zeros((HALO, LANES), F32)
        for f in range(FORWARD):
            span = slice(BASE + HALO * f, BASE + HALO * (f + 1))
            value = jnp.where(use_odd, got_odd[span, :LANES], got_even[span, :LANES])
            here = (lane >= STRIP * f) & (lane < STRIP * (f + 1))
            near = jnp.where(here, turn(value, STRIP * f), near)
        span = slice(EXTRA, EXTRA + HALO)
        far = jnp.where(use_odd, got_odd[span, :LANES], got_even[span, :LANES])
        if side == 0:
            rows_in[BASE:EDGE, :] = near
            rows_in[:BASE, :] = far[HALO - BASE :]
            rows_in[LANES - (HALO - BASE) :, :] = far[: HALO - BASE]
        else:
            rows_in[EDGE + rows : EDGE + rows + HALO, :] = near
            rows_in[EDGE + rows + HALO : EDGE + rows + 2 * HALO, :] = far
    turned = rows_in[...].T
    values = [turned[STRIP * f : STRIP * (f + 1)] for f in range(FORWARD)]
    state[...] = jnp.zeros(state.shape, F32)
    for f in range(5):
        state[f, 0, PAD : PAD + STRIP, :] = values[f]
    buoyancy, lame, shear = (NEAR * value for value in values[5:])
    for k, value in enumerate((buoyancy, lame + 2.0 * shear, lame, shear)):
        media[k, 0] = value
        media_out[k] = value
    rates_out[...] = strip_steps(state, media)[0]


def gradient_kernel(sums, rates, media, base, strains, end, lambda_out, mu_out, end_out, state, sems):
    copy = pltpu.make_async_copy(end, end_out, sems.at[0])
    copy.start()
    rows = base.shape[1]
    near = jnp.concatenate([rates[8 * t : 8 * t + 4, :] for t in range(MOMENTS)], axis=0)
    lane = lane_ids(IMAGE)
    reached = (lane >= BASE) & (lane < EDGE + rows + HALO) & (lax.axis_index("depth") == 0)
    found = jnp.where(reached, sums[IMAGE:, :] * near - sums[:IMAGE, :], 0.0)
    nothing = jnp.zeros((8 - FIBRE_ROWS, LANES), F32)
    sources = [
        jnp.concatenate([found[FIBRE_ROWS * t : FIBRE_ROWS * (t + 1)], nothing], axis=0) for t in range(MOMENTS)
    ]
    added = response(state, media, sources, strains)
    added = jnp.concatenate(added + [jnp.zeros((LANES - 32, LANES), F32)], axis=0).T[EDGE : EDGE + rows]
    lane = lane_ids(rows)
    for k, out in enumerate((lambda_out, mu_out)):
        more = jnp.where(lane < STRIP, turn(added, -STRIP * k), 0.0)
        out[:, :LANES] = (NEAR * NEAR) * (base[k, :, :LANES] + more)
        out[:, LANES:] = (NEAR * NEAR) * base[k, :, LANES:]
    copy.wait()


def residual_kernel(tracks, columns, notes, beside, obs, cells, residual_out, state, media, low, high):
    depth = lax.axis_index("depth")
    low[...] = jnp.where(depth == 0, notes[...], beside[...])
    high[...] = jnp.where(depth == 0, beside[...], notes[...])
    along, row = cells[0], cells[1]
    channels = along.shape[1]
    rate = recorded_rates(state, media, low, high, along, tracks, columns)
    mask = row_ids(8, channels) == row
    traces = [
        jnp.sum(jnp.where(mask, rate[8 * t : 8 * t + 8], 0.0), axis=0, keepdims=True) - obs[t : t + 1, :]
        for t in range(MOMENTS)
    ]
    residual_out[...] = jnp.where(
        depth == 0, jnp.concatenate(traces[:2], axis=0), jnp.concatenate(traces[2:], axis=0)
    )


def adjoint_kernel(
    held, got_even, got_odd, got_depth, corner, media, saved, inner_media, inner_saved,
    base_out, strains_out, state, sums,
):
    states, totals = each(state, 3, 1), each(sums, 3, 1)
    rows = held.shape[1]
    load_state(states, FORWARD, (0, 1, 2), held, got_even, got_odd, got_depth, corner)
    medias = each(media, 2, 1) + each(inner_media, 1, 1)
    saveds = each(saved, 2, 2) + each(inner_saved, 1, 2)
    sums[...] = jnp.zeros(sums.shape, F32)
    for step in range(MOMENTS):
        fast, slow = spans(step, rows)
        moment = MOMENTS - 1 - step
        velocities(states, medias, fast)

        def gather(i, r, exx, ezz, shear):
            if 0 <= r < rows:
                fxx, fzz, fxz = (saveds[i][moment, k, r : r + 8, :] for k in range(3))
                totals[i][0, r : r + 8, :] += (fxx + fzz) * (exx + ezz)
                totals[i][1, r : r + 8, :] += 2.0 * (fxx * exx + fzz * ezz) + fxz * shear

        stresses(states, medias, slow, step < MOMENTS - 1, gather)
    for k in range(2):
        first, last = joined(*(total[k] for total in totals))
        base_out[k, :, :LANES] = first
        base_out[k, :, LANES:] = last
    lane = lane_ids(rows)
    for group in range(2):
        packed = jnp.zeros((rows, LANES), F32)
        for j in range(8 * group, min(8 * group + 8, 3 * MOMENTS)):
            spot = STRIP * (j % 8)
            here = (lane >= spot) & (lane < spot + STRIP)
            packed = jnp.where(here, turn(saveds[0][j // 3, j % 3], spot - EDGE), packed)
        turned = packed.T
        strains_out[group] = turn(jnp.concatenate([turned, jnp.zeros_like(turned)], axis=1), EDGE)


def per_device(
    velocity,
    stress,
    adjoint_velocity,
    adjoint_stress,
    buoyancy,
    lame_lambda,
    shear_modulus,
    observed,
    owner_track,
    fibre_cell,
):
    tracks = lax.axis_size("track")
    rows, depth_cells = buoyancy.shape
    moments, channels = observed.shape
    owner = owner_track.reshape(1, channels)
    cell = fibre_cell.reshape(1, channels)
    pinned = lambda array: pltpu.with_memory_space_constraint(array, pltpu.HBM)
    arrays = (velocity, stress, adjoint_velocity, adjoint_stress, buoyancy, lame_lambda, shear_modulus)
    arrays = tuple(pinned(array) for array in arrays)
    channel_arrays = (pinned(observed), pinned(owner), pinned(cell))
    extent = rows + 2 * EDGE
    block = jax.ShapeDtypeStruct((rows, depth_cells), F32)
    edges = jax.ShapeDtypeStruct((EXTRA + EDGE, depth_cells), F32)
    inside = pl.BlockSpec(memory_space=VMEM)
    outside = pl.BlockSpec(memory_space=pltpu.HBM)
    anywhere = pl.BlockSpec(memory_space=pl.ANY)
    held, held_adj, to_depth, to_even, to_odd, strip, traces, cells, strip_rows = pl.pallas_call(
        pack_kernel,
        out_shape=(
            jax.ShapeDtypeStruct((FORWARD, rows, depth_cells), F32),
            jax.ShapeDtypeStruct((ADJOINT, rows, depth_cells), F32),
            jax.ShapeDtypeStruct((rows + STRIP, depth_cells), F32),
            edges,
            edges,
            jax.ShapeDtypeStruct((2 * STRIP, LANES), F32),
            jax.ShapeDtypeStruct((moments, channels), F32),
            jax.ShapeDtypeStruct((2, 1, channels), jnp.int32),
            jax.ShapeDtypeStruct((rows, LANES), F32),
        ),
        in_specs=[outside] * 10,
        out_specs=(inside,) * 9,
        scratch_shapes=[VMEM((2, 1, channels), jnp.int32), pltpu.SemaphoreType.DMA((10,))],
        compiler_params=params(),
        cost_estimate=cost(5),
        name="pack",
    )(*arrays, *channel_arrays)
    depth_swap = [(0, 1), (1, 0)]
    got_depth = lax.ppermute(to_depth, "depth", depth_swap)
    swap = lambda k: [pair for i in range(k, tracks - 1, 2) for pair in ((i, i + 1), (i + 1, i))]
    got_odd = lax.ppermute(to_odd, "track", swap(1))
    got_even = lax.ppermute(to_even, "track", swap(0))

    def state_of(planes):
        return VMEM((5, planes, extent + 2 * PAD, LANES), F32)

    note = pl.pallas_call(
        note_kernel,
        out_shape=jax.ShapeDtypeStruct((tracks, 2 * STRIP + 8, LANES), F32),
        in_specs=[inside] * 4,
        out_specs=inside,
        compiler_params=params(),
        cost_estimate=cost(1),
        name="note",
    )(strip, got_depth, traces, cells)
    notes = lax.all_to_all(note, "track", split_axis=0, concat_axis=0, tiled=True)

    corner = pl.pallas_call(
        corner_kernel,
        out_shape=jax.ShapeDtypeStruct((2 * EDGE, depth_cells), F32),
        in_specs=[inside] * 2,
        out_specs=inside,
        compiler_params=params(),
        cost_estimate=cost(1),
        name="corners",
    )(got_even, got_odd)
    got_corner = lax.ppermute(corner, "depth", depth_swap)

    def media_of(planes):
        return jax.ShapeDtypeStruct((4, planes, extent, LANES), F32)

    def saved_of(planes):
        return jax.ShapeDtypeStruct((moments, 3, planes, rows, LANES), F32)

    media, saved, end = pl.pallas_call(
        forward_kernel,
        out_shape=(media_of(2), saved_of(2), jax.ShapeDtypeStruct((2, 2, rows, LANES), F32)),
        in_specs=[inside] * 3,
        out_specs=(inside,) * 3,
        scratch_shapes=[state_of(2)],
        compiler_params=params(),
        cost_estimate=cost(20),
        name="forward",
    )(held, got_even, got_odd)

    inner_media, inner_saved, end = pl.pallas_call(
        forward_inner_kernel,
        out_shape=(media_of(1), saved_of(1), jax.ShapeDtypeStruct(velocity.shape, F32)),
        in_specs=[inside] * 6,
        out_specs=(inside,) * 3,
        scratch_shapes=[state_of(1)],
        compiler_params=params(),
        cost_estimate=cost(20),
        name="forward_inner",
    )(held, got_even, got_odd, got_depth, got_corner, end)

    base, strains = pl.pallas_call(
        adjoint_kernel,
        out_shape=(
            jax.ShapeDtypeStruct((2, rows, depth_cells), F32),
            jax.ShapeDtypeStruct((2, LANES, LANES), F32),
        ),
        in_specs=[inside] * 9,
        out_specs=(inside,) * 2,
        scratch_shapes=[state_of(3), VMEM((2, 3, rows, LANES), F32)],
        compiler_params=params(),
        cost_estimate=cost(20),
        name="adjoint",
    )(held_adj, got_even, got_odd, got_depth, got_corner, media, saved, inner_media, inner_saved)

    rates, own_media = pl.pallas_call(
        fibre_kernel,
        out_shape=(
            jax.ShapeDtypeStruct((8 * MOMENTS, LANES), F32),
            jax.ShapeDtypeStruct((4, STRIP, LANES), F32),
        ),
        in_specs=[inside] * 3,
        out_specs=(inside,) * 2,
        scratch_shapes=[
            VMEM((5, 1, 2 * PAD + STRIP, LANES), F32),
            VMEM((4, 1, STRIP, LANES), F32),
            VMEM((LANES, LANES), F32),
        ],
        compiler_params=params(),
        cost_estimate=cost(5),
        name="fibre",
    )(strip_rows, got_even, got_odd)

    mine = pl.pallas_call(
        relay_kernel,
        out_shape=jax.ShapeDtypeStruct(note.shape, F32),
        in_specs=[inside, anywhere, anywhere],
        out_specs=inside,
        compiler_params=params(),
        cost_estimate=cost(1),
        name="relay",
    )(notes, base, rates)
    beside = lax.ppermute(mine, "depth", depth_swap)

    sums = pl.pallas_call(
        lambda *refs: sums_kernel(tracks, rows, *refs),
        out_shape=jax.ShapeDtypeStruct((2 * IMAGE, LANES), F32),
        in_specs=[inside],
        out_specs=inside,
        compiler_params=params(),
        cost_estimate=cost(20),
        name="sums",
    )(mine)

    gradient_lambda, gradient_mu, velocity_end = pl.pallas_call(
        gradient_kernel,
        out_shape=(block, block, jax.ShapeDtypeStruct(velocity.shape, F32)),
        in_specs=[inside] * 6,
        out_specs=(inside, inside, outside),
        scratch_shapes=[VMEM((5, 2 * PAD + STRIP, LANES), F32), pltpu.SemaphoreType.DMA((1,))],
        compiler_params=params(),
        cost_estimate=cost(20),
        name="gradient",
    )(sums, rates, own_media, base, strains, end)

    residual = pl.pallas_call(
        lambda *refs: residual_kernel(tracks, rows, *refs),
        out_shape=jax.ShapeDtypeStruct((moments // 2, channels), F32),
        in_specs=[inside] * 4,
        out_specs=inside,
        scratch_shapes=[
            VMEM((5, BATCH, 2 * PAD + STRIP, LANES), F32),
            VMEM((4, BATCH, STRIP, LANES), F32),
            VMEM(note.shape, F32),
            VMEM(note.shape, F32),
        ],
        compiler_params=params(),
        cost_estimate=cost(2),
        name="residual",
    )(mine, beside, traces, cells)
    return gradient_lambda, gradient_mu, velocity_end, residual


def solution(mesh):
    return jax.shard_map(
        per_device,
        mesh=mesh,
        in_specs=(
            P("shots", "track", "depth"),
            P("shots", "track", "depth"),
            P("shots", "track", "depth"),
            P("shots", "track", "depth"),
            P("track", "depth"),
            P("track", "depth"),
            P("track", "depth"),
            P("shots", "track"),
            P("track", None),
            P("track"),
        ),
        out_specs=(
            P(("shots", "track"), "depth"),
            P(("shots", "track"), "depth"),
            P("shots", "track", "depth"),
            P(("shots", "depth"), "track"),
        ),
        check_vma=False,
    )
```

```python
import jax
import jax.numpy as jnp
from jax import lax
from jax.experimental import pallas as pl
from jax.experimental.pallas import tpu as pltpu
from jax.sharding import PartitionSpec as P

FIBRE_ROWS = 4
NEAR = 9.0 / 8.0
RATIO = -1.0 / 27.0
HALO = 12
EDGE = 16
LANES = 128
PAD = 8
FORWARD = 8
ADJOINT = 5
FIELDS = FORWARD + ADJOINT
STRIP = 16
CELL_ROWS = (14, 15, 30, 31)
EXTRA = 168
BASE = EDGE - HALO
MOMENTS = 4
IMAGE = MOMENTS * FIBRE_ROWS
VMEM = pltpu.VMEM
F32 = jnp.float32
BF16 = jnp.bfloat16


def lane_ids(rows):
    return lax.broadcasted_iota(jnp.int32, (rows, LANES), 1)


def row_ids(rows, columns):
    return lax.broadcasted_iota(jnp.int32, (rows, columns), 0)


def params():
    return pltpu.CompilerParams(vmem_limit_bytes=16 * 1024 * 1024)


def cost(microseconds):
    return pl.CostEstimate(flops=int(microseconds * 1e9), bytes_accessed=1 << 20, transcendentals=0)


def turn(value, by):
    return pltpu.roll(value, by % LANES, 1)


def is_even():
    return lax.rem(lax.axis_index("track"), 2) == 0


def fetch(sources, targets, sems):
    copies = [pltpu.make_async_copy(s, t, sems.at[i]) for i, (s, t) in enumerate(zip(sources, targets))]
    for copy in copies:
        copy.start()
    return copies


def pack_kernel(*refs):
    sources, channel_arrays = refs[:7], refs[7:10]
    held, held_adj, depth_out, edge_outs, strip_out, traces_out, cells_out = *refs[10:13], refs[13:15], *refs[15:18]
    rows_out, numbers, sems = refs[18:]
    targets = (
        held.at[pl.ds(0, 2)],
        held.at[pl.ds(2, 3)],
        held.at[5],
        held.at[6],
        held.at[7],
        held_adj.at[pl.ds(0, 2)],
        held_adj.at[pl.ds(2, 3)],
        traces_out,
        numbers.at[0],
        numbers.at[1],
    )
    copies = fetch((*sources[:2], *sources[4:], *sources[2:4], *channel_arrays), targets, sems)
    depth = lax.axis_index("depth")
    even = is_even()
    rows = held.shape[1]
    lane = lane_ids(rows)
    tail = BASE + HALO * FIELDS
    for out in edge_outs:
        out[:BASE, :] = jnp.zeros((BASE, 2 * LANES), F32)
        out[tail:, :] = jnp.zeros((out.shape[0] - tail, 2 * LANES), F32)
    for copy in copies:
        copy.wait()
    packed = [jnp.zeros((rows, LANES), F32) for _ in range(2)]
    strip = jnp.zeros((rows, LANES), F32)
    for f in range(FIELDS):
        ref = held.at[f] if f < FORWARD else held_adj.at[f - FORWARD]
        first, last = ref[:, :LANES], ref[:, LANES:]
        group, place = divmod(f, FORWARD)
        spot = EDGE * place
        here = (lane >= spot) & (lane < spot + EDGE)
        edge = jnp.where(depth == 0, last, first)
        shift = lax.rem(spot + EDGE * (1 - depth), LANES)
        packed[group] = jnp.where(here, pltpu.roll(edge, shift, 1), packed[group])
        if f < FORWARD:
            strip = jnp.where(here, turn(first, spot), strip)
        low, high = ref[:HALO, :], ref[rows - HALO :, :]
        at = BASE + HALO * f
        edge_outs[0][at : at + HALO, :] = jnp.where(even, high, low)
        edge_outs[1][at : at + HALO, :] = jnp.where(even, low, high)
    depth_out[:rows, :LANES] = packed[0]
    depth_out[:rows, LANES:] = packed[1]
    rows_out[...] = strip
    low, high = strip[HALO : 2 * HALO], strip[rows - 2 * HALO : rows - HALO]
    edge_outs[0][EXTRA : EXTRA + HALO, :LANES] = jnp.where(even, high, low)
    edge_outs[1][EXTRA : EXTRA + HALO, :LANES] = jnp.where(even, low, high)
    turned = strip.T
    strip_out[:, :rows] = turned[: 2 * STRIP]
    strip_out[:, rows:] = turned[2 * STRIP : 4 * STRIP]
    depth_out[rows:, :rows] = turned[4 * STRIP : 5 * STRIP]
    depth_out[rows:, rows : 2 * rows] = turned[6 * STRIP : 7 * STRIP]
    depth_out[rows:, 2 * rows : 3 * rows] = turned[5 * STRIP : 6 * STRIP]
    depth_out[rows:, 3 * rows :] = turned[7 * STRIP :]
    cells_out[0] = numbers[0] * rows + lax.shift_right_logical(numbers[1], 2)
    cells_out[1] = numbers[1] & 3


def edge_rows(f, side, got_even, got_odd):
    at = BASE + HALO * f
    span = slice(at - BASE, at + HALO) if side == 0 else slice(at, at + EDGE)
    use_odd = is_even() if side == 0 else ~is_even()
    return jnp.where(use_odd, got_odd[span, :], got_even[span, :])


def corner_kernel(got_even, got_odd, corner_out):
    depth = lax.axis_index("depth")
    lane = lane_ids(EDGE)
    for side in range(2):
        packed = [jnp.zeros((EDGE, LANES), F32) for _ in range(2)]
        for f in range(FIELDS):
            group, place = divmod(f, FORWARD)
            spot = EDGE * place
            value = edge_rows(f, side, got_even, got_odd)
            edge = jnp.where(depth == 0, value[:, LANES:], value[:, :LANES])
            shift = lax.rem(spot + EDGE * (1 - depth), LANES)
            here = (lane >= spot) & (lane < spot + EDGE)
            packed[group] = jnp.where(here, pltpu.roll(edge, shift, 1), packed[group])
        corner_out[EDGE * side : EDGE * (side + 1), :LANES] = packed[0]
        corner_out[EDGE * side : EDGE * (side + 1), LANES:] = packed[1]


def window(plane, f, value, halo):
    depth = lax.axis_index("depth")
    surface = depth == 0
    first, last = value[:, :LANES], value[:, LANES:]
    lane = lane_ids(first.shape[0])
    low = jnp.where(surface, lane, LANES - 1 - lane)
    if plane == 0:
        shift = jnp.where(surface, EDGE, LANES - EDGE)
        return jnp.where(low >= EDGE, pltpu.roll(jnp.where(surface, first, last), shift, 1), 0.0)
    if plane == 1:
        return jnp.where(lane < LANES // 2, turn(first, LANES // 2), turn(last, LANES // 2))
    shift = jnp.where(surface, LANES - EDGE, EDGE)
    beside = lax.rem(LANES - EDGE * (f % FORWARD) + (LANES - EDGE) * (1 - depth), LANES)
    own = pltpu.roll(jnp.where(surface, last, first), shift, 1)
    return jnp.where(low < LANES - EDGE, own, pltpu.roll(halo, beside, 1))


def field_windows(f, planes, held, got_even, got_odd, got_depth=None, corner=None):
    rows = held.shape[1]
    col = LANES * (f // FORWARD)
    blocks = (
        (0, edge_rows(f, 0, got_even, got_odd), corner, 0),
        (EDGE, held[f % FORWARD], got_depth, 0),
        (EDGE + rows, edge_rows(f, 1, got_even, got_odd), corner, EDGE),
    )
    found = [[] for _ in planes]
    for at, value, halo, start in blocks:
        if halo is not None:
            halo = halo[start : start + value.shape[0], col : col + LANES]
        for parts, p in zip(found, planes):
            parts.append((at, window(p, f, value, halo)))
    return found


def joined(outer, middle, inner):
    surface = lax.axis_index("depth") == 0
    lane = lane_ids(outer.shape[0])
    first, last = jnp.where(surface, outer, inner), jnp.where(surface, inner, outer)
    middle = turn(middle, LANES // 2)
    return jnp.where(lane < 88, turn(first, -EDGE), middle), jnp.where(lane < 40, middle, turn(last, EDGE))


def load_state(states, base, planes, held, *got):
    extent = held.shape[1] + 2 * EDGE
    for f in range(5):
        for state, parts in zip(states, field_windows(base + f, planes, held, *got)):
            state[f, :PAD, :] = jnp.zeros((PAD, LANES), F32)
            state[f, PAD + extent :, :] = jnp.zeros((PAD, LANES), F32)
            for at, part in parts:
                state[f, PAD + at : PAD + at + part.shape[0], :] = part


def velocities(states, medias, span):
    for r in range(8 * span[0], 8 * span[1], 8):
        for state, media in zip(states, medias):

            def at(f, by=0):
                return state[f, r + PAD + by : r + PAD + by + 8, :]

            xx, xz, zz = at(2), at(4), at(3)
            b = media[0, r : r + 8, :]
            near = (xx - at(2, -1)) + (xz - turn(xz, 1))
            far = (at(2, 1) - at(2, -2)) + (turn(xz, -1) - turn(xz, 2))
            state[0, r + PAD : r + PAD + 8, :] = at(0) + b * (near + RATIO * far)
            near = (at(4, 1) - xz) + (turn(zz, -1) - zz)
            far = (at(4, 2) - at(4, -1)) + (turn(zz, -2) - turn(zz, 1))
            state[1, r + PAD : r + PAD + 8, :] = at(1) + b * (near + RATIO * far)


def stresses(states, medias, span, update, keep):
    for r in range(8 * span[0], 8 * span[1], 8):
        for i, (state, media) in enumerate(zip(states, medias)):

            def at(f, by=0):
                return state[f, r + PAD + by : r + PAD + by + 8, :]

            vx, vz = at(0), at(1)
            exx = (at(0, 1) - vx) + RATIO * (at(0, 2) - at(0, -1))
            ezz = (vz - turn(vz, 1)) + RATIO * (turn(vz, -1) - turn(vz, 2))
            near = (turn(vx, -1) - vx) + (vz - at(1, -1))
            far = (turn(vx, -2) - turn(vx, 1)) + (at(1, 1) - at(1, -2))
            shear = near + RATIO * far
            keep(i, r - EDGE, exx, ezz, shear)
            if update:
                whole, lam, mu = (media[k, r : r + 8, :] for k in (1, 2, 3))
                state[2, r + PAD : r + PAD + 8, :] = at(2) + (whole * exx + lam * ezz)
                state[3, r + PAD : r + PAD + 8, :] = at(3) + (lam * exx + whole * ezz)
                state[4, r + PAD : r + PAD + 8, :] = at(4) + mu * shear


def spans(step, rows):
    tiles = (rows + 2 * EDGE) // 8
    if step == 0:
        return (0, tiles), (0, tiles)
    inner = (1, tiles - 1)
    return inner, inner if step < MOMENTS - 1 else (EDGE // 8, tiles - EDGE // 8)


def run_forward(states, medias, saveds, planes, held, *got):
    rows = held.shape[1]
    given = [field_windows(f, planes, held, *got) for f in (5, 6, 7)]
    for i, media in enumerate(medias):
        for k in range(3):
            at = given[0][i][k][0]
            b, lam, mu = (NEAR * given[m][i][k][1] for m in range(3))
            span = slice(at, at + b.shape[0])
            media[0, span, :] = b
            media[1, span, :] = lam + 2.0 * mu
            media[2, span, :] = lam
            media[3, span, :] = mu
    load_state(states, 0, planes, held, *got)
    for step in range(MOMENTS):
        fast, slow = spans(step, rows)
        velocities(states, medias, fast)

        def save(i, r, exx, ezz, shear):
            if 0 <= r < rows:
                saveds[i][step, 0, r : r + 8, :] = exx
                saveds[i][step, 1, r : r + 8, :] = ezz
                saveds[i][step, 2, r : r + 8, :] = shear

        stresses(states, medias, slow, step < MOMENTS - 1, save)


def each(ref, count, axis):
    return [ref.at[(slice(None),) * axis + (i,)] for i in range(count)]


def forward_kernel(held, got_even, got_odd, media, saved, end_out, state):
    states = each(state, 2, 1)
    run_forward(states, each(media, 2, 1), each(saved, 2, 2), (0, 1), held, got_even, got_odd)
    top, rows = PAD + EDGE, held.shape[1]
    for f in range(2):
        for i in range(2):
            end_out[f, i] = states[i][f, top : top + rows, :]


def forward_inner_kernel(held, got_even, got_odd, got_depth, corner, end, media, saved, end_out, state):
    states = each(state, 1, 1)
    run_forward(
        states, each(media, 1, 1), each(saved, 1, 2), (2,), held, got_even, got_odd, got_depth, corner
    )
    top, rows = PAD + EDGE, held.shape[1]
    for f in range(2):
        first, last = joined(end[f, 0], end[f, 1], states[0][f, top : top + rows, :])
        end_out[f, :, :LANES] = first
        end_out[f, :, LANES:] = last


def note_kernel(strip, got_depth, traces, cells, note_out):
    first = lax.axis_index("depth") == 0
    beside = got_depth[got_depth.shape[0] - STRIP :, :]
    beside = jnp.concatenate([beside[:, :LANES], beside[:, LANES:]], axis=0)
    seen = jnp.concatenate([traces[:, :LANES], traces[:, LANES:]], axis=0)
    value = jnp.where(first, strip[...], beside)
    row = row_ids(2 * STRIP, LANES)
    for i, place in enumerate(CELL_ROWS):
        cell = cells[i // 2][:, LANES * (i % 2) : LANES * (i % 2 + 1)].astype(F32)
        value = jnp.where((row == place) & first, cell, value)
    block = jnp.concatenate([value, seen], axis=0)
    for k in range(note_out.shape[0]):
        note_out[k] = block


def relay_kernel(notes, base, rates, notes_out):
    del base, rates
    notes_out[...] = notes[...]


def three(value):
    high = value.astype(BF16)
    rest = value - high.astype(F32)
    middle = rest.astype(BF16)
    low = (rest - middle.astype(F32)).astype(BF16)
    return [high, middle, low]


def add_up(value, count):
    return (value[2 * count : 3 * count] + value[count : 2 * count]) + value[:count]


BATCH = 5
OWN = LANES - 2 * HALO


def strip_window(f, low, high, base, offset, tracks, columns):
    lane = lane_ids(STRIP)
    part = lax.div(offset + lane, columns)
    spot = base * columns + offset + lane
    source, q = (low, high)[f // 4], f % 4
    value = jnp.zeros((STRIP, LANES), F32)
    for step in range(3):
        who = jnp.clip(base + step, 0, tracks - 1)
        block = source[who, STRIP * (q % 2) : STRIP * (q % 2 + 1), :]
        shift = (4 * LANES - offset + columns * step - columns * (q // 2)) % LANES
        value = jnp.where(part == step, pltpu.roll(block, shift, 1), value)
    return jnp.where((spot >= 0) & (spot < tracks * columns), value, 0.0)


def fill_strip(state, media, low, high, first, tracks, columns):
    state[...] = jnp.zeros(state.shape, F32)
    for w in range(BATCH):
        begin = (first + w) * OWN - HALO
        base = (begin + columns) // columns - 1
        offset = begin - base * columns
        values = [strip_window(f, low, high, base, offset, tracks, columns) for f in range(FORWARD)]
        for f in range(5):
            state[f, w, PAD : PAD + STRIP, :] = values[f]
        buoyancy, lame, shear = (NEAR * value for value in values[5:])
        media[0, w] = buoyancy
        media[1, w] = lame + 2.0 * shear
        media[2, w] = lame
        media[3, w] = shear


def strip_steps(state, media):
    def at(f, w, r, by=0):
        return state[f, w, PAD + r + by : PAD + r + by + 8, :]

    count = state.shape[1]
    strains = [[] for _ in range(count)]
    for moment in range(MOMENTS):
        last = moment == MOMENTS - 1
        for r in (0, 8) if moment < 2 else (0,):
            for w in range(count):
                here = slice(PAD + r, PAD + r + 8)
                xx, xz, zz = at(2, w, r), at(4, w, r), at(3, w, r)
                b = media[0, w, r : r + 8, :]
                near = (xx - turn(xx, 1)) + (xz - at(4, w, r, -1))
                far = (turn(xx, -1) - turn(xx, 2)) + (at(4, w, r, 1) - at(4, w, r, -2))
                state[0, w, here, :] = at(0, w, r) + b * (near + RATIO * far)
                if not last:
                    near = (turn(xz, -1) - xz) + (at(3, w, r, 1) - zz)
                    far = (turn(xz, -2) - turn(xz, 1)) + (at(3, w, r, 2) - at(3, w, r, -1))
                    state[1, w, here, :] = at(1, w, r) + b * (near + RATIO * far)
        for r in (0, 8) if moment < 1 else (0,):
            for w in range(count):
                here = slice(PAD + r, PAD + r + 8)
                vx, vz = at(0, w, r), at(1, w, r)
                exx = (turn(vx, -1) - vx) + RATIO * (turn(vx, -2) - turn(vx, 1))
                if r == 0:
                    strains[w].append(NEAR * exx)
                if not last:
                    ezz = (vz - at(1, w, r, -1)) + RATIO * (at(1, w, r, 1) - at(1, w, r, -2))
                    near = (at(0, w, r, 1) - vx) + (vz - turn(vz, 1))
                    far = (at(0, w, r, 2) - at(0, w, r, -1)) + (turn(vz, -1) - turn(vz, 2))
                    whole, lam, mu = (media[k, w, r : r + 8, :] for k in (1, 2, 3))
                    state[2, w, here, :] = at(2, w, r) + (whole * exx + lam * ezz)
                    state[3, w, here, :] = at(3, w, r) + (lam * exx + whole * ezz)
                    state[4, w, here, :] = at(4, w, r) + mu * (near + RATIO * far)
    return [jnp.concatenate(parts, axis=0) for parts in strains]


def recorded_rates(state, media, low, high, wanted, tracks, columns):
    lane = lane_ids(8 * MOMENTS)
    mine = (lane >= HALO) & (lane < HALO + OWN)

    def body(number, rate):
        first = number * BATCH
        fill_strip(state, media, low, high, first, tracks, columns)
        images = [three(jnp.where(mine, image, 0.0)) for image in strip_steps(state, media)]
        parts = [jnp.concatenate([image[i] for image in images], axis=1) for i in range(3)]
        spots = [
            (first + w) * OWN - HALO + row_ids(LANES, wanted.shape[1]) for w in range(BATCH)
        ]
        hot = (jnp.concatenate(spots, axis=0) == wanted).astype(F32).astype(BF16)
        return rate + jnp.dot(jnp.concatenate(parts, axis=0), hot, preferred_element_type=F32)

    rate = jnp.zeros((3 * 8 * MOMENTS, wanted.shape[1]), F32)
    batches = -(-(-(-tracks * columns // OWN)) // BATCH)
    rate = body(0, rate) if batches == 1 else lax.fori_loop(0, batches, body, rate)
    return add_up(rate, 8 * MOMENTS)


def sums_kernel(tracks, columns, notes, sums_out):
    start = lax.axis_index("track") * columns - EDGE
    group = min(8, tracks)
    row16 = row_ids(IMAGE, LANES)

    def body(number, image):
        weights, hots = [], []
        for k in range(group):
            who = number * group + k
            traces = notes[who, 2 * STRIP :, :]
            places = [notes[who, place : place + 1, :] for place in CELL_ROWS]
            for h in range(2):
                mask = (row16 & 3).astype(F32) == places[2 + h]
                seen = [traces[4 * h + t : 4 * h + t + 1] for t in range(MOMENTS)]
                value = jnp.where(
                    row16 < 8,
                    jnp.where(row16 < 4, seen[0], seen[1]),
                    jnp.where(row16 < 12, seen[2], seen[3]),
                )
                pieces = three(jnp.where(mask, value, 0.0)) + [mask.astype(F32).astype(BF16)]
                weights.append(jnp.concatenate(pieces, axis=0))
                spot = (start + row_ids(LANES, LANES)).astype(F32)
                hots.append((spot == places[h]).astype(F32).astype(BF16))
        return image + lax.dot_general(
            jnp.concatenate(weights, axis=1),
            jnp.concatenate(hots, axis=1),
            (((1,), (1,)), ((), ())),
            preferred_element_type=F32,
        )

    image = jnp.zeros((4 * IMAGE, LANES), F32)
    image = body(0, image) if tracks == group else lax.fori_loop(0, tracks // group, body, image)
    sums_out[:IMAGE, :] = add_up(image, IMAGE)
    sums_out[IMAGE:, :] = image[3 * IMAGE :]


def response(state, media, sources, strains):
    state[...] = jnp.zeros(state.shape, F32)
    tiles = (0, 8)
    sums = [[jnp.zeros((8, LANES), F32) for _ in tiles] for _ in range(2)]

    def at(f, r, by=0):
        return state[f, PAD + r + by : PAD + r + by + 8, :]

    def put(f, r, value):
        state[f, PAD + r : PAD + r + 8, :] = value

    for moment in reversed(range(MOMENTS)):
        put(2, 0, at(2, 0) + sources[moment])
        for r in tiles:
            xx, xz, zz = at(2, r), at(4, r), at(3, r)
            b = media[0, r : r + 8, :]
            near = (xx - turn(xx, 1)) + (xz - at(4, r, -1))
            far = (turn(xx, -1) - turn(xx, 2)) + (at(4, r, 1) - at(4, r, -2))
            put(0, r, at(0, r) + b * (near + RATIO * far))
            near = (turn(xz, -1) - xz) + (at(3, r, 1) - zz)
            far = (turn(xz, -2) - turn(xz, 1)) + (at(3, r, 2) - at(3, r, -1))
            put(1, r, at(1, r) + b * (near + RATIO * far))
        for i, r in enumerate(tiles):
            vx, vz = at(0, r), at(1, r)
            exx = (turn(vx, -1) - vx) + RATIO * (turn(vx, -2) - turn(vx, 1))
            ezz = (vz - at(1, r, -1)) + RATIO * (at(1, r, 1) - at(1, r, -2))
            near = (at(0, r, 1) - vx) + (vz - turn(vz, 1))
            far = (at(0, r, 2) - at(0, r, -1)) + (turn(vz, -1) - turn(vz, 2))
            shear = near + RATIO * far
            fxx, fzz, fxz = (
                strains[j // 8, STRIP * (j % 8) + r : STRIP * (j % 8) + r + 8, :]
                for j in range(3 * moment, 3 * moment + 3)
            )
            sums[0][i] += (fxx + fzz) * (exx + ezz)
            sums[1][i] += 2.0 * (fxx * exx + fzz * ezz) + fxz * shear
            if moment > 0:
                whole, lam, mu = (media[k, r : r + 8, :] for k in (1, 2, 3))
                put(2, r, at(2, r) + (whole * exx + lam * ezz))
                put(3, r, at(3, r) + (lam * exx + whole * ezz))
                put(4, r, at(4, r) + mu * shear)
    return sums[0] + sums[1]


def fibre_kernel(strip, got_even, got_odd, rates_out, media_out, state, media, rows_in):
    rows = strip.shape[0]
    rows_in[...] = jnp.zeros(rows_in.shape, F32)
    rows_in[EDGE : EDGE + rows, :] = strip[...]
    lane = lane_ids(HALO)
    for side in range(2):
        use_odd = is_even() if side == 0 else ~is_even()
        near = jnp.zeros((HALO, LANES), F32)
        for f in range(FORWARD):
            span = slice(BASE + HALO * f, BASE + HALO * (f + 1))
            value = jnp.where(use_odd, got_odd[span, :LANES], got_even[span, :LANES])
            here = (lane >= STRIP * f) & (lane < STRIP * (f + 1))
            near = jnp.where(here, turn(value, STRIP * f), near)
        span = slice(EXTRA, EXTRA + HALO)
        far = jnp.where(use_odd, got_odd[span, :LANES], got_even[span, :LANES])
        if side == 0:
            rows_in[BASE:EDGE, :] = near
            rows_in[:BASE, :] = far[HALO - BASE :]
            rows_in[LANES - (HALO - BASE) :, :] = far[: HALO - BASE]
        else:
            rows_in[EDGE + rows : EDGE + rows + HALO, :] = near
            rows_in[EDGE + rows + HALO : EDGE + rows + 2 * HALO, :] = far
    turned = rows_in[...].T
    values = [turned[STRIP * f : STRIP * (f + 1)] for f in range(FORWARD)]
    state[...] = jnp.zeros(state.shape, F32)
    for f in range(5):
        state[f, 0, PAD : PAD + STRIP, :] = values[f]
    buoyancy, lame, shear = (NEAR * value for value in values[5:])
    for k, value in enumerate((buoyancy, lame + 2.0 * shear, lame, shear)):
        media[k, 0] = value
        media_out[k] = value
    rates_out[...] = strip_steps(state, media)[0]


def gradient_kernel(sums, rates, media, base, strains, gradients_out, state):
    rows = base.shape[1]
    near = jnp.concatenate([rates[8 * t : 8 * t + 4, :] for t in range(MOMENTS)], axis=0)
    lane = lane_ids(IMAGE)
    reached = (lane >= BASE) & (lane < EDGE + rows + HALO) & (lax.axis_index("depth") == 0)
    found = jnp.where(reached, sums[IMAGE:, :] * near - sums[:IMAGE, :], 0.0)
    nothing = jnp.zeros((8 - FIBRE_ROWS, LANES), F32)
    sources = [
        jnp.concatenate([found[FIBRE_ROWS * t : FIBRE_ROWS * (t + 1)], nothing], axis=0) for t in range(MOMENTS)
    ]
    added = response(state, media, sources, strains)
    added = jnp.concatenate(added + [jnp.zeros((LANES - 32, LANES), F32)], axis=0).T[EDGE : EDGE + rows]
    lane = lane_ids(rows)
    for k in range(2):
        more = jnp.where(lane < STRIP, turn(added, -STRIP * k), 0.0)
        gradients_out[k, :, :LANES] = (NEAR * NEAR) * (base[k, :, :LANES] + more)
        gradients_out[k, :, LANES:] = (NEAR * NEAR) * base[k, :, LANES:]


def residual_kernel(
    tracks, columns, notes, beside, obs, cells, gradients, end,
    residual_out, lambda_out, mu_out, end_out, state, media, low, high, sems,
):
    copies = fetch((gradients.at[0], gradients.at[1], end), (lambda_out, mu_out, end_out), sems)
    depth = lax.axis_index("depth")
    low[...] = jnp.where(depth == 0, notes[...], beside[...])
    high[...] = jnp.where(depth == 0, beside[...], notes[...])
    along, row = cells[0], cells[1]
    channels = along.shape[1]
    rate = recorded_rates(state, media, low, high, along, tracks, columns)
    mask = row_ids(8, channels) == row
    traces = [
        jnp.sum(jnp.where(mask, rate[8 * t : 8 * t + 8], 0.0), axis=0, keepdims=True) - obs[t : t + 1, :]
        for t in range(MOMENTS)
    ]
    residual_out[...] = jnp.where(
        depth == 0, jnp.concatenate(traces[:2], axis=0), jnp.concatenate(traces[2:], axis=0)
    )
    for copy in copies:
        copy.wait()


def adjoint_kernel(
    held, got_even, got_odd, got_depth, corner, media, saved, inner_media, inner_saved,
    base_out, strains_out, state, sums,
):
    states, totals = each(state, 3, 1), each(sums, 3, 1)
    rows = held.shape[1]
    load_state(states, FORWARD, (0, 1, 2), held, got_even, got_odd, got_depth, corner)
    medias = each(media, 2, 1) + each(inner_media, 1, 1)
    saveds = each(saved, 2, 2) + each(inner_saved, 1, 2)
    sums[...] = jnp.zeros(sums.shape, F32)
    for step in range(MOMENTS):
        fast, slow = spans(step, rows)
        moment = MOMENTS - 1 - step
        velocities(states, medias, fast)

        def gather(i, r, exx, ezz, shear):
            if 0 <= r < rows:
                fxx, fzz, fxz = (saveds[i][moment, k, r : r + 8, :] for k in range(3))
                totals[i][0, r : r + 8, :] += (fxx + fzz) * (exx + ezz)
                totals[i][1, r : r + 8, :] += 2.0 * (fxx * exx + fzz * ezz) + fxz * shear

        stresses(states, medias, slow, step < MOMENTS - 1, gather)
    for k in range(2):
        first, last = joined(*(total[k] for total in totals))
        base_out[k, :, :LANES] = first
        base_out[k, :, LANES:] = last
    lane = lane_ids(rows)
    for group in range(2):
        packed = jnp.zeros((rows, LANES), F32)
        for j in range(8 * group, min(8 * group + 8, 3 * MOMENTS)):
            spot = STRIP * (j % 8)
            here = (lane >= spot) & (lane < spot + STRIP)
            packed = jnp.where(here, turn(saveds[0][j // 3, j % 3], spot - EDGE), packed)
        turned = packed.T
        strains_out[group] = turn(jnp.concatenate([turned, jnp.zeros_like(turned)], axis=1), EDGE)


def per_device(
    velocity,
    stress,
    adjoint_velocity,
    adjoint_stress,
    buoyancy,
    lame_lambda,
    shear_modulus,
    observed,
    owner_track,
    fibre_cell,
):
    tracks = lax.axis_size("track")
    rows, depth_cells = buoyancy.shape
    moments, channels = observed.shape
    owner = owner_track.reshape(1, channels)
    cell = fibre_cell.reshape(1, channels)
    pinned = lambda array: pltpu.with_memory_space_constraint(array, pltpu.HBM)
    arrays = (velocity, stress, adjoint_velocity, adjoint_stress, buoyancy, lame_lambda, shear_modulus)
    arrays = tuple(pinned(array) for array in arrays)
    channel_arrays = (pinned(observed), pinned(owner), pinned(cell))
    extent = rows + 2 * EDGE
    block = jax.ShapeDtypeStruct((rows, depth_cells), F32)
    edges = jax.ShapeDtypeStruct((EXTRA + EDGE, depth_cells), F32)
    inside = pl.BlockSpec(memory_space=VMEM)
    outside = pl.BlockSpec(memory_space=pltpu.HBM)
    anywhere = pl.BlockSpec(memory_space=pl.ANY)
    held, held_adj, to_depth, to_even, to_odd, strip, traces, cells, strip_rows = pl.pallas_call(
        pack_kernel,
        out_shape=(
            jax.ShapeDtypeStruct((FORWARD, rows, depth_cells), F32),
            jax.ShapeDtypeStruct((ADJOINT, rows, depth_cells), F32),
            jax.ShapeDtypeStruct((rows + STRIP, depth_cells), F32),
            edges,
            edges,
            jax.ShapeDtypeStruct((2 * STRIP, LANES), F32),
            jax.ShapeDtypeStruct((moments, channels), F32),
            jax.ShapeDtypeStruct((2, 1, channels), jnp.int32),
            jax.ShapeDtypeStruct((rows, LANES), F32),
        ),
        in_specs=[outside] * 10,
        out_specs=(inside,) * 9,
        scratch_shapes=[VMEM((2, 1, channels), jnp.int32), pltpu.SemaphoreType.DMA((10,))],
        compiler_params=params(),
        cost_estimate=cost(5),
        name="pack",
    )(*arrays, *channel_arrays)
    depth_swap = [(0, 1), (1, 0)]
    got_depth = lax.ppermute(to_depth, "depth", depth_swap)
    swap = lambda k: [pair for i in range(k, tracks - 1, 2) for pair in ((i, i + 1), (i + 1, i))]
    got_odd = lax.ppermute(to_odd, "track", swap(1))
    got_even = lax.ppermute(to_even, "track", swap(0))

    def state_of(planes):
        return VMEM((5, planes, extent + 2 * PAD, LANES), F32)

    note = pl.pallas_call(
        note_kernel,
        out_shape=jax.ShapeDtypeStruct((tracks, 2 * STRIP + 8, LANES), F32),
        in_specs=[inside] * 4,
        out_specs=inside,
        compiler_params=params(),
        cost_estimate=cost(20),
        name="note",
    )(strip, got_depth, traces, cells)
    notes = lax.all_to_all(note, "track", split_axis=0, concat_axis=0, tiled=True)

    corner = pl.pallas_call(
        corner_kernel,
        out_shape=jax.ShapeDtypeStruct((2 * EDGE, depth_cells), F32),
        in_specs=[inside] * 2,
        out_specs=inside,
        compiler_params=params(),
        cost_estimate=cost(1),
        name="corners",
    )(got_even, got_odd)
    got_corner = lax.ppermute(corner, "depth", depth_swap)

    def media_of(planes):
        return jax.ShapeDtypeStruct((4, planes, extent, LANES), F32)

    def saved_of(planes):
        return jax.ShapeDtypeStruct((moments, 3, planes, rows, LANES), F32)

    media, saved, end = pl.pallas_call(
        forward_kernel,
        out_shape=(media_of(2), saved_of(2), jax.ShapeDtypeStruct((2, 2, rows, LANES), F32)),
        in_specs=[inside] * 3,
        out_specs=(inside,) * 3,
        scratch_shapes=[state_of(2)],
        compiler_params=params(),
        cost_estimate=cost(20),
        name="forward",
    )(held, got_even, got_odd)

    inner_media, inner_saved, end = pl.pallas_call(
        forward_inner_kernel,
        out_shape=(media_of(1), saved_of(1), jax.ShapeDtypeStruct(velocity.shape, F32)),
        in_specs=[inside] * 6,
        out_specs=(inside,) * 3,
        scratch_shapes=[state_of(1)],
        compiler_params=params(),
        cost_estimate=cost(20),
        name="forward_inner",
    )(held, got_even, got_odd, got_depth, got_corner, end)

    base, strains = pl.pallas_call(
        adjoint_kernel,
        out_shape=(
            jax.ShapeDtypeStruct((2, rows, depth_cells), F32),
            jax.ShapeDtypeStruct((2, LANES, LANES), F32),
        ),
        in_specs=[inside] * 9,
        out_specs=(inside,) * 2,
        scratch_shapes=[state_of(3), VMEM((2, 3, rows, LANES), F32)],
        compiler_params=params(),
        cost_estimate=cost(20),
        name="adjoint",
    )(held_adj, got_even, got_odd, got_depth, got_corner, media, saved, inner_media, inner_saved)

    rates, own_media = pl.pallas_call(
        fibre_kernel,
        out_shape=(
            jax.ShapeDtypeStruct((8 * MOMENTS, LANES), F32),
            jax.ShapeDtypeStruct((4, STRIP, LANES), F32),
        ),
        in_specs=[inside] * 3,
        out_specs=(inside,) * 2,
        scratch_shapes=[
            VMEM((5, 1, 2 * PAD + STRIP, LANES), F32),
            VMEM((4, 1, STRIP, LANES), F32),
            VMEM((LANES, LANES), F32),
        ],
        compiler_params=params(),
        cost_estimate=cost(5),
        name="fibre",
    )(strip_rows, got_even, got_odd)

    mine = pl.pallas_call(
        relay_kernel,
        out_shape=jax.ShapeDtypeStruct(note.shape, F32),
        in_specs=[inside, anywhere, anywhere],
        out_specs=inside,
        compiler_params=params(),
        cost_estimate=cost(1),
        name="relay",
    )(notes, base, rates)
    beside = lax.ppermute(mine, "depth", depth_swap)

    sums = pl.pallas_call(
        lambda *refs: sums_kernel(tracks, rows, *refs),
        out_shape=jax.ShapeDtypeStruct((2 * IMAGE, LANES), F32),
        in_specs=[inside],
        out_specs=inside,
        compiler_params=params(),
        cost_estimate=cost(20),
        name="sums",
    )(mine)

    gradients = pl.pallas_call(
        gradient_kernel,
        out_shape=jax.ShapeDtypeStruct((2, rows, depth_cells), F32),
        in_specs=[inside] * 5,
        out_specs=inside,
        scratch_shapes=[VMEM((5, 2 * PAD + STRIP, LANES), F32)],
        compiler_params=params(),
        cost_estimate=cost(20),
        name="gradient",
    )(sums, rates, own_media, base, strains)

    residual, gradient_lambda, gradient_mu, velocity_end = pl.pallas_call(
        lambda *refs: residual_kernel(tracks, rows, *refs),
        out_shape=(
            jax.ShapeDtypeStruct((moments // 2, channels), F32),
            block,
            block,
            jax.ShapeDtypeStruct(velocity.shape, F32),
        ),
        in_specs=[inside] * 6,
        out_specs=(inside, outside, outside, outside),
        scratch_shapes=[
            VMEM((5, BATCH, 2 * PAD + STRIP, LANES), F32),
            VMEM((4, BATCH, STRIP, LANES), F32),
            VMEM(note.shape, F32),
            VMEM(note.shape, F32),
            pltpu.SemaphoreType.DMA((3,)),
        ],
        compiler_params=params(),
        cost_estimate=cost(2),
        name="residual",
    )(mine, beside, traces, cells, gradients, end)
    return gradient_lambda, gradient_mu, velocity_end, residual


def solution(mesh):
    return jax.shard_map(
        per_device,
        mesh=mesh,
        in_specs=(
            P("shots", "track", "depth"),
            P("shots", "track", "depth"),
            P("shots", "track", "depth"),
            P("shots", "track", "depth"),
            P("track", "depth"),
            P("track", "depth"),
            P("track", "depth"),
            P("shots", "track"),
            P("track", None),
            P("track"),
        ),
        out_specs=(
            P(("shots", "track"), "depth"),
            P(("shots", "track"), "depth"),
            P("shots", "track", "depth"),
            P(("shots", "depth"), "track"),
        ),
        check_vma=False,
    )
```

```python
import jax
import jax.numpy as jnp
from jax import lax
from jax.experimental import pallas as pl
from jax.experimental.pallas import tpu as pltpu
from jax.sharding import PartitionSpec as P

FIBRE_ROWS = 4
NEAR = 9.0 / 8.0
RATIO = -1.0 / 27.0
HALO = 12
EDGE = 16
LANES = 128
PAD = 8
FORWARD = 8
ADJOINT = 5
FIELDS = FORWARD + ADJOINT
STRIP = 16
CELL_ROWS = (14, 15, 30, 31)
EXTRA = 168
BASE = EDGE - HALO
MOMENTS = 4
IMAGE = MOMENTS * FIBRE_ROWS
VMEM = pltpu.VMEM
F32 = jnp.float32
BF16 = jnp.bfloat16


def lane_ids(rows):
    return lax.broadcasted_iota(jnp.int32, (rows, LANES), 1)


def row_ids(rows, columns):
    return lax.broadcasted_iota(jnp.int32, (rows, columns), 0)


def params():
    return pltpu.CompilerParams(vmem_limit_bytes=16 * 1024 * 1024)


def cost(microseconds):
    return pl.CostEstimate(flops=int(microseconds * 1e9), bytes_accessed=1 << 20, transcendentals=0)


def turn(value, by):
    return pltpu.roll(value, by % LANES, 1)


def is_even():
    return lax.rem(lax.axis_index("track"), 2) == 0


def fetch(sources, targets, sems):
    copies = [pltpu.make_async_copy(s, t, sems.at[i]) for i, (s, t) in enumerate(zip(sources, targets))]
    for copy in copies:
        copy.start()
    return copies


def pack_kernel(*refs):
    sources, channel_arrays = refs[:7], refs[7:10]
    held, held_adj, depth_out, edge_outs, strip_out, traces_out, cells_out = *refs[10:13], refs[13:15], *refs[15:18]
    rows_out, numbers, sems = refs[18:]
    targets = (
        held.at[pl.ds(0, 2)],
        held.at[pl.ds(2, 3)],
        held.at[5],
        held.at[6],
        held.at[7],
        held_adj.at[pl.ds(0, 2)],
        held_adj.at[pl.ds(2, 3)],
        traces_out,
        numbers.at[0],
        numbers.at[1],
    )
    copies = fetch((*sources[:2], *sources[4:], *sources[2:4], *channel_arrays), targets, sems)
    depth = lax.axis_index("depth")
    even = is_even()
    rows = held.shape[1]
    lane = lane_ids(rows)
    tail = BASE + HALO * FIELDS
    for out in edge_outs:
        out[:BASE, :] = jnp.zeros((BASE, 2 * LANES), F32)
        out[tail:, :] = jnp.zeros((out.shape[0] - tail, 2 * LANES), F32)
    for copy in copies:
        copy.wait()
    packed = [jnp.zeros((rows, LANES), F32) for _ in range(2)]
    strip = jnp.zeros((rows, LANES), F32)
    for f in range(FIELDS):
        ref = held.at[f] if f < FORWARD else held_adj.at[f - FORWARD]
        first, last = ref[:, :LANES], ref[:, LANES:]
        group, place = divmod(f, FORWARD)
        spot = EDGE * place
        here = (lane >= spot) & (lane < spot + EDGE)
        edge = jnp.where(depth == 0, last, first)
        shift = lax.rem(spot + EDGE * (1 - depth), LANES)
        packed[group] = jnp.where(here, pltpu.roll(edge, shift, 1), packed[group])
        if f < FORWARD:
            strip = jnp.where(here, turn(first, spot), strip)
        low, high = ref[:HALO, :], ref[rows - HALO :, :]
        at = BASE + HALO * f
        edge_outs[0][at : at + HALO, :] = jnp.where(even, high, low)
        edge_outs[1][at : at + HALO, :] = jnp.where(even, low, high)
    depth_out[:rows, :LANES] = packed[0]
    depth_out[:rows, LANES:] = packed[1]
    rows_out[...] = strip
    low, high = strip[HALO : 2 * HALO], strip[rows - 2 * HALO : rows - HALO]
    edge_outs[0][EXTRA : EXTRA + HALO, :LANES] = jnp.where(even, high, low)
    edge_outs[1][EXTRA : EXTRA + HALO, :LANES] = jnp.where(even, low, high)
    turned = strip.T
    strip_out[:, :rows] = turned[: 2 * STRIP]
    strip_out[:, rows:] = turned[2 * STRIP : 4 * STRIP]
    depth_out[rows:, :rows] = turned[4 * STRIP : 5 * STRIP]
    depth_out[rows:, rows : 2 * rows] = turned[6 * STRIP : 7 * STRIP]
    depth_out[rows:, 2 * rows : 3 * rows] = turned[5 * STRIP : 6 * STRIP]
    depth_out[rows:, 3 * rows :] = turned[7 * STRIP :]
    cells_out[0] = numbers[0] * rows + lax.shift_right_logical(numbers[1], 2)
    cells_out[1] = numbers[1] & 3


def edge_rows(f, side, got_even, got_odd):
    at = BASE + HALO * f
    span = slice(at - BASE, at + HALO) if side == 0 else slice(at, at + EDGE)
    use_odd = is_even() if side == 0 else ~is_even()
    return jnp.where(use_odd, got_odd[span, :], got_even[span, :])


def corner_kernel(got_even, got_odd, corner_out):
    depth = lax.axis_index("depth")
    lane = lane_ids(EDGE)
    for side in range(2):
        packed = [jnp.zeros((EDGE, LANES), F32) for _ in range(2)]
        for f in range(FIELDS):
            group, place = divmod(f, FORWARD)
            spot = EDGE * place
            value = edge_rows(f, side, got_even, got_odd)
            edge = jnp.where(depth == 0, value[:, LANES:], value[:, :LANES])
            shift = lax.rem(spot + EDGE * (1 - depth), LANES)
            here = (lane >= spot) & (lane < spot + EDGE)
            packed[group] = jnp.where(here, pltpu.roll(edge, shift, 1), packed[group])
        corner_out[EDGE * side : EDGE * (side + 1), :LANES] = packed[0]
        corner_out[EDGE * side : EDGE * (side + 1), LANES:] = packed[1]


def window(plane, f, value, halo):
    depth = lax.axis_index("depth")
    surface = depth == 0
    first, last = value[:, :LANES], value[:, LANES:]
    lane = lane_ids(first.shape[0])
    low = jnp.where(surface, lane, LANES - 1 - lane)
    if plane == 0:
        shift = jnp.where(surface, EDGE, LANES - EDGE)
        return jnp.where(low >= EDGE, pltpu.roll(jnp.where(surface, first, last), shift, 1), 0.0)
    if plane == 1:
        return jnp.where(lane < LANES // 2, turn(first, LANES // 2), turn(last, LANES // 2))
    shift = jnp.where(surface, LANES - EDGE, EDGE)
    beside = lax.rem(LANES - EDGE * (f % FORWARD) + (LANES - EDGE) * (1 - depth), LANES)
    own = pltpu.roll(jnp.where(surface, last, first), shift, 1)
    return jnp.where(low < LANES - EDGE, own, pltpu.roll(halo, beside, 1))


def field_windows(f, planes, held, got_even, got_odd, got_depth=None, corner=None):
    rows = held.shape[1]
    col = LANES * (f // FORWARD)
    blocks = (
        (0, edge_rows(f, 0, got_even, got_odd), corner, 0),
        (EDGE, held[f % FORWARD], got_depth, 0),
        (EDGE + rows, edge_rows(f, 1, got_even, got_odd), corner, EDGE),
    )
    found = [[] for _ in planes]
    for at, value, halo, start in blocks:
        if halo is not None:
            halo = halo[start : start + value.shape[0], col : col + LANES]
        for parts, p in zip(found, planes):
            parts.append((at, window(p, f, value, halo)))
    return found


def joined(outer, middle, inner):
    surface = lax.axis_index("depth") == 0
    lane = lane_ids(outer.shape[0])
    first, last = jnp.where(surface, outer, inner), jnp.where(surface, inner, outer)
    middle = turn(middle, LANES // 2)
    return jnp.where(lane < 88, turn(first, -EDGE), middle), jnp.where(lane < 40, middle, turn(last, EDGE))


def load_state(states, base, planes, held, *got):
    extent = held.shape[1] + 2 * EDGE
    for f in range(5):
        for state, parts in zip(states, field_windows(base + f, planes, held, *got)):
            state[f, :PAD, :] = jnp.zeros((PAD, LANES), F32)
            state[f, PAD + extent :, :] = jnp.zeros((PAD, LANES), F32)
            for at, part in parts:
                state[f, PAD + at : PAD + at + part.shape[0], :] = part


def velocities(states, medias, span):
    for r in range(8 * span[0], 8 * span[1], 8):
        for state, media in zip(states, medias):

            def at(f, by=0):
                return state[f, r + PAD + by : r + PAD + by + 8, :]

            xx, xz, zz = at(2), at(4), at(3)
            b = media[0, r : r + 8, :]
            near = (xx - at(2, -1)) + (xz - turn(xz, 1))
            far = (at(2, 1) - at(2, -2)) + (turn(xz, -1) - turn(xz, 2))
            state[0, r + PAD : r + PAD + 8, :] = at(0) + b * (near + RATIO * far)
            near = (at(4, 1) - xz) + (turn(zz, -1) - zz)
            far = (at(4, 2) - at(4, -1)) + (turn(zz, -2) - turn(zz, 1))
            state[1, r + PAD : r + PAD + 8, :] = at(1) + b * (near + RATIO * far)


def stresses(states, medias, span, update, keep):
    for r in range(8 * span[0], 8 * span[1], 8):
        for i, (state, media) in enumerate(zip(states, medias)):

            def at(f, by=0):
                return state[f, r + PAD + by : r + PAD + by + 8, :]

            vx, vz = at(0), at(1)
            exx = (at(0, 1) - vx) + RATIO * (at(0, 2) - at(0, -1))
            ezz = (vz - turn(vz, 1)) + RATIO * (turn(vz, -1) - turn(vz, 2))
            near = (turn(vx, -1) - vx) + (vz - at(1, -1))
            far = (turn(vx, -2) - turn(vx, 1)) + (at(1, 1) - at(1, -2))
            shear = near + RATIO * far
            keep(i, r - EDGE, exx, ezz, shear)
            if update:
                whole, lam, mu = (media[k, r : r + 8, :] for k in (1, 2, 3))
                state[2, r + PAD : r + PAD + 8, :] = at(2) + (whole * exx + lam * ezz)
                state[3, r + PAD : r + PAD + 8, :] = at(3) + (lam * exx + whole * ezz)
                state[4, r + PAD : r + PAD + 8, :] = at(4) + mu * shear


def spans(step, rows):
    tiles = (rows + 2 * EDGE) // 8
    if step == 0:
        return (0, tiles), (0, tiles)
    inner = (1, tiles - 1)
    return inner, inner if step < MOMENTS - 1 else (EDGE // 8, tiles - EDGE // 8)


def run_forward(states, medias, saveds, planes, held, *got):
    rows = held.shape[1]
    given = [field_windows(f, planes, held, *got) for f in (5, 6, 7)]
    for i, media in enumerate(medias):
        for k in range(3):
            at = given[0][i][k][0]
            b, lam, mu = (NEAR * given[m][i][k][1] for m in range(3))
            span = slice(at, at + b.shape[0])
            media[0, span, :] = b
            media[1, span, :] = lam + 2.0 * mu
            media[2, span, :] = lam
            media[3, span, :] = mu
    load_state(states, 0, planes, held, *got)
    for step in range(MOMENTS):
        fast, slow = spans(step, rows)
        velocities(states, medias, fast)

        def save(i, r, exx, ezz, shear):
            if 0 <= r < rows:
                saveds[i][step, 0, r : r + 8, :] = exx
                saveds[i][step, 1, r : r + 8, :] = ezz
                saveds[i][step, 2, r : r + 8, :] = shear

        stresses(states, medias, slow, step < MOMENTS - 1, save)


def each(ref, count, axis):
    return [ref.at[(slice(None),) * axis + (i,)] for i in range(count)]


def forward_kernel(held, got_even, got_odd, media, saved, end_out, state):
    states = each(state, 2, 1)
    run_forward(states, each(media, 2, 1), each(saved, 2, 2), (0, 1), held, got_even, got_odd)
    top, rows = PAD + EDGE, held.shape[1]
    for f in range(2):
        for i in range(2):
            end_out[f, i] = states[i][f, top : top + rows, :]


def forward_inner_kernel(held, got_even, got_odd, got_depth, corner, end, media, saved, end_out, state):
    states = each(state, 1, 1)
    run_forward(
        states, each(media, 1, 1), each(saved, 1, 2), (2,), held, got_even, got_odd, got_depth, corner
    )
    top, rows = PAD + EDGE, held.shape[1]
    for f in range(2):
        first, last = joined(end[f, 0], end[f, 1], states[0][f, top : top + rows, :])
        end_out[f, :, :LANES] = first
        end_out[f, :, LANES:] = last


def note_kernel(strip, got_depth, traces, cells, note_out):
    first = lax.axis_index("depth") == 0
    beside = got_depth[got_depth.shape[0] - STRIP :, :]
    beside = jnp.concatenate([beside[:, :LANES], beside[:, LANES:]], axis=0)
    seen = jnp.concatenate([traces[:, :LANES], traces[:, LANES:]], axis=0)
    value = jnp.where(first, strip[...], beside)
    row = row_ids(2 * STRIP, LANES)
    for i, place in enumerate(CELL_ROWS):
        cell = cells[i // 2][:, LANES * (i % 2) : LANES * (i % 2 + 1)].astype(F32)
        value = jnp.where((row == place) & first, cell, value)
    block = jnp.concatenate([value, seen], axis=0)
    for k in range(note_out.shape[0]):
        note_out[k] = block


def relay_kernel(notes, base, rates, notes_out):
    del base, rates
    notes_out[...] = notes[...]


def three(value):
    high = value.astype(BF16)
    rest = value - high.astype(F32)
    middle = rest.astype(BF16)
    low = (rest - middle.astype(F32)).astype(BF16)
    return [high, middle, low]


def add_up(value, count):
    return (value[2 * count : 3 * count] + value[count : 2 * count]) + value[:count]


BATCH = 5
OWN = LANES - 2 * HALO


def strip_window(f, low, high, base, offset, tracks, columns):
    lane = lane_ids(STRIP)
    part = lax.div(offset + lane, columns)
    spot = base * columns + offset + lane
    source, q = (low, high)[f // 4], f % 4
    value = jnp.zeros((STRIP, LANES), F32)
    for step in range(3):
        who = jnp.clip(base + step, 0, tracks - 1)
        block = source[who, STRIP * (q % 2) : STRIP * (q % 2 + 1), :]
        shift = (4 * LANES - offset + columns * step - columns * (q // 2)) % LANES
        value = jnp.where(part == step, pltpu.roll(block, shift, 1), value)
    return jnp.where((spot >= 0) & (spot < tracks * columns), value, 0.0)


def fill_strip(state, media, low, high, first, tracks, columns):
    state[...] = jnp.zeros(state.shape, F32)
    for w in range(BATCH):
        begin = (first + w) * OWN - HALO
        base = (begin + columns) // columns - 1
        offset = begin - base * columns
        values = [strip_window(f, low, high, base, offset, tracks, columns) for f in range(FORWARD)]
        for f in range(5):
            state[f, w, PAD : PAD + STRIP, :] = values[f]
        buoyancy, lame, shear = (NEAR * value for value in values[5:])
        media[0, w] = buoyancy
        media[1, w] = lame + 2.0 * shear
        media[2, w] = lame
        media[3, w] = shear


def strip_steps(state, media):
    def at(f, w, r, by=0):
        return state[f, w, PAD + r + by : PAD + r + by + 8, :]

    count = state.shape[1]
    strains = [[] for _ in range(count)]
    for moment in range(MOMENTS):
        last = moment == MOMENTS - 1
        for r in (0, 8) if moment < 2 else (0,):
            for w in range(count):
                here = slice(PAD + r, PAD + r + 8)
                xx, xz, zz = at(2, w, r), at(4, w, r), at(3, w, r)
                b = media[0, w, r : r + 8, :]
                near = (xx - turn(xx, 1)) + (xz - at(4, w, r, -1))
                far = (turn(xx, -1) - turn(xx, 2)) + (at(4, w, r, 1) - at(4, w, r, -2))
                state[0, w, here, :] = at(0, w, r) + b * (near + RATIO * far)
                if not last:
                    near = (turn(xz, -1) - xz) + (at(3, w, r, 1) - zz)
                    far = (turn(xz, -2) - turn(xz, 1)) + (at(3, w, r, 2) - at(3, w, r, -1))
                    state[1, w, here, :] = at(1, w, r) + b * (near + RATIO * far)
        for r in (0, 8) if moment < 1 else (0,):
            for w in range(count):
                here = slice(PAD + r, PAD + r + 8)
                vx, vz = at(0, w, r), at(1, w, r)
                exx = (turn(vx, -1) - vx) + RATIO * (turn(vx, -2) - turn(vx, 1))
                if r == 0:
                    strains[w].append(NEAR * exx)
                if not last:
                    ezz = (vz - at(1, w, r, -1)) + RATIO * (at(1, w, r, 1) - at(1, w, r, -2))
                    near = (at(0, w, r, 1) - vx) + (vz - turn(vz, 1))
                    far = (at(0, w, r, 2) - at(0, w, r, -1)) + (turn(vz, -1) - turn(vz, 2))
                    whole, lam, mu = (media[k, w, r : r + 8, :] for k in (1, 2, 3))
                    state[2, w, here, :] = at(2, w, r) + (whole * exx + lam * ezz)
                    state[3, w, here, :] = at(3, w, r) + (lam * exx + whole * ezz)
                    state[4, w, here, :] = at(4, w, r) + mu * (near + RATIO * far)
    return [jnp.concatenate(parts, axis=0) for parts in strains]


def recorded_rates(state, media, low, high, wanted, tracks, columns):
    lane = lane_ids(8 * MOMENTS)
    mine = (lane >= HALO) & (lane < HALO + OWN)

    def body(number, rate):
        first = number * BATCH
        fill_strip(state, media, low, high, first, tracks, columns)
        images = [three(jnp.where(mine, image, 0.0)) for image in strip_steps(state, media)]
        parts = [jnp.concatenate([image[i] for image in images], axis=1) for i in range(3)]
        spots = [
            (first + w) * OWN - HALO + row_ids(LANES, wanted.shape[1]) for w in range(BATCH)
        ]
        hot = (jnp.concatenate(spots, axis=0) == wanted).astype(F32).astype(BF16)
        return rate + jnp.dot(jnp.concatenate(parts, axis=0), hot, preferred_element_type=F32)

    rate = jnp.zeros((3 * 8 * MOMENTS, wanted.shape[1]), F32)
    batches = -(-(-(-tracks * columns // OWN)) // BATCH)
    rate = body(0, rate) if batches == 1 else lax.fori_loop(0, batches, body, rate)
    return add_up(rate, 8 * MOMENTS)


def sums_kernel(tracks, columns, notes, sums_out):
    start = lax.axis_index("track") * columns - EDGE
    group = min(8, tracks)
    row16 = row_ids(IMAGE, LANES)

    def body(number, image):
        weights, hots = [], []
        for k in range(group):
            who = number * group + k
            traces = notes[who, 2 * STRIP :, :]
            places = [notes[who, place : place + 1, :] for place in CELL_ROWS]
            for h in range(2):
                mask = (row16 & 3).astype(F32) == places[2 + h]
                seen = [traces[4 * h + t : 4 * h + t + 1] for t in range(MOMENTS)]
                value = jnp.where(
                    row16 < 8,
                    jnp.where(row16 < 4, seen[0], seen[1]),
                    jnp.where(row16 < 12, seen[2], seen[3]),
                )
                pieces = three(jnp.where(mask, value, 0.0)) + [mask.astype(F32).astype(BF16)]
                weights.append(jnp.concatenate(pieces, axis=0))
                spot = (start + row_ids(LANES, LANES)).astype(F32)
                hots.append((spot == places[h]).astype(F32).astype(BF16))
        return image + lax.dot_general(
            jnp.concatenate(weights, axis=1),
            jnp.concatenate(hots, axis=1),
            (((1,), (1,)), ((), ())),
            preferred_element_type=F32,
        )

    image = jnp.zeros((4 * IMAGE, LANES), F32)
    image = body(0, image) if tracks == group else lax.fori_loop(0, tracks // group, body, image)
    sums_out[:IMAGE, :] = add_up(image, IMAGE)
    sums_out[IMAGE:, :] = image[3 * IMAGE :]


def response(state, media, sources, strains):
    state[...] = jnp.zeros(state.shape, F32)
    tiles = (0, 8)
    sums = [[jnp.zeros((8, LANES), F32) for _ in tiles] for _ in range(2)]

    def at(f, r, by=0):
        return state[f, PAD + r + by : PAD + r + by + 8, :]

    def put(f, r, value):
        state[f, PAD + r : PAD + r + 8, :] = value

    for moment in reversed(range(MOMENTS)):
        put(2, 0, at(2, 0) + sources[moment])
        for r in tiles:
            xx, xz, zz = at(2, r), at(4, r), at(3, r)
            b = media[0, r : r + 8, :]
            near = (xx - turn(xx, 1)) + (xz - at(4, r, -1))
            far = (turn(xx, -1) - turn(xx, 2)) + (at(4, r, 1) - at(4, r, -2))
            put(0, r, at(0, r) + b * (near + RATIO * far))
            near = (turn(xz, -1) - xz) + (at(3, r, 1) - zz)
            far = (turn(xz, -2) - turn(xz, 1)) + (at(3, r, 2) - at(3, r, -1))
            put(1, r, at(1, r) + b * (near + RATIO * far))
        for i, r in enumerate(tiles):
            vx, vz = at(0, r), at(1, r)
            exx = (turn(vx, -1) - vx) + RATIO * (turn(vx, -2) - turn(vx, 1))
            ezz = (vz - at(1, r, -1)) + RATIO * (at(1, r, 1) - at(1, r, -2))
            near = (at(0, r, 1) - vx) + (vz - turn(vz, 1))
            far = (at(0, r, 2) - at(0, r, -1)) + (turn(vz, -1) - turn(vz, 2))
            shear = near + RATIO * far
            fxx, fzz, fxz = (
                strains[j // 8, STRIP * (j % 8) + r : STRIP * (j % 8) + r + 8, :]
                for j in range(3 * moment, 3 * moment + 3)
            )
            sums[0][i] += (fxx + fzz) * (exx + ezz)
            sums[1][i] += 2.0 * (fxx * exx + fzz * ezz) + fxz * shear
            if moment > 0:
                whole, lam, mu = (media[k, r : r + 8, :] for k in (1, 2, 3))
                put(2, r, at(2, r) + (whole * exx + lam * ezz))
                put(3, r, at(3, r) + (lam * exx + whole * ezz))
                put(4, r, at(4, r) + mu * shear)
    return sums[0] + sums[1]


def fibre_kernel(strip, got_even, got_odd, rates_out, media_out, state, media, rows_in):
    rows = strip.shape[0]
    rows_in[...] = jnp.zeros(rows_in.shape, F32)
    rows_in[EDGE : EDGE + rows, :] = strip[...]
    lane = lane_ids(HALO)
    for side in range(2):
        use_odd = is_even() if side == 0 else ~is_even()
        near = jnp.zeros((HALO, LANES), F32)
        for f in range(FORWARD):
            span = slice(BASE + HALO * f, BASE + HALO * (f + 1))
            value = jnp.where(use_odd, got_odd[span, :LANES], got_even[span, :LANES])
            here = (lane >= STRIP * f) & (lane < STRIP * (f + 1))
            near = jnp.where(here, turn(value, STRIP * f), near)
        span = slice(EXTRA, EXTRA + HALO)
        far = jnp.where(use_odd, got_odd[span, :LANES], got_even[span, :LANES])
        if side == 0:
            rows_in[BASE:EDGE, :] = near
            rows_in[:BASE, :] = far[HALO - BASE :]
            rows_in[LANES - (HALO - BASE) :, :] = far[: HALO - BASE]
        else:
            rows_in[EDGE + rows : EDGE + rows + HALO, :] = near
            rows_in[EDGE + rows + HALO : EDGE + rows + 2 * HALO, :] = far
    turned = rows_in[...].T
    values = [turned[STRIP * f : STRIP * (f + 1)] for f in range(FORWARD)]
    state[...] = jnp.zeros(state.shape, F32)
    for f in range(5):
        state[f, 0, PAD : PAD + STRIP, :] = values[f]
    buoyancy, lame, shear = (NEAR * value for value in values[5:])
    for k, value in enumerate((buoyancy, lame + 2.0 * shear, lame, shear)):
        media[k, 0] = value
        media_out[k] = value
    rates_out[...] = strip_steps(state, media)[0]


def gradient_kernel(sums, rates, media, base, strains, gradients_out, state):
    rows = base.shape[1]
    near = jnp.concatenate([rates[8 * t : 8 * t + 4, :] for t in range(MOMENTS)], axis=0)
    lane = lane_ids(IMAGE)
    reached = (lane >= BASE) & (lane < EDGE + rows + HALO) & (lax.axis_index("depth") == 0)
    found = jnp.where(reached, sums[IMAGE:, :] * near - sums[:IMAGE, :], 0.0)
    nothing = jnp.zeros((8 - FIBRE_ROWS, LANES), F32)
    sources = [
        jnp.concatenate([found[FIBRE_ROWS * t : FIBRE_ROWS * (t + 1)], nothing], axis=0) for t in range(MOMENTS)
    ]
    added = response(state, media, sources, strains)
    added = jnp.concatenate(added + [jnp.zeros((LANES - 32, LANES), F32)], axis=0).T[EDGE : EDGE + rows]
    lane = lane_ids(rows)
    for k in range(2):
        more = jnp.where(lane < STRIP, turn(added, -STRIP * k), 0.0)
        gradients_out[k, :, :LANES] = (NEAR * NEAR) * (base[k, :, :LANES] + more)
        gradients_out[k, :, LANES:] = (NEAR * NEAR) * base[k, :, LANES:]


def residual_kernel(
    tracks, columns, notes, beside, obs, cells, gradients,
    residual_out, lambda_out, mu_out, state, media, low, high, sems,
):
    copies = fetch((gradients.at[0], gradients.at[1]), (lambda_out, mu_out), sems)
    depth = lax.axis_index("depth")
    low[...] = jnp.where(depth == 0, notes[...], beside[...])
    high[...] = jnp.where(depth == 0, beside[...], notes[...])
    along, row = cells[0], cells[1]
    channels = along.shape[1]
    rate = recorded_rates(state, media, low, high, along, tracks, columns)
    mask = row_ids(8, channels) == row
    traces = [
        jnp.sum(jnp.where(mask, rate[8 * t : 8 * t + 8], 0.0), axis=0, keepdims=True) - obs[t : t + 1, :]
        for t in range(MOMENTS)
    ]
    residual_out[...] = jnp.where(
        depth == 0, jnp.concatenate(traces[:2], axis=0), jnp.concatenate(traces[2:], axis=0)
    )
    for copy in copies:
        copy.wait()


def adjoint_kernel(
    held, got_even, got_odd, got_depth, corner, media, saved, inner_media, inner_saved, end,
    base_out, strains_out, end_out, state, sums, sems,
):
    (copy,) = fetch((end,), (end_out,), sems)
    states, totals = each(state, 3, 1), each(sums, 3, 1)
    rows = held.shape[1]
    load_state(states, FORWARD, (0, 1, 2), held, got_even, got_odd, got_depth, corner)
    medias = each(media, 2, 1) + each(inner_media, 1, 1)
    saveds = each(saved, 2, 2) + each(inner_saved, 1, 2)
    sums[...] = jnp.zeros(sums.shape, F32)
    for step in range(MOMENTS):
        fast, slow = spans(step, rows)
        moment = MOMENTS - 1 - step
        velocities(states, medias, fast)

        def gather(i, r, exx, ezz, shear):
            if 0 <= r < rows:
                fxx, fzz, fxz = (saveds[i][moment, k, r : r + 8, :] for k in range(3))
                totals[i][0, r : r + 8, :] += (fxx + fzz) * (exx + ezz)
                totals[i][1, r : r + 8, :] += 2.0 * (fxx * exx + fzz * ezz) + fxz * shear

        stresses(states, medias, slow, step < MOMENTS - 1, gather)
    for k in range(2):
        first, last = joined(*(total[k] for total in totals))
        base_out[k, :, :LANES] = first
        base_out[k, :, LANES:] = last
    lane = lane_ids(rows)
    for group in range(2):
        packed = jnp.zeros((rows, LANES), F32)
        for j in range(8 * group, min(8 * group + 8, 3 * MOMENTS)):
            spot = STRIP * (j % 8)
            here = (lane >= spot) & (lane < spot + STRIP)
            packed = jnp.where(here, turn(saveds[0][j // 3, j % 3], spot - EDGE), packed)
        turned = packed.T
        strains_out[group] = turn(jnp.concatenate([turned, jnp.zeros_like(turned)], axis=1), EDGE)
    copy.wait()


def per_device(
    velocity,
    stress,
    adjoint_velocity,
    adjoint_stress,
    buoyancy,
    lame_lambda,
    shear_modulus,
    observed,
    owner_track,
    fibre_cell,
):
    tracks = lax.axis_size("track")
    rows, depth_cells = buoyancy.shape
    moments, channels = observed.shape
    owner = owner_track.reshape(1, channels)
    cell = fibre_cell.reshape(1, channels)
    pinned = lambda array: pltpu.with_memory_space_constraint(array, pltpu.HBM)
    arrays = (velocity, stress, adjoint_velocity, adjoint_stress, buoyancy, lame_lambda, shear_modulus)
    arrays = tuple(pinned(array) for array in arrays)
    channel_arrays = (pinned(observed), pinned(owner), pinned(cell))
    extent = rows + 2 * EDGE
    block = jax.ShapeDtypeStruct((rows, depth_cells), F32)
    edges = jax.ShapeDtypeStruct((EXTRA + EDGE, depth_cells), F32)
    inside = pl.BlockSpec(memory_space=VMEM)
    outside = pl.BlockSpec(memory_space=pltpu.HBM)
    anywhere = pl.BlockSpec(memory_space=pl.ANY)
    held, held_adj, to_depth, to_even, to_odd, strip, traces, cells, strip_rows = pl.pallas_call(
        pack_kernel,
        out_shape=(
            jax.ShapeDtypeStruct((FORWARD, rows, depth_cells), F32),
            jax.ShapeDtypeStruct((ADJOINT, rows, depth_cells), F32),
            jax.ShapeDtypeStruct((rows + STRIP, depth_cells), F32),
            edges,
            edges,
            jax.ShapeDtypeStruct((2 * STRIP, LANES), F32),
            jax.ShapeDtypeStruct((moments, channels), F32),
            jax.ShapeDtypeStruct((2, 1, channels), jnp.int32),
            jax.ShapeDtypeStruct((rows, LANES), F32),
        ),
        in_specs=[outside] * 10,
        out_specs=(inside,) * 9,
        scratch_shapes=[VMEM((2, 1, channels), jnp.int32), pltpu.SemaphoreType.DMA((10,))],
        compiler_params=params(),
        cost_estimate=cost(5),
        name="pack",
    )(*arrays, *channel_arrays)
    depth_swap = [(0, 1), (1, 0)]
    got_depth = lax.ppermute(to_depth, "depth", depth_swap)
    swap = lambda k: [pair for i in range(k, tracks - 1, 2) for pair in ((i, i + 1), (i + 1, i))]
    got_odd = lax.ppermute(to_odd, "track", swap(1))
    got_even = lax.ppermute(to_even, "track", swap(0))

    def state_of(planes):
        return VMEM((5, planes, extent + 2 * PAD, LANES), F32)

    note = pl.pallas_call(
        note_kernel,
        out_shape=jax.ShapeDtypeStruct((tracks, 2 * STRIP + 8, LANES), F32),
        in_specs=[inside] * 4,
        out_specs=inside,
        compiler_params=params(),
        cost_estimate=cost(20),
        name="note",
    )(strip, got_depth, traces, cells)
    notes = lax.all_to_all(note, "track", split_axis=0, concat_axis=0, tiled=True)

    corner = pl.pallas_call(
        corner_kernel,
        out_shape=jax.ShapeDtypeStruct((2 * EDGE, depth_cells), F32),
        in_specs=[inside] * 2,
        out_specs=inside,
        compiler_params=params(),
        cost_estimate=cost(1),
        name="corners",
    )(got_even, got_odd)
    got_corner = lax.ppermute(corner, "depth", depth_swap)

    def media_of(planes):
        return jax.ShapeDtypeStruct((4, planes, extent, LANES), F32)

    def saved_of(planes):
        return jax.ShapeDtypeStruct((moments, 3, planes, rows, LANES), F32)

    media, saved, end = pl.pallas_call(
        forward_kernel,
        out_shape=(media_of(2), saved_of(2), jax.ShapeDtypeStruct((2, 2, rows, LANES), F32)),
        in_specs=[inside] * 3,
        out_specs=(inside,) * 3,
        scratch_shapes=[state_of(2)],
        compiler_params=params(),
        cost_estimate=cost(20),
        name="forward",
    )(held, got_even, got_odd)

    inner_media, inner_saved, end = pl.pallas_call(
        forward_inner_kernel,
        out_shape=(media_of(1), saved_of(1), jax.ShapeDtypeStruct(velocity.shape, F32)),
        in_specs=[inside] * 6,
        out_specs=(inside,) * 3,
        scratch_shapes=[state_of(1)],
        compiler_params=params(),
        cost_estimate=cost(20),
        name="forward_inner",
    )(held, got_even, got_odd, got_depth, got_corner, end)

    base, strains, velocity_end = pl.pallas_call(
        adjoint_kernel,
        out_shape=(
            jax.ShapeDtypeStruct((2, rows, depth_cells), F32),
            jax.ShapeDtypeStruct((2, LANES, LANES), F32),
            jax.ShapeDtypeStruct(velocity.shape, F32),
        ),
        in_specs=[inside] * 10,
        out_specs=(inside, inside, outside),
        scratch_shapes=[state_of(3), VMEM((2, 3, rows, LANES), F32), pltpu.SemaphoreType.DMA((1,))],
        compiler_params=params(),
        cost_estimate=cost(20),
        name="adjoint",
    )(held_adj, got_even, got_odd, got_depth, got_corner, media, saved, inner_media, inner_saved, end)

    rates, own_media = pl.pallas_call(
        fibre_kernel,
        out_shape=(
            jax.ShapeDtypeStruct((8 * MOMENTS, LANES), F32),
            jax.ShapeDtypeStruct((4, STRIP, LANES), F32),
        ),
        in_specs=[inside] * 3,
        out_specs=(inside,) * 2,
        scratch_shapes=[
            VMEM((5, 1, 2 * PAD + STRIP, LANES), F32),
            VMEM((4, 1, STRIP, LANES), F32),
            VMEM((LANES, LANES), F32),
        ],
        compiler_params=params(),
        cost_estimate=cost(5),
        name="fibre",
    )(strip_rows, got_even, got_odd)

    mine = pl.pallas_call(
        relay_kernel,
        out_shape=jax.ShapeDtypeStruct(note.shape, F32),
        in_specs=[inside, anywhere, anywhere],
        out_specs=inside,
        compiler_params=params(),
        cost_estimate=cost(1),
        name="relay",
    )(notes, base, rates)
    beside = lax.ppermute(mine, "depth", depth_swap)

    sums = pl.pallas_call(
        lambda *refs: sums_kernel(tracks, rows, *refs),
        out_shape=jax.ShapeDtypeStruct((2 * IMAGE, LANES), F32),
        in_specs=[inside],
        out_specs=inside,
        compiler_params=params(),
        cost_estimate=cost(2),
        name="sums",
    )(mine)

    gradients = pl.pallas_call(
        gradient_kernel,
        out_shape=jax.ShapeDtypeStruct((2, rows, depth_cells), F32),
        in_specs=[inside] * 5,
        out_specs=inside,
        scratch_shapes=[VMEM((5, 2 * PAD + STRIP, LANES), F32)],
        compiler_params=params(),
        cost_estimate=cost(2),
        name="gradient",
    )(sums, rates, own_media, base, strains)

    residual, gradient_lambda, gradient_mu = pl.pallas_call(
        lambda *refs: residual_kernel(tracks, rows, *refs),
        out_shape=(
            jax.ShapeDtypeStruct((moments // 2, channels), F32),
            block,
            block,
        ),
        in_specs=[inside] * 5,
        out_specs=(inside, outside, outside),
        scratch_shapes=[
            VMEM((5, BATCH, 2 * PAD + STRIP, LANES), F32),
            VMEM((4, BATCH, STRIP, LANES), F32),
            VMEM(note.shape, F32),
            VMEM(note.shape, F32),
            pltpu.SemaphoreType.DMA((2,)),
        ],
        compiler_params=params(),
        cost_estimate=cost(2),
        name="residual",
    )(mine, beside, traces, cells, gradients)
    return gradient_lambda, gradient_mu, velocity_end, residual


def solution(mesh):
    return jax.shard_map(
        per_device,
        mesh=mesh,
        in_specs=(
            P("shots", "track", "depth"),
            P("shots", "track", "depth"),
            P("shots", "track", "depth"),
            P("shots", "track", "depth"),
            P("track", "depth"),
            P("track", "depth"),
            P("track", "depth"),
            P("shots", "track"),
            P("track", None),
            P("track"),
        ),
        out_specs=(
            P(("shots", "track"), "depth"),
            P(("shots", "track"), "depth"),
            P("shots", "track", "depth"),
            P(("shots", "depth"), "track"),
        ),
        check_vma=False,
    )
```

```python
import jax
import jax.numpy as jnp
from jax import lax
from jax.experimental import pallas as pl
from jax.experimental.pallas import tpu as pltpu
from jax.sharding import PartitionSpec as P

FIBRE_ROWS = 4
NEAR = 9.0 / 8.0
RATIO = -1.0 / 27.0
HALO = 12
EDGE = 16
LANES = 128
PAD = 8
FORWARD = 8
ADJOINT = 5
FIELDS = FORWARD + ADJOINT
STRIP = 16
CELL_ROWS = (14, 15, 30, 31)
EXTRA = 168
BASE = EDGE - HALO
MOMENTS = 4
IMAGE = MOMENTS * FIBRE_ROWS
VMEM = pltpu.VMEM
F32 = jnp.float32
BF16 = jnp.bfloat16


def lane_ids(rows):
    return lax.broadcasted_iota(jnp.int32, (rows, LANES), 1)


def row_ids(rows, columns):
    return lax.broadcasted_iota(jnp.int32, (rows, columns), 0)


def params():
    return pltpu.CompilerParams(vmem_limit_bytes=16 * 1024 * 1024)


def cost(microseconds):
    return pl.CostEstimate(flops=int(microseconds * 1e9), bytes_accessed=1 << 20, transcendentals=0)


def turn(value, by):
    return pltpu.roll(value, by % LANES, 1)


def is_even():
    return lax.rem(lax.axis_index("track"), 2) == 0


def fetch(sources, targets, sems):
    copies = [pltpu.make_async_copy(s, t, sems.at[i]) for i, (s, t) in enumerate(zip(sources, targets))]
    for copy in copies:
        copy.start()
    return copies


def pack_kernel(*refs):
    sources, channel_arrays = refs[:7], refs[7:10]
    held, held_adj, depth_out, edge_outs, strip_out, traces_out, cells_out = *refs[10:13], refs[13:15], *refs[15:18]
    rows_out, numbers, sems = refs[18:]
    targets = (
        held.at[pl.ds(0, 2)],
        held.at[pl.ds(2, 3)],
        held.at[5],
        held.at[6],
        held.at[7],
        held_adj.at[pl.ds(0, 2)],
        held_adj.at[pl.ds(2, 3)],
        traces_out,
        numbers.at[0],
        numbers.at[1],
    )
    copies = fetch((*sources[:2], *sources[4:], *sources[2:4], *channel_arrays), targets, sems)
    depth = lax.axis_index("depth")
    even = is_even()
    rows = held.shape[1]
    lane = lane_ids(rows)
    tail = BASE + HALO * FIELDS
    for out in edge_outs:
        out[:BASE, :] = jnp.zeros((BASE, 2 * LANES), F32)
        out[tail:, :] = jnp.zeros((out.shape[0] - tail, 2 * LANES), F32)
    for copy in copies:
        copy.wait()
    packed = [jnp.zeros((rows, LANES), F32) for _ in range(2)]
    strip = jnp.zeros((rows, LANES), F32)
    for f in range(FIELDS):
        ref = held.at[f] if f < FORWARD else held_adj.at[f - FORWARD]
        first, last = ref[:, :LANES], ref[:, LANES:]
        group, place = divmod(f, FORWARD)
        spot = EDGE * place
        here = (lane >= spot) & (lane < spot + EDGE)
        edge = jnp.where(depth == 0, last, first)
        shift = lax.rem(spot + EDGE * (1 - depth), LANES)
        packed[group] = jnp.where(here, pltpu.roll(edge, shift, 1), packed[group])
        if f < FORWARD:
            strip = jnp.where(here, turn(first, spot), strip)
        low, high = ref[:HALO, :], ref[rows - HALO :, :]
        at = BASE + HALO * f
        edge_outs[0][at : at + HALO, :] = jnp.where(even, high, low)
        edge_outs[1][at : at + HALO, :] = jnp.where(even, low, high)
    depth_out[:rows, :LANES] = packed[0]
    depth_out[:rows, LANES:] = packed[1]
    rows_out[...] = strip
    low, high = strip[HALO : 2 * HALO], strip[rows - 2 * HALO : rows - HALO]
    edge_outs[0][EXTRA : EXTRA + HALO, :LANES] = jnp.where(even, high, low)
    edge_outs[1][EXTRA : EXTRA + HALO, :LANES] = jnp.where(even, low, high)
    turned = strip.T
    strip_out[:, :rows] = turned[: 2 * STRIP]
    strip_out[:, rows:] = turned[2 * STRIP : 4 * STRIP]
    depth_out[rows:, :rows] = turned[4 * STRIP : 5 * STRIP]
    depth_out[rows:, rows : 2 * rows] = turned[6 * STRIP : 7 * STRIP]
    depth_out[rows:, 2 * rows : 3 * rows] = turned[5 * STRIP : 6 * STRIP]
    depth_out[rows:, 3 * rows :] = turned[7 * STRIP :]
    cells_out[0] = numbers[0] * rows + lax.shift_right_logical(numbers[1], 2)
    cells_out[1] = numbers[1] & 3


def edge_rows(f, side, got_even, got_odd):
    at = BASE + HALO * f
    span = slice(at - BASE, at + HALO) if side == 0 else slice(at, at + EDGE)
    use_odd = is_even() if side == 0 else ~is_even()
    return jnp.where(use_odd, got_odd[span, :], got_even[span, :])


def corner_kernel(got_even, got_odd, corner_out):
    depth = lax.axis_index("depth")
    lane = lane_ids(EDGE)
    for side in range(2):
        packed = [jnp.zeros((EDGE, LANES), F32) for _ in range(2)]
        for f in range(FIELDS):
            group, place = divmod(f, FORWARD)
            spot = EDGE * place
            value = edge_rows(f, side, got_even, got_odd)
            edge = jnp.where(depth == 0, value[:, LANES:], value[:, :LANES])
            shift = lax.rem(spot + EDGE * (1 - depth), LANES)
            here = (lane >= spot) & (lane < spot + EDGE)
            packed[group] = jnp.where(here, pltpu.roll(edge, shift, 1), packed[group])
        corner_out[EDGE * side : EDGE * (side + 1), :LANES] = packed[0]
        corner_out[EDGE * side : EDGE * (side + 1), LANES:] = packed[1]


def window(plane, f, value, halo):
    depth = lax.axis_index("depth")
    surface = depth == 0
    first, last = value[:, :LANES], value[:, LANES:]
    lane = lane_ids(first.shape[0])
    low = jnp.where(surface, lane, LANES - 1 - lane)
    if plane == 0:
        shift = jnp.where(surface, EDGE, LANES - EDGE)
        return jnp.where(low >= EDGE, pltpu.roll(jnp.where(surface, first, last), shift, 1), 0.0)
    if plane == 1:
        return jnp.where(lane < LANES // 2, turn(first, LANES // 2), turn(last, LANES // 2))
    shift = jnp.where(surface, LANES - EDGE, EDGE)
    beside = lax.rem(LANES - EDGE * (f % FORWARD) + (LANES - EDGE) * (1 - depth), LANES)
    own = pltpu.roll(jnp.where(surface, last, first), shift, 1)
    return jnp.where(low < LANES - EDGE, own, pltpu.roll(halo, beside, 1))


def field_windows(f, planes, held, got_even, got_odd, got_depth=None, corner=None):
    rows = held.shape[1]
    col = LANES * (f // FORWARD)
    blocks = (
        (0, edge_rows(f, 0, got_even, got_odd), corner, 0),
        (EDGE, held[f % FORWARD], got_depth, 0),
        (EDGE + rows, edge_rows(f, 1, got_even, got_odd), corner, EDGE),
    )
    found = [[] for _ in planes]
    for at, value, halo, start in blocks:
        if halo is not None:
            halo = halo[start : start + value.shape[0], col : col + LANES]
        for parts, p in zip(found, planes):
            parts.append((at, window(p, f, value, halo)))
    return found


def joined(outer, middle, inner):
    surface = lax.axis_index("depth") == 0
    lane = lane_ids(outer.shape[0])
    first, last = jnp.where(surface, outer, inner), jnp.where(surface, inner, outer)
    middle = turn(middle, LANES // 2)
    return jnp.where(lane < 88, turn(first, -EDGE), middle), jnp.where(lane < 40, middle, turn(last, EDGE))


def load_state(states, base, planes, held, *got):
    extent = held.shape[1] + 2 * EDGE
    for f in range(5):
        for state, parts in zip(states, field_windows(base + f, planes, held, *got)):
            state[f, :PAD, :] = jnp.zeros((PAD, LANES), F32)
            state[f, PAD + extent :, :] = jnp.zeros((PAD, LANES), F32)
            for at, part in parts:
                state[f, PAD + at : PAD + at + part.shape[0], :] = part


def velocities(states, medias, span):
    for r in range(8 * span[0], 8 * span[1], 8):
        for state, media in zip(states, medias):

            def at(f, by=0):
                return state[f, r + PAD + by : r + PAD + by + 8, :]

            xx, xz, zz = at(2), at(4), at(3)
            b = media[0, r : r + 8, :]
            near = (xx - at(2, -1)) + (xz - turn(xz, 1))
            far = (at(2, 1) - at(2, -2)) + (turn(xz, -1) - turn(xz, 2))
            state[0, r + PAD : r + PAD + 8, :] = at(0) + b * (near + RATIO * far)
            near = (at(4, 1) - xz) + (turn(zz, -1) - zz)
            far = (at(4, 2) - at(4, -1)) + (turn(zz, -2) - turn(zz, 1))
            state[1, r + PAD : r + PAD + 8, :] = at(1) + b * (near + RATIO * far)


def stresses(states, medias, span, update, keep):
    for r in range(8 * span[0], 8 * span[1], 8):
        for i, (state, media) in enumerate(zip(states, medias)):

            def at(f, by=0):
                return state[f, r + PAD + by : r + PAD + by + 8, :]

            vx, vz = at(0), at(1)
            exx = (at(0, 1) - vx) + RATIO * (at(0, 2) - at(0, -1))
            ezz = (vz - turn(vz, 1)) + RATIO * (turn(vz, -1) - turn(vz, 2))
            near = (turn(vx, -1) - vx) + (vz - at(1, -1))
            far = (turn(vx, -2) - turn(vx, 1)) + (at(1, 1) - at(1, -2))
            shear = near + RATIO * far
            keep(i, r - EDGE, exx, ezz, shear)
            if update:
                whole, lam, mu = (media[k, r : r + 8, :] for k in (1, 2, 3))
                state[2, r + PAD : r + PAD + 8, :] = at(2) + (whole * exx + lam * ezz)
                state[3, r + PAD : r + PAD + 8, :] = at(3) + (lam * exx + whole * ezz)
                state[4, r + PAD : r + PAD + 8, :] = at(4) + mu * shear


def spans(step, rows):
    tiles = (rows + 2 * EDGE) // 8
    if step == 0:
        return (0, tiles), (0, tiles)
    inner = (1, tiles - 1)
    return inner, inner if step < MOMENTS - 1 else (EDGE // 8, tiles - EDGE // 8)


def run_forward(states, medias, saveds, planes, held, *got):
    rows = held.shape[1]
    given = [field_windows(f, planes, held, *got) for f in (5, 6, 7)]
    for i, media in enumerate(medias):
        for k in range(3):
            at = given[0][i][k][0]
            b, lam, mu = (NEAR * given[m][i][k][1] for m in range(3))
            span = slice(at, at + b.shape[0])
            media[0, span, :] = b
            media[1, span, :] = lam + 2.0 * mu
            media[2, span, :] = lam
            media[3, span, :] = mu
    load_state(states, 0, planes, held, *got)
    for step in range(MOMENTS):
        fast, slow = spans(step, rows)
        velocities(states, medias, fast)

        def save(i, r, exx, ezz, shear):
            if 0 <= r < rows:
                saveds[i][step, 0, r : r + 8, :] = exx
                saveds[i][step, 1, r : r + 8, :] = ezz
                saveds[i][step, 2, r : r + 8, :] = shear

        stresses(states, medias, slow, step < MOMENTS - 1, save)


def each(ref, count, axis):
    return [ref.at[(slice(None),) * axis + (i,)] for i in range(count)]


def forward_kernel(held, got_even, got_odd, media, saved, end_out, state):
    states = each(state, 2, 1)
    run_forward(states, each(media, 2, 1), each(saved, 2, 2), (0, 1), held, got_even, got_odd)
    top, rows = PAD + EDGE, held.shape[1]
    for f in range(2):
        for i in range(2):
            end_out[f, i] = states[i][f, top : top + rows, :]


def forward_inner_kernel(held, got_even, got_odd, got_depth, corner, end, media, saved, end_out, state):
    states = each(state, 1, 1)
    run_forward(
        states, each(media, 1, 1), each(saved, 1, 2), (2,), held, got_even, got_odd, got_depth, corner
    )
    top, rows = PAD + EDGE, held.shape[1]
    for f in range(2):
        first, last = joined(end[f, 0], end[f, 1], states[0][f, top : top + rows, :])
        end_out[f, :, :LANES] = first
        end_out[f, :, LANES:] = last


def note_kernel(strip, got_depth, traces, cells, note_out):
    first = lax.axis_index("depth") == 0
    beside = got_depth[got_depth.shape[0] - STRIP :, :]
    beside = jnp.concatenate([beside[:, :LANES], beside[:, LANES:]], axis=0)
    seen = jnp.concatenate([traces[:, :LANES], traces[:, LANES:]], axis=0)
    value = jnp.where(first, strip[...], beside)
    row = row_ids(2 * STRIP, LANES)
    for i, place in enumerate(CELL_ROWS):
        cell = cells[i // 2][:, LANES * (i % 2) : LANES * (i % 2 + 1)].astype(F32)
        value = jnp.where((row == place) & first, cell, value)
    block = jnp.concatenate([value, seen], axis=0)
    for k in range(note_out.shape[0]):
        note_out[k] = block


def relay_kernel(notes, base, rates, notes_out):
    del base, rates
    notes_out[...] = notes[...]


def three(value):
    high = value.astype(BF16)
    rest = value - high.astype(F32)
    middle = rest.astype(BF16)
    low = (rest - middle.astype(F32)).astype(BF16)
    return [high, middle, low]


def add_up(value, count):
    return (value[2 * count : 3 * count] + value[count : 2 * count]) + value[:count]


BATCH = 5
OWN = LANES - 2 * HALO


def strip_window(f, low, high, base, offset, tracks, columns):
    lane = lane_ids(STRIP)
    part = lax.div(offset + lane, columns)
    spot = base * columns + offset + lane
    source, q = (low, high)[f // 4], f % 4
    value = jnp.zeros((STRIP, LANES), F32)
    for step in range(3):
        who = jnp.clip(base + step, 0, tracks - 1)
        block = source[who, STRIP * (q % 2) : STRIP * (q % 2 + 1), :]
        shift = (4 * LANES - offset + columns * step - columns * (q // 2)) % LANES
        value = jnp.where(part == step, pltpu.roll(block, shift, 1), value)
    return jnp.where((spot >= 0) & (spot < tracks * columns), value, 0.0)


def fill_strip(state, media, low, high, first, tracks, columns):
    state[...] = jnp.zeros(state.shape, F32)
    for w in range(BATCH):
        begin = (first + w) * OWN - HALO
        base = (begin + columns) // columns - 1
        offset = begin - base * columns
        values = [strip_window(f, low, high, base, offset, tracks, columns) for f in range(FORWARD)]
        for f in range(5):
            state[f, w, PAD : PAD + STRIP, :] = values[f]
        buoyancy, lame, shear = (NEAR * value for value in values[5:])
        media[0, w] = buoyancy
        media[1, w] = lame + 2.0 * shear
        media[2, w] = lame
        media[3, w] = shear


def strip_steps(state, media):
    def at(f, w, r, by=0):
        return state[f, w, PAD + r + by : PAD + r + by + 8, :]

    count = state.shape[1]
    strains = [[] for _ in range(count)]
    for moment in range(MOMENTS):
        last = moment == MOMENTS - 1
        for r in (0, 8) if moment < 2 else (0,):
            for w in range(count):
                here = slice(PAD + r, PAD + r + 8)
                xx, xz, zz = at(2, w, r), at(4, w, r), at(3, w, r)
                b = media[0, w, r : r + 8, :]
                near = (xx - turn(xx, 1)) + (xz - at(4, w, r, -1))
                far = (turn(xx, -1) - turn(xx, 2)) + (at(4, w, r, 1) - at(4, w, r, -2))
                state[0, w, here, :] = at(0, w, r) + b * (near + RATIO * far)
                if not last:
                    near = (turn(xz, -1) - xz) + (at(3, w, r, 1) - zz)
                    far = (turn(xz, -2) - turn(xz, 1)) + (at(3, w, r, 2) - at(3, w, r, -1))
                    state[1, w, here, :] = at(1, w, r) + b * (near + RATIO * far)
        for r in (0, 8) if moment < 1 else (0,):
            for w in range(count):
                here = slice(PAD + r, PAD + r + 8)
                vx, vz = at(0, w, r), at(1, w, r)
                exx = (turn(vx, -1) - vx) + RATIO * (turn(vx, -2) - turn(vx, 1))
                if r == 0:
                    strains[w].append(NEAR * exx)
                if not last:
                    ezz = (vz - at(1, w, r, -1)) + RATIO * (at(1, w, r, 1) - at(1, w, r, -2))
                    near = (at(0, w, r, 1) - vx) + (vz - turn(vz, 1))
                    far = (at(0, w, r, 2) - at(0, w, r, -1)) + (turn(vz, -1) - turn(vz, 2))
                    whole, lam, mu = (media[k, w, r : r + 8, :] for k in (1, 2, 3))
                    state[2, w, here, :] = at(2, w, r) + (whole * exx + lam * ezz)
                    state[3, w, here, :] = at(3, w, r) + (lam * exx + whole * ezz)
                    state[4, w, here, :] = at(4, w, r) + mu * (near + RATIO * far)
    return [jnp.concatenate(parts, axis=0) for parts in strains]


def recorded_rates(state, media, low, high, wanted, tracks, columns):
    lane = lane_ids(8 * MOMENTS)
    mine = (lane >= HALO) & (lane < HALO + OWN)

    def body(number, rate):
        first = number * BATCH
        fill_strip(state, media, low, high, first, tracks, columns)
        images = [three(jnp.where(mine, image, 0.0)) for image in strip_steps(state, media)]
        parts = [jnp.concatenate([image[i] for image in images], axis=1) for i in range(3)]
        spots = [
            (first + w) * OWN - HALO + row_ids(LANES, wanted.shape[1]) for w in range(BATCH)
        ]
        hot = (jnp.concatenate(spots, axis=0) == wanted).astype(F32).astype(BF16)
        return rate + jnp.dot(jnp.concatenate(parts, axis=0), hot, preferred_element_type=F32)

    rate = jnp.zeros((3 * 8 * MOMENTS, wanted.shape[1]), F32)
    batches = -(-(-(-tracks * columns // OWN)) // BATCH)
    rate = body(0, rate) if batches == 1 else lax.fori_loop(0, batches, body, rate)
    return add_up(rate, 8 * MOMENTS)


def window_sums(tracks, columns, notes, sums_out):
    start = lax.axis_index("track") * columns - EDGE
    group = min(8, tracks)
    row16 = row_ids(IMAGE, LANES)

    def body(number, image):
        weights, hots = [], []
        for k in range(group):
            who = number * group + k
            traces = notes[who, 2 * STRIP :, :]
            places = [notes[who, place : place + 1, :] for place in CELL_ROWS]
            for h in range(2):
                mask = (row16 & 3).astype(F32) == places[2 + h]
                seen = [traces[4 * h + t : 4 * h + t + 1] for t in range(MOMENTS)]
                value = jnp.where(
                    row16 < 8,
                    jnp.where(row16 < 4, seen[0], seen[1]),
                    jnp.where(row16 < 12, seen[2], seen[3]),
                )
                pieces = three(jnp.where(mask, value, 0.0)) + [mask.astype(F32).astype(BF16)]
                weights.append(jnp.concatenate(pieces, axis=0))
                spot = (start + row_ids(LANES, LANES)).astype(F32)
                hots.append((spot == places[h]).astype(F32).astype(BF16))
        return image + lax.dot_general(
            jnp.concatenate(weights, axis=1),
            jnp.concatenate(hots, axis=1),
            (((1,), (1,)), ((), ())),
            preferred_element_type=F32,
        )

    image = jnp.zeros((4 * IMAGE, LANES), F32)
    image = body(0, image) if tracks == group else lax.fori_loop(0, tracks // group, body, image)
    sums_out[:IMAGE, :] = add_up(image, IMAGE)
    sums_out[IMAGE:, :] = image[3 * IMAGE :]


def response(state, media, sources, strains):
    state[...] = jnp.zeros(state.shape, F32)
    tiles = (0, 8)
    sums = [[jnp.zeros((8, LANES), F32) for _ in tiles] for _ in range(2)]

    def at(f, r, by=0):
        return state[f, PAD + r + by : PAD + r + by + 8, :]

    def put(f, r, value):
        state[f, PAD + r : PAD + r + 8, :] = value

    for moment in reversed(range(MOMENTS)):
        put(2, 0, at(2, 0) + sources[moment])
        for r in tiles:
            xx, xz, zz = at(2, r), at(4, r), at(3, r)
            b = media[0, r : r + 8, :]
            near = (xx - turn(xx, 1)) + (xz - at(4, r, -1))
            far = (turn(xx, -1) - turn(xx, 2)) + (at(4, r, 1) - at(4, r, -2))
            put(0, r, at(0, r) + b * (near + RATIO * far))
            near = (turn(xz, -1) - xz) + (at(3, r, 1) - zz)
            far = (turn(xz, -2) - turn(xz, 1)) + (at(3, r, 2) - at(3, r, -1))
            put(1, r, at(1, r) + b * (near + RATIO * far))
        for i, r in enumerate(tiles):
            vx, vz = at(0, r), at(1, r)
            exx = (turn(vx, -1) - vx) + RATIO * (turn(vx, -2) - turn(vx, 1))
            ezz = (vz - at(1, r, -1)) + RATIO * (at(1, r, 1) - at(1, r, -2))
            near = (at(0, r, 1) - vx) + (vz - turn(vz, 1))
            far = (at(0, r, 2) - at(0, r, -1)) + (turn(vz, -1) - turn(vz, 2))
            shear = near + RATIO * far
            fxx, fzz, fxz = (
                strains[j // 8, STRIP * (j % 8) + r : STRIP * (j % 8) + r + 8, :]
                for j in range(3 * moment, 3 * moment + 3)
            )
            sums[0][i] += (fxx + fzz) * (exx + ezz)
            sums[1][i] += 2.0 * (fxx * exx + fzz * ezz) + fxz * shear
            if moment > 0:
                whole, lam, mu = (media[k, r : r + 8, :] for k in (1, 2, 3))
                put(2, r, at(2, r) + (whole * exx + lam * ezz))
                put(3, r, at(3, r) + (lam * exx + whole * ezz))
                put(4, r, at(4, r) + mu * shear)
    return sums[0] + sums[1]


def fibre_kernel(strip, got_even, got_odd, rates_out, media_out, state, media, rows_in):
    rows = strip.shape[0]
    rows_in[...] = jnp.zeros(rows_in.shape, F32)
    rows_in[EDGE : EDGE + rows, :] = strip[...]
    lane = lane_ids(HALO)
    for side in range(2):
        use_odd = is_even() if side == 0 else ~is_even()
        near = jnp.zeros((HALO, LANES), F32)
        for f in range(FORWARD):
            span = slice(BASE + HALO * f, BASE + HALO * (f + 1))
            value = jnp.where(use_odd, got_odd[span, :LANES], got_even[span, :LANES])
            here = (lane >= STRIP * f) & (lane < STRIP * (f + 1))
            near = jnp.where(here, turn(value, STRIP * f), near)
        span = slice(EXTRA, EXTRA + HALO)
        far = jnp.where(use_odd, got_odd[span, :LANES], got_even[span, :LANES])
        if side == 0:
            rows_in[BASE:EDGE, :] = near
            rows_in[:BASE, :] = far[HALO - BASE :]
            rows_in[LANES - (HALO - BASE) :, :] = far[: HALO - BASE]
        else:
            rows_in[EDGE + rows : EDGE + rows + HALO, :] = near
            rows_in[EDGE + rows + HALO : EDGE + rows + 2 * HALO, :] = far
    turned = rows_in[...].T
    values = [turned[STRIP * f : STRIP * (f + 1)] for f in range(FORWARD)]
    state[...] = jnp.zeros(state.shape, F32)
    for f in range(5):
        state[f, 0, PAD : PAD + STRIP, :] = values[f]
    buoyancy, lame, shear = (NEAR * value for value in values[5:])
    for k, value in enumerate((buoyancy, lame + 2.0 * shear, lame, shear)):
        media[k, 0] = value
        media_out[k] = value
    rates_out[...] = strip_steps(state, media)[0]


def gradient_kernel(tracks, columns, notes, rates, media, base, strains, gradients_out, state, sums):
    window_sums(tracks, columns, notes, sums)
    rows = base.shape[1]
    near = jnp.concatenate([rates[8 * t : 8 * t + 4, :] for t in range(MOMENTS)], axis=0)
    lane = lane_ids(IMAGE)
    reached = (lane >= BASE) & (lane < EDGE + rows + HALO) & (lax.axis_index("depth") == 0)
    found = jnp.where(reached, sums[IMAGE:, :] * near - sums[:IMAGE, :], 0.0)
    nothing = jnp.zeros((8 - FIBRE_ROWS, LANES), F32)
    sources = [
        jnp.concatenate([found[FIBRE_ROWS * t : FIBRE_ROWS * (t + 1)], nothing], axis=0) for t in range(MOMENTS)
    ]
    added = response(state, media, sources, strains)
    added = jnp.concatenate(added + [jnp.zeros((LANES - 32, LANES), F32)], axis=0).T[EDGE : EDGE + rows]
    lane = lane_ids(rows)
    for k in range(2):
        more = jnp.where(lane < STRIP, turn(added, -STRIP * k), 0.0)
        gradients_out[k, :, :LANES] = (NEAR * NEAR) * (base[k, :, :LANES] + more)
        gradients_out[k, :, LANES:] = (NEAR * NEAR) * base[k, :, LANES:]


def residual_kernel(
    tracks, columns, notes, beside, obs, cells, gradients, end,
    residual_out, lambda_out, mu_out, end_out, state, media, low, high, sems,
):
    copies = fetch((gradients.at[0], gradients.at[1], end), (lambda_out, mu_out, end_out), sems)
    depth = lax.axis_index("depth")
    low[...] = jnp.where(depth == 0, notes[...], beside[...])
    high[...] = jnp.where(depth == 0, beside[...], notes[...])
    along, row = cells[0], cells[1]
    channels = along.shape[1]
    rate = recorded_rates(state, media, low, high, along, tracks, columns)
    mask = row_ids(8, channels) == row
    traces = [
        jnp.sum(jnp.where(mask, rate[8 * t : 8 * t + 8], 0.0), axis=0, keepdims=True) - obs[t : t + 1, :]
        for t in range(MOMENTS)
    ]
    residual_out[...] = jnp.where(
        depth == 0, jnp.concatenate(traces[:2], axis=0), jnp.concatenate(traces[2:], axis=0)
    )
    for copy in copies:
        copy.wait()


def adjoint_kernel(
    held, got_even, got_odd, got_depth, corner, media, saved, inner_media, inner_saved,
    base_out, strains_out, state, sums,
):
    states, totals = each(state, 3, 1), each(sums, 3, 1)
    rows = held.shape[1]
    load_state(states, FORWARD, (0, 1, 2), held, got_even, got_odd, got_depth, corner)
    medias = each(media, 2, 1) + each(inner_media, 1, 1)
    saveds = each(saved, 2, 2) + each(inner_saved, 1, 2)
    sums[...] = jnp.zeros(sums.shape, F32)
    for step in range(MOMENTS):
        fast, slow = spans(step, rows)
        moment = MOMENTS - 1 - step
        velocities(states, medias, fast)

        def gather(i, r, exx, ezz, shear):
            if 0 <= r < rows:
                fxx, fzz, fxz = (saveds[i][moment, k, r : r + 8, :] for k in range(3))
                totals[i][0, r : r + 8, :] += (fxx + fzz) * (exx + ezz)
                totals[i][1, r : r + 8, :] += 2.0 * (fxx * exx + fzz * ezz) + fxz * shear

        stresses(states, medias, slow, step < MOMENTS - 1, gather)
    for k in range(2):
        first, last = joined(*(total[k] for total in totals))
        base_out[k, :, :LANES] = first
        base_out[k, :, LANES:] = last
    lane = lane_ids(rows)
    for group in range(2):
        packed = jnp.zeros((rows, LANES), F32)
        for j in range(8 * group, min(8 * group + 8, 3 * MOMENTS)):
            spot = STRIP * (j % 8)
            here = (lane >= spot) & (lane < spot + STRIP)
            packed = jnp.where(here, turn(saveds[0][j // 3, j % 3], spot - EDGE), packed)
        turned = packed.T
        strains_out[group] = turn(jnp.concatenate([turned, jnp.zeros_like(turned)], axis=1), EDGE)


def per_device(
    velocity,
    stress,
    adjoint_velocity,
    adjoint_stress,
    buoyancy,
    lame_lambda,
    shear_modulus,
    observed,
    owner_track,
    fibre_cell,
):
    tracks = lax.axis_size("track")
    rows, depth_cells = buoyancy.shape
    moments, channels = observed.shape
    owner = owner_track.reshape(1, channels)
    cell = fibre_cell.reshape(1, channels)
    pinned = lambda array: pltpu.with_memory_space_constraint(array, pltpu.HBM)
    arrays = (velocity, stress, adjoint_velocity, adjoint_stress, buoyancy, lame_lambda, shear_modulus)
    arrays = tuple(pinned(array) for array in arrays)
    channel_arrays = (pinned(observed), pinned(owner), pinned(cell))
    extent = rows + 2 * EDGE
    block = jax.ShapeDtypeStruct((rows, depth_cells), F32)
    edges = jax.ShapeDtypeStruct((EXTRA + EDGE, depth_cells), F32)
    inside = pl.BlockSpec(memory_space=VMEM)
    outside = pl.BlockSpec(memory_space=pltpu.HBM)
    anywhere = pl.BlockSpec(memory_space=pl.ANY)
    held, held_adj, to_depth, to_even, to_odd, strip, traces, cells, strip_rows = pl.pallas_call(
        pack_kernel,
        out_shape=(
            jax.ShapeDtypeStruct((FORWARD, rows, depth_cells), F32),
            jax.ShapeDtypeStruct((ADJOINT, rows, depth_cells), F32),
            jax.ShapeDtypeStruct((rows + STRIP, depth_cells), F32),
            edges,
            edges,
            jax.ShapeDtypeStruct((2 * STRIP, LANES), F32),
            jax.ShapeDtypeStruct((moments, channels), F32),
            jax.ShapeDtypeStruct((2, 1, channels), jnp.int32),
            jax.ShapeDtypeStruct((rows, LANES), F32),
        ),
        in_specs=[outside] * 10,
        out_specs=(inside,) * 9,
        scratch_shapes=[VMEM((2, 1, channels), jnp.int32), pltpu.SemaphoreType.DMA((10,))],
        compiler_params=params(),
        cost_estimate=cost(5),
        name="pack",
    )(*arrays, *channel_arrays)
    depth_swap = [(0, 1), (1, 0)]
    got_depth = lax.ppermute(to_depth, "depth", depth_swap)
    swap = lambda k: [pair for i in range(k, tracks - 1, 2) for pair in ((i, i + 1), (i + 1, i))]
    got_odd = lax.ppermute(to_odd, "track", swap(1))
    got_even = lax.ppermute(to_even, "track", swap(0))

    def state_of(planes):
        return VMEM((5, planes, extent + 2 * PAD, LANES), F32)

    note = pl.pallas_call(
        note_kernel,
        out_shape=jax.ShapeDtypeStruct((tracks, 2 * STRIP + 8, LANES), F32),
        in_specs=[inside] * 4,
        out_specs=inside,
        compiler_params=params(),
        cost_estimate=cost(20),
        name="note",
    )(strip, got_depth, traces, cells)
    notes = lax.all_to_all(note, "track", split_axis=0, concat_axis=0, tiled=True)

    corner = pl.pallas_call(
        corner_kernel,
        out_shape=jax.ShapeDtypeStruct((2 * EDGE, depth_cells), F32),
        in_specs=[inside] * 2,
        out_specs=inside,
        compiler_params=params(),
        cost_estimate=cost(1),
        name="corners",
    )(got_even, got_odd)
    got_corner = lax.ppermute(corner, "depth", depth_swap)

    def media_of(planes):
        return jax.ShapeDtypeStruct((4, planes, extent, LANES), F32)

    def saved_of(planes):
        return jax.ShapeDtypeStruct((moments, 3, planes, rows, LANES), F32)

    media, saved, end = pl.pallas_call(
        forward_kernel,
        out_shape=(media_of(2), saved_of(2), jax.ShapeDtypeStruct((2, 2, rows, LANES), F32)),
        in_specs=[inside] * 3,
        out_specs=(inside,) * 3,
        scratch_shapes=[state_of(2)],
        compiler_params=params(),
        cost_estimate=cost(20),
        name="forward",
    )(held, got_even, got_odd)

    inner_media, inner_saved, end = pl.pallas_call(
        forward_inner_kernel,
        out_shape=(media_of(1), saved_of(1), jax.ShapeDtypeStruct(velocity.shape, F32)),
        in_specs=[inside] * 6,
        out_specs=(inside,) * 3,
        scratch_shapes=[state_of(1)],
        compiler_params=params(),
        cost_estimate=cost(20),
        name="forward_inner",
    )(held, got_even, got_odd, got_depth, got_corner, end)

    base, strains = pl.pallas_call(
        adjoint_kernel,
        out_shape=(
            jax.ShapeDtypeStruct((2, rows, depth_cells), F32),
            jax.ShapeDtypeStruct((2, LANES, LANES), F32),
        ),
        in_specs=[inside] * 9,
        out_specs=(inside,) * 2,
        scratch_shapes=[state_of(3), VMEM((2, 3, rows, LANES), F32)],
        compiler_params=params(),
        cost_estimate=cost(20),
        name="adjoint",
    )(held_adj, got_even, got_odd, got_depth, got_corner, media, saved, inner_media, inner_saved)

    rates, own_media = pl.pallas_call(
        fibre_kernel,
        out_shape=(
            jax.ShapeDtypeStruct((8 * MOMENTS, LANES), F32),
            jax.ShapeDtypeStruct((4, STRIP, LANES), F32),
        ),
        in_specs=[inside] * 3,
        out_specs=(inside,) * 2,
        scratch_shapes=[
            VMEM((5, 1, 2 * PAD + STRIP, LANES), F32),
            VMEM((4, 1, STRIP, LANES), F32),
            VMEM((LANES, LANES), F32),
        ],
        compiler_params=params(),
        cost_estimate=cost(5),
        name="fibre",
    )(strip_rows, got_even, got_odd)

    mine = pl.pallas_call(
        relay_kernel,
        out_shape=jax.ShapeDtypeStruct(note.shape, F32),
        in_specs=[inside, anywhere, anywhere],
        out_specs=inside,
        compiler_params=params(),
        cost_estimate=cost(1),
        name="relay",
    )(notes, base, rates)
    beside = lax.ppermute(mine, "depth", depth_swap)

    gradients = pl.pallas_call(
        lambda *refs: gradient_kernel(tracks, rows, *refs),
        out_shape=jax.ShapeDtypeStruct((2, rows, depth_cells), F32),
        in_specs=[inside] * 5,
        out_specs=inside,
        scratch_shapes=[VMEM((5, 2 * PAD + STRIP, LANES), F32), VMEM((2 * IMAGE, LANES), F32)],
        compiler_params=params(),
        cost_estimate=cost(20),
        name="gradient",
    )(mine, rates, own_media, base, strains)

    residual, gradient_lambda, gradient_mu, velocity_end = pl.pallas_call(
        lambda *refs: residual_kernel(tracks, rows, *refs),
        out_shape=(
            jax.ShapeDtypeStruct((moments // 2, channels), F32),
            block,
            block,
            jax.ShapeDtypeStruct(velocity.shape, F32),
        ),
        in_specs=[inside] * 6,
        out_specs=(inside, outside, outside, outside),
        scratch_shapes=[
            VMEM((5, BATCH, 2 * PAD + STRIP, LANES), F32),
            VMEM((4, BATCH, STRIP, LANES), F32),
            VMEM(note.shape, F32),
            VMEM(note.shape, F32),
            pltpu.SemaphoreType.DMA((3,)),
        ],
        compiler_params=params(),
        cost_estimate=cost(2),
        name="residual",
    )(mine, beside, traces, cells, gradients, end)
    return gradient_lambda, gradient_mu, velocity_end, residual


def solution(mesh):
    return jax.shard_map(
        per_device,
        mesh=mesh,
        in_specs=(
            P("shots", "track", "depth"),
            P("shots", "track", "depth"),
            P("shots", "track", "depth"),
            P("shots", "track", "depth"),
            P("track", "depth"),
            P("track", "depth"),
            P("track", "depth"),
            P("shots", "track"),
            P("track", None),
            P("track"),
        ),
        out_specs=(
            P(("shots", "track"), "depth"),
            P(("shots", "track"), "depth"),
            P("shots", "track", "depth"),
            P(("shots", "depth"), "track"),
        ),
        check_vma=False,
    )
```
